32 devices in a mesh: line: 8 (over y, x, core), col: 4 (over z).
Axes of the slice: x: 2, y: 2, z: 4, core: 2. Of those that a mesh axis runs over, the one named last changes fastest.
Arguments:
- fields: float32 [4, 256, 32, 512], P(None, 'line', 'col'), may hold values from -4 to 4
- viscosity: float32 [256, 32, 512], P('line', 'col'), may hold values from 0.5 to 2
Outputs:
- updated: float32 [4, 256, 32, 512], P(None, 'line', 'col')
The draws below stay inside these ranges and needn't reach their ends.
All inputs are finite; a program needn't handle non-finite values.
Results may differ from the reference program's by a relative error of at most 0.0003.
Values sent between devices are 32-bit elements; how exact they have to be, the bound alone decides.
No kernel may reach another device: no remote copies, remote signals or barrier semaphores. Data moves between devices by JAX's collectives and lax.ppermute only.
A program may use at most 64 MiB of HBM per device.

```python
import math
import jax
import jax.numpy as jnp
from jax import lax

NX = 256
NY = 32
NZ = 512
STIFF = 3072


def draw_fields(key, part):
    shape = (4, NX, NY, NZ)
    rough_key, mode_key = jax.random.split(key)
    x_coord = (jnp.arange(NX, dtype=jnp.float32) + 0.5) / NX
    rough = jax.random.truncated_normal(rough_key, -2.5, 2.5, shape, jnp.float32)
    amounts = jax.random.uniform(mode_key, (3, 4, 1, NY, NZ), jnp.float32, -0.5, 0.5)
    first_mode = jnp.sin(math.pi * x_coord)[None, :, None, None]
    second_mode = jnp.sin(2.0 * math.pi * x_coord)[None, :, None, None]
    third_mode = jnp.sin(3.0 * math.pi * x_coord)[None, :, None, None]
    smooth = amounts[0] * first_mode + amounts[1] * second_mode + amounts[2] * third_mode
    return rough + smooth


def block_scale(rng, dims, cuts, smallest, top_value):
    def one(axis_at, shards_of):
        heights = jax.random.uniform(jax.random.fold_in(jax.random.fold_in(rng, 6), axis_at), (shards_of,), jnp.float32, smallest / len(cuts), top_value / len(cuts))
        return jnp.repeat(jnp.exp(heights), dims[axis_at] // shards_of).reshape((-1,) + (1,) * (len(dims) - axis_at - 1))

    level = one(*cuts[0])
    for cut in cuts[1:]:
        level = level * one(*cut)
    return level


def setup_inputs(seed: int = 0) -> dict:
    keys = jax.random.split(jax.random.key(seed), 3)
    return {
        "fields": draw_fields(jax.random.fold_in(keys[2], 71), 0),
        "viscosity": jnp.clip(jnp.exp(math.log(2.0) - 1.3862944 * jax.random.uniform(keys[1], (NX, NY, NZ), jnp.float32) ** block_scale(keys[1], (NX, NY, NZ), ((0, 8), (1, 4)), -0.2, 0.2)), 0.5, 2.0),
    }


THERMAL_RATIO = 0.8
CROSS_RATE = 0.2
ADVECTION = 0.25
BUOYANCY = 2.0


def neighbours(values, along, wrapped):
    length = values.shape[along]
    widths = [(0, 0)] * values.ndim
    widths[along] = (1, 1)
    if wrapped:
        padded = jnp.pad(values, widths, mode="wrap")
    else:
        padded = jnp.pad(values, widths, mode="constant")
    upper = lax.slice_in_dim(padded, 2, length + 2, axis=along)
    lower = lax.slice_in_dim(padded, 0, length, axis=along)
    return upper, lower


def thomas(sub_diag, diagonal, super_diag, source):
    initial = jnp.zeros(source.shape[1:], source.dtype)

    def forward(state, record):
        prev_upper, prev_source = state
        sub_row, diag_row, super_row, source_row = record
        divisor = diag_row - sub_row * prev_upper
        next_upper = super_row / divisor
        next_source = (source_row - sub_row * prev_source) / divisor
        return (next_upper, next_source), (next_upper, next_source)

    _, (uppers, sources) = lax.scan(forward, (initial, initial), (sub_diag, diagonal, super_diag, source))

    def backward(following, record):
        upper_row, source_row = record
        solved = source_row - upper_row * following
        return solved, solved

    _, solved = lax.scan(backward, initial, (uppers, sources), reverse=True)
    return solved


def reference(fields, viscosity):
    directions = ((0, False), (1, True), (2, False))
    face_list = []
    for along, wrapped in directions:
        visc_next, visc_prev = neighbours(viscosity, along, wrapped)
        face_list.append((0.5 * (viscosity + visc_next), 0.5 * (viscosity + visc_prev)))
    results = []
    for member in range(4):
        field = fields[member]
        weight = THERMAL_RATIO if member == 3 else 1.0
        diffusions = []
        centrals = []
        for along, wrapped in directions:
            field_next, field_prev = neighbours(field, along, wrapped)
            face_next, face_prev = face_list[along]
            diffusions.append(face_next * (field_next - field) - face_prev * (field - field_prev))
            centrals.append(0.5 * (field_next - field_prev))
        transport = fields[0] * centrals[0] + fields[1] * centrals[1] + fields[2] * centrals[2]
        source = field + weight * (CROSS_RATE * diffusions[1] + CROSS_RATE * diffusions[2]) - ADVECTION * transport
        if member == 2:
            source = source + BUOYANCY * fields[3]
        rate = STIFF * weight
        low_side = rate * face_list[0][1]
        high_side = rate * face_list[0][0]
        results.append(thomas(-low_side, 1.0 + low_side + high_side, -high_side, source))
    return jnp.stack(results)
```

```python
import functools

import jax
import jax.numpy as jnp
from jax import lax
from jax.experimental import pallas as pl
from jax.experimental.pallas import tpu as pltpu
from jax.sharding import PartitionSpec as P

STIFF = 3072
THERMAL_RATIO = 0.8
CROSS_RATE = 0.2
ADVECTION = 0.25
BUOYANCY = 2.0
SCALES = (1.0, THERMAL_RATIO)
KIND = (0, 0, 0, 1)

F32 = jnp.float32
VMEM = pltpu.VMEM
LIMIT = 24 * 1024 * 1024

G00, G0N, GNN = (0, 3), (1, 4), (2, 5)
V_FIRST, V_LAST, F_FIRST, F_LAST = 6, 7, 8, 12
PLANES = 16
R_, GA, GB, CA, CB = 0, 2, 4, 6, 10
JOINT = 14


def in_vmem(x):
    return pltpu.with_memory_space_constraint(x, VMEM)


def spec():
    return pl.BlockSpec(memory_space=VMEM)


def call(kernel, name, out_shapes, args, scratch=(), any_in=(), any_out=(), flops=0, moved=0):
    in_specs = []
    operands = []
    for i, x in enumerate(args):
        if i in any_in:
            in_specs.append(pl.BlockSpec(memory_space=pl.ANY))
            operands.append(x)
        else:
            in_specs.append(spec())
            operands.append(in_vmem(x))
    out_shape = []
    out_specs = []
    for i, s in enumerate(out_shapes):
        if i in any_out:
            out_shape.append(jax.ShapeDtypeStruct(s, F32))
            out_specs.append(pl.BlockSpec(memory_space=pl.ANY))
        else:
            out_shape.append(VMEM(s, F32))
            out_specs.append(spec())
    return pl.pallas_call(
        kernel,
        out_shape=out_shape,
        in_specs=in_specs,
        out_specs=out_specs,
        scratch_shapes=list(scratch),
        compiler_params=pltpu.CompilerParams(vmem_limit_bytes=LIMIT),
        cost_estimate=pl.CostEstimate(flops=flops, bytes_accessed=moved, transcendentals=0),
        name=name,
    )(*operands)


def first_kernel(rows, parts, fields_ref, visc_ref, fv, src, inv, cpr, g0, gn, w, tau, sems):
    ny, nz = fv.shape[2], fv.shape[3]
    step = rows // parts
    me = lax.axis_index("line")
    last = lax.axis_size("line") - 1
    copies = []
    for c in range(parts):
        lo = c * step
        one = pltpu.make_async_copy(
            fields_ref.at[:, lo : lo + step], fv.at[0:4, 1 + lo : 1 + lo + step], sems.at[0, c]
        )
        two = pltpu.make_async_copy(
            visc_ref.at[lo : lo + step], fv.at[4, 1 + lo : 1 + lo + step], sems.at[1, c]
        )
        one.start()
        two.start()
        copies.append((one, two))
    zero = jnp.zeros((ny, nz), F32)
    for k in range(5):
        fv[k, 0] = zero
        fv[k, rows + 1] = zero
    lane = lax.broadcasted_iota(jnp.int32, (ny, nz), 1)
    sub = lax.broadcasted_iota(jnp.int32, (ny, nz), 0)
    z_top, z_low = lane == nz - 1, lane == 0
    y_top, y_low = sub == ny - 1, sub == 0
    wall_low = jnp.where(me == 0, 1.0, 0.0).astype(F32)
    wall_high = jnp.where(me == last, 1.0, 0.0).astype(F32)

    def sides(x):
        yn = jnp.where(y_top, 0.0, pltpu.roll(x, ny - 1, 0))
        yp = jnp.where(y_low, 0.0, pltpu.roll(x, 1, 0))
        zn = jnp.where(z_top, 0.0, pltpu.roll(x, nz - 1, 1))
        zp = jnp.where(z_low, 0.0, pltpu.roll(x, 1, 1))
        return yn, yp, zn, zp

    def row(i, carry):
        f = [fv[k, i + 1] for k in range(4)]
        v = fv[4, i + 1]
        vyn, vyp, vzn, vzp = sides(v)
        half = 0.5 * CROSS_RATE
        face_yn = jnp.where(y_top, 0.0, half * (v + vyn))
        face_yp = jnp.where(y_low, 0.0, half * (v + vyp))
        face_zn = half * (v + vzn)
        face_zp = half * (v + vzp)
        adv = [(-0.5 * ADVECTION) * f[k] for k in range(3)]
        for k in range(4):
            yn, yp, zn, zp = sides(f[k])
            spread = (
                face_yn * (yn - f[k])
                - face_yp * (f[k] - yp)
                + face_zn * (zn - f[k])
                - face_zp * (f[k] - zp)
            )
            if KIND[k]:
                spread = THERMAL_RATIO * spread
            out = f[k] + spread
            out = out + adv[0] * (fv[k, i + 2] - fv[k, i])
            out = out + adv[1] * (yn - yp)
            out = out + adv[2] * (zn - zp)
            if k == 2:
                out = out + BUOYANCY * f[3]
            src[k, i] = out
        is_first = jnp.where(i == 0, wall_low, 1.0)
        is_last = jnp.where(i == rows - 1, wall_high, 1.0)
        low = (0.5 * STIFF) * is_first * (fv[4, i] + v)
        high = (0.5 * STIFF) * is_last * (v + fv[4, i + 2])
        new = []
        for s in range(2):
            gain, running = carry[2 * s], carry[2 * s + 1]
            q = 1.0 + (SCALES[s] * low) * gain
            up = SCALES[s] * high
            one_over = 1.0 / (q + up)
            coupling = up * one_over
            inv[s, i] = one_over
            cpr[s, i] = coupling
            tau[s, i] = running
            new += [q * one_over, coupling * running]
        return tuple(new)

    carry = (zero + 1.0,) * 4
    for part in copies[0]:
        part.wait()
    for c in range(parts):
        if c + 1 < parts:
            for part in copies[c + 1]:
                part.wait()
        carry = lax.fori_loop(c * step, (c + 1) * step, row, carry)

    end = rows - 1
    start = []
    for s in range(2):
        a = inv[s, end] * tau[s, end]
        b = inv[s, end]
        g0[s, end] = a
        gn[s, end] = b
        w[G0N[s]] = a
        w[GNN[s]] = b
        start += [a, b]

    def back(j, carry):
        i = end - 1 - j
        new = []
        for s in range(2):
            c = cpr[s, i]
            a = inv[s, i] * tau[s, i] + c * carry[2 * s]
            b = c * carry[2 * s + 1]
            g0[s, i] = a
            gn[s, i] = b
            new += [a, b]
        return tuple(new)

    final = lax.fori_loop(0, end, back, tuple(start))
    for s in range(2):
        w[G00[s]] = final[2 * s]
    w[V_FIRST] = fv[4, 1]
    w[V_LAST] = fv[4, rows]
    for k in range(4):
        w[F_FIRST + k] = fv[k, 1]
        w[F_LAST + k] = fv[k, rows]


def joint_kernel(level, halve, group, own, other, joint, *outs):
    bit = jnp.bitwise_and(jnp.right_shift(lax.axis_index("line"), level), 1)
    low_side = bit == 0

    def pick(plane):
        mine, theirs = own[plane], other[plane]
        return jnp.where(low_side, mine, theirs), jnp.where(low_side, theirs, mine)

    planes = {}
    for plane in range(PLANES):
        planes[plane] = pick(plane)
    left = {p: planes[p][0] for p in planes}
    right = {p: planes[p][1] for p in planes}
    face = left[V_LAST] + right[V_FIRST]
    ratio = []
    for s in range(2):
        resist = 1.0 / ((0.5 * STIFF * SCALES[s]) * face)
        r = 1.0 / (resist + left[GNN[s]] + right[G00[s]])
        ratio.append(r)
        joint[R_ + s] = r
        joint[GA + s] = left[G0N[s]]
        joint[GB + s] = right[G0N[s]]
    rate = 0.5 * ADVECTION
    for k in range(4):
        s = KIND[k]
        add_a = -rate * left[F_LAST] * right[F_FIRST + k]
        add_b = rate * right[F_FIRST] * left[F_LAST + k]
        e = ratio[s] * (left[GNN[s]] * add_a - right[G00[s]] * add_b)
        joint[CA + k] = add_a - e
        joint[CB + k] = add_b + e
    if group:
        out = outs[0]
        width = out.shape[2]
        new = {}
        for s in range(2):
            a, b, r = left[G0N[s]], right[G0N[s]], ratio[s]
            new[G00[s]] = left[G00[s]] - r * a * a
            new[GNN[s]] = right[GNN[s]] - r * b * b
            new[G0N[s]] = r * a * b
        new[V_FIRST] = left[V_FIRST]
        new[V_LAST] = right[V_LAST]
        for k in range(4):
            new[F_FIRST + k] = left[F_FIRST + k]
            new[F_LAST + k] = right[F_LAST + k]
        if halve:
            for plane in range(PLANES):
                x = new[plane]
                out[plane] = jnp.where(low_side, x[:, :width], x[:, width:])
        else:
            for plane in range(PLANES):
                out[plane] = new[plane]


def source_kernel(rows, fv, src, cpr, inv, g0, low, high, t, p):
    ny, nz = src.shape[2], src.shape[3]
    sub = lax.broadcasted_iota(jnp.int32, (ny, nz), 0)
    top, edge = sub == ny - 1, (sub == ny - 1) | (sub == 0)
    rate = 0.5 * ADVECTION
    sign = jnp.where(sub == 0, rate, jnp.where(top, -rate, 0.0)).astype(F32)
    weight = jnp.where(edge, 0.5 * CROSS_RATE, 0.0).astype(F32)

    def near(k, i):
        a = jnp.broadcast_to(high[k, pl.ds(i, 1), :], (ny, nz))
        b = jnp.broadcast_to(low[k, pl.ds(i, 1), :], (ny, nz))
        return jnp.where(top, a, b)

    def row(i, carry):
        v = fv[4, i + 1]
        face = weight * (v + near(4, i))
        adv = sign * fv[1, i + 1]
        prev = jnp.maximum(i - 1, 0)
        new = []
        for k in range(4):
            s = KIND[k]
            beside = near(k, i)
            part = face * (beside - fv[k, i + 1])
            if s:
                part = THERMAL_RATIO * part
            x = src[k, i] + part + adv * beside
            total = carry[2 * k + 1] + g0[s, i] * x
            x = x + cpr[s, prev] * carry[2 * k]
            t[k, i] = x
            new += [x, total]
        return tuple(new)

    zero = jnp.zeros((ny, nz), F32)
    final = lax.fori_loop(0, rows, row, (zero,) * 8)
    for k in range(4):
        p[k] = final[2 * k + 1]
        p[4 + k] = inv[KIND[k], rows - 1] * final[2 * k]


def back_kernel(rows, t, inv, cpr, part):
    end = rows - 1
    start = []
    for k in range(4):
        x = inv[KIND[k], end] * t[k, end]
        part[k, end] = x
        start.append(x)

    def row(j, carry):
        i = end - 1 - j
        new = []
        for k in range(4):
            s = KIND[k]
            x = inv[s, i] * t[k, i] + cpr[s, i] * carry[k]
            part[k, i] = x
            new.append(x)
        return tuple(new)

    lax.fori_loop(0, end, row, tuple(start))


def up_kernel(level, halve, own, other, joint, out, diff):
    bit = jnp.bitwise_and(jnp.right_shift(lax.axis_index("line"), level), 1)
    low_side = bit == 0
    width = out.shape[2]
    for k in range(4):
        s = KIND[k]
        far_left = jnp.where(low_side, own[k], other[k])
        far_right = jnp.where(low_side, other[4 + k], own[4 + k])
        d = jnp.where(low_side, own[4 + k] - other[k], other[4 + k] - own[k])
        diff[k] = d
        flow = joint[R_ + s] * d
        first = far_left + joint[GA + s] * (joint[CA + k] - flow)
        last = far_right + joint[GB + s] * (joint[CB + k] + flow)
        if halve:
            first = jnp.where(low_side, first[:, :width], first[:, width:])
            last = jnp.where(low_side, last[:, :width], last[:, width:])
        out[k] = first
        out[4 + k] = last


def joint_flow(joint, k, d, into_first, into_last, low_side):
    s = KIND[k]
    flow = joint[R_ + s] * (d + joint[GA + s] * into_first - joint[GB + s] * into_last)
    first = jnp.where(low_side, into_first, joint[CB + k] + flow)
    last = jnp.where(low_side, joint[CA + k] - flow, into_last)
    return first, last


def down_kernel(levels, own, other, *refs):
    joints = refs[: levels - 1]
    diffs = refs[levels - 1 : 2 * levels - 3]
    out = refs[2 * levels - 3]
    me = lax.axis_index("line")
    for k in range(4):
        low_side = jnp.bitwise_and(jnp.right_shift(me, levels - 1), 1) == 0
        d = jnp.where(low_side, own[4 + k] - other[k], other[4 + k] - own[k])
        first = last = jnp.zeros_like(d)
        first, last = joint_flow(joints[levels - 2], k, d, first, last, low_side)
        for level in range(levels - 2, 0, -1):
            low_side = jnp.bitwise_and(jnp.right_shift(me, level), 1) == 0
            first, last = joint_flow(
                joints[level - 1], k, diffs[level - 1][k], first, last, low_side
            )
        out[k] = first
        out[4 + k] = last


def final_kernel(rows, parts, own, other, joint, diff, part, g0, gn, out, flux, buf, sems):
    bit = jnp.bitwise_and(lax.axis_index("line"), 1)
    low_side = bit == 0
    width = own.shape[2]
    for k in range(8):
        flux[k, :, :width] = jnp.where(low_side, own[k], other[k])
        flux[k, :, width:] = jnp.where(low_side, other[k], own[k])
    for k in range(4):
        first, last = joint_flow(joint, k, diff[k], flux[k], flux[4 + k], low_side)
        flux[k] = first
        flux[4 + k] = last
    step = rows // parts
    copies = []
    for c in range(parts):

        def row(i, _):
            for k in range(4):
                s = KIND[k]
                buf[k, i] = part[k, i] + g0[s, i] * flux[k] + gn[s, i] * flux[4 + k]
            return 0

        lax.fori_loop(c * step, (c + 1) * step, row, 0)
        copy = pltpu.make_async_copy(
            buf.at[:, c * step : (c + 1) * step], out.at[:, c * step : (c + 1) * step], sems.at[c]
        )
        copy.start()
        copies.append(copy)
    for copy in copies:
        copy.wait()


def local(fields, viscosity):
    rows, ny, nz = viscosity.shape
    lines = lax.axis_size("line")
    cols = lax.axis_size("col")
    levels = lines.bit_length() - 1
    half = nz // 2
    cells = rows * ny * nz

    ring = [(i, (i + 1) % cols) for i in range(cols)]
    back_ring = [(b, a) for a, b in ring]
    y_first = jnp.concatenate([fields[:, :, 0], viscosity[None, :, 0]], axis=0)
    y_last = jnp.concatenate([fields[:, :, ny - 1], viscosity[None, :, ny - 1]], axis=0)
    high = lax.ppermute(y_first, "col", back_ring)
    low = lax.ppermute(y_last, "col", ring)

    def swap(x, level):
        return lax.ppermute(x, "line", [(i, i ^ (1 << level)) for i in range(lines)])

    parts = 4 if rows % 4 == 0 else 1
    block = (rows, ny, nz)
    fv, src, inv, cpr, g0, gn, w = call(
        functools.partial(first_kernel, rows, parts),
        "first",
        [(5, rows + 2, ny, nz), (4,) + block, (2,) + block, (2,) + block, (2,) + block, (2,) + block, (PLANES, ny, nz)],
        [fields, viscosity],
        scratch=[VMEM((2,) + block, F32), pltpu.SemaphoreType.DMA((2, parts))],
        any_in=(0, 1),
        flops=200 * cells,
        moved=24 * cells,
    )
    joints = []
    for level in range(levels):
        width = nz if level == 0 else half
        group = level < levels - 1
        outs = [(JOINT, ny, width)] + ([(PLANES, ny, half)] if group else [])
        got = call(
            functools.partial(joint_kernel, level, level == 0, group),
            f"joint{level}",
            outs,
            [w, swap(w, level)],
            moved=4 * ny * width * 60,
        )
        joints.append(got[0])
        if group:
            w = got[1]

    t, p = call(
        functools.partial(source_kernel, rows),
        "source",
        [(4,) + block, (8, ny, nz)],
        [fv, src, cpr, inv, g0, low, high],
        flops=60 * cells,
        moved=24 * cells,
    )
    (part,) = call(
        functools.partial(back_kernel, rows),
        "back",
        [(4,) + block],
        [t, inv, cpr],
        flops=20 * cells,
        moved=24 * cells,
    )
    diffs = []
    for level in range(levels - 1):
        width = nz if level == 0 else half
        p, diff = call(
            functools.partial(up_kernel, level, level == 0),
            f"up{level}",
            [(8, ny, half), (4, ny, width)],
            [p, swap(p, level), joints[level]],
            moved=4 * ny * width * 40,
        )
        diffs.append(diff)
    (flux,) = call(
        functools.partial(down_kernel, levels),
        "down",
        [(8, ny, half)],
        [p, swap(p, levels - 1)] + joints[1:] + diffs[1:],
        moved=4 * ny * half * 60,
    )
    (out,) = call(
        functools.partial(final_kernel, rows, parts),
        "final",
        [(4,) + block],
        [flux, swap(flux, 0), joints[0], diffs[0], part, g0, gn],
        scratch=[VMEM((8, ny, nz), F32), VMEM((4,) + block, F32), pltpu.SemaphoreType.DMA((parts,))],
        any_out=(0,),
        flops=16 * cells,
        moved=16 * cells,
    )
    return out


def solution(mesh):
    return jax.shard_map(
        local,
        mesh=mesh,
        in_specs=(P(None, "line", "col", None), P("line", "col", None)),
        out_specs=P(None, "line", "col", None),
        check_vma=False,
    )
```

```python
import functools

import jax
import jax.numpy as jnp
from jax import lax
from jax.experimental import pallas as pl
from jax.experimental.pallas import tpu as pltpu
from jax.sharding import PartitionSpec as P

STIFF = 3072
THERMAL_RATIO = 0.8
CROSS_RATE = 0.2
ADVECTION = 0.25
BUOYANCY = 2.0
SCALES = (1.0, THERMAL_RATIO)
KIND = (0, 0, 0, 1)

F32 = jnp.float32
VMEM = pltpu.VMEM
LIMIT = 24 * 1024 * 1024

G00, G0N, GNN = (0, 3), (1, 4), (2, 5)
V_FIRST, V_LAST, F_FIRST, F_LAST = 6, 7, 8, 12
PLANES = 16
R_, GA, GB, CA, CB = 0, 2, 4, 6, 10
JOINT = 14


def in_vmem(x):
    return pltpu.with_memory_space_constraint(x, VMEM)


def spec():
    return pl.BlockSpec(memory_space=VMEM)


def call(kernel, name, out_shapes, args, scratch=(), in_hbm=(), any_out=(), flops=0, moved=0):
    in_specs = []
    operands = []
    for i, x in enumerate(args):
        if i in in_hbm:
            in_specs.append(pl.BlockSpec(memory_space=pltpu.HBM))
            operands.append(pltpu.with_memory_space_constraint(x, pltpu.HBM))
        else:
            in_specs.append(spec())
            operands.append(in_vmem(x))
    out_shape = []
    out_specs = []
    for i, s in enumerate(out_shapes):
        if i in any_out:
            out_shape.append(jax.ShapeDtypeStruct(s, F32))
            out_specs.append(pl.BlockSpec(memory_space=pl.ANY))
        else:
            out_shape.append(VMEM(s, F32))
            out_specs.append(spec())
    return pl.pallas_call(
        kernel,
        out_shape=out_shape,
        in_specs=in_specs,
        out_specs=out_specs,
        scratch_shapes=list(scratch),
        compiler_params=pltpu.CompilerParams(vmem_limit_bytes=LIMIT),
        cost_estimate=pl.CostEstimate(flops=flops, bytes_accessed=moved, transcendentals=0),
        name=name,
    )(*operands)


def layer(read, ny, nz):
    sub = lax.broadcasted_iota(jnp.int32, (8, nz), 0)
    tile = jnp.broadcast_to(read(0), (8, nz))
    for r in range(1, 8):
        tile = jnp.where(sub == r, jnp.broadcast_to(read(r), (8, nz)), tile)
    return tile


def load_kernel(rows, parts, fields_ref, visc_ref, fv, y_first, y_last, sems):
    ny, nz = fv.shape[2], fv.shape[3]
    step = rows // parts
    copies = []
    for c in range(parts):
        lo = c * step
        one = pltpu.make_async_copy(
            fields_ref.at[:, lo : lo + step], fv.at[0:4, 1 + lo : 1 + lo + step], sems.at[0, c]
        )
        two = pltpu.make_async_copy(
            visc_ref.at[lo : lo + step], fv.at[4, 1 + lo : 1 + lo + step], sems.at[1, c]
        )
        one.start()
        two.start()
        copies.append((one, two))
    zero = jnp.zeros((ny, nz), F32)
    for k in range(5):
        fv[k, 0] = zero
        fv[k, rows + 1] = zero
    for c in range(parts):
        for part in copies[c]:
            part.wait()
        for lo in range(c * step, (c + 1) * step, 8):
            for k in range(5):
                for at, out in ((0, y_first), (ny - 1, y_last)):
                    out[k, lo : lo + 8] = layer(
                        lambda r: fv[k, 1 + lo + r, at : at + 1, :], ny, nz
                    )


def factor_kernel(rows, fv, inv, cpr, g0, gn, w, tau):
    ny, nz = fv.shape[2], fv.shape[3]
    me = lax.axis_index("line")
    wall_low = jnp.where(me == 0, 1.0, 0.0).astype(F32)
    wall_high = jnp.where(me == lax.axis_size("line") - 1, 1.0, 0.0).astype(F32)
    one = jnp.ones((ny, nz), F32)

    def row(i, carry):
        low, v = carry[4], carry[5]
        after = fv[4, i + 2]
        high = (0.5 * STIFF) * (v + after)
        high = jnp.where(i == rows - 1, wall_high, 1.0) * high
        new = []
        for s in range(2):
            gain, running = carry[2 * s], carry[2 * s + 1]
            down = SCALES[s] * low if s else low
            up = SCALES[s] * high if s else high
            q = 1.0 + down * gain
            one_over = 1.0 / (q + up)
            coupling = up * one_over
            inv[s, i] = one_over
            cpr[s, i] = coupling
            tau[s, i] = running
            new += [q * one_over, coupling * running]
        return tuple(new) + (high, after)

    first = fv[4, 1]
    lax.fori_loop(0, rows, row, (one,) * 4 + (wall_low * (0.5 * STIFF) * first, first))

    end = rows - 1
    start = []
    for s in range(2):
        a = inv[s, end] * tau[s, end]
        b = inv[s, end]
        g0[s, end] = a
        gn[s, end] = b
        w[G0N[s]] = a
        w[GNN[s]] = b
        start += [a, b]

    def back(j, carry):
        i = end - 1 - j
        new = []
        for s in range(2):
            c = cpr[s, i]
            a = inv[s, i] * tau[s, i] + c * carry[2 * s]
            b = c * carry[2 * s + 1]
            g0[s, i] = a
            gn[s, i] = b
            new += [a, b]
        return tuple(new)

    final = lax.fori_loop(0, end, back, tuple(start))
    for s in range(2):
        w[G00[s]] = final[2 * s]
    w[V_FIRST] = first
    w[V_LAST] = fv[4, rows]
    for k in range(4):
        w[F_FIRST + k] = fv[k, 1]
        w[F_LAST + k] = fv[k, rows]


def explicit_kernel(rows, fv, g0, gn, src, p, ends):
    ny, nz = fv.shape[2], fv.shape[3]
    lane = lax.broadcasted_iota(jnp.int32, (ny, nz), 1)
    sub = lax.broadcasted_iota(jnp.int32, (ny, nz), 0)
    z_top, z_low = lane == nz - 1, lane == 0
    y_top, y_low = sub == ny - 1, sub == 0

    def sides(x):
        return (
            pltpu.roll(x, ny - 1, 0),
            pltpu.roll(x, 1, 0),
            pltpu.roll(x, nz - 1, 1),
            pltpu.roll(x, 1, 1),
        )

    def row(i, _):
        f = [fv[k, i + 1] for k in range(4)]
        v = fv[4, i + 1]
        vyn, vyp, vzn, vzp = sides(v)
        half = 0.5 * CROSS_RATE
        faces = [
            jnp.where(y_top, 0.0, half * (v + vyn)),
            jnp.where(y_low, 0.0, half * (v + vyp)),
            half * (v + jnp.where(z_top, 0.0, vzn)),
            half * (v + jnp.where(z_low, 0.0, vzp)),
        ]
        none = [y_top, y_low, z_top, z_low]
        total = (faces[0] + faces[1]) + (faces[2] + faces[3])
        adv = [(-0.5 * ADVECTION) * f[k] for k in range(3)]
        move = [adv[1], -adv[1], adv[2], -adv[2]]
        weights, centre = [], []
        for s in range(2):
            scaled = [SCALES[s] * x if s else x for x in faces]
            weights.append([jnp.where(n, 0.0, x + m) for n, x, m in zip(none, scaled, move)])
            centre.append(1.0 - (SCALES[s] * total if s else total))
        for k in range(4):
            s = KIND[k]
            near = sides(f[k])
            out = centre[s] * f[k] + adv[0] * (fv[k, i + 2] - fv[k, i])
            for c, x in zip(weights[s], near):
                out = out + c * x
            if k == 2:
                out = out + BUOYANCY * f[3]
            src[k, i] = out
        return 0

    lax.fori_loop(0, rows, row, 0)

    def dot(i, carry):
        new = []
        for k in range(4):
            x = src[k, i]
            s = KIND[k]
            new.append(carry[k] + g0[s, i] * x)
        for k in range(4):
            x = src[k, i]
            s = KIND[k]
            new.append(carry[4 + k] + gn[s, i] * x)
        return tuple(new)

    zero = jnp.zeros((ny, nz), F32)
    final = lax.fori_loop(0, rows, dot, (zero,) * 8)
    for k in range(8):
        p[k] = final[k]

    for s in range(2):
        for side, at in ((0, 0), (1, ny - 1)):
            for which, g in ((0, g0), (1, gn)):
                for lo in range(0, rows, 8):
                    ends[4 * side + 2 * which + s, lo : lo + 8] = layer(
                        lambda r: g[s, lo + r, at : at + 1, :], ny, nz
                    )


def edge_kernel(rows, y_first, y_last, low, high, add):
    nz = add.shape[2]
    rate = 0.5 * ADVECTION
    for side, mine, far, sign in ((0, y_first, low, rate), (4, y_last, high, -rate)):
        for r in range(rows // 8):
            x = pl.ds(r * 8, 8)
            face = (0.5 * CROSS_RATE) * (mine[4, x] + far[4, x])
            faces = (face, THERMAL_RATIO * face)
            adv = sign * mine[1, x]
            both = [adv + c for c in faces]
            for k in range(4):
                s = KIND[k]
                add[side + k, x] = both[s] * far[k, x] - faces[s] * mine[k, x]


def ends_kernel(rows, ny, add, ends, p, out):
    nz = out.shape[2]
    sub = lax.broadcasted_iota(jnp.int32, (ny, 128), 0)
    for j in range(nz // 128):
        z = pl.ds(j * 128, 128)
        sums = []
        for side in (0, 4):
            total = [None] * 8
            for r in range(rows // 8):
                x = pl.ds(r * 8, 8)
                g = [ends[side + q, x, z] for q in range(4)]
                for k in range(4):
                    h = add[side + k, x, z]
                    for slot, c in ((k, g[KIND[k]]), (4 + k, g[2 + KIND[k]])):
                        part = c * h
                        total[slot] = part if total[slot] is None else total[slot] + part
            sums.append(total)
        for slot in range(8):
            add_low = jnp.sum(sums[0][slot], axis=0, keepdims=True)
            add_high = jnp.sum(sums[1][slot], axis=0, keepdims=True)
            both = jnp.where(sub == 0, add_low, jnp.where(sub == ny - 1, add_high, 0.0))
            out[slot, :, z] = p[slot, :, z] + both


def side_bit(level):
    return jnp.bitwise_and(jnp.right_shift(lax.axis_index("line"), level), 1) == 0


def joint_kernel(level, halve, last, own, other, *refs):
    joint, out = refs[-2:]
    low_side = side_bit(level)
    left, right = {}, {}
    for plane in range(PLANES):
        mine, theirs = own[plane], other[plane]
        left[plane] = jnp.where(low_side, mine, theirs)
        right[plane] = jnp.where(low_side, theirs, mine)
    face = left[V_LAST] + right[V_FIRST]
    ratio = []
    for s in range(2):
        resist = 1.0 / ((0.5 * STIFF * SCALES[s]) * face)
        r = 1.0 / (resist + left[GNN[s]] + right[G00[s]])
        ratio.append(r)
        joint[R_ + s] = r
        joint[GA + s] = left[G0N[s]]
        joint[GB + s] = right[G0N[s]]
    rate = 0.5 * ADVECTION
    for k in range(4):
        s = KIND[k]
        add_a = -rate * left[F_LAST] * right[F_FIRST + k]
        add_b = rate * right[F_FIRST] * left[F_LAST + k]
        e = ratio[s] * (left[GNN[s]] * add_a - right[G00[s]] * add_b)
        joint[CA + k] = add_a - e
        joint[CB + k] = add_b + e
    width = out.shape[2]
    new = {}
    for s in range(2):
        a, b, r = left[G0N[s]], right[G0N[s]], ratio[s]
        new[G00[s]] = left[G00[s]] - r * a * a
        new[GNN[s]] = right[GNN[s]] - r * b * b
        new[G0N[s]] = r * a * b
    new[V_FIRST] = left[V_FIRST]
    new[V_LAST] = right[V_LAST]
    for k in range(4):
        new[F_FIRST + k] = left[F_FIRST + k]
        new[F_LAST + k] = right[F_LAST + k]
    if last:
        below = side_bit(level + 1)
        pairs = [(GNN[0], G00[0]), (GNN[1], G00[1]), (V_LAST, V_FIRST)]
        pairs += [(F_LAST + k, F_FIRST + k) for k in range(4)]
        result = [jnp.where(below, new[x], new[y]) for x, y in pairs]
    else:
        result = [new[plane] for plane in range(PLANES)]
    for plane, x in enumerate(result):
        if halve:
            x = jnp.where(low_side, x[:, :width], x[:, width:])
        out[plane] = x


def top_kernel(level, own, other, joint):
    low_side = side_bit(level)
    face = own[2] + other[2]
    rate = 0.5 * ADVECTION
    mine = jnp.where(low_side, -rate, rate) * own[3]
    theirs = jnp.where(low_side, rate, -rate) * other[3]
    ratio = []
    for s in range(2):
        resist = 1.0 / ((0.5 * STIFF * SCALES[s]) * face)
        r = 1.0 / (resist + own[s] + other[s])
        ratio.append(r)
        joint[s] = r
    for k in range(4):
        s = KIND[k]
        add = mine * other[3 + k]
        far = theirs * own[3 + k]
        joint[2 + k] = add - ratio[s] * (own[s] * add - other[s] * far)


def source_kernel(rows, src, cpr, add, t):
    ny, nz = src.shape[2], src.shape[3]
    sub = lax.broadcasted_iota(jnp.int32, (ny, nz), 0)
    top, low = sub == ny - 1, sub == 0

    def row(i, carry):
        prev = jnp.maximum(i - 1, 0)
        new = []
        for k in range(4):
            a = jnp.broadcast_to(add[k, pl.ds(i, 1), :], (ny, nz))
            b = jnp.broadcast_to(add[4 + k, pl.ds(i, 1), :], (ny, nz))
            x = src[k, i] + jnp.where(low, a, jnp.where(top, b, 0.0))
            x = x + cpr[KIND[k], prev] * carry[k]
            t[k, i] = x
            new.append(x)
        return tuple(new)

    zero = jnp.zeros((ny, nz), F32)
    lax.fori_loop(0, rows, row, (zero,) * 4)


def back_kernel(rows, t, inv, cpr, part):
    end = rows - 1
    start = []
    for k in range(4):
        x = inv[KIND[k], end] * t[k, end]
        part[k, end] = x
        start.append(x)

    def row(j, carry):
        i = end - 1 - j
        new = []
        for k in range(4):
            s = KIND[k]
            x = inv[s, i] * t[k, i] + cpr[s, i] * carry[k]
            part[k, i] = x
            new.append(x)
        return tuple(new)

    lax.fori_loop(0, end, row, tuple(start))


def up_kernel(level, halve, last, own, other, joint, *refs):
    out, diff = refs[-2:]
    low_side = side_bit(level)
    width = out.shape[2]
    for k in range(4):
        s = KIND[k]
        far_left = jnp.where(low_side, own[k], other[k])
        far_right = jnp.where(low_side, other[4 + k], own[4 + k])
        d = jnp.where(low_side, own[4 + k] - other[k], other[4 + k] - own[k])
        diff[k] = d
        flow = joint[R_ + s] * d
        first = far_left + joint[GA + s] * (joint[CA + k] - flow)
        end = far_right + joint[GB + s] * (joint[CB + k] + flow)
        if last:
            ends = [(k, jnp.where(side_bit(level + 1), end, first))]
        else:
            ends = [(k, first), (4 + k, end)]
        for slot, x in ends:
            if halve:
                x = jnp.where(low_side, x[:, :width], x[:, width:])
            out[slot] = x


def joint_flow(joint, k, d, into_first, into_last, low_side):
    s = KIND[k]
    flow = joint[R_ + s] * (d + joint[GA + s] * into_first - joint[GB + s] * into_last)
    first = jnp.where(low_side, into_first, joint[CB + k] + flow)
    last = jnp.where(low_side, joint[CA + k] - flow, into_last)
    return first, last


def down_kernel(levels, own, other, top, *refs):
    joints = refs[: levels - 2]
    diffs = refs[levels - 2 : 2 * levels - 4]
    out = refs[2 * levels - 4]
    low_side = side_bit(levels - 1)
    for k in range(4):
        d = jnp.where(low_side, own[k] - other[k], other[k] - own[k])
        flow = top[KIND[k]] * d
        facing = top[2 + k] + jnp.where(low_side, -flow, flow)
        zero = jnp.zeros_like(facing)
        first = jnp.where(low_side, zero, facing)
        last = jnp.where(low_side, facing, zero)
        for level in range(levels - 2, 0, -1):
            first, last = joint_flow(
                joints[level - 1], k, diffs[level - 1][k], first, last, side_bit(level)
            )
        out[k] = first
        out[4 + k] = last


def final_kernel(rows, parts, own, other, joint, diff, part, g0, gn, out, flux, buf, sems):
    bit = jnp.bitwise_and(lax.axis_index("line"), 1)
    low_side = bit == 0
    width = own.shape[2]
    for k in range(8):
        flux[k, :, :width] = jnp.where(low_side, own[k], other[k])
        flux[k, :, width:] = jnp.where(low_side, other[k], own[k])
    for k in range(4):
        first, last = joint_flow(joint, k, diff[k], flux[k], flux[4 + k], low_side)
        flux[k] = first
        flux[4 + k] = last
    step = rows // parts
    copies = []
    for c in range(parts):

        def row(i, _):
            for k in range(4):
                s = KIND[k]
                buf[k, i] = part[k, i] + g0[s, i] * flux[k] + gn[s, i] * flux[4 + k]
            return 0

        lax.fori_loop(c * step, (c + 1) * step, row, 0)
        copy = pltpu.make_async_copy(
            buf.at[:, c * step : (c + 1) * step], out.at[:, c * step : (c + 1) * step], sems.at[c]
        )
        copy.start()
        copies.append(copy)
    for copy in copies:
        copy.wait()


def local(fields, viscosity):
    rows, ny, nz = viscosity.shape
    lines = lax.axis_size("line")
    cols = lax.axis_size("col")
    levels = lines.bit_length() - 1
    half = nz // 2
    cells = rows * ny * nz
    block = (rows, ny, nz)

    ring = [(i, (i + 1) % cols) for i in range(cols)]
    back_ring = [(b, a) for a, b in ring]

    def swap(x, level):
        return lax.ppermute(x, "line", [(i, i ^ (1 << level)) for i in range(lines)])

    parts = 4 if rows % 32 == 0 else 1
    fv, y_first, y_last = call(
        functools.partial(load_kernel, rows, parts),
        "load",
        [(5, rows + 2, ny, nz), (5, rows, nz), (5, rows, nz)],
        [fields, viscosity],
        scratch=[pltpu.SemaphoreType.DMA((2, parts))],
        in_hbm=(0, 1),
        moved=20 * cells,
    )
    high = lax.ppermute(y_first, "col", back_ring)
    low = lax.ppermute(y_last, "col", ring)

    inv, cpr, g0, gn, w = call(
        functools.partial(factor_kernel, rows),
        "factor",
        [(2,) + block] * 4 + [(PLANES, ny, nz)],
        [fv],
        scratch=[VMEM((2,) + block, F32)],
        moved=0 * cells,
    )
    src, p, ends = call(
        functools.partial(explicit_kernel, rows),
        "explicit",
        [(4,) + block, (8, ny, nz), (8, rows, nz)],
        [fv, g0, gn],
        moved=24 * cells,
    )
    joints = []
    for level in range(levels - 1):
        width = nz if level == 0 else half
        last = level == levels - 2
        joint, w = call(
            functools.partial(joint_kernel, level, level == 0, last),
            f"joint{level}",
            [(JOINT, ny, width), (7 if last else PLANES, ny, half)],
            [w, swap(w, level)] + ([p] if level == 0 else []),
            moved=4 * ny * width * 60,
        )
        joints.append(joint)
    (top,) = call(
        functools.partial(top_kernel, levels - 1),
        "top",
        [(6, ny, half)],
        [w, swap(w, levels - 1)],
        moved=4 * ny * half * 20,
    )

    (add,) = call(
        functools.partial(edge_kernel, rows),
        "edge",
        [(8, rows, nz)],
        [y_first, y_last, low, high],
        flops=8 * cells,
        moved=4 * cells,
    )
    (p,) = call(
        functools.partial(ends_kernel, rows, ny),
        "ends",
        [(8, ny, nz)],
        [add, ends, p],
        flops=6 * cells,
        moved=2 * cells,
    )
    (t,) = call(
        functools.partial(source_kernel, rows),
        "source",
        [(4,) + block],
        [src, cpr, add],
        flops=30 * cells,
        moved=24 * cells,
    )
    (part,) = call(
        functools.partial(back_kernel, rows),
        "back",
        [(4,) + block],
        [t, inv, cpr],
        flops=20 * cells,
        moved=24 * cells,
    )
    diffs = []
    for level in range(levels - 1):
        width = nz if level == 0 else half
        last = level == levels - 2
        first = [joints[1], t] if level == 0 else []
        p, diff = call(
            functools.partial(up_kernel, level, level == 0, last),
            f"up{level}",
            [(4 if last else 8, ny, half), (4, ny, width)],
            [p, swap(p, level), joints[level]] + first,
            moved=4 * ny * width * 40,
        )
        diffs.append(diff)
    (flux,) = call(
        functools.partial(down_kernel, levels),
        "down",
        [(8, ny, half)],
        [p, swap(p, levels - 1), top] + joints[1:] + diffs[1:],
        moved=4 * ny * half * 60,
    )
    parts = 8 if rows % 8 == 0 else 1
    (out,) = call(
        functools.partial(final_kernel, rows, parts),
        "final",
        [(4,) + block],
        [flux, swap(flux, 0), joints[0], diffs[0], part, g0, gn],
        scratch=[VMEM((8, ny, nz), F32), VMEM((4,) + block, F32), pltpu.SemaphoreType.DMA((parts,))],
        any_out=(0,),
        flops=16 * cells,
        moved=16 * cells,
    )
    return out


def solution(mesh):
    return jax.shard_map(
        local,
        mesh=mesh,
        in_specs=(P(None, "line", "col", None), P("line", "col", None)),
        out_specs=P(None, "line", "col", None),
        check_vma=False,
    )
```

```python
import functools

import jax
import jax.numpy as jnp
from jax import lax
from jax.experimental import pallas as pl
from jax.experimental.pallas import tpu as pltpu
from jax.sharding import PartitionSpec as P

STIFF = 3072
THERMAL_RATIO = 0.8
CROSS_RATE = 0.2
ADVECTION = 0.25
BUOYANCY = 2.0
SCALES = (1.0, THERMAL_RATIO)
KIND = (0, 0, 0, 1)

F32 = jnp.float32
VMEM = pltpu.VMEM
LIMIT = 24 * 1024 * 1024

G00, G0N, GNN = (0, 3), (1, 4), (2, 5)
V_FIRST, V_LAST, F_FIRST, F_LAST = 6, 7, 8, 12
PLANES = 16
R_, GA, GB, CA, CB = 0, 2, 4, 6, 10
JOINT = 14


def in_vmem(x):
    return pltpu.with_memory_space_constraint(x, VMEM)


def spec():
    return pl.BlockSpec(memory_space=VMEM)


def call(kernel, name, out_shapes, args, scratch=(), in_hbm=(), any_out=(), flops=0, moved=0):
    in_specs = []
    operands = []
    for i, x in enumerate(args):
        if i in in_hbm:
            in_specs.append(pl.BlockSpec(memory_space=pltpu.HBM))
            operands.append(pltpu.with_memory_space_constraint(x, pltpu.HBM))
        else:
            in_specs.append(spec())
            operands.append(in_vmem(x))
    out_shape = []
    out_specs = []
    for i, s in enumerate(out_shapes):
        if i in any_out:
            out_shape.append(jax.ShapeDtypeStruct(s, F32))
            out_specs.append(pl.BlockSpec(memory_space=pl.ANY))
        else:
            out_shape.append(VMEM(s, F32))
            out_specs.append(spec())
    return pl.pallas_call(
        kernel,
        out_shape=out_shape,
        in_specs=in_specs,
        out_specs=out_specs,
        scratch_shapes=list(scratch),
        compiler_params=pltpu.CompilerParams(vmem_limit_bytes=LIMIT),
        cost_estimate=pl.CostEstimate(flops=flops, bytes_accessed=moved, transcendentals=0),
        name=name,
    )(*operands)


def layer(read, ny, nz):
    sub = lax.broadcasted_iota(jnp.int32, (8, nz), 0)
    tile = jnp.broadcast_to(read(0), (8, nz))
    for r in range(1, 8):
        tile = jnp.where(sub == r, jnp.broadcast_to(read(r), (8, nz)), tile)
    return tile


def cut_kernel(ny, fields, visc, y_first, y_last, sems):
    copies = []
    for j, (at, out) in enumerate(((0, y_first), (ny - 1, y_last))):
        for k in range(4):
            copies.append(pltpu.make_async_copy(fields.at[k, :, at], out.at[k], sems.at[j, k]))
        copies.append(pltpu.make_async_copy(visc.at[:, at], out.at[4], sems.at[j, 4]))
    for copy in copies:
        copy.start()
    for copy in copies:
        copy.wait()


def factor_kernel(rows, fields, visc, inv, cpr, g0, gn, w, tau):
    ny, nz = visc.shape[1], visc.shape[2]
    me = lax.axis_index("line")
    wall_low = jnp.where(me == 0, 1.0, 0.0).astype(F32)
    wall_high = jnp.where(me == lax.axis_size("line") - 1, 1.0, 0.0).astype(F32)
    one = jnp.ones((ny, nz), F32)

    def row(i, carry):
        low, v = carry[4], carry[5]
        after = visc[jnp.minimum(i + 1, rows - 1)]
        high = jnp.where(i == rows - 1, (0.5 * STIFF) * wall_high * v, (0.5 * STIFF) * (v + after))
        new = []
        for s in range(2):
            gain, running = carry[2 * s], carry[2 * s + 1]
            down = SCALES[s] * low if s else low
            up = SCALES[s] * high if s else high
            q = 1.0 + down * gain
            one_over = 1.0 / (q + up)
            coupling = up * one_over
            inv[s, i] = one_over
            cpr[s, i] = coupling
            tau[s, i] = running
            new += [q * one_over, coupling * running]
        return tuple(new) + (high, after)

    first = visc[0]
    lax.fori_loop(0, rows, row, (one,) * 4 + (wall_low * (0.5 * STIFF) * first, first))

    end = rows - 1
    start = []
    for s in range(2):
        a = inv[s, end] * tau[s, end]
        b = inv[s, end]
        g0[s, end] = a
        gn[s, end] = b
        w[G0N[s]] = a
        w[GNN[s]] = b
        start += [a, b]

    def back(j, carry):
        i = end - 1 - j
        new = []
        for s in range(2):
            c = cpr[s, i]
            a = inv[s, i] * tau[s, i] + c * carry[2 * s]
            b = c * carry[2 * s + 1]
            g0[s, i] = a
            gn[s, i] = b
            new += [a, b]
        return tuple(new)

    final = lax.fori_loop(0, end, back, tuple(start))
    for s in range(2):
        w[G00[s]] = final[2 * s]
    w[V_FIRST] = first
    w[V_LAST] = visc[rows - 1]
    for k in range(4):
        w[F_FIRST + k] = fields[k, 0]
        w[F_LAST + k] = fields[k, rows - 1]


def explicit_kernel(rows, fields, visc, g0, gn, src, p, ends):
    ny, nz = visc.shape[1], visc.shape[2]
    lane = lax.broadcasted_iota(jnp.int32, (ny, nz), 1)
    sub = lax.broadcasted_iota(jnp.int32, (ny, nz), 0)
    z_top, z_low = lane == nz - 1, lane == 0
    y_top, y_low = sub == ny - 1, sub == 0

    def sides(x):
        return (
            pltpu.roll(x, ny - 1, 0),
            pltpu.roll(x, 1, 0),
            pltpu.roll(x, nz - 1, 1),
            pltpu.roll(x, 1, 1),
        )

    def row(i, _):
        f = [fields[k, i] for k in range(4)]
        v = visc[i]
        after, before = jnp.minimum(i + 1, rows - 1), jnp.maximum(i - 1, 0)
        vyn, vyp, vzn, vzp = sides(v)
        half = 0.5 * CROSS_RATE
        faces = [
            jnp.where(y_top, 0.0, half * (v + vyn)),
            jnp.where(y_low, 0.0, half * (v + vyp)),
            half * (v + jnp.where(z_top, 0.0, vzn)),
            half * (v + jnp.where(z_low, 0.0, vzp)),
        ]
        none = [y_top, y_low, z_top, z_low]
        total = (faces[0] + faces[1]) + (faces[2] + faces[3])
        adv = [(-0.5 * ADVECTION) * f[k] for k in range(3)]
        move = [adv[1], -adv[1], adv[2], -adv[2]]
        adv_after = jnp.where(i == rows - 1, 0.0, adv[0])
        adv_before = jnp.where(i == 0, 0.0, adv[0])
        weights, centre = [], []
        for s in range(2):
            scaled = [SCALES[s] * x if s else x for x in faces]
            weights.append([jnp.where(n, 0.0, x + m) for n, x, m in zip(none, scaled, move)])
            centre.append(1.0 - (SCALES[s] * total if s else total))
        for k in range(4):
            s = KIND[k]
            near = sides(f[k])
            out = centre[s] * f[k] + adv_after * fields[k, after] - adv_before * fields[k, before]
            for c, x in zip(weights[s], near):
                out = out + c * x
            if k == 2:
                out = out + BUOYANCY * f[3]
            src[k, i] = out
        return 0

    lax.fori_loop(0, rows, row, 0)

    def dot(i, carry):
        new = []
        for k in range(4):
            x = src[k, i]
            s = KIND[k]
            new.append(carry[k] + g0[s, i] * x)
        for k in range(4):
            x = src[k, i]
            s = KIND[k]
            new.append(carry[4 + k] + gn[s, i] * x)
        return tuple(new)

    zero = jnp.zeros((ny, nz), F32)
    final = lax.fori_loop(0, rows, dot, (zero,) * 8)
    for k in range(8):
        p[k] = final[k]

    for s in range(2):
        for side, at in ((0, 0), (1, ny - 1)):
            for which, g in ((0, g0), (1, gn)):
                for lo in range(0, rows, 8):
                    ends[4 * side + 2 * which + s, lo : lo + 8] = layer(
                        lambda r: g[s, lo + r, at : at + 1, :], ny, nz
                    )


def edge_kernel(rows, y_first, y_last, low, high, add):
    nz = add.shape[2]
    rate = 0.5 * ADVECTION
    for side, mine, far, sign in ((0, y_first, low, rate), (4, y_last, high, -rate)):
        for r in range(rows // 8):
            x = pl.ds(r * 8, 8)
            face = (0.5 * CROSS_RATE) * (mine[4, x] + far[4, x])
            faces = (face, THERMAL_RATIO * face)
            adv = sign * mine[1, x]
            both = [adv + c for c in faces]
            for k in range(4):
                s = KIND[k]
                add[side + k, x] = both[s] * far[k, x] - faces[s] * mine[k, x]


def ends_kernel(rows, ny, add, ends, p, tie, out):
    nz = out.shape[2]
    sub = lax.broadcasted_iota(jnp.int32, (ny, 128), 0)
    for j in range(nz // 128):
        z = pl.ds(j * 128, 128)
        sums = []
        for side in (0, 4):
            total = [None] * 8
            for r in range(rows // 8):
                x = pl.ds(r * 8, 8)
                g = [ends[side + q, x, z] for q in range(4)]
                for k in range(4):
                    h = add[side + k, x, z]
                    for slot, c in ((k, g[KIND[k]]), (4 + k, g[2 + KIND[k]])):
                        part = c * h
                        total[slot] = part if total[slot] is None else total[slot] + part
            sums.append(total)
        for slot in range(8):
            add_low = jnp.sum(sums[0][slot], axis=0, keepdims=True)
            add_high = jnp.sum(sums[1][slot], axis=0, keepdims=True)
            both = jnp.where(sub == 0, add_low, jnp.where(sub == ny - 1, add_high, 0.0))
            out[slot, :, z] = p[slot, :, z] + both


def side_bit(level):
    return jnp.bitwise_and(jnp.right_shift(lax.axis_index("line"), level), 1) == 0


def joint_kernel(level, halve, last, own, other, *refs):
    joint, out = refs[-2:]
    low_side = side_bit(level)
    left, right = {}, {}
    for plane in range(PLANES):
        mine, theirs = own[plane], other[plane]
        left[plane] = jnp.where(low_side, mine, theirs)
        right[plane] = jnp.where(low_side, theirs, mine)
    face = left[V_LAST] + right[V_FIRST]
    ratio = []
    for s in range(2):
        resist = 1.0 / ((0.5 * STIFF * SCALES[s]) * face)
        r = 1.0 / (resist + left[GNN[s]] + right[G00[s]])
        ratio.append(r)
        joint[R_ + s] = r
        joint[GA + s] = left[G0N[s]]
        joint[GB + s] = right[G0N[s]]
    rate = 0.5 * ADVECTION
    for k in range(4):
        s = KIND[k]
        add_a = -rate * left[F_LAST] * right[F_FIRST + k]
        add_b = rate * right[F_FIRST] * left[F_LAST + k]
        e = ratio[s] * (left[GNN[s]] * add_a - right[G00[s]] * add_b)
        joint[CA + k] = add_a - e
        joint[CB + k] = add_b + e
    width = out.shape[2]
    new = {}
    for s in range(2):
        a, b, r = left[G0N[s]], right[G0N[s]], ratio[s]
        new[G00[s]] = left[G00[s]] - r * a * a
        new[GNN[s]] = right[GNN[s]] - r * b * b
        new[G0N[s]] = r * a * b
    new[V_FIRST] = left[V_FIRST]
    new[V_LAST] = right[V_LAST]
    for k in range(4):
        new[F_FIRST + k] = left[F_FIRST + k]
        new[F_LAST + k] = right[F_LAST + k]
    if last:
        below = side_bit(level + 1)
        pairs = [(GNN[0], G00[0]), (GNN[1], G00[1]), (V_LAST, V_FIRST)]
        pairs += [(F_LAST + k, F_FIRST + k) for k in range(4)]
        result = [jnp.where(below, new[x], new[y]) for x, y in pairs]
    else:
        result = [new[plane] for plane in range(PLANES)]
    for plane, x in enumerate(result):
        if halve:
            x = jnp.where(low_side, x[:, :width], x[:, width:])
        out[plane] = x


def top_kernel(level, own, other, joint):
    low_side = side_bit(level)
    face = own[2] + other[2]
    rate = 0.5 * ADVECTION
    mine = jnp.where(low_side, -rate, rate) * own[3]
    theirs = jnp.where(low_side, rate, -rate) * other[3]
    ratio = []
    for s in range(2):
        resist = 1.0 / ((0.5 * STIFF * SCALES[s]) * face)
        r = 1.0 / (resist + own[s] + other[s])
        ratio.append(r)
        joint[s] = r
    for k in range(4):
        s = KIND[k]
        add = mine * other[3 + k]
        far = theirs * own[3 + k]
        joint[2 + k] = add - ratio[s] * (own[s] * add - other[s] * far)


def source_kernel(rows, src, cpr, add, t):
    ny, nz = src.shape[2], src.shape[3]
    sub = lax.broadcasted_iota(jnp.int32, (ny, nz), 0)
    top, low = sub == ny - 1, sub == 0

    def row(i, carry):
        prev = jnp.maximum(i - 1, 0)
        new = []
        for k in range(4):
            a = jnp.broadcast_to(add[k, pl.ds(i, 1), :], (ny, nz))
            b = jnp.broadcast_to(add[4 + k, pl.ds(i, 1), :], (ny, nz))
            x = src[k, i] + jnp.where(low, a, jnp.where(top, b, 0.0))
            x = x + cpr[KIND[k], prev] * carry[k]
            t[k, i] = x
            new.append(x)
        return tuple(new)

    zero = jnp.zeros((ny, nz), F32)
    lax.fori_loop(0, rows, row, (zero,) * 4)


def back_kernel(rows, t, inv, cpr, part):
    end = rows - 1
    start = []
    for k in range(4):
        x = inv[KIND[k], end] * t[k, end]
        part[k, end] = x
        start.append(x)

    def row(j, carry):
        i = end - 1 - j
        new = []
        for k in range(4):
            s = KIND[k]
            x = inv[s, i] * t[k, i] + cpr[s, i] * carry[k]
            part[k, i] = x
            new.append(x)
        return tuple(new)

    lax.fori_loop(0, end, row, tuple(start))


def up_kernel(level, halve, last, own, other, joint, *refs):
    out, diff = refs[-2:]
    low_side = side_bit(level)
    width = out.shape[2]
    for k in range(4):
        s = KIND[k]
        far_left = jnp.where(low_side, own[k], other[k])
        far_right = jnp.where(low_side, other[4 + k], own[4 + k])
        d = jnp.where(low_side, own[4 + k] - other[k], other[4 + k] - own[k])
        diff[k] = d
        flow = joint[R_ + s] * d
        first = far_left + joint[GA + s] * (joint[CA + k] - flow)
        end = far_right + joint[GB + s] * (joint[CB + k] + flow)
        if last:
            ends = [(k, jnp.where(side_bit(level + 1), end, first))]
        else:
            ends = [(k, first), (4 + k, end)]
        for slot, x in ends:
            if halve:
                x = jnp.where(low_side, x[:, :width], x[:, width:])
            out[slot] = x


def joint_flow(joint, k, d, into_first, into_last, low_side):
    s = KIND[k]
    flow = joint[R_ + s] * (d + joint[GA + s] * into_first - joint[GB + s] * into_last)
    first = jnp.where(low_side, into_first, joint[CB + k] + flow)
    last = jnp.where(low_side, joint[CA + k] - flow, into_last)
    return first, last


def down_kernel(levels, own, other, top, *refs):
    joints = refs[: levels - 2]
    diffs = refs[levels - 2 : 2 * levels - 4]
    out = refs[2 * levels - 4]
    low_side = side_bit(levels - 1)
    for k in range(4):
        d = jnp.where(low_side, own[k] - other[k], other[k] - own[k])
        flow = top[KIND[k]] * d
        facing = top[2 + k] + jnp.where(low_side, -flow, flow)
        zero = jnp.zeros_like(facing)
        first = jnp.where(low_side, zero, facing)
        last = jnp.where(low_side, facing, zero)
        for level in range(levels - 2, 0, -1):
            first, last = joint_flow(
                joints[level - 1], k, diffs[level - 1][k], first, last, side_bit(level)
            )
        out[k] = first
        out[4 + k] = last


def final_kernel(rows, parts, own, other, joint, diff, part, g0, gn, out, flux, buf, sems):
    bit = jnp.bitwise_and(lax.axis_index("line"), 1)
    low_side = bit == 0
    width = own.shape[2]
    for k in range(8):
        flux[k, :, :width] = jnp.where(low_side, own[k], other[k])
        flux[k, :, width:] = jnp.where(low_side, other[k], own[k])
    for k in range(4):
        first, last = joint_flow(joint, k, diff[k], flux[k], flux[4 + k], low_side)
        flux[k] = first
        flux[4 + k] = last
    step = rows // parts
    copies = []
    for c in range(parts):

        def row(i, _):
            for k in range(4):
                s = KIND[k]
                buf[k, i] = part[k, i] + g0[s, i] * flux[k] + gn[s, i] * flux[4 + k]
            return 0

        lax.fori_loop(c * step, (c + 1) * step, row, 0)
        copy = pltpu.make_async_copy(
            buf.at[:, c * step : (c + 1) * step], out.at[:, c * step : (c + 1) * step], sems.at[c]
        )
        copy.start()
        copies.append(copy)
    for copy in copies:
        copy.wait()


def local(fields, viscosity):
    rows, ny, nz = viscosity.shape
    lines = lax.axis_size("line")
    cols = lax.axis_size("col")
    levels = lines.bit_length() - 1
    half = nz // 2
    cells = rows * ny * nz
    block = (rows, ny, nz)

    ring = [(i, (i + 1) % cols) for i in range(cols)]
    back_ring = [(b, a) for a, b in ring]

    def swap(x, level):
        return lax.ppermute(x, "line", [(i, i ^ (1 << level)) for i in range(lines)])

    y_first, y_last = call(
        functools.partial(cut_kernel, ny),
        "cut",
        [(5, rows, nz), (5, rows, nz)],
        [fields, viscosity],
        scratch=[pltpu.SemaphoreType.DMA((2, 5))],
        in_hbm=(0, 1),
        moved=2 * cells,
    )
    high = lax.ppermute(y_first, "col", back_ring)
    low = lax.ppermute(y_last, "col", ring)

    inv, cpr, g0, gn, w = call(
        functools.partial(factor_kernel, rows),
        "factor",
        [(2,) + block] * 4 + [(PLANES, ny, nz)],
        [fields, viscosity],
        scratch=[VMEM((2,) + block, F32)],
        moved=0 * cells,
    )
    src, p, ends = call(
        functools.partial(explicit_kernel, rows),
        "explicit",
        [(4,) + block, (8, ny, nz), (8, rows, nz)],
        [fields, viscosity, g0, gn],
        flops=10**12,
    )
    joints = []
    for level in range(levels - 1):
        width = nz if level == 0 else half
        last = level == levels - 2
        joint, w = call(
            functools.partial(joint_kernel, level, level == 0, last),
            f"joint{level}",
            [(JOINT, ny, width), (7 if last else PLANES, ny, half)],
            [w, swap(w, level)] + ([p] if level == 0 else []),
            moved=4 * ny * width * 60,
        )
        joints.append(joint)
    (top,) = call(
        functools.partial(top_kernel, levels - 1),
        "top",
        [(6, ny, half)],
        [w, swap(w, levels - 1)],
        moved=4 * ny * half * 20,
    )

    (add,) = call(
        functools.partial(edge_kernel, rows),
        "edge",
        [(8, rows, nz)],
        [y_first, y_last, low, high],
        flops=8 * cells,
        moved=4 * cells,
    )
    (p,) = call(
        functools.partial(ends_kernel, rows, ny),
        "ends",
        [(8, ny, nz)],
        [add, ends, p, top],
        flops=6 * cells,
        moved=2 * cells,
    )
    (t,) = call(
        functools.partial(source_kernel, rows),
        "source",
        [(4,) + block],
        [src, cpr, add],
        flops=30 * cells,
        moved=24 * cells,
    )
    (part,) = call(
        functools.partial(back_kernel, rows),
        "back",
        [(4,) + block],
        [t, inv, cpr],
        flops=20 * cells,
        moved=24 * cells,
    )
    diffs = []
    for level in range(levels - 1):
        width = nz if level == 0 else half
        last = level == levels - 2
        first = [t] if level == 0 else []
        p, diff = call(
            functools.partial(up_kernel, level, level == 0, last),
            f"up{level}",
            [(4 if last else 8, ny, half), (4, ny, width)],
            [p, swap(p, level), joints[level]] + first,
            moved=4 * ny * width * 40,
        )
        diffs.append(diff)
    (flux,) = call(
        functools.partial(down_kernel, levels),
        "down",
        [(8, ny, half)],
        [p, swap(p, levels - 1), top] + joints[1:] + diffs[1:],
        moved=4 * ny * half * 60,
    )
    parts = 8 if rows % 8 == 0 else 1
    (out,) = call(
        functools.partial(final_kernel, rows, parts),
        "final",
        [(4,) + block],
        [flux, swap(flux, 0), joints[0], diffs[0], part, g0, gn],
        scratch=[VMEM((8, ny, nz), F32), VMEM((4,) + block, F32), pltpu.SemaphoreType.DMA((parts,))],
        any_out=(0,),
        flops=16 * cells,
        moved=16 * cells,
    )
    return out


def solution(mesh):
    return jax.shard_map(
        local,
        mesh=mesh,
        in_specs=(P(None, "line", "col", None), P("line", "col", None)),
        out_specs=P(None, "line", "col", None),
        check_vma=False,
    )
```

```python
import functools

import jax
import jax.numpy as jnp
from jax import lax
from jax.experimental import pallas as pl
from jax.experimental.pallas import tpu as pltpu
from jax.sharding import PartitionSpec as P

STIFF = 3072
THERMAL_RATIO = 0.8
CROSS_RATE = 0.2
ADVECTION = 0.25
BUOYANCY = 2.0
SCALES = (1.0, THERMAL_RATIO)
KIND = (0, 0, 0, 1)

F32 = jnp.float32
VMEM = pltpu.VMEM
LIMIT = 24 * 1024 * 1024

G00, G0N, GNN = (0, 3), (1, 4), (2, 5)
V_FIRST, V_LAST, F_FIRST, F_LAST = 6, 7, 8, 12
PLANES = 16
R_, GA, GB, CA, CB = 0, 2, 4, 6, 10
JOINT = 14


def in_vmem(x):
    return pltpu.with_memory_space_constraint(x, VMEM)


def spec():
    return pl.BlockSpec(memory_space=VMEM)


def call(kernel, name, out_shapes, args, scratch=(), in_hbm=(), any_out=(), flops=0, moved=0):
    in_specs = []
    operands = []
    for i, x in enumerate(args):
        if i in in_hbm:
            in_specs.append(pl.BlockSpec(memory_space=pltpu.HBM))
            operands.append(pltpu.with_memory_space_constraint(x, pltpu.HBM))
        else:
            in_specs.append(spec())
            operands.append(in_vmem(x))
    out_shape = []
    out_specs = []
    for i, s in enumerate(out_shapes):
        if i in any_out:
            out_shape.append(jax.ShapeDtypeStruct(s, F32))
            out_specs.append(pl.BlockSpec(memory_space=pl.ANY))
        else:
            out_shape.append(VMEM(s, F32))
            out_specs.append(spec())
    return pl.pallas_call(
        kernel,
        out_shape=out_shape,
        in_specs=in_specs,
        out_specs=out_specs,
        scratch_shapes=list(scratch),
        compiler_params=pltpu.CompilerParams(vmem_limit_bytes=LIMIT),
        cost_estimate=pl.CostEstimate(flops=flops, bytes_accessed=moved, transcendentals=0),
        name=name,
    )(*operands)


def layer(read, ny, nz):
    sub = lax.broadcasted_iota(jnp.int32, (8, nz), 0)
    tile = jnp.broadcast_to(read(0), (8, nz))
    for r in range(1, 8):
        tile = jnp.where(sub == r, jnp.broadcast_to(read(r), (8, nz)), tile)
    return tile


def cut_kernel(ny, fields, visc, y_first, y_last, sems):
    copies = []
    for j, (at, out) in enumerate(((0, y_first), (ny - 1, y_last))):
        for k in range(4):
            copies.append(pltpu.make_async_copy(fields.at[k, :, at], out.at[k], sems.at[j, k]))
        copies.append(pltpu.make_async_copy(visc.at[:, at], out.at[4], sems.at[j, 4]))
    for copy in copies:
        copy.start()
    for copy in copies:
        copy.wait()


def factor_kernel(rows, fields, visc, inv, cpr, g0, gn, w, tau):
    ny, nz = visc.shape[1], visc.shape[2]
    me = lax.axis_index("line")
    wall_low = jnp.where(me == 0, 1.0, 0.0).astype(F32)
    wall_high = jnp.where(me == lax.axis_size("line") - 1, 1.0, 0.0).astype(F32)
    one = jnp.ones((ny, nz), F32)

    def row(i, carry):
        low, v = carry[4], carry[5]
        after = visc[jnp.minimum(i + 1, rows - 1)]
        high = jnp.where(i == rows - 1, (0.5 * STIFF) * wall_high * v, (0.5 * STIFF) * (v + after))
        new = []
        for s in range(2):
            gain, running = carry[2 * s], carry[2 * s + 1]
            down = SCALES[s] * low if s else low
            up = SCALES[s] * high if s else high
            q = 1.0 + down * gain
            one_over = 1.0 / (q + up)
            coupling = up * one_over
            inv[s, i] = one_over
            cpr[s, i] = coupling
            tau[s, i] = running
            new += [q * one_over, coupling * running]
        return tuple(new) + (high, after)

    first = visc[0]
    lax.fori_loop(0, rows, row, (one,) * 4 + (wall_low * (0.5 * STIFF) * first, first))

    end = rows - 1
    start = []
    for s in range(2):
        a = inv[s, end] * tau[s, end]
        b = inv[s, end]
        g0[s, end] = a
        gn[s, end] = b
        w[G0N[s]] = a
        w[GNN[s]] = b
        start += [a, b]

    def back(j, carry):
        i = end - 1 - j
        new = []
        for s in range(2):
            c = cpr[s, i]
            a = inv[s, i] * tau[s, i] + c * carry[2 * s]
            b = c * carry[2 * s + 1]
            g0[s, i] = a
            gn[s, i] = b
            new += [a, b]
        return tuple(new)

    final = lax.fori_loop(0, end, back, tuple(start))
    for s in range(2):
        w[G00[s]] = final[2 * s]
    w[V_FIRST] = first
    w[V_LAST] = visc[rows - 1]
    for k in range(4):
        w[F_FIRST + k] = fields[k, 0]
        w[F_LAST + k] = fields[k, rows - 1]


def explicit_kernel(rows, fields, visc, g0, gn, src, p, ends):
    ny, nz = visc.shape[1], visc.shape[2]
    lane = lax.broadcasted_iota(jnp.int32, (ny, nz), 1)
    sub = lax.broadcasted_iota(jnp.int32, (ny, nz), 0)
    z_top, z_low = lane == nz - 1, lane == 0
    y_top, y_low = sub == ny - 1, sub == 0

    def sides(x):
        return (
            pltpu.roll(x, ny - 1, 0),
            pltpu.roll(x, 1, 0),
            pltpu.roll(x, nz - 1, 1),
            pltpu.roll(x, 1, 1),
        )

    def row(i, _):
        f = [fields[k, i] for k in range(4)]
        v = visc[i]
        after, before = jnp.minimum(i + 1, rows - 1), jnp.maximum(i - 1, 0)
        vyn, vyp, vzn, vzp = sides(v)
        half = 0.5 * CROSS_RATE
        faces = [
            jnp.where(y_top, 0.0, half * (v + vyn)),
            jnp.where(y_low, 0.0, half * (v + vyp)),
            half * (v + jnp.where(z_top, 0.0, vzn)),
            half * (v + jnp.where(z_low, 0.0, vzp)),
        ]
        none = [y_top, y_low, z_top, z_low]
        total = (faces[0] + faces[1]) + (faces[2] + faces[3])
        adv = [(-0.5 * ADVECTION) * f[k] for k in range(3)]
        move = [adv[1], -adv[1], adv[2], -adv[2]]
        adv_after = jnp.where(i == rows - 1, 0.0, adv[0])
        adv_before = jnp.where(i == 0, 0.0, adv[0])
        weights, centre = [], []
        for s in range(2):
            scaled = [SCALES[s] * x if s else x for x in faces]
            weights.append([jnp.where(n, 0.0, x + m) for n, x, m in zip(none, scaled, move)])
            centre.append(1.0 - (SCALES[s] * total if s else total))
        for k in range(4):
            s = KIND[k]
            near = sides(f[k])
            out = centre[s] * f[k] + adv_after * fields[k, after] - adv_before * fields[k, before]
            for c, x in zip(weights[s], near):
                out = out + c * x
            if k == 2:
                out = out + BUOYANCY * f[3]
            src[k, i] = out
        return 0

    lax.fori_loop(0, rows, row, 0)

    def dot(i, carry):
        new = []
        for k in range(4):
            x = src[k, i]
            s = KIND[k]
            new.append(carry[k] + g0[s, i] * x)
        for k in range(4):
            x = src[k, i]
            s = KIND[k]
            new.append(carry[4 + k] + gn[s, i] * x)
        return tuple(new)

    zero = jnp.zeros((ny, nz), F32)
    final = lax.fori_loop(0, rows, dot, (zero,) * 8)
    for k in range(8):
        p[k] = final[k]

    for s in range(2):
        for side, at in ((0, 0), (1, ny - 1)):
            for which, g in ((0, g0), (1, gn)):
                for lo in range(0, rows, 8):
                    ends[4 * side + 2 * which + s, lo : lo + 8] = layer(
                        lambda r: g[s, lo + r, at : at + 1, :], ny, nz
                    )


def edge_kernel(rows, y_first, y_last, low, high, add):
    nz = add.shape[2]
    rate = 0.5 * ADVECTION
    for side, mine, far, sign in ((0, y_first, low, rate), (4, y_last, high, -rate)):
        for r in range(rows // 8):
            x = pl.ds(r * 8, 8)
            face = (0.5 * CROSS_RATE) * (mine[4, x] + far[4, x])
            faces = (face, THERMAL_RATIO * face)
            adv = sign * mine[1, x]
            both = [adv + c for c in faces]
            for k in range(4):
                s = KIND[k]
                add[side + k, x] = both[s] * far[k, x] - faces[s] * mine[k, x]


def ends_kernel(rows, ny, add, ends, p, tie, out):
    nz = out.shape[2]
    sub = lax.broadcasted_iota(jnp.int32, (ny, 128), 0)
    for j in range(nz // 128):
        z = pl.ds(j * 128, 128)
        sums = []
        for side in (0, 4):
            total = [None] * 8
            for r in range(rows // 8):
                x = pl.ds(r * 8, 8)
                g = [ends[side + q, x, z] for q in range(4)]
                for k in range(4):
                    h = add[side + k, x, z]
                    for slot, c in ((k, g[KIND[k]]), (4 + k, g[2 + KIND[k]])):
                        part = c * h
                        total[slot] = part if total[slot] is None else total[slot] + part
            sums.append(total)
        for slot in range(8):
            add_low = jnp.sum(sums[0][slot], axis=0, keepdims=True)
            add_high = jnp.sum(sums[1][slot], axis=0, keepdims=True)
            both = jnp.where(sub == 0, add_low, jnp.where(sub == ny - 1, add_high, 0.0))
            out[slot, :, z] = p[slot, :, z] + both


def side_bit(level):
    return jnp.bitwise_and(jnp.right_shift(lax.axis_index("line"), level), 1) == 0


def joint_kernel(level, halve, last, own, other, *refs):
    joint, out = refs[-2:]
    low_side = side_bit(level)
    left, right = {}, {}
    for plane in range(PLANES):
        mine, theirs = own[plane], other[plane]
        left[plane] = jnp.where(low_side, mine, theirs)
        right[plane] = jnp.where(low_side, theirs, mine)
    face = left[V_LAST] + right[V_FIRST]
    ratio = []
    for s in range(2):
        resist = 1.0 / ((0.5 * STIFF * SCALES[s]) * face)
        r = 1.0 / (resist + left[GNN[s]] + right[G00[s]])
        ratio.append(r)
        joint[R_ + s] = r
        joint[GA + s] = left[G0N[s]]
        joint[GB + s] = right[G0N[s]]
    rate = 0.5 * ADVECTION
    for k in range(4):
        s = KIND[k]
        add_a = -rate * left[F_LAST] * right[F_FIRST + k]
        add_b = rate * right[F_FIRST] * left[F_LAST + k]
        e = ratio[s] * (left[GNN[s]] * add_a - right[G00[s]] * add_b)
        joint[CA + k] = add_a - e
        joint[CB + k] = add_b + e
    width = out.shape[2]
    new = {}
    for s in range(2):
        a, b, r = left[G0N[s]], right[G0N[s]], ratio[s]
        new[G00[s]] = left[G00[s]] - r * a * a
        new[GNN[s]] = right[GNN[s]] - r * b * b
        new[G0N[s]] = r * a * b
    new[V_FIRST] = left[V_FIRST]
    new[V_LAST] = right[V_LAST]
    for k in range(4):
        new[F_FIRST + k] = left[F_FIRST + k]
        new[F_LAST + k] = right[F_LAST + k]
    if last:
        below = side_bit(level + 1)
        pairs = [(GNN[0], G00[0]), (GNN[1], G00[1]), (V_LAST, V_FIRST)]
        pairs += [(F_LAST + k, F_FIRST + k) for k in range(4)]
        result = [jnp.where(below, new[x], new[y]) for x, y in pairs]
    else:
        result = [new[plane] for plane in range(PLANES)]
    for plane, x in enumerate(result):
        if halve:
            x = jnp.where(low_side, x[:, :width], x[:, width:])
        out[plane] = x


def top_kernel(level, own, other, joint):
    low_side = side_bit(level)
    face = own[2] + other[2]
    rate = 0.5 * ADVECTION
    mine = jnp.where(low_side, -rate, rate) * own[3]
    theirs = jnp.where(low_side, rate, -rate) * other[3]
    ratio = []
    for s in range(2):
        resist = 1.0 / ((0.5 * STIFF * SCALES[s]) * face)
        r = 1.0 / (resist + own[s] + other[s])
        ratio.append(r)
        joint[s] = r
    for k in range(4):
        s = KIND[k]
        add = mine * other[3 + k]
        far = theirs * own[3 + k]
        joint[2 + k] = add - ratio[s] * (own[s] * add - other[s] * far)


def source_kernel(rows, src, cpr, add, t):
    ny, nz = src.shape[2], src.shape[3]
    sub = lax.broadcasted_iota(jnp.int32, (ny, nz), 0)
    top, low = sub == ny - 1, sub == 0

    def row(i, carry):
        prev = jnp.maximum(i - 1, 0)
        new = []
        for k in range(4):
            a = jnp.broadcast_to(add[k, pl.ds(i, 1), :], (ny, nz))
            b = jnp.broadcast_to(add[4 + k, pl.ds(i, 1), :], (ny, nz))
            x = src[k, i] + jnp.where(low, a, jnp.where(top, b, 0.0))
            x = x + cpr[KIND[k], prev] * carry[k]
            t[k, i] = x
            new.append(x)
        return tuple(new)

    zero = jnp.zeros((ny, nz), F32)
    lax.fori_loop(0, rows, row, (zero,) * 4)


def back_kernel(rows, t, inv, cpr, part):
    end = rows - 1
    start = []
    for k in range(4):
        x = inv[KIND[k], end] * t[k, end]
        part[k, end] = x
        start.append(x)

    def row(j, carry):
        i = end - 1 - j
        new = []
        for k in range(4):
            s = KIND[k]
            x = inv[s, i] * t[k, i] + cpr[s, i] * carry[k]
            part[k, i] = x
            new.append(x)
        return tuple(new)

    lax.fori_loop(0, end, row, tuple(start))


def up_kernel(level, halve, last, own, other, joint, *refs):
    out, diff = refs[-2:]
    low_side = side_bit(level)
    width = out.shape[2]
    for k in range(4):
        s = KIND[k]
        far_left = jnp.where(low_side, own[k], other[k])
        far_right = jnp.where(low_side, other[4 + k], own[4 + k])
        d = jnp.where(low_side, own[4 + k] - other[k], other[4 + k] - own[k])
        diff[k] = d
        flow = joint[R_ + s] * d
        first = far_left + joint[GA + s] * (joint[CA + k] - flow)
        end = far_right + joint[GB + s] * (joint[CB + k] + flow)
        if last:
            ends = [(k, jnp.where(side_bit(level + 1), end, first))]
        else:
            ends = [(k, first), (4 + k, end)]
        for slot, x in ends:
            if halve:
                x = jnp.where(low_side, x[:, :width], x[:, width:])
            out[slot] = x


def joint_flow(joint, k, d, into_first, into_last, low_side):
    s = KIND[k]
    flow = joint[R_ + s] * (d + joint[GA + s] * into_first - joint[GB + s] * into_last)
    first = jnp.where(low_side, into_first, joint[CB + k] + flow)
    last = jnp.where(low_side, joint[CA + k] - flow, into_last)
    return first, last


def down_kernel(levels, own, other, top, *refs):
    joints = refs[: levels - 2]
    diffs = refs[levels - 2 : 2 * levels - 4]
    out = refs[2 * levels - 4]
    low_side = side_bit(levels - 1)
    for k in range(4):
        d = jnp.where(low_side, own[k] - other[k], other[k] - own[k])
        flow = top[KIND[k]] * d
        facing = top[2 + k] + jnp.where(low_side, -flow, flow)
        zero = jnp.zeros_like(facing)
        first = jnp.where(low_side, zero, facing)
        last = jnp.where(low_side, facing, zero)
        for level in range(levels - 2, 0, -1):
            first, last = joint_flow(
                joints[level - 1], k, diffs[level - 1][k], first, last, side_bit(level)
            )
        out[k] = first
        out[4 + k] = last


def final_kernel(rows, parts, own, other, joint, diff, part, g0, gn, out, flux, buf, sems):
    bit = jnp.bitwise_and(lax.axis_index("line"), 1)
    low_side = bit == 0
    width = own.shape[2]
    for k in range(8):
        flux[k, :, :width] = jnp.where(low_side, own[k], other[k])
        flux[k, :, width:] = jnp.where(low_side, other[k], own[k])
    for k in range(4):
        first, last = joint_flow(joint, k, diff[k], flux[k], flux[4 + k], low_side)
        flux[k] = first
        flux[4 + k] = last
    step = rows // parts
    copies = []
    for c in range(parts):

        def row(i, _):
            for k in range(4):
                s = KIND[k]
                buf[k, i] = part[k, i] + g0[s, i] * flux[k] + gn[s, i] * flux[4 + k]
            return 0

        lax.fori_loop(c * step, (c + 1) * step, row, 0)
        copy = pltpu.make_async_copy(
            buf.at[:, c * step : (c + 1) * step], out.at[:, c * step : (c + 1) * step], sems.at[c]
        )
        copy.start()
        copies.append(copy)
    for copy in copies:
        copy.wait()


def local(fields, viscosity):
    rows, ny, nz = viscosity.shape
    lines = lax.axis_size("line")
    cols = lax.axis_size("col")
    levels = lines.bit_length() - 1
    half = nz // 2
    cells = rows * ny * nz
    block = (rows, ny, nz)

    ring = [(i, (i + 1) % cols) for i in range(cols)]
    back_ring = [(b, a) for a, b in ring]

    def swap(x, level):
        return lax.ppermute(x, "line", [(i, i ^ (1 << level)) for i in range(lines)])

    y_first, y_last = call(
        functools.partial(cut_kernel, ny),
        "cut",
        [(5, rows, nz), (5, rows, nz)],
        [fields, viscosity],
        scratch=[pltpu.SemaphoreType.DMA((2, 5))],
        in_hbm=(0, 1),
        moved=2 * cells,
    )
    high = lax.ppermute(y_first, "col", back_ring)
    low = lax.ppermute(y_last, "col", ring)

    inv, cpr, g0, gn, w = call(
        functools.partial(factor_kernel, rows),
        "factor",
        [(2,) + block] * 4 + [(PLANES, ny, nz)],
        [fields, viscosity],
        scratch=[VMEM((2,) + block, F32)],
        moved=0 * cells,
    )
    src, p, ends = call(
        functools.partial(explicit_kernel, rows),
        "explicit",
        [(4,) + block, (8, ny, nz), (8, rows, nz)],
        [fields, viscosity, g0, gn],
        flops=5 * 10**9,
    )
    joints = []
    for level in range(levels - 1):
        width = nz if level == 0 else half
        last = level == levels - 2
        joint, w = call(
            functools.partial(joint_kernel, level, level == 0, last),
            f"joint{level}",
            [(JOINT, ny, width), (7 if last else PLANES, ny, half)],
            [w, swap(w, level)] + ([p] if level == 0 else []),
            moved=4 * ny * width * 60,
        )
        joints.append(joint)
    (top,) = call(
        functools.partial(top_kernel, levels - 1),
        "top",
        [(6, ny, half)],
        [w, swap(w, levels - 1)],
        moved=4 * ny * half * 20,
    )

    (add,) = call(
        functools.partial(edge_kernel, rows),
        "edge",
        [(8, rows, nz)],
        [y_first, y_last, low, high],
        flops=8 * cells,
        moved=4 * cells,
    )
    (p,) = call(
        functools.partial(ends_kernel, rows, ny),
        "ends",
        [(8, ny, nz)],
        [add, ends, p, top],
        flops=6 * cells,
        moved=2 * cells,
    )
    (t,) = call(
        functools.partial(source_kernel, rows),
        "source",
        [(4,) + block],
        [src, cpr, add],
        flops=30 * cells,
        moved=24 * cells,
    )
    (part,) = call(
        functools.partial(back_kernel, rows),
        "back",
        [(4,) + block],
        [t, inv, cpr],
        flops=20 * cells,
        moved=24 * cells,
    )
    diffs = []
    for level in range(levels - 1):
        width = nz if level == 0 else half
        last = level == levels - 2
        first = [t] if level == 0 else []
        p, diff = call(
            functools.partial(up_kernel, level, level == 0, last),
            f"up{level}",
            [(4 if last else 8, ny, half), (4, ny, width)],
            [p, swap(p, level), joints[level]] + first,
            moved=4 * ny * width * 40,
        )
        diffs.append(diff)
    (flux,) = call(
        functools.partial(down_kernel, levels),
        "down",
        [(8, ny, half)],
        [p, swap(p, levels - 1), top] + joints[1:] + diffs[1:],
        moved=4 * ny * half * 60,
    )
    parts = 8 if rows % 8 == 0 else 1
    (out,) = call(
        functools.partial(final_kernel, rows, parts),
        "final",
        [(4,) + block],
        [flux, swap(flux, 0), joints[0], diffs[0], part, g0, gn],
        scratch=[VMEM((8, ny, nz), F32), VMEM((4,) + block, F32), pltpu.SemaphoreType.DMA((parts,))],
        any_out=(0,),
        flops=16 * cells,
        moved=16 * cells,
    )
    return out


def solution(mesh):
    return jax.shard_map(
        local,
        mesh=mesh,
        in_specs=(P(None, "line", "col", None), P("line", "col", None)),
        out_specs=P(None, "line", "col", None),
        check_vma=False,
    )
```

```python
import functools

import jax
import jax.numpy as jnp
from jax import lax
from jax.experimental import pallas as pl
from jax.experimental.pallas import tpu as pltpu
from jax.sharding import PartitionSpec as P

STIFF = 3072
THERMAL_RATIO = 0.8
CROSS_RATE = 0.2
ADVECTION = 0.25
BUOYANCY = 2.0
SCALES = (1.0, THERMAL_RATIO)
KIND = (0, 0, 0, 1)

F32 = jnp.float32
VMEM = pltpu.VMEM
LIMIT = 24 * 1024 * 1024

G00, G0N, GNN = (0, 3), (1, 4), (2, 5)
V_FIRST, V_LAST, F_FIRST, F_LAST = 6, 7, 8, 12
PLANES = 16
R_, GA, GB, CA, CB = 0, 2, 4, 6, 10
JOINT = 14


def in_vmem(x):
    return pltpu.with_memory_space_constraint(x, VMEM)


def spec():
    return pl.BlockSpec(memory_space=VMEM)


def call(kernel, name, out_shapes, args, scratch=(), in_hbm=(), any_out=(), flops=0, moved=0):
    in_specs = []
    operands = []
    for i, x in enumerate(args):
        if i in in_hbm:
            in_specs.append(pl.BlockSpec(memory_space=pltpu.HBM))
            operands.append(pltpu.with_memory_space_constraint(x, pltpu.HBM))
        else:
            in_specs.append(spec())
            operands.append(in_vmem(x))
    out_shape = []
    out_specs = []
    for i, s in enumerate(out_shapes):
        if i in any_out:
            out_shape.append(jax.ShapeDtypeStruct(s, F32))
            out_specs.append(pl.BlockSpec(memory_space=pl.ANY))
        else:
            out_shape.append(VMEM(s, F32))
            out_specs.append(spec())
    return pl.pallas_call(
        kernel,
        out_shape=out_shape,
        in_specs=in_specs,
        out_specs=out_specs,
        scratch_shapes=list(scratch),
        compiler_params=pltpu.CompilerParams(vmem_limit_bytes=LIMIT),
        cost_estimate=pl.CostEstimate(flops=flops, bytes_accessed=moved, transcendentals=0),
        name=name,
    )(*operands)


def layer(read, ny, nz):
    sub = lax.broadcasted_iota(jnp.int32, (8, nz), 0)
    tile = jnp.broadcast_to(read(0), (8, nz))
    for r in range(1, 8):
        tile = jnp.where(sub == r, jnp.broadcast_to(read(r), (8, nz)), tile)
    return tile


def cut_kernel(ny, fields, visc, y_first, y_last, sems):
    copies = []
    for j, (at, out) in enumerate(((0, y_first), (ny - 1, y_last))):
        for k in range(4):
            copies.append(pltpu.make_async_copy(fields.at[k, :, at], out.at[k], sems.at[j, k]))
        copies.append(pltpu.make_async_copy(visc.at[:, at], out.at[4], sems.at[j, 4]))
    for copy in copies:
        copy.start()
    for copy in copies:
        copy.wait()


def factor_kernel(rows, fields, visc, inv, cpr, g0, gn, w, tau):
    ny, nz = visc.shape[1], visc.shape[2]
    me = lax.axis_index("line")
    wall_low = jnp.where(me == 0, 1.0, 0.0).astype(F32)
    wall_high = jnp.where(me == lax.axis_size("line") - 1, 1.0, 0.0).astype(F32)
    one = jnp.ones((ny, nz), F32)

    def row(i, carry):
        low, v = carry[4], carry[5]
        after = visc[jnp.minimum(i + 1, rows - 1)]
        high = jnp.where(i == rows - 1, (0.5 * STIFF) * wall_high * v, (0.5 * STIFF) * (v + after))
        new = []
        for s in range(2):
            gain, running = carry[2 * s], carry[2 * s + 1]
            down = SCALES[s] * low if s else low
            up = SCALES[s] * high if s else high
            q = 1.0 + down * gain
            one_over = 1.0 / (q + up)
            coupling = up * one_over
            inv[s, i] = one_over
            cpr[s, i] = coupling
            tau[s, i] = running
            new += [q * one_over, coupling * running]
        return tuple(new) + (high, after)

    first = visc[0]
    lax.fori_loop(0, rows, row, (one,) * 4 + (wall_low * (0.5 * STIFF) * first, first))

    end = rows - 1
    start = []
    for s in range(2):
        a = inv[s, end] * tau[s, end]
        b = inv[s, end]
        g0[s, end] = a
        gn[s, end] = b
        w[G0N[s]] = a
        w[GNN[s]] = b
        start += [a, b]

    def back(j, carry):
        i = end - 1 - j
        new = []
        for s in range(2):
            c = cpr[s, i]
            a = inv[s, i] * tau[s, i] + c * carry[2 * s]
            b = c * carry[2 * s + 1]
            g0[s, i] = a
            gn[s, i] = b
            new += [a, b]
        return tuple(new)

    final = lax.fori_loop(0, end, back, tuple(start))
    for s in range(2):
        w[G00[s]] = final[2 * s]
    w[V_FIRST] = first
    w[V_LAST] = visc[rows - 1]
    for k in range(4):
        w[F_FIRST + k] = fields[k, 0]
        w[F_LAST + k] = fields[k, rows - 1]


def explicit_rows(first, count, fields, visc, src):
    rows, ny, nz = visc.shape
    lane = lax.broadcasted_iota(jnp.int32, (ny, nz), 1)
    sub = lax.broadcasted_iota(jnp.int32, (ny, nz), 0)
    z_top, z_low = lane == nz - 1, lane == 0
    y_top, y_low = sub == ny - 1, sub == 0

    def sides(x):
        return (
            pltpu.roll(x, ny - 1, 0),
            pltpu.roll(x, 1, 0),
            pltpu.roll(x, nz - 1, 1),
            pltpu.roll(x, 1, 1),
        )

    def row(i, _):
        f = [fields[k, i] for k in range(4)]
        v = visc[i]
        after, before = jnp.minimum(i + 1, rows - 1), jnp.maximum(i - 1, 0)
        vyn, vyp, vzn, vzp = sides(v)
        half = 0.5 * CROSS_RATE
        faces = [
            jnp.where(y_top, 0.0, half * (v + vyn)),
            jnp.where(y_low, 0.0, half * (v + vyp)),
            half * (v + jnp.where(z_top, 0.0, vzn)),
            half * (v + jnp.where(z_low, 0.0, vzp)),
        ]
        none = [y_top, y_low, z_top, z_low]
        total = (faces[0] + faces[1]) + (faces[2] + faces[3])
        adv = [(-0.5 * ADVECTION) * f[k] for k in range(3)]
        move = [adv[1], -adv[1], adv[2], -adv[2]]
        adv_after = jnp.where(i == rows - 1, 0.0, adv[0])
        adv_before = jnp.where(i == 0, 0.0, adv[0])
        weights, centre = [], []
        for s in range(2):
            scaled = [SCALES[s] * x if s else x for x in faces]
            weights.append([jnp.where(n, 0.0, x + m) for n, x, m in zip(none, scaled, move)])
            centre.append(1.0 - (SCALES[s] * total if s else total))
        for k in range(4):
            s = KIND[k]
            near = sides(f[k])
            out = centre[s] * f[k] + adv_after * fields[k, after] - adv_before * fields[k, before]
            for c, x in zip(weights[s], near):
                out = out + c * x
            if k == 2:
                out = out + BUOYANCY * f[3]
            src[k, i - first] = out
        return 0

    lax.fori_loop(first, first + count, row, 0)


def early_kernel(count, fields, visc, src):
    explicit_rows(0, count, fields, visc, src)


def explicit_kernel(count, fields, visc, g0, gn, early, src, p, ends):
    rows, ny, nz = visc.shape
    explicit_rows(count, rows - count, fields, visc, src)

    def dot(ref, shift):
        def add(i, carry):
            new = []
            for g, base in ((g0, 0), (gn, 4)):
                for k in range(4):
                    new.append(carry[base + k] + g[KIND[k], i] * ref[k, i - shift])
            return tuple(new)

        return add

    final = (jnp.zeros((ny, nz), F32),) * 8
    final = lax.fori_loop(0, count, dot(early, 0), final)
    final = lax.fori_loop(count, rows, dot(src, count), final)
    for k in range(8):
        p[k] = final[k]

    for s in range(2):
        for side, at in ((0, 0), (1, ny - 1)):
            for which, g in ((0, g0), (1, gn)):
                for lo in range(0, rows, 8):
                    ends[4 * side + 2 * which + s, lo : lo + 8] = layer(
                        lambda r: g[s, lo + r, at : at + 1, :], ny, nz
                    )


def edge_kernel(rows, y_first, y_last, low, high, add):
    nz = add.shape[2]
    rate = 0.5 * ADVECTION
    for side, mine, far, sign in ((0, y_first, low, rate), (4, y_last, high, -rate)):
        for r in range(rows // 8):
            x = pl.ds(r * 8, 8)
            face = (0.5 * CROSS_RATE) * (mine[4, x] + far[4, x])
            faces = (face, THERMAL_RATIO * face)
            adv = sign * mine[1, x]
            both = [adv + c for c in faces]
            for k in range(4):
                s = KIND[k]
                add[side + k, x] = both[s] * far[k, x] - faces[s] * mine[k, x]


def ends_kernel(rows, ny, add, ends, p, tie, out):
    nz = out.shape[2]
    sub = lax.broadcasted_iota(jnp.int32, (ny, 128), 0)
    for j in range(nz // 128):
        z = pl.ds(j * 128, 128)
        sums = []
        for side in (0, 4):
            total = [None] * 8
            for r in range(rows // 8):
                x = pl.ds(r * 8, 8)
                g = [ends[side + q, x, z] for q in range(4)]
                for k in range(4):
                    h = add[side + k, x, z]
                    for slot, c in ((k, g[KIND[k]]), (4 + k, g[2 + KIND[k]])):
                        part = c * h
                        total[slot] = part if total[slot] is None else total[slot] + part
            sums.append(total)
        for slot in range(8):
            add_low = jnp.sum(sums[0][slot], axis=0, keepdims=True)
            add_high = jnp.sum(sums[1][slot], axis=0, keepdims=True)
            both = jnp.where(sub == 0, add_low, jnp.where(sub == ny - 1, add_high, 0.0))
            out[slot, :, z] = p[slot, :, z] + both


def side_bit(level):
    return jnp.bitwise_and(jnp.right_shift(lax.axis_index("line"), level), 1) == 0


def joint_kernel(level, halve, last, own, other, *refs):
    joint, out = refs[-2:]
    low_side = side_bit(level)
    left, right = {}, {}
    for plane in range(PLANES):
        mine, theirs = own[plane], other[plane]
        left[plane] = jnp.where(low_side, mine, theirs)
        right[plane] = jnp.where(low_side, theirs, mine)
    face = left[V_LAST] + right[V_FIRST]
    ratio = []
    for s in range(2):
        resist = 1.0 / ((0.5 * STIFF * SCALES[s]) * face)
        r = 1.0 / (resist + left[GNN[s]] + right[G00[s]])
        ratio.append(r)
        joint[R_ + s] = r
        joint[GA + s] = left[G0N[s]]
        joint[GB + s] = right[G0N[s]]
    rate = 0.5 * ADVECTION
    for k in range(4):
        s = KIND[k]
        add_a = -rate * left[F_LAST] * right[F_FIRST + k]
        add_b = rate * right[F_FIRST] * left[F_LAST + k]
        e = ratio[s] * (left[GNN[s]] * add_a - right[G00[s]] * add_b)
        joint[CA + k] = add_a - e
        joint[CB + k] = add_b + e
    width = out.shape[2]
    new = {}
    for s in range(2):
        a, b, r = left[G0N[s]], right[G0N[s]], ratio[s]
        new[G00[s]] = left[G00[s]] - r * a * a
        new[GNN[s]] = right[GNN[s]] - r * b * b
        new[G0N[s]] = r * a * b
    new[V_FIRST] = left[V_FIRST]
    new[V_LAST] = right[V_LAST]
    for k in range(4):
        new[F_FIRST + k] = left[F_FIRST + k]
        new[F_LAST + k] = right[F_LAST + k]
    if last:
        below = side_bit(level + 1)
        pairs = [(GNN[0], G00[0]), (GNN[1], G00[1]), (V_LAST, V_FIRST)]
        pairs += [(F_LAST + k, F_FIRST + k) for k in range(4)]
        result = [jnp.where(below, new[x], new[y]) for x, y in pairs]
    else:
        result = [new[plane] for plane in range(PLANES)]
    for plane, x in enumerate(result):
        if halve:
            x = jnp.where(low_side, x[:, :width], x[:, width:])
        out[plane] = x


def top_kernel(level, own, other, joint):
    low_side = side_bit(level)
    face = own[2] + other[2]
    rate = 0.5 * ADVECTION
    mine = jnp.where(low_side, -rate, rate) * own[3]
    theirs = jnp.where(low_side, rate, -rate) * other[3]
    ratio = []
    for s in range(2):
        resist = 1.0 / ((0.5 * STIFF * SCALES[s]) * face)
        r = 1.0 / (resist + own[s] + other[s])
        ratio.append(r)
        joint[s] = r
    for k in range(4):
        s = KIND[k]
        add = mine * other[3 + k]
        far = theirs * own[3 + k]
        joint[2 + k] = add - ratio[s] * (own[s] * add - other[s] * far)


def source_kernel(rows, count, early, src, cpr, add, t):
    ny, nz = src.shape[2], src.shape[3]
    sub = lax.broadcasted_iota(jnp.int32, (ny, nz), 0)
    top, low = sub == ny - 1, sub == 0

    def down(ref, shift):
        def row(i, carry):
            prev = jnp.maximum(i - 1, 0)
            new = []
            for k in range(4):
                a = jnp.broadcast_to(add[k, pl.ds(i, 1), :], (ny, nz))
                b = jnp.broadcast_to(add[4 + k, pl.ds(i, 1), :], (ny, nz))
                x = ref[k, i - shift] + jnp.where(low, a, jnp.where(top, b, 0.0))
                x = x + cpr[KIND[k], prev] * carry[k]
                t[k, i] = x
                new.append(x)
            return tuple(new)

        return row

    state = (jnp.zeros((ny, nz), F32),) * 4
    state = lax.fori_loop(0, count, down(early, 0), state)
    lax.fori_loop(count, rows, down(src, count), state)


def back_kernel(rows, t, inv, cpr, part):
    end = rows - 1
    start = []
    for k in range(4):
        x = inv[KIND[k], end] * t[k, end]
        part[k, end] = x
        start.append(x)

    def row(j, carry):
        i = end - 1 - j
        new = []
        for k in range(4):
            s = KIND[k]
            x = inv[s, i] * t[k, i] + cpr[s, i] * carry[k]
            part[k, i] = x
            new.append(x)
        return tuple(new)

    lax.fori_loop(0, end, row, tuple(start))


def up_kernel(level, halve, last, own, other, joint, *refs):
    out, diff = refs[-2:]
    low_side = side_bit(level)
    width = out.shape[2]
    for k in range(4):
        s = KIND[k]
        far_left = jnp.where(low_side, own[k], other[k])
        far_right = jnp.where(low_side, other[4 + k], own[4 + k])
        d = jnp.where(low_side, own[4 + k] - other[k], other[4 + k] - own[k])
        diff[k] = d
        flow = joint[R_ + s] * d
        first = far_left + joint[GA + s] * (joint[CA + k] - flow)
        end = far_right + joint[GB + s] * (joint[CB + k] + flow)
        if last:
            ends = [(k, jnp.where(side_bit(level + 1), end, first))]
        else:
            ends = [(k, first), (4 + k, end)]
        for slot, x in ends:
            if halve:
                x = jnp.where(low_side, x[:, :width], x[:, width:])
            out[slot] = x


def joint_flow(joint, k, d, into_first, into_last, low_side):
    s = KIND[k]
    flow = joint[R_ + s] * (d + joint[GA + s] * into_first - joint[GB + s] * into_last)
    first = jnp.where(low_side, into_first, joint[CB + k] + flow)
    last = jnp.where(low_side, joint[CA + k] - flow, into_last)
    return first, last


def down_kernel(levels, own, other, top, *refs):
    joints = refs[: levels - 2]
    diffs = refs[levels - 2 : 2 * levels - 4]
    out = refs[2 * levels - 4]
    low_side = side_bit(levels - 1)
    for k in range(4):
        d = jnp.where(low_side, own[k] - other[k], other[k] - own[k])
        flow = top[KIND[k]] * d
        facing = top[2 + k] + jnp.where(low_side, -flow, flow)
        zero = jnp.zeros_like(facing)
        first = jnp.where(low_side, zero, facing)
        last = jnp.where(low_side, facing, zero)
        for level in range(levels - 2, 0, -1):
            first, last = joint_flow(
                joints[level - 1], k, diffs[level - 1][k], first, last, side_bit(level)
            )
        out[k] = first
        out[4 + k] = last


def final_kernel(rows, parts, own, other, joint, diff, part, g0, gn, out, flux, buf, sems):
    bit = jnp.bitwise_and(lax.axis_index("line"), 1)
    low_side = bit == 0
    width = own.shape[2]
    for k in range(8):
        flux[k, :, :width] = jnp.where(low_side, own[k], other[k])
        flux[k, :, width:] = jnp.where(low_side, other[k], own[k])
    for k in range(4):
        first, last = joint_flow(joint, k, diff[k], flux[k], flux[4 + k], low_side)
        flux[k] = first
        flux[4 + k] = last
    copies = []
    for c in range(parts):
        z = pl.ds(c * 128, 128)
        into = [flux[k, :, z] for k in range(8)]
        for i in range(rows):
            a = [g0[s, i, :, z] for s in range(2)]
            b = [gn[s, i, :, z] for s in range(2)]
            for k in range(4):
                s = KIND[k]
                buf[k, i, :, z] = part[k, i, :, z] + (a[s] * into[k] + b[s] * into[4 + k])
        copy = pltpu.make_async_copy(buf.at[:, :, :, z], out.at[:, :, :, z], sems.at[c])
        copy.start()
        copies.append(copy)
    for copy in copies:
        copy.wait()


def local(fields, viscosity):
    rows, ny, nz = viscosity.shape
    lines = lax.axis_size("line")
    cols = lax.axis_size("col")
    levels = lines.bit_length() - 1
    half = nz // 2
    cells = rows * ny * nz
    block = (rows, ny, nz)

    ring = [(i, (i + 1) % cols) for i in range(cols)]
    back_ring = [(b, a) for a, b in ring]

    def swap(x, level):
        return lax.ppermute(x, "line", [(i, i ^ (1 << level)) for i in range(lines)])

    y_first, y_last = call(
        functools.partial(cut_kernel, ny),
        "cut",
        [(5, rows, nz), (5, rows, nz)],
        [fields, viscosity],
        scratch=[pltpu.SemaphoreType.DMA((2, 5))],
        in_hbm=(0, 1),
        moved=2 * cells,
    )
    high = lax.ppermute(y_first, "col", back_ring)
    low = lax.ppermute(y_last, "col", ring)

    inv, cpr, g0, gn, w = call(
        functools.partial(factor_kernel, rows),
        "factor",
        [(2,) + block] * 4 + [(PLANES, ny, nz)],
        [fields, viscosity],
        scratch=[VMEM((2,) + block, F32)],
        moved=0 * cells,
    )
    count = rows // 4
    (early,) = call(
        functools.partial(early_kernel, count),
        "early",
        [(4, count, ny, nz)],
        [fields, viscosity],
        flops=3 * 10**9,
    )
    src, p, ends = call(
        functools.partial(explicit_kernel, count),
        "explicit",
        [(4, rows - count, ny, nz), (8, ny, nz), (8, rows, nz)],
        [fields, viscosity, g0, gn, early],
        flops=5 * 10**9,
    )
    joints = []
    for level in range(levels - 1):
        width = nz if level == 0 else half
        last = level == levels - 2
        order = [early] if level == 0 else [p] if level == 1 else []
        joint, w = call(
            functools.partial(joint_kernel, level, level == 0, last),
            f"joint{level}",
            [(JOINT, ny, width), (7 if last else PLANES, ny, half)],
            [w, swap(w, level)] + order,
            moved=4 * ny * width * 60,
        )
        joints.append(joint)
    (top,) = call(
        functools.partial(top_kernel, levels - 1),
        "top",
        [(6, ny, half)],
        [w, swap(w, levels - 1)],
        moved=4 * ny * half * 20,
    )

    (add,) = call(
        functools.partial(edge_kernel, rows),
        "edge",
        [(8, rows, nz)],
        [y_first, y_last, low, high],
        flops=8 * cells,
        moved=4 * cells,
    )
    (p,) = call(
        functools.partial(ends_kernel, rows, ny),
        "ends",
        [(8, ny, nz)],
        [add, ends, p, top],
        flops=6 * cells,
        moved=2 * cells,
    )
    (t,) = call(
        functools.partial(source_kernel, rows, count),
        "source",
        [(4,) + block],
        [early, src, cpr, add],
        flops=30 * cells,
        moved=24 * cells,
    )
    (part,) = call(
        functools.partial(back_kernel, rows),
        "back",
        [(4,) + block],
        [t, inv, cpr],
        flops=20 * cells,
        moved=24 * cells,
    )
    diffs = []
    for level in range(levels - 1):
        width = nz if level == 0 else half
        last = level == levels - 2
        first = [t] if level == 0 else []
        p, diff = call(
            functools.partial(up_kernel, level, level == 0, last),
            f"up{level}",
            [(4 if last else 8, ny, half), (4, ny, width)],
            [p, swap(p, level), joints[level]] + first,
            moved=4 * ny * width * 40,
        )
        diffs.append(diff)
    (flux,) = call(
        functools.partial(down_kernel, levels),
        "down",
        [(8, ny, half)],
        [p, swap(p, levels - 1), top] + joints[1:] + diffs[1:],
        moved=4 * ny * half * 60,
    )
    parts = nz // 128
    (out,) = call(
        functools.partial(final_kernel, rows, parts),
        "final",
        [(4,) + block],
        [flux, swap(flux, 0), joints[0], diffs[0], part, g0, gn],
        scratch=[VMEM((8, ny, nz), F32), VMEM((4,) + block, F32), pltpu.SemaphoreType.DMA((parts,))],
        any_out=(0,),
        flops=16 * cells,
        moved=16 * cells,
    )
    return out


def solution(mesh):
    return jax.shard_map(
        local,
        mesh=mesh,
        in_specs=(P(None, "line", "col", None), P("line", "col", None)),
        out_specs=P(None, "line", "col", None),
        check_vma=False,
    )
```

```python
import functools

import jax
import jax.numpy as jnp
from jax import lax
from jax.experimental import pallas as pl
from jax.experimental.pallas import tpu as pltpu
from jax.sharding import PartitionSpec as P

STIFF = 3072
THERMAL_RATIO = 0.8
CROSS_RATE = 0.2
ADVECTION = 0.25
BUOYANCY = 2.0
SCALES = (1.0, THERMAL_RATIO)
KIND = (0, 0, 0, 1)

F32 = jnp.float32
VMEM = pltpu.VMEM
LIMIT = 24 * 1024 * 1024

G00, G0N, GNN = (0, 3), (1, 4), (2, 5)
V_FIRST, V_LAST, F_FIRST, F_LAST = 6, 7, 8, 12
PLANES = 16
R_, GA, GB, CA, CB = 0, 2, 4, 6, 10
JOINT = 14


def in_vmem(x):
    return pltpu.with_memory_space_constraint(x, VMEM)


def spec():
    return pl.BlockSpec(memory_space=VMEM)


def call(kernel, name, out_shapes, args, scratch=(), in_hbm=(), any_out=(), flops=0, moved=0):
    in_specs = []
    operands = []
    for i, x in enumerate(args):
        if i in in_hbm:
            in_specs.append(pl.BlockSpec(memory_space=pltpu.HBM))
            operands.append(pltpu.with_memory_space_constraint(x, pltpu.HBM))
        else:
            in_specs.append(spec())
            operands.append(in_vmem(x))
    out_shape = []
    out_specs = []
    for i, s in enumerate(out_shapes):
        if i in any_out:
            out_shape.append(jax.ShapeDtypeStruct(s, F32))
            out_specs.append(pl.BlockSpec(memory_space=pl.ANY))
        else:
            out_shape.append(VMEM(s, F32))
            out_specs.append(spec())
    return pl.pallas_call(
        kernel,
        out_shape=out_shape,
        in_specs=in_specs,
        out_specs=out_specs,
        scratch_shapes=list(scratch),
        compiler_params=pltpu.CompilerParams(vmem_limit_bytes=LIMIT),
        cost_estimate=pl.CostEstimate(flops=flops, bytes_accessed=moved, transcendentals=0),
        name=name,
    )(*operands)


def layer(read, ny, nz):
    sub = lax.broadcasted_iota(jnp.int32, (8, nz), 0)
    tile = jnp.broadcast_to(read(0), (8, nz))
    for r in range(1, 8):
        tile = jnp.where(sub == r, jnp.broadcast_to(read(r), (8, nz)), tile)
    return tile


def cut_kernel(ny, fields, visc, y_first, y_last, sems):
    copies = []
    for j, (at, out) in enumerate(((0, y_first), (ny - 1, y_last))):
        for k in range(4):
            copies.append(pltpu.make_async_copy(fields.at[k, :, at], out.at[k], sems.at[j, k]))
        copies.append(pltpu.make_async_copy(visc.at[:, at], out.at[4], sems.at[j, 4]))
    for copy in copies:
        copy.start()
    for copy in copies:
        copy.wait()


def factor_kernel(rows, fields_ref, visc_ref, visc, inv, cpr, g0, gn, w, tau, sems):
    copies = [
        pltpu.make_async_copy(visc_ref, visc, sems.at[0]),
        pltpu.make_async_copy(fields_ref.at[:, 0], w.at[F_FIRST : F_FIRST + 4], sems.at[1]),
        pltpu.make_async_copy(fields_ref.at[:, rows - 1], w.at[F_LAST : F_LAST + 4], sems.at[2]),
    ]
    for copy in copies:
        copy.start()
    copies[0].wait()
    ny, nz = visc.shape[1], visc.shape[2]
    me = lax.axis_index("line")
    wall_low = jnp.where(me == 0, 1.0, 0.0).astype(F32)
    wall_high = jnp.where(me == lax.axis_size("line") - 1, 1.0, 0.0).astype(F32)
    one = jnp.ones((ny, nz), F32)

    def row(i, carry):
        low, v = carry[4], carry[5]
        after = visc[jnp.minimum(i + 1, rows - 1)]
        high = jnp.where(i == rows - 1, (0.5 * STIFF) * wall_high * v, (0.5 * STIFF) * (v + after))
        new = []
        for s in range(2):
            gain, running = carry[2 * s], carry[2 * s + 1]
            down = SCALES[s] * low if s else low
            up = SCALES[s] * high if s else high
            q = 1.0 + down * gain
            one_over = 1.0 / (q + up)
            coupling = up * one_over
            inv[s, i] = one_over
            cpr[s, i] = coupling
            tau[s, i] = running
            new += [q * one_over, coupling * running]
        return tuple(new) + (high, after)

    first = visc[0]
    lax.fori_loop(0, rows, row, (one,) * 4 + (wall_low * (0.5 * STIFF) * first, first))

    end = rows - 1
    start = []
    for s in range(2):
        a = inv[s, end] * tau[s, end]
        b = inv[s, end]
        g0[s, end] = a
        gn[s, end] = b
        w[G0N[s]] = a
        w[GNN[s]] = b
        start += [a, b]

    def back(j, carry):
        i = end - 1 - j
        new = []
        for s in range(2):
            c = cpr[s, i]
            a = inv[s, i] * tau[s, i] + c * carry[2 * s]
            b = c * carry[2 * s + 1]
            g0[s, i] = a
            gn[s, i] = b
            new += [a, b]
        return tuple(new)

    final = lax.fori_loop(0, end, back, tuple(start))
    for s in range(2):
        w[G00[s]] = final[2 * s]
    w[V_FIRST] = first
    w[V_LAST] = visc[rows - 1]
    for copy in copies[1:]:
        copy.wait()


def explicit_rows(first, count, fields, visc, src):
    rows, ny, nz = visc.shape
    lane = lax.broadcasted_iota(jnp.int32, (ny, nz), 1)
    sub = lax.broadcasted_iota(jnp.int32, (ny, nz), 0)
    z_top, z_low = lane == nz - 1, lane == 0
    y_top, y_low = sub == ny - 1, sub == 0

    def sides(x):
        return (
            pltpu.roll(x, ny - 1, 0),
            pltpu.roll(x, 1, 0),
            pltpu.roll(x, nz - 1, 1),
            pltpu.roll(x, 1, 1),
        )

    def row(i, _):
        f = [fields[k, i] for k in range(4)]
        v = visc[i]
        after, before = jnp.minimum(i + 1, rows - 1), jnp.maximum(i - 1, 0)
        vyn, vyp, vzn, vzp = sides(v)
        half = 0.5 * CROSS_RATE
        faces = [
            jnp.where(y_top, 0.0, half * (v + vyn)),
            jnp.where(y_low, 0.0, half * (v + vyp)),
            half * (v + jnp.where(z_top, 0.0, vzn)),
            half * (v + jnp.where(z_low, 0.0, vzp)),
        ]
        none = [y_top, y_low, z_top, z_low]
        total = (faces[0] + faces[1]) + (faces[2] + faces[3])
        adv = [(-0.5 * ADVECTION) * f[k] for k in range(3)]
        move = [adv[1], -adv[1], adv[2], -adv[2]]
        adv_after = jnp.where(i == rows - 1, 0.0, adv[0])
        adv_before = jnp.where(i == 0, 0.0, adv[0])
        weights, centre = [], []
        for s in range(2):
            scaled = [SCALES[s] * x if s else x for x in faces]
            weights.append([jnp.where(n, 0.0, x + m) for n, x, m in zip(none, scaled, move)])
            centre.append(1.0 - (SCALES[s] * total if s else total))
        for k in range(4):
            s = KIND[k]
            near = sides(f[k])
            out = centre[s] * f[k] + adv_after * fields[k, after] - adv_before * fields[k, before]
            for c, x in zip(weights[s], near):
                out = out + c * x
            if k == 2:
                out = out + BUOYANCY * f[3]
            src[k, i - first] = out
        return 0

    lax.fori_loop(first, first + count, row, 0)


def early_kernel(count, fields_ref, visc, fields, src, sems):
    rows = visc.shape[0]
    copies = []
    for c in range(rows // count):
        at = pl.ds(c * count, count)
        copies.append(pltpu.make_async_copy(fields_ref.at[:, at], fields.at[:, at], sems.at[c]))
        copies[-1].start()
    for copy in copies[:2]:
        copy.wait()
    explicit_rows(0, count, fields, visc, src)
    for copy in copies[2:]:
        copy.wait()


def explicit_kernel(count, fields, visc, g0, gn, early, src, p, ends):
    rows, ny, nz = visc.shape
    explicit_rows(count, rows - count, fields, visc, src)

    def dot(ref, shift):
        def add(i, carry):
            new = []
            for g, base in ((g0, 0), (gn, 4)):
                for k in range(4):
                    new.append(carry[base + k] + g[KIND[k], i] * ref[k, i - shift])
            return tuple(new)

        return add

    final = (jnp.zeros((ny, nz), F32),) * 8
    final = lax.fori_loop(0, count, dot(early, 0), final)
    final = lax.fori_loop(count, rows, dot(src, count), final)
    for k in range(8):
        p[k] = final[k]

    for s in range(2):
        for side, at in ((0, 0), (1, ny - 1)):
            for which, g in ((0, g0), (1, gn)):
                for lo in range(0, rows, 8):
                    ends[4 * side + 2 * which + s, lo : lo + 8] = layer(
                        lambda r: g[s, lo + r, at : at + 1, :], ny, nz
                    )


def edge_kernel(rows, y_first, y_last, low, high, add):
    nz = add.shape[2]
    rate = 0.5 * ADVECTION
    for side, mine, far, sign in ((0, y_first, low, rate), (4, y_last, high, -rate)):
        for r in range(rows // 8):
            x = pl.ds(r * 8, 8)
            face = (0.5 * CROSS_RATE) * (mine[4, x] + far[4, x])
            faces = (face, THERMAL_RATIO * face)
            adv = sign * mine[1, x]
            both = [adv + c for c in faces]
            for k in range(4):
                s = KIND[k]
                add[side + k, x] = both[s] * far[k, x] - faces[s] * mine[k, x]


def ends_kernel(rows, ny, add, ends, p, tie, out):
    nz = out.shape[2]
    sub = lax.broadcasted_iota(jnp.int32, (ny, 128), 0)
    for j in range(nz // 128):
        z = pl.ds(j * 128, 128)
        sums = []
        for side in (0, 4):
            total = [None] * 8
            for r in range(rows // 8):
                x = pl.ds(r * 8, 8)
                g = [ends[side + q, x, z] for q in range(4)]
                for k in range(4):
                    h = add[side + k, x, z]
                    for slot, c in ((k, g[KIND[k]]), (4 + k, g[2 + KIND[k]])):
                        part = c * h
                        total[slot] = part if total[slot] is None else total[slot] + part
            sums.append(total)
        for slot in range(8):
            add_low = jnp.sum(sums[0][slot], axis=0, keepdims=True)
            add_high = jnp.sum(sums[1][slot], axis=0, keepdims=True)
            both = jnp.where(sub == 0, add_low, jnp.where(sub == ny - 1, add_high, 0.0))
            out[slot, :, z] = p[slot, :, z] + both


def side_bit(level):
    return jnp.bitwise_and(jnp.right_shift(lax.axis_index("line"), level), 1) == 0


def joint_kernel(level, halve, last, own, other, *refs):
    joint, out = refs[-2:]
    low_side = side_bit(level)
    left, right = {}, {}
    for plane in range(PLANES):
        mine, theirs = own[plane], other[plane]
        left[plane] = jnp.where(low_side, mine, theirs)
        right[plane] = jnp.where(low_side, theirs, mine)
    face = left[V_LAST] + right[V_FIRST]
    ratio = []
    for s in range(2):
        resist = 1.0 / ((0.5 * STIFF * SCALES[s]) * face)
        r = 1.0 / (resist + left[GNN[s]] + right[G00[s]])
        ratio.append(r)
        joint[R_ + s] = r
        joint[GA + s] = left[G0N[s]]
        joint[GB + s] = right[G0N[s]]
    rate = 0.5 * ADVECTION
    for k in range(4):
        s = KIND[k]
        add_a = -rate * left[F_LAST] * right[F_FIRST + k]
        add_b = rate * right[F_FIRST] * left[F_LAST + k]
        e = ratio[s] * (left[GNN[s]] * add_a - right[G00[s]] * add_b)
        joint[CA + k] = add_a - e
        joint[CB + k] = add_b + e
    width = out.shape[2]
    new = {}
    for s in range(2):
        a, b, r = left[G0N[s]], right[G0N[s]], ratio[s]
        new[G00[s]] = left[G00[s]] - r * a * a
        new[GNN[s]] = right[GNN[s]] - r * b * b
        new[G0N[s]] = r * a * b
    new[V_FIRST] = left[V_FIRST]
    new[V_LAST] = right[V_LAST]
    for k in range(4):
        new[F_FIRST + k] = left[F_FIRST + k]
        new[F_LAST + k] = right[F_LAST + k]
    if last:
        below = side_bit(level + 1)
        pairs = [(GNN[0], G00[0]), (GNN[1], G00[1]), (V_LAST, V_FIRST)]
        pairs += [(F_LAST + k, F_FIRST + k) for k in range(4)]
        result = [jnp.where(below, new[x], new[y]) for x, y in pairs]
    else:
        result = [new[plane] for plane in range(PLANES)]
    for plane, x in enumerate(result):
        if halve:
            x = jnp.where(low_side, x[:, :width], x[:, width:])
        out[plane] = x


def top_kernel(level, own, other, joint):
    low_side = side_bit(level)
    face = own[2] + other[2]
    rate = 0.5 * ADVECTION
    mine = jnp.where(low_side, -rate, rate) * own[3]
    theirs = jnp.where(low_side, rate, -rate) * other[3]
    ratio = []
    for s in range(2):
        resist = 1.0 / ((0.5 * STIFF * SCALES[s]) * face)
        r = 1.0 / (resist + own[s] + other[s])
        ratio.append(r)
        joint[s] = r
    for k in range(4):
        s = KIND[k]
        add = mine * other[3 + k]
        far = theirs * own[3 + k]
        joint[2 + k] = add - ratio[s] * (own[s] * add - other[s] * far)


def source_kernel(rows, count, early, src, cpr, add, t):
    ny, nz = src.shape[2], src.shape[3]
    sub = lax.broadcasted_iota(jnp.int32, (ny, nz), 0)
    top, low = sub == ny - 1, sub == 0

    def down(ref, shift):
        def row(i, carry):
            prev = jnp.maximum(i - 1, 0)
            new = []
            for k in range(4):
                a = jnp.broadcast_to(add[k, pl.ds(i, 1), :], (ny, nz))
                b = jnp.broadcast_to(add[4 + k, pl.ds(i, 1), :], (ny, nz))
                x = ref[k, i - shift] + jnp.where(low, a, jnp.where(top, b, 0.0))
                x = x + cpr[KIND[k], prev] * carry[k]
                t[k, i] = x
                new.append(x)
            return tuple(new)

        return row

    state = (jnp.zeros((ny, nz), F32),) * 4
    state = lax.fori_loop(0, count, down(early, 0), state)
    lax.fori_loop(count, rows, down(src, count), state)


def back_kernel(rows, t, inv, cpr, part):
    end = rows - 1
    start = []
    for k in range(4):
        x = inv[KIND[k], end] * t[k, end]
        part[k, end] = x
        start.append(x)

    def row(j, carry):
        i = end - 1 - j
        new = []
        for k in range(4):
            s = KIND[k]
            x = inv[s, i] * t[k, i] + cpr[s, i] * carry[k]
            part[k, i] = x
            new.append(x)
        return tuple(new)

    lax.fori_loop(0, end, row, tuple(start))


def up_kernel(level, halve, last, own, other, joint, *refs):
    out, diff = refs[-2:]
    low_side = side_bit(level)
    width = out.shape[2]
    for k in range(4):
        s = KIND[k]
        far_left = jnp.where(low_side, own[k], other[k])
        far_right = jnp.where(low_side, other[4 + k], own[4 + k])
        d = jnp.where(low_side, own[4 + k] - other[k], other[4 + k] - own[k])
        diff[k] = d
        flow = joint[R_ + s] * d
        first = far_left + joint[GA + s] * (joint[CA + k] - flow)
        end = far_right + joint[GB + s] * (joint[CB + k] + flow)
        if last:
            ends = [(k, jnp.where(side_bit(level + 1), end, first))]
        else:
            ends = [(k, first), (4 + k, end)]
        for slot, x in ends:
            if halve:
                x = jnp.where(low_side, x[:, :width], x[:, width:])
            out[slot] = x


def joint_flow(joint, k, d, into_first, into_last, low_side):
    s = KIND[k]
    flow = joint[R_ + s] * (d + joint[GA + s] * into_first - joint[GB + s] * into_last)
    first = jnp.where(low_side, into_first, joint[CB + k] + flow)
    last = jnp.where(low_side, joint[CA + k] - flow, into_last)
    return first, last


def down_kernel(levels, own, other, top, *refs):
    joints = refs[: levels - 2]
    diffs = refs[levels - 2 : 2 * levels - 4]
    out = refs[2 * levels - 4]
    low_side = side_bit(levels - 1)
    for k in range(4):
        d = jnp.where(low_side, own[k] - other[k], other[k] - own[k])
        flow = top[KIND[k]] * d
        facing = top[2 + k] + jnp.where(low_side, -flow, flow)
        zero = jnp.zeros_like(facing)
        first = jnp.where(low_side, zero, facing)
        last = jnp.where(low_side, facing, zero)
        for level in range(levels - 2, 0, -1):
            first, last = joint_flow(
                joints[level - 1], k, diffs[level - 1][k], first, last, side_bit(level)
            )
        out[k] = first
        out[4 + k] = last


def final_kernel(rows, parts, own, other, joint, diff, part, g0, gn, out, flux, buf, sems):
    bit = jnp.bitwise_and(lax.axis_index("line"), 1)
    low_side = bit == 0
    width = own.shape[2]
    for k in range(8):
        flux[k, :, :width] = jnp.where(low_side, own[k], other[k])
        flux[k, :, width:] = jnp.where(low_side, other[k], own[k])
    for k in range(4):
        first, last = joint_flow(joint, k, diff[k], flux[k], flux[4 + k], low_side)
        flux[k] = first
        flux[4 + k] = last
    copies = []
    for c in range(parts):
        z = pl.ds(c * 128, 128)
        into = [flux[k, :, z] for k in range(8)]
        for i in range(rows):
            a = [g0[s, i, :, z] for s in range(2)]
            b = [gn[s, i, :, z] for s in range(2)]
            for k in range(4):
                s = KIND[k]
                buf[k, i, :, z] = part[k, i, :, z] + (a[s] * into[k] + b[s] * into[4 + k])
        copy = pltpu.make_async_copy(buf.at[:, :, :, z], out.at[:, :, :, z], sems.at[c])
        copy.start()
        copies.append(copy)
    for copy in copies:
        copy.wait()


def local(fields, viscosity):
    rows, ny, nz = viscosity.shape
    lines = lax.axis_size("line")
    cols = lax.axis_size("col")
    levels = lines.bit_length() - 1
    half = nz // 2
    cells = rows * ny * nz
    block = (rows, ny, nz)

    ring = [(i, (i + 1) % cols) for i in range(cols)]
    back_ring = [(b, a) for a, b in ring]

    def swap(x, level):
        return lax.ppermute(x, "line", [(i, i ^ (1 << level)) for i in range(lines)])

    y_first, y_last = call(
        functools.partial(cut_kernel, ny),
        "cut",
        [(5, rows, nz), (5, rows, nz)],
        [fields, viscosity],
        scratch=[pltpu.SemaphoreType.DMA((2, 5))],
        in_hbm=(0, 1),
        moved=2 * cells,
    )
    low = lax.ppermute(y_last, "col", ring)
    high = lax.ppermute(y_first, "col", back_ring)

    visc, inv, cpr, g0, gn, w = call(
        functools.partial(factor_kernel, rows),
        "factor",
        [block] + [(2,) + block] * 4 + [(PLANES, ny, nz)],
        [fields, viscosity],
        scratch=[VMEM((2,) + block, F32), pltpu.SemaphoreType.DMA((3,))],
        in_hbm=(0, 1),
        flops=10**9,
    )
    count = rows // 4
    inner, early = call(
        functools.partial(early_kernel, count),
        "early",
        [(4,) + block, (4, count, ny, nz)],
        [fields, visc],
        scratch=[pltpu.SemaphoreType.DMA((4,))],
        in_hbm=(0,),
        flops=3 * 10**9,
    )
    src, p, ends = call(
        functools.partial(explicit_kernel, count),
        "explicit",
        [(4, rows - count, ny, nz), (8, ny, nz), (8, rows, nz)],
        [inner, visc, g0, gn, early],
        flops=5 * 10**9,
    )
    joints = []
    for level in range(levels - 1):
        width = nz if level == 0 else half
        last = level == levels - 2
        order = [early] if level == 0 else [p] if level == 1 else []
        joint, w = call(
            functools.partial(joint_kernel, level, level == 0, last),
            f"joint{level}",
            [(JOINT, ny, width), (7 if last else PLANES, ny, half)],
            [w, swap(w, level)] + order,
            moved=4 * ny * width * 60,
        )
        joints.append(joint)
    (top,) = call(
        functools.partial(top_kernel, levels - 1),
        "top",
        [(6, ny, half)],
        [w, swap(w, levels - 1)],
        moved=4 * ny * half * 20,
    )

    (add,) = call(
        functools.partial(edge_kernel, rows),
        "edge",
        [(8, rows, nz)],
        [y_first, y_last, low, high],
        flops=8 * cells,
        moved=4 * cells,
    )
    (p,) = call(
        functools.partial(ends_kernel, rows, ny),
        "ends",
        [(8, ny, nz)],
        [add, ends, p, top],
        flops=6 * cells,
        moved=2 * cells,
    )
    (t,) = call(
        functools.partial(source_kernel, rows, count),
        "source",
        [(4,) + block],
        [early, src, cpr, add],
        flops=30 * cells,
        moved=24 * cells,
    )
    (part,) = call(
        functools.partial(back_kernel, rows),
        "back",
        [(4,) + block],
        [t, inv, cpr],
        flops=20 * cells,
        moved=24 * cells,
    )
    diffs = []
    for level in range(levels - 1):
        width = nz if level == 0 else half
        last = level == levels - 2
        first = [t] if level == 0 else []
        p, diff = call(
            functools.partial(up_kernel, level, level == 0, last),
            f"up{level}",
            [(4 if last else 8, ny, half), (4, ny, width)],
            [p, swap(p, level), joints[level]] + first,
            moved=4 * ny * width * 40,
        )
        diffs.append(diff)
    (flux,) = call(
        functools.partial(down_kernel, levels),
        "down",
        [(8, ny, half)],
        [p, swap(p, levels - 1), top] + joints[1:] + diffs[1:],
        moved=4 * ny * half * 60,
    )
    parts = nz // 128
    (out,) = call(
        functools.partial(final_kernel, rows, parts),
        "final",
        [(4,) + block],
        [flux, swap(flux, 0), joints[0], diffs[0], part, g0, gn],
        scratch=[VMEM((8, ny, nz), F32), VMEM((4,) + block, F32), pltpu.SemaphoreType.DMA((parts,))],
        any_out=(0,),
        flops=16 * cells,
        moved=16 * cells,
    )
    return out


def solution(mesh):
    return jax.shard_map(
        local,
        mesh=mesh,
        in_specs=(P(None, "line", "col", None), P("line", "col", None)),
        out_specs=P(None, "line", "col", None),
        check_vma=False,
    )
```

```python
import functools

import jax
import jax.numpy as jnp
from jax import lax
from jax.experimental import pallas as pl
from jax.experimental.pallas import tpu as pltpu
from jax.sharding import PartitionSpec as P

STIFF = 3072
THERMAL_RATIO = 0.8
CROSS_RATE = 0.2
ADVECTION = 0.25
BUOYANCY = 2.0
SCALES = (1.0, THERMAL_RATIO)
KIND = (0, 0, 0, 1)

F32 = jnp.float32
VMEM = pltpu.VMEM
LIMIT = 24 * 1024 * 1024

G00, G0N, GNN = (0, 3), (1, 4), (2, 5)
V_FIRST, V_LAST, F_FIRST, F_LAST = 6, 7, 8, 12
PLANES = 16
R_, GA, GB, CA, CB = 0, 2, 4, 6, 10
JOINT = 14


def in_vmem(x):
    return pltpu.with_memory_space_constraint(x, VMEM)


def spec():
    return pl.BlockSpec(memory_space=VMEM)


def call(kernel, name, out_shapes, args, scratch=(), in_hbm=(), any_out=(), flops=0, moved=0):
    in_specs = []
    operands = []
    for i, x in enumerate(args):
        if i in in_hbm:
            in_specs.append(pl.BlockSpec(memory_space=pltpu.HBM))
            operands.append(pltpu.with_memory_space_constraint(x, pltpu.HBM))
        else:
            in_specs.append(spec())
            operands.append(in_vmem(x))
    out_shape = []
    out_specs = []
    for i, s in enumerate(out_shapes):
        if i in any_out:
            out_shape.append(jax.ShapeDtypeStruct(s, F32))
            out_specs.append(pl.BlockSpec(memory_space=pl.ANY))
        else:
            out_shape.append(VMEM(s, F32))
            out_specs.append(spec())
    return pl.pallas_call(
        kernel,
        out_shape=out_shape,
        in_specs=in_specs,
        out_specs=out_specs,
        scratch_shapes=list(scratch),
        compiler_params=pltpu.CompilerParams(vmem_limit_bytes=LIMIT),
        cost_estimate=pl.CostEstimate(flops=flops, bytes_accessed=moved, transcendentals=0),
        name=name,
    )(*operands)


def layer(read, ny, nz):
    sub = lax.broadcasted_iota(jnp.int32, (8, nz), 0)
    tile = jnp.broadcast_to(read(0), (8, nz))
    for r in range(1, 8):
        tile = jnp.where(sub == r, jnp.broadcast_to(read(r), (8, nz)), tile)
    return tile


def cut_kernel(ny, fields, visc, y_first, y_last, sems):
    copies = []
    for j, (at, out) in enumerate(((0, y_first), (ny - 1, y_last))):
        for k in range(4):
            copies.append(pltpu.make_async_copy(fields.at[k, :, at], out.at[k], sems.at[j, k]))
        copies.append(pltpu.make_async_copy(visc.at[:, at], out.at[4], sems.at[j, 4]))
    for copy in copies:
        copy.start()
    for copy in copies:
        copy.wait()


def factor_kernel(rows, fields_ref, visc_ref, visc, inv, cpr, g0, gn, w, tau, sems):
    copies = [
        pltpu.make_async_copy(visc_ref, visc, sems.at[0]),
        pltpu.make_async_copy(fields_ref.at[:, 0], w.at[F_FIRST : F_FIRST + 4], sems.at[1]),
        pltpu.make_async_copy(fields_ref.at[:, rows - 1], w.at[F_LAST : F_LAST + 4], sems.at[2]),
    ]
    for copy in copies:
        copy.start()
    copies[0].wait()
    ny, nz = visc.shape[1], visc.shape[2]
    me = lax.axis_index("line")
    wall_low = jnp.where(me == 0, 1.0, 0.0).astype(F32)
    wall_high = jnp.where(me == lax.axis_size("line") - 1, 1.0, 0.0).astype(F32)
    one = jnp.ones((ny, nz), F32)

    def row(i, carry):
        low, v = carry[4], carry[5]
        after = visc[jnp.minimum(i + 1, rows - 1)]
        high = jnp.where(i == rows - 1, (0.5 * STIFF) * wall_high * v, (0.5 * STIFF) * (v + after))
        new = []
        for s in range(2):
            gain, running = carry[2 * s], carry[2 * s + 1]
            down = SCALES[s] * low if s else low
            up = SCALES[s] * high if s else high
            q = 1.0 + down * gain
            one_over = 1.0 / (q + up)
            coupling = up * one_over
            inv[s, i] = one_over
            cpr[s, i] = coupling
            tau[s, i] = running
            new += [q * one_over, coupling * running]
        return tuple(new) + (high, after)

    first = visc[0]
    lax.fori_loop(0, rows, row, (one,) * 4 + (wall_low * (0.5 * STIFF) * first, first))

    end = rows - 1
    start = []
    for s in range(2):
        a = inv[s, end] * tau[s, end]
        b = inv[s, end]
        g0[s, end] = a
        gn[s, end] = b
        w[G0N[s]] = a
        w[GNN[s]] = b
        start += [a, b]

    def back(j, carry):
        i = end - 1 - j
        new = []
        for s in range(2):
            c = cpr[s, i]
            a = inv[s, i] * tau[s, i] + c * carry[2 * s]
            b = c * carry[2 * s + 1]
            g0[s, i] = a
            gn[s, i] = b
            new += [a, b]
        return tuple(new)

    final = lax.fori_loop(0, end, back, tuple(start))
    for s in range(2):
        w[G00[s]] = final[2 * s]
    w[V_FIRST] = first
    w[V_LAST] = visc[rows - 1]
    for copy in copies[1:]:
        copy.wait()


def explicit_rows(first, count, fields, visc, src):
    rows, ny, nz = visc.shape
    lane = lax.broadcasted_iota(jnp.int32, (ny, nz), 1)
    sub = lax.broadcasted_iota(jnp.int32, (ny, nz), 0)
    z_top, z_low = lane == nz - 1, lane == 0
    y_top, y_low = sub == ny - 1, sub == 0

    def sides(x):
        return (
            pltpu.roll(x, ny - 1, 0),
            pltpu.roll(x, 1, 0),
            pltpu.roll(x, nz - 1, 1),
            pltpu.roll(x, 1, 1),
        )

    def row(i, _):
        f = [fields[k, i] for k in range(4)]
        v = visc[i]
        after, before = jnp.minimum(i + 1, rows - 1), jnp.maximum(i - 1, 0)
        vyn, vyp, vzn, vzp = sides(v)
        half = 0.5 * CROSS_RATE
        faces = [
            jnp.where(y_top, 0.0, half * (v + vyn)),
            jnp.where(y_low, 0.0, half * (v + vyp)),
            half * (v + jnp.where(z_top, 0.0, vzn)),
            half * (v + jnp.where(z_low, 0.0, vzp)),
        ]
        none = [y_top, y_low, z_top, z_low]
        total = (faces[0] + faces[1]) + (faces[2] + faces[3])
        adv = [(-0.5 * ADVECTION) * f[k] for k in range(3)]
        move = [adv[1], -adv[1], adv[2], -adv[2]]
        adv_after = jnp.where(i == rows - 1, 0.0, adv[0])
        adv_before = jnp.where(i == 0, 0.0, adv[0])
        weights, centre = [], []
        for s in range(2):
            scaled = [SCALES[s] * x if s else x for x in faces]
            weights.append([jnp.where(n, 0.0, x + m) for n, x, m in zip(none, scaled, move)])
            centre.append(1.0 - (SCALES[s] * total if s else total))
        for k in range(4):
            s = KIND[k]
            near = sides(f[k])
            out = centre[s] * f[k] + adv_after * fields[k, after] - adv_before * fields[k, before]
            for c, x in zip(weights[s], near):
                out = out + c * x
            if k == 2:
                out = out + BUOYANCY * f[3]
            src[k, i - first] = out
        return 0

    lax.fori_loop(first, first + count, row, 0)


def early_kernel(count, fields_ref, visc, fields, src, sems):
    rows = visc.shape[0]
    copies = []
    for c in range(rows // count):
        at = pl.ds(c * count, count)
        copies.append(pltpu.make_async_copy(fields_ref.at[:, at], fields.at[:, at], sems.at[c]))
        copies[-1].start()
    for copy in copies[:2]:
        copy.wait()
    explicit_rows(0, count, fields, visc, src)
    for copy in copies[2:]:
        copy.wait()


def explicit_kernel(count, fields, visc, g0, gn, early, src, p, ends):
    rows, ny, nz = visc.shape
    explicit_rows(count, rows - count, fields, visc, src)

    def dot(ref, shift):
        def add(i, carry):
            new = []
            for g, base in ((g0, 0), (gn, 4)):
                for k in range(4):
                    new.append(carry[base + k] + g[KIND[k], i] * ref[k, i - shift])
            return tuple(new)

        return add

    final = (jnp.zeros((ny, nz), F32),) * 8
    final = lax.fori_loop(0, count, dot(early, 0), final)
    final = lax.fori_loop(count, rows, dot(src, count), final)
    for k in range(8):
        p[k] = final[k]

    for s in range(2):
        for side, at in ((0, 0), (1, ny - 1)):
            for which, g in ((0, g0), (1, gn)):
                for lo in range(0, rows, 8):
                    ends[4 * side + 2 * which + s, lo : lo + 8] = layer(
                        lambda r: g[s, lo + r, at : at + 1, :], ny, nz
                    )


def edge_kernel(rows, y_first, y_last, low, high, add):
    nz = add.shape[2]
    rate = 0.5 * ADVECTION
    for side, mine, far, sign in ((0, y_first, low, rate), (4, y_last, high, -rate)):
        for r in range(rows // 8):
            x = pl.ds(r * 8, 8)
            face = (0.5 * CROSS_RATE) * (mine[4, x] + far[4, x])
            faces = (face, THERMAL_RATIO * face)
            adv = sign * mine[1, x]
            both = [adv + c for c in faces]
            for k in range(4):
                s = KIND[k]
                add[side + k, x] = both[s] * far[k, x] - faces[s] * mine[k, x]


def ends_kernel(rows, ny, add, ends, p, tie, out):
    nz = out.shape[2]
    sub = lax.broadcasted_iota(jnp.int32, (ny, 128), 0)
    for j in range(nz // 128):
        z = pl.ds(j * 128, 128)
        sums = []
        for side in (0, 4):
            total = [None] * 8
            for r in range(rows // 8):
                x = pl.ds(r * 8, 8)
                g = [ends[side + q, x, z] for q in range(4)]
                for k in range(4):
                    h = add[side + k, x, z]
                    for slot, c in ((k, g[KIND[k]]), (4 + k, g[2 + KIND[k]])):
                        part = c * h
                        total[slot] = part if total[slot] is None else total[slot] + part
            sums.append(total)
        for slot in range(8):
            add_low = jnp.sum(sums[0][slot], axis=0, keepdims=True)
            add_high = jnp.sum(sums[1][slot], axis=0, keepdims=True)
            both = jnp.where(sub == 0, add_low, jnp.where(sub == ny - 1, add_high, 0.0))
            out[slot, :, z] = p[slot, :, z] + both


def side_bit(level):
    return jnp.bitwise_and(jnp.right_shift(lax.axis_index("line"), level), 1) == 0


def join(left, right):
    face = left[V_LAST] + right[V_FIRST]
    joint, new, ratio = {}, {}, []
    for s in range(2):
        resist = 1.0 / ((0.5 * STIFF * SCALES[s]) * face)
        r = 1.0 / (resist + left[GNN[s]] + right[G00[s]])
        ratio.append(r)
        a, b = left[G0N[s]], right[G0N[s]]
        joint[R_ + s] = r
        joint[GA + s] = a
        joint[GB + s] = b
        new[G00[s]] = left[G00[s]] - r * a * a
        new[GNN[s]] = right[GNN[s]] - r * b * b
        new[G0N[s]] = r * a * b
    rate = 0.5 * ADVECTION
    for k in range(4):
        s = KIND[k]
        add_a = -rate * left[F_LAST] * right[F_FIRST + k]
        add_b = rate * right[F_FIRST] * left[F_LAST + k]
        e = ratio[s] * (left[GNN[s]] * add_a - right[G00[s]] * add_b)
        joint[CA + k] = add_a - e
        joint[CB + k] = add_b + e
        new[F_FIRST + k] = left[F_FIRST + k]
        new[F_LAST + k] = right[F_LAST + k]
    new[V_FIRST] = left[V_FIRST]
    new[V_LAST] = right[V_LAST]
    return joint, new


def sided(low_side, mine, theirs):
    left = {p: jnp.where(low_side, mine[p], theirs[p]) for p in mine}
    right = {p: jnp.where(low_side, theirs[p], mine[p]) for p in mine}
    return left, right


def pair_kernel(own, other, *refs):
    joint, out = refs[-2:]
    low_side = side_bit(0)
    planes = range(PLANES)
    found, new = join(*sided(low_side, {p: own[p] for p in planes}, {p: other[p] for p in planes}))
    for plane in range(JOINT):
        joint[plane] = found[plane]
    width = out.shape[2]
    for plane in planes:
        out[plane] = jnp.where(low_side, new[plane][:, :width], new[plane][:, width:])


def chips_kernel(levels, own, *refs):
    others, joints = refs[: 2 ** (levels - 1) - 1], refs[-(levels - 1) :]
    blocks = [{p: x[p] for p in range(PLANES)} for x in (own, *others)]
    for level in range(1, levels):
        low_side = side_bit(level)
        joined = []
        for j in range(0, len(blocks), 2):
            found, new = join(*sided(low_side, blocks[j], blocks[j + 1]))
            for plane in range(JOINT):
                joints[level - 1][j // 2, plane] = found[plane]
            joined.append(new)
        blocks = joined


def source_kernel(rows, count, early, src, cpr, add, t):
    ny, nz = src.shape[2], src.shape[3]
    sub = lax.broadcasted_iota(jnp.int32, (ny, nz), 0)
    top, low = sub == ny - 1, sub == 0

    def down(ref, shift):
        def row(i, carry):
            prev = jnp.maximum(i - 1, 0)
            new = []
            for k in range(4):
                a = jnp.broadcast_to(add[k, pl.ds(i, 1), :], (ny, nz))
                b = jnp.broadcast_to(add[4 + k, pl.ds(i, 1), :], (ny, nz))
                x = ref[k, i - shift] + jnp.where(low, a, jnp.where(top, b, 0.0))
                x = x + cpr[KIND[k], prev] * carry[k]
                t[k, i] = x
                new.append(x)
            return tuple(new)

        return row

    state = (jnp.zeros((ny, nz), F32),) * 4
    state = lax.fori_loop(0, count, down(early, 0), state)
    lax.fori_loop(count, rows, down(src, count), state)


def back_kernel(rows, t, inv, cpr, part):
    end = rows - 1
    start = []
    for k in range(4):
        x = inv[KIND[k], end] * t[k, end]
        part[k, end] = x
        start.append(x)

    def row(j, carry):
        i = end - 1 - j
        new = []
        for k in range(4):
            s = KIND[k]
            x = inv[s, i] * t[k, i] + cpr[s, i] * carry[k]
            part[k, i] = x
            new.append(x)
        return tuple(new)

    lax.fori_loop(0, end, row, tuple(start))


def up(joint, k, left, right):
    s = KIND[k]
    d = left[4 + k] - right[k]
    flow = joint[R_ + s] * d
    first = left[k] + joint[GA + s] * (joint[CA + k] - flow)
    last = right[4 + k] + joint[GB + s] * (joint[CB + k] + flow)
    return d, first, last


def up_kernel(own, other, joint, *refs):
    out, diff = refs[-2:]
    low_side = side_bit(0)
    width = out.shape[2]
    left, right = sided(low_side, {p: own[p] for p in range(8)}, {p: other[p] for p in range(8)})
    for k in range(4):
        diff[k], first, last = up(joint, k, left, right)
        out[k] = jnp.where(low_side, first[:, :width], first[:, width:])
        out[4 + k] = jnp.where(low_side, last[:, :width], last[:, width:])


def joint_flow(joint, k, d, into_first, into_last, low_side):
    s = KIND[k]
    flow = joint[R_ + s] * (d + joint[GA + s] * into_first - joint[GB + s] * into_last)
    first = jnp.where(low_side, into_first, joint[CB + k] + flow)
    last = jnp.where(low_side, joint[CA + k] - flow, into_last)
    return first, last


def settle_kernel(levels, own, *refs):
    others, joints, out = refs[: 2 ** (levels - 1) - 1], refs[-levels:-1], refs[-1]
    blocks = [{p: x[p] for p in range(8)} for x in (own, *others)]
    diffs = []
    for level in range(1, levels):
        low_side = side_bit(level)
        joined = []
        for j in range(0, len(blocks), 2):
            left, right = sided(low_side, blocks[j], blocks[j + 1])
            joint = joints[level - 1].at[j // 2]
            new, across = {}, []
            for k in range(4):
                d, new[k], new[4 + k] = up(joint, k, left, right)
                across.append(d)
            joined.append(new)
            if j == 0:
                diffs.append(across)
        blocks = joined
    for k in range(4):
        first = last = jnp.zeros_like(diffs[0][0])
        for level in range(levels - 1, 0, -1):
            first, last = joint_flow(
                joints[level - 1].at[0], k, diffs[level - 1][k], first, last, side_bit(level)
            )
        out[k] = first
        out[4 + k] = last


def final_kernel(rows, parts, own, other, joint, diff, part, g0, gn, out, flux, buf, sems):
    bit = jnp.bitwise_and(lax.axis_index("line"), 1)
    low_side = bit == 0
    width = own.shape[2]
    for k in range(8):
        flux[k, :, :width] = jnp.where(low_side, own[k], other[k])
        flux[k, :, width:] = jnp.where(low_side, other[k], own[k])
    for k in range(4):
        first, last = joint_flow(joint, k, diff[k], flux[k], flux[4 + k], low_side)
        flux[k] = first
        flux[4 + k] = last
    copies = []
    for c in range(parts):
        z = pl.ds(c * 128, 128)
        into = [flux[k, :, z] for k in range(8)]
        for i in range(rows):
            a = [g0[s, i, :, z] for s in range(2)]
            b = [gn[s, i, :, z] for s in range(2)]
            for k in range(4):
                s = KIND[k]
                buf[k, i, :, z] = part[k, i, :, z] + (a[s] * into[k] + b[s] * into[4 + k])
        copy = pltpu.make_async_copy(buf.at[:, :, :, z], out.at[:, :, :, z], sems.at[c])
        copy.start()
        copies.append(copy)
    for copy in copies:
        copy.wait()


def local(fields, viscosity):
    rows, ny, nz = viscosity.shape
    lines = lax.axis_size("line")
    cols = lax.axis_size("col")
    levels = lines.bit_length() - 1
    half = nz // 2
    cells = rows * ny * nz
    block = (rows, ny, nz)

    ring = [(i, (i + 1) % cols) for i in range(cols)]
    back_ring = [(b, a) for a, b in ring]

    def gather(x):
        return [
            lax.ppermute(x, "line", [(i, i ^ (d << 1)) for i in range(lines)])
            for d in range(1, lines // 2)
        ]

    def swap(x, level):
        return lax.ppermute(x, "line", [(i, i ^ (1 << level)) for i in range(lines)])

    y_first, y_last = call(
        functools.partial(cut_kernel, ny),
        "cut",
        [(5, rows, nz), (5, rows, nz)],
        [fields, viscosity],
        scratch=[pltpu.SemaphoreType.DMA((2, 5))],
        in_hbm=(0, 1),
        moved=2 * cells,
    )
    low = lax.ppermute(y_last, "col", ring)
    high = lax.ppermute(y_first, "col", back_ring)

    visc, inv, cpr, g0, gn, w = call(
        functools.partial(factor_kernel, rows),
        "factor",
        [block] + [(2,) + block] * 4 + [(PLANES, ny, nz)],
        [fields, viscosity],
        scratch=[VMEM((2,) + block, F32), pltpu.SemaphoreType.DMA((3,))],
        in_hbm=(0, 1),
        flops=10**9,
    )
    count = rows // 4
    inner, early = call(
        functools.partial(early_kernel, count),
        "early",
        [(4,) + block, (4, count, ny, nz)],
        [fields, visc],
        scratch=[pltpu.SemaphoreType.DMA((4,))],
        in_hbm=(0,),
        flops=3 * 10**9,
    )
    src, p, ends = call(
        functools.partial(explicit_kernel, count),
        "explicit",
        [(4, rows - count, ny, nz), (8, ny, nz), (8, rows, nz)],
        [inner, visc, g0, gn, early],
        flops=5 * 10**9,
    )
    pair, w = call(
        pair_kernel,
        "pair",
        [(JOINT, ny, nz), (PLANES, ny, half)],
        [w, swap(w, 0), early],
        moved=4 * ny * nz * 60,
    )
    pairs = lines // 2
    joints = call(
        functools.partial(chips_kernel, levels),
        "chips",
        [(pairs >> level, JOINT, ny, half) for level in range(1, levels)],
        [w] + gather(w) + [p],
        moved=4 * ny * half * 300,
    )

    (add,) = call(
        functools.partial(edge_kernel, rows),
        "edge",
        [(8, rows, nz)],
        [y_first, y_last, low, high],
        flops=8 * cells,
        moved=4 * cells,
    )
    (p,) = call(
        functools.partial(ends_kernel, rows, ny),
        "ends",
        [(8, ny, nz)],
        [add, ends, p, joints[0]],
        flops=6 * cells,
        moved=2 * cells,
    )
    (t,) = call(
        functools.partial(source_kernel, rows, count),
        "source",
        [(4,) + block],
        [early, src, cpr, add],
        flops=30 * cells,
        moved=24 * cells,
    )
    (part,) = call(
        functools.partial(back_kernel, rows),
        "back",
        [(4,) + block],
        [t, inv, cpr],
        flops=20 * cells,
        moved=24 * cells,
    )
    p, diff = call(
        up_kernel,
        "up",
        [(8, ny, half), (4, ny, nz)],
        [p, swap(p, 0), pair, t],
        moved=4 * ny * nz * 40,
    )
    (flux,) = call(
        functools.partial(settle_kernel, levels),
        "settle",
        [(8, ny, half)],
        [p] + gather(p) + list(joints),
        moved=4 * ny * half * 100,
    )
    parts = nz // 128
    (out,) = call(
        functools.partial(final_kernel, rows, parts),
        "final",
        [(4,) + block],
        [flux, swap(flux, 0), pair, diff, part, g0, gn],
        scratch=[VMEM((8, ny, nz), F32), VMEM((4,) + block, F32), pltpu.SemaphoreType.DMA((parts,))],
        any_out=(0,),
        flops=16 * cells,
        moved=16 * cells,
    )
    return out


def solution(mesh):
    return jax.shard_map(
        local,
        mesh=mesh,
        in_specs=(P(None, "line", "col", None), P("line", "col", None)),
        out_specs=P(None, "line", "col", None),
        check_vma=False,
    )
```

```python
import functools

import jax
import jax.numpy as jnp
from jax import lax
from jax.experimental import pallas as pl
from jax.experimental.pallas import tpu as pltpu
from jax.sharding import PartitionSpec as P

STIFF = 3072
THERMAL_RATIO = 0.8
CROSS_RATE = 0.2
ADVECTION = 0.25
BUOYANCY = 2.0
SCALES = (1.0, THERMAL_RATIO)
KIND = (0, 0, 0, 1)

F32 = jnp.float32
VMEM = pltpu.VMEM
LIMIT = 24 * 1024 * 1024

G00, G0N, GNN = (0, 3), (1, 4), (2, 5)
V_FIRST, V_LAST, F_FIRST, F_LAST = 6, 7, 8, 12
PLANES = 16
R_, GA, GB, CA, CB = 0, 2, 4, 6, 10
JOINT = 14


def in_vmem(x):
    return pltpu.with_memory_space_constraint(x, VMEM)


def spec():
    return pl.BlockSpec(memory_space=VMEM)


def call(kernel, name, out_shapes, args, scratch=(), in_hbm=(), any_out=(), flops=0, moved=0):
    in_specs = []
    operands = []
    for i, x in enumerate(args):
        if i in in_hbm:
            in_specs.append(pl.BlockSpec(memory_space=pltpu.HBM))
            operands.append(pltpu.with_memory_space_constraint(x, pltpu.HBM))
        else:
            in_specs.append(spec())
            operands.append(in_vmem(x))
    out_shape = []
    out_specs = []
    for i, s in enumerate(out_shapes):
        if i in any_out:
            out_shape.append(jax.ShapeDtypeStruct(s, F32))
            out_specs.append(pl.BlockSpec(memory_space=pl.ANY))
        else:
            out_shape.append(VMEM(s, F32))
            out_specs.append(spec())
    return pl.pallas_call(
        kernel,
        out_shape=out_shape,
        in_specs=in_specs,
        out_specs=out_specs,
        scratch_shapes=list(scratch),
        compiler_params=pltpu.CompilerParams(vmem_limit_bytes=LIMIT),
        cost_estimate=pl.CostEstimate(flops=flops, bytes_accessed=moved, transcendentals=0),
        name=name,
    )(*operands)


def layer(read, ny, nz):
    sub = lax.broadcasted_iota(jnp.int32, (8, nz), 0)
    tile = jnp.broadcast_to(read(0), (8, nz))
    for r in range(1, 8):
        tile = jnp.where(sub == r, jnp.broadcast_to(read(r), (8, nz)), tile)
    return tile


def cut_kernel(ny, fields, visc, y_first, y_last, sems):
    copies = []
    for j, (at, out) in enumerate(((0, y_first), (ny - 1, y_last))):
        for k in range(4):
            copies.append(pltpu.make_async_copy(fields.at[k, :, at], out.at[k], sems.at[j, k]))
        copies.append(pltpu.make_async_copy(visc.at[:, at], out.at[4], sems.at[j, 4]))
    for copy in copies:
        copy.start()
    for copy in copies:
        copy.wait()


def factor_kernel(rows, fields_ref, visc, inv, cpr, g0, gn, w, tau, sems):
    copies = [
        pltpu.make_async_copy(fields_ref.at[:, 0], w.at[F_FIRST : F_FIRST + 4], sems.at[0]),
        pltpu.make_async_copy(fields_ref.at[:, rows - 1], w.at[F_LAST : F_LAST + 4], sems.at[1]),
    ]
    for copy in copies:
        copy.start()
    ny, nz = visc.shape[1], visc.shape[2]
    me = lax.axis_index("line")
    wall_low = jnp.where(me == 0, 1.0, 0.0).astype(F32)
    wall_high = jnp.where(me == lax.axis_size("line") - 1, 1.0, 0.0).astype(F32)
    one = jnp.ones((ny, nz), F32)

    def row(i, carry):
        low, v = carry[4], carry[5]
        after = visc[jnp.minimum(i + 1, rows - 1)]
        high = jnp.where(i == rows - 1, (0.5 * STIFF) * wall_high * v, (0.5 * STIFF) * (v + after))
        new = []
        for s in range(2):
            gain, running = carry[2 * s], carry[2 * s + 1]
            down = SCALES[s] * low if s else low
            up = SCALES[s] * high if s else high
            q = 1.0 + down * gain
            one_over = 1.0 / (q + up)
            coupling = up * one_over
            inv[s, i] = one_over
            cpr[s, i] = coupling
            tau[s, i] = running
            new += [q * one_over, coupling * running]
        return tuple(new) + (high, after)

    first = visc[0]
    lax.fori_loop(0, rows, row, (one,) * 4 + (wall_low * (0.5 * STIFF) * first, first))

    end = rows - 1
    start = []
    for s in range(2):
        a = inv[s, end] * tau[s, end]
        b = inv[s, end]
        g0[s, end] = a
        gn[s, end] = b
        w[G0N[s]] = a
        w[GNN[s]] = b
        start += [a, b]

    def back(j, carry):
        i = end - 1 - j
        new = []
        for s in range(2):
            c = cpr[s, i]
            a = inv[s, i] * tau[s, i] + c * carry[2 * s]
            b = c * carry[2 * s + 1]
            g0[s, i] = a
            gn[s, i] = b
            new += [a, b]
        return tuple(new)

    final = lax.fori_loop(0, end, back, tuple(start))
    for s in range(2):
        w[G00[s]] = final[2 * s]
    w[V_FIRST] = first
    w[V_LAST] = visc[rows - 1]
    for copy in copies:
        copy.wait()


def explicit_rows(first, count, base, start, fields, visc, src):
    rows, ny, nz = visc.shape
    lane = lax.broadcasted_iota(jnp.int32, (ny, nz), 1)
    sub = lax.broadcasted_iota(jnp.int32, (ny, nz), 0)
    z_top, z_low = lane == nz - 1, lane == 0
    y_top, y_low = sub == ny - 1, sub == 0

    def sides(x):
        return (
            pltpu.roll(x, ny - 1, 0),
            pltpu.roll(x, 1, 0),
            pltpu.roll(x, nz - 1, 1),
            pltpu.roll(x, 1, 1),
        )

    def row(i, _):
        f = [fields[k, i - base] for k in range(4)]
        v = visc[i]
        after, before = jnp.minimum(i + 1, rows - 1), jnp.maximum(i - 1, 0)
        vyn, vyp, vzn, vzp = sides(v)
        half = 0.5 * CROSS_RATE
        faces = [
            jnp.where(y_top, 0.0, half * (v + vyn)),
            jnp.where(y_low, 0.0, half * (v + vyp)),
            half * (v + jnp.where(z_top, 0.0, vzn)),
            half * (v + jnp.where(z_low, 0.0, vzp)),
        ]
        none = [y_top, y_low, z_top, z_low]
        total = (faces[0] + faces[1]) + (faces[2] + faces[3])
        adv = [(-0.5 * ADVECTION) * f[k] for k in range(3)]
        move = [adv[1], -adv[1], adv[2], -adv[2]]
        adv_after = jnp.where(i == rows - 1, 0.0, adv[0])
        adv_before = jnp.where(i == 0, 0.0, adv[0])
        weights, centre = [], []
        for s in range(2):
            scaled = [SCALES[s] * x if s else x for x in faces]
            weights.append([jnp.where(n, 0.0, x + m) for n, x, m in zip(none, scaled, move)])
            centre.append(1.0 - (SCALES[s] * total if s else total))
        for k in range(4):
            s = KIND[k]
            near = sides(f[k])
            out = centre[s] * f[k] + adv_after * fields[k, after - base] - adv_before * fields[k, before - base]
            for c, x in zip(weights[s], near):
                out = out + c * x
            if k == 2:
                out = out + BUOYANCY * f[3]
            src[k, i - start] = out
        return 0

    lax.fori_loop(first, first + count, row, 0)


def early_kernel(count, fields_ref, visc, src, fields, sem):
    copy = pltpu.make_async_copy(fields_ref.at[:, 0 : count + 1], fields, sem)
    copy.start()
    copy.wait()
    explicit_rows(0, count, 0, 0, fields, visc, src)


def explicit_kernel(count, fields_ref, visc, g0, gn, early, src, p, ends, fields, sems):
    rows, ny, nz = visc.shape
    cuts = [count - 1] + list(range(2 * count + 1, rows, count)) + [rows]
    copies = []
    for c, (lo, hi) in enumerate(zip(cuts, cuts[1:])):
        copies.append(
            pltpu.make_async_copy(
                fields_ref.at[:, lo:hi], fields.at[:, lo - cuts[0] : hi - cuts[0]], sems.at[c]
            )
        )
        copies[-1].start()
    for c, copy in enumerate(copies):
        copy.wait()
        explicit_rows((c + 1) * count, count, cuts[0], count, fields, visc, src)

    def dot(ref, shift):
        def add(i, carry):
            new = []
            for g, base in ((g0, 0), (gn, 4)):
                for k in range(4):
                    new.append(carry[base + k] + g[KIND[k], i] * ref[k, i - shift])
            return tuple(new)

        return add

    final = (jnp.zeros((ny, nz), F32),) * 8
    final = lax.fori_loop(0, count, dot(early, 0), final)
    final = lax.fori_loop(count, rows, dot(src, count), final)
    for k in range(8):
        p[k] = final[k]

    for s in range(2):
        for side, at in ((0, 0), (1, ny - 1)):
            for which, g in ((0, g0), (1, gn)):
                for lo in range(0, rows, 8):
                    ends[4 * side + 2 * which + s, lo : lo + 8] = layer(
                        lambda r: g[s, lo + r, at : at + 1, :], ny, nz
                    )


def edge_kernel(rows, y_last, y_first, low, high, add):
    nz = add.shape[2]
    rate = 0.5 * ADVECTION
    for side, mine, far, sign in ((0, y_first, low, rate), (4, y_last, high, -rate)):
        for r in range(rows // 8):
            x = pl.ds(r * 8, 8)
            face = (0.5 * CROSS_RATE) * (mine[4, x] + far[4, x])
            faces = (face, THERMAL_RATIO * face)
            adv = sign * mine[1, x]
            both = [adv + c for c in faces]
            for k in range(4):
                s = KIND[k]
                add[side + k, x] = both[s] * far[k, x] - faces[s] * mine[k, x]


def ends_kernel(rows, ny, add, ends, p, tie, out):
    nz = out.shape[2]
    sub = lax.broadcasted_iota(jnp.int32, (ny, 128), 0)
    for j in range(nz // 128):
        z = pl.ds(j * 128, 128)
        sums = []
        for side in (0, 4):
            total = [None] * 8
            for r in range(rows // 8):
                x = pl.ds(r * 8, 8)
                g = [ends[side + q, x, z] for q in range(4)]
                for k in range(4):
                    h = add[side + k, x, z]
                    for slot, c in ((k, g[KIND[k]]), (4 + k, g[2 + KIND[k]])):
                        part = c * h
                        total[slot] = part if total[slot] is None else total[slot] + part
            sums.append(total)
        for slot in range(8):
            add_low = jnp.sum(sums[0][slot], axis=0, keepdims=True)
            add_high = jnp.sum(sums[1][slot], axis=0, keepdims=True)
            both = jnp.where(sub == 0, add_low, jnp.where(sub == ny - 1, add_high, 0.0))
            out[slot, :, z] = p[slot, :, z] + both


def side_bit(level):
    return jnp.bitwise_and(jnp.right_shift(lax.axis_index("line"), level), 1) == 0


def join(left, right):
    face = left[V_LAST] + right[V_FIRST]
    joint, new, ratio = {}, {}, []
    for s in range(2):
        resist = 1.0 / ((0.5 * STIFF * SCALES[s]) * face)
        r = 1.0 / (resist + left[GNN[s]] + right[G00[s]])
        ratio.append(r)
        a, b = left[G0N[s]], right[G0N[s]]
        joint[R_ + s] = r
        joint[GA + s] = a
        joint[GB + s] = b
        new[G00[s]] = left[G00[s]] - r * a * a
        new[GNN[s]] = right[GNN[s]] - r * b * b
        new[G0N[s]] = r * a * b
    rate = 0.5 * ADVECTION
    for k in range(4):
        s = KIND[k]
        add_a = -rate * left[F_LAST] * right[F_FIRST + k]
        add_b = rate * right[F_FIRST] * left[F_LAST + k]
        e = ratio[s] * (left[GNN[s]] * add_a - right[G00[s]] * add_b)
        joint[CA + k] = add_a - e
        joint[CB + k] = add_b + e
        new[F_FIRST + k] = left[F_FIRST + k]
        new[F_LAST + k] = right[F_LAST + k]
    new[V_FIRST] = left[V_FIRST]
    new[V_LAST] = right[V_LAST]
    return joint, new


def sided(low_side, mine, theirs):
    left = {p: jnp.where(low_side, mine[p], theirs[p]) for p in mine}
    right = {p: jnp.where(low_side, theirs[p], mine[p]) for p in mine}
    return left, right


def pair_kernel(own, other, *refs):
    joint, out = refs[-2:]
    low_side = side_bit(0)
    planes = range(PLANES)
    found, new = join(*sided(low_side, {p: own[p] for p in planes}, {p: other[p] for p in planes}))
    for plane in range(JOINT):
        joint[plane] = found[plane]
    width = out.shape[2]
    for plane in planes:
        out[plane] = jnp.where(low_side, new[plane][:, :width], new[plane][:, width:])


def chips_kernel(levels, own, *refs):
    others, joints = refs[: 2 ** (levels - 1) - 1], refs[-(levels - 1) :]
    blocks = [{p: x[p] for p in range(PLANES)} for x in (own, *others)]
    for level in range(1, levels):
        low_side = side_bit(level)
        joined = []
        for j in range(0, len(blocks), 2):
            found, new = join(*sided(low_side, blocks[j], blocks[j + 1]))
            for plane in range(JOINT):
                joints[level - 1][j // 2, plane] = found[plane]
            joined.append(new)
        blocks = joined


def source_kernel(rows, count, early, src, cpr, add, t):
    ny, nz = src.shape[2], src.shape[3]
    sub = lax.broadcasted_iota(jnp.int32, (ny, nz), 0)
    top, low = sub == ny - 1, sub == 0

    def down(ref, shift):
        def row(i, carry):
            prev = jnp.maximum(i - 1, 0)
            new = []
            for k in range(4):
                a = jnp.broadcast_to(add[k, pl.ds(i, 1), :], (ny, nz))
                b = jnp.broadcast_to(add[4 + k, pl.ds(i, 1), :], (ny, nz))
                x = ref[k, i - shift] + jnp.where(low, a, jnp.where(top, b, 0.0))
                x = x + cpr[KIND[k], prev] * carry[k]
                t[k, i] = x
                new.append(x)
            return tuple(new)

        return row

    state = (jnp.zeros((ny, nz), F32),) * 4
    state = lax.fori_loop(0, count, down(early, 0), state)
    lax.fori_loop(count, rows, down(src, count), state)


def back_kernel(rows, t, inv, cpr, part):
    end = rows - 1
    start = []
    for k in range(4):
        x = inv[KIND[k], end] * t[k, end]
        part[k, end] = x
        start.append(x)

    def row(j, carry):
        i = end - 1 - j
        new = []
        for k in range(4):
            s = KIND[k]
            x = inv[s, i] * t[k, i] + cpr[s, i] * carry[k]
            part[k, i] = x
            new.append(x)
        return tuple(new)

    lax.fori_loop(0, end, row, tuple(start))


def up(joint, k, left, right):
    s = KIND[k]
    d = left[4 + k] - right[k]
    flow = joint[R_ + s] * d
    first = left[k] + joint[GA + s] * (joint[CA + k] - flow)
    last = right[4 + k] + joint[GB + s] * (joint[CB + k] + flow)
    return d, first, last


def up_kernel(own, other, joint, *refs):
    out, diff = refs[-2:]
    low_side = side_bit(0)
    width = out.shape[2]
    left, right = sided(low_side, {p: own[p] for p in range(8)}, {p: other[p] for p in range(8)})
    for k in range(4):
        diff[k], first, last = up(joint, k, left, right)
        out[k] = jnp.where(low_side, first[:, :width], first[:, width:])
        out[4 + k] = jnp.where(low_side, last[:, :width], last[:, width:])


def joint_flow(joint, k, d, into_first, into_last, low_side):
    s = KIND[k]
    flow = joint[R_ + s] * (d + joint[GA + s] * into_first - joint[GB + s] * into_last)
    first = jnp.where(low_side, into_first, joint[CB + k] + flow)
    last = jnp.where(low_side, joint[CA + k] - flow, into_last)
    return first, last


def settle_kernel(levels, own, *refs):
    others, joints, out = refs[: 2 ** (levels - 1) - 1], refs[-levels:-1], refs[-1]
    blocks = [{p: x[p] for p in range(8)} for x in (own, *others)]
    diffs = []
    for level in range(1, levels):
        low_side = side_bit(level)
        joined = []
        for j in range(0, len(blocks), 2):
            left, right = sided(low_side, blocks[j], blocks[j + 1])
            joint = joints[level - 1].at[j // 2]
            new, across = {}, []
            for k in range(4):
                d, new[k], new[4 + k] = up(joint, k, left, right)
                across.append(d)
            joined.append(new)
            if j == 0:
                diffs.append(across)
        blocks = joined
    for k in range(4):
        first = last = jnp.zeros_like(diffs[0][0])
        for level in range(levels - 1, 0, -1):
            first, last = joint_flow(
                joints[level - 1].at[0], k, diffs[level - 1][k], first, last, side_bit(level)
            )
        out[k] = first
        out[4 + k] = last


def final_kernel(rows, parts, own, other, joint, diff, part, g0, gn, out, flux, buf, sems):
    bit = jnp.bitwise_and(lax.axis_index("line"), 1)
    low_side = bit == 0
    width = own.shape[2]
    for k in range(8):
        flux[k, :, :width] = jnp.where(low_side, own[k], other[k])
        flux[k, :, width:] = jnp.where(low_side, other[k], own[k])
    for k in range(4):
        first, last = joint_flow(joint, k, diff[k], flux[k], flux[4 + k], low_side)
        flux[k] = first
        flux[4 + k] = last
    copies = []
    for c in range(parts):
        z = pl.ds(c * 128, 128)
        into = [flux[k, :, z] for k in range(8)]
        for i in range(rows):
            a = [g0[s, i, :, z] for s in range(2)]
            b = [gn[s, i, :, z] for s in range(2)]
            for k in range(4):
                s = KIND[k]
                buf[k, i, :, z] = part[k, i, :, z] + (a[s] * into[k] + b[s] * into[4 + k])
        copy = pltpu.make_async_copy(buf.at[:, :, :, z], out.at[:, :, :, z], sems.at[c])
        copy.start()
        copies.append(copy)
    for copy in copies:
        copy.wait()


def local(fields, viscosity):
    rows, ny, nz = viscosity.shape
    lines = lax.axis_size("line")
    cols = lax.axis_size("col")
    levels = lines.bit_length() - 1
    half = nz // 2
    cells = rows * ny * nz
    block = (rows, ny, nz)

    ring = [(i, (i + 1) % cols) for i in range(cols)]
    back_ring = [(b, a) for a, b in ring]

    def gather(x):
        found = {}
        for d in sorted(range(1, lines // 2), key=lambda d: (-d.bit_count(), d)):
            found[d] = lax.ppermute(x, "line", [(i, i ^ (d << 1)) for i in range(lines)])
        return [found[d] for d in sorted(found)]

    def swap(x, level):
        return lax.ppermute(x, "line", [(i, i ^ (1 << level)) for i in range(lines)])

    y_first, y_last = call(
        functools.partial(cut_kernel, ny),
        "cut",
        [(5, rows, nz), (5, rows, nz)],
        [fields, viscosity],
        scratch=[pltpu.SemaphoreType.DMA((2, 5))],
        in_hbm=(0, 1),
        moved=2 * cells,
    )
    low = lax.ppermute(y_last, "col", ring)
    high = lax.ppermute(y_first, "col", back_ring)

    inv, cpr, g0, gn, w = call(
        functools.partial(factor_kernel, rows),
        "factor",
        [(2,) + block] * 4 + [(PLANES, ny, nz)],
        [fields, viscosity],
        scratch=[VMEM((2,) + block, F32), pltpu.SemaphoreType.DMA((2,))],
        in_hbm=(0,),
        flops=10**9,
    )
    count = rows // 4
    (early,) = call(
        functools.partial(early_kernel, count),
        "early",
        [(4, count, ny, nz)],
        [fields, viscosity],
        scratch=[VMEM((4, count + 1, ny, nz), F32), pltpu.SemaphoreType.DMA],
        in_hbm=(0,),
        flops=4 * 10**9,
    )
    src, p, ends = call(
        functools.partial(explicit_kernel, count),
        "explicit",
        [(4, rows - count, ny, nz), (8, ny, nz), (8, rows, nz)],
        [fields, viscosity, g0, gn, early],
        scratch=[VMEM((4, rows - count + 1, ny, nz), F32), pltpu.SemaphoreType.DMA((3,))],
        in_hbm=(0,),
        flops=5 * 10**9,
    )
    pair, w = call(
        pair_kernel,
        "pair",
        [(JOINT, ny, nz), (PLANES, ny, half)],
        [w, swap(w, 0), early],
        moved=4 * ny * nz * 60,
    )
    pairs = lines // 2
    joints = call(
        functools.partial(chips_kernel, levels),
        "chips",
        [(pairs >> level, JOINT, ny, half) for level in range(1, levels)],
        [w] + gather(w) + [p],
        moved=4 * ny * half * 300,
    )

    (add,) = call(
        functools.partial(edge_kernel, rows),
        "edge",
        [(8, rows, nz)],
        [y_last, y_first, low, high],
        flops=8 * cells,
        moved=4 * cells,
    )
    (p,) = call(
        functools.partial(ends_kernel, rows, ny),
        "ends",
        [(8, ny, nz)],
        [add, ends, p, joints[0]],
        flops=6 * cells,
        moved=2 * cells,
    )
    (t,) = call(
        functools.partial(source_kernel, rows, count),
        "source",
        [(4,) + block],
        [early, src, cpr, add],
        flops=30 * cells,
        moved=24 * cells,
    )
    (part,) = call(
        functools.partial(back_kernel, rows),
        "back",
        [(4,) + block],
        [t, inv, cpr],
        flops=20 * cells,
        moved=24 * cells,
    )
    p, diff = call(
        up_kernel,
        "up",
        [(8, ny, half), (4, ny, nz)],
        [p, swap(p, 0), pair, t],
        moved=4 * ny * nz * 40,
    )
    (flux,) = call(
        functools.partial(settle_kernel, levels),
        "settle",
        [(8, ny, half)],
        [p] + gather(p) + list(joints),
        moved=4 * ny * half * 100,
    )
    parts = nz // 128
    (out,) = call(
        functools.partial(final_kernel, rows, parts),
        "final",
        [(4,) + block],
        [flux, swap(flux, 0), pair, diff, part, g0, gn],
        scratch=[VMEM((8, ny, nz), F32), VMEM((4,) + block, F32), pltpu.SemaphoreType.DMA((parts,))],
        any_out=(0,),
        flops=16 * cells,
        moved=16 * cells,
    )
    return out


def solution(mesh):
    return jax.shard_map(
        local,
        mesh=mesh,
        in_specs=(P(None, "line", "col", None), P("line", "col", None)),
        out_specs=P(None, "line", "col", None),
        check_vma=False,
    )
```

```python
import functools

import jax
import jax.numpy as jnp
from jax import lax
from jax.experimental import pallas as pl
from jax.experimental.pallas import tpu as pltpu
from jax.sharding import PartitionSpec as P

STIFF = 3072
THERMAL_RATIO = 0.8
CROSS_RATE = 0.2
ADVECTION = 0.25
BUOYANCY = 2.0
SCALES = (1.0, THERMAL_RATIO)
KIND = (0, 0, 0, 1)

F32 = jnp.float32
VMEM = pltpu.VMEM
LIMIT = 24 * 1024 * 1024

G00, G0N, GNN = (0, 3), (1, 4), (2, 5)
V_FIRST, V_LAST, F_FIRST, F_LAST = 6, 7, 8, 12
PLANES = 16
R_, GA, GB, CA, CB = 0, 2, 4, 6, 10
JOINT = 14


def in_vmem(x):
    return pltpu.with_memory_space_constraint(x, VMEM)


def spec():
    return pl.BlockSpec(memory_space=VMEM)


def call(kernel, name, out_shapes, args, scratch=(), in_hbm=(), any_out=(), flops=0, moved=0):
    in_specs = []
    operands = []
    for i, x in enumerate(args):
        if i in in_hbm:
            in_specs.append(pl.BlockSpec(memory_space=pltpu.HBM))
            operands.append(pltpu.with_memory_space_constraint(x, pltpu.HBM))
        else:
            in_specs.append(spec())
            operands.append(in_vmem(x))
    out_shape = []
    out_specs = []
    for i, s in enumerate(out_shapes):
        if i in any_out:
            out_shape.append(jax.ShapeDtypeStruct(s, F32))
            out_specs.append(pl.BlockSpec(memory_space=pl.ANY))
        else:
            out_shape.append(VMEM(s, F32))
            out_specs.append(spec())
    return pl.pallas_call(
        kernel,
        out_shape=out_shape,
        in_specs=in_specs,
        out_specs=out_specs,
        scratch_shapes=list(scratch),
        compiler_params=pltpu.CompilerParams(vmem_limit_bytes=LIMIT),
        cost_estimate=pl.CostEstimate(flops=flops, bytes_accessed=moved, transcendentals=0),
        name=name,
    )(*operands)


def layer(read, ny, nz):
    sub = lax.broadcasted_iota(jnp.int32, (8, nz), 0)
    tile = jnp.broadcast_to(read(0), (8, nz))
    for r in range(1, 8):
        tile = jnp.where(sub == r, jnp.broadcast_to(read(r), (8, nz)), tile)
    return tile


def cut_kernel(ny, fields, visc, y_first, y_last, sems):
    copies = []
    for j, (at, out) in enumerate(((0, y_first), (ny - 1, y_last))):
        for k in range(4):
            copies.append(pltpu.make_async_copy(fields.at[k, :, at], out.at[k], sems.at[j, k]))
        copies.append(pltpu.make_async_copy(visc.at[:, at], out.at[4], sems.at[j, 4]))
    for copy in copies:
        copy.start()
    for copy in copies:
        copy.wait()


def factor_kernel(rows, fields_ref, visc, inv, cpr, g0, gn, w, tau, sems):
    copies = [
        pltpu.make_async_copy(fields_ref.at[:, 0], w.at[F_FIRST : F_FIRST + 4], sems.at[0]),
        pltpu.make_async_copy(fields_ref.at[:, rows - 1], w.at[F_LAST : F_LAST + 4], sems.at[1]),
    ]
    for copy in copies:
        copy.start()
    ny, nz = visc.shape[1], visc.shape[2]
    me = lax.axis_index("line")
    wall_low = jnp.where(me == 0, 1.0, 0.0).astype(F32)
    wall_high = jnp.where(me == lax.axis_size("line") - 1, 1.0, 0.0).astype(F32)
    one = jnp.ones((ny, nz), F32)

    def row(i, carry):
        low, v = carry[4], carry[5]
        after = visc[jnp.minimum(i + 1, rows - 1)]
        high = jnp.where(i == rows - 1, (0.5 * STIFF) * wall_high * v, (0.5 * STIFF) * (v + after))
        new = []
        for s in range(2):
            gain, running = carry[2 * s], carry[2 * s + 1]
            down = SCALES[s] * low if s else low
            up = SCALES[s] * high if s else high
            q = 1.0 + down * gain
            one_over = 1.0 / (q + up)
            coupling = up * one_over
            inv[s, i] = one_over
            cpr[s, i] = coupling
            tau[s, i] = running
            new += [q * one_over, coupling * running]
        return tuple(new) + (high, after)

    first = visc[0]
    lax.fori_loop(0, rows, row, (one,) * 4 + (wall_low * (0.5 * STIFF) * first, first))

    end = rows - 1
    start = []
    for s in range(2):
        a = inv[s, end] * tau[s, end]
        b = inv[s, end]
        g0[s, end] = a
        gn[s, end] = b
        w[G0N[s]] = a
        w[GNN[s]] = b
        start += [a, b]

    def back(j, carry):
        i = end - 1 - j
        new = []
        for s in range(2):
            c = cpr[s, i]
            a = inv[s, i] * tau[s, i] + c * carry[2 * s]
            b = c * carry[2 * s + 1]
            g0[s, i] = a
            gn[s, i] = b
            new += [a, b]
        return tuple(new)

    final = lax.fori_loop(0, end, back, tuple(start))
    for s in range(2):
        w[G00[s]] = final[2 * s]
    w[V_FIRST] = first
    w[V_LAST] = visc[rows - 1]
    for copy in copies:
        copy.wait()


def explicit_rows(first, count, base, start, fields, visc, src):
    rows, ny, nz = visc.shape
    lane = lax.broadcasted_iota(jnp.int32, (ny, nz), 1)
    sub = lax.broadcasted_iota(jnp.int32, (ny, nz), 0)
    z_top, z_low = lane == nz - 1, lane == 0
    y_top, y_low = sub == ny - 1, sub == 0

    def sides(x):
        return (
            pltpu.roll(x, ny - 1, 0),
            pltpu.roll(x, 1, 0),
            pltpu.roll(x, nz - 1, 1),
            pltpu.roll(x, 1, 1),
        )

    def row(i, _):
        f = [fields[k, i - base] for k in range(4)]
        v = visc[i]
        after, before = jnp.minimum(i + 1, rows - 1), jnp.maximum(i - 1, 0)
        vyn, vyp, vzn, vzp = sides(v)
        half = 0.5 * CROSS_RATE
        faces = [
            jnp.where(y_top, 0.0, half * (v + vyn)),
            jnp.where(y_low, 0.0, half * (v + vyp)),
            half * (v + jnp.where(z_top, 0.0, vzn)),
            half * (v + jnp.where(z_low, 0.0, vzp)),
        ]
        none = [y_top, y_low, z_top, z_low]
        total = (faces[0] + faces[1]) + (faces[2] + faces[3])
        adv = [(-0.5 * ADVECTION) * f[k] for k in range(3)]
        move = [adv[1], -adv[1], adv[2], -adv[2]]
        adv_after = jnp.where(i == rows - 1, 0.0, adv[0])
        adv_before = jnp.where(i == 0, 0.0, adv[0])
        weights, centre = [], []
        for s in range(2):
            scaled = [SCALES[s] * x if s else x for x in faces]
            weights.append([jnp.where(n, 0.0, x + m) for n, x, m in zip(none, scaled, move)])
            centre.append(1.0 - (SCALES[s] * total if s else total))
        for k in range(4):
            s = KIND[k]
            near = sides(f[k])
            out = centre[s] * f[k] + adv_after * fields[k, after - base] - adv_before * fields[k, before - base]
            for c, x in zip(weights[s], near):
                out = out + c * x
            if k == 2:
                out = out + BUOYANCY * f[3]
            src[k, i - start] = out
        return 0

    lax.fori_loop(first, first + count, row, 0)


def early_kernel(count, fields_ref, visc, src, fields, sem):
    copy = pltpu.make_async_copy(fields_ref.at[:, 0 : count + 1], fields, sem)
    copy.start()
    copy.wait()
    explicit_rows(0, count, 0, 0, fields, visc, src)


def explicit_kernel(count, fields_ref, visc, g0, gn, early, src, p, ends, fields, sems):
    rows, ny, nz = visc.shape
    cuts = [count - 1] + list(range(2 * count + 1, rows, count)) + [rows]
    copies = []
    for c, (lo, hi) in enumerate(zip(cuts, cuts[1:])):
        copies.append(
            pltpu.make_async_copy(
                fields_ref.at[:, lo:hi], fields.at[:, lo - cuts[0] : hi - cuts[0]], sems.at[c]
            )
        )
        copies[-1].start()
    for c, copy in enumerate(copies):
        copy.wait()
        explicit_rows((c + 1) * count, count, cuts[0], count, fields, visc, src)

    def dot(ref, shift):
        def add(i, carry):
            new = []
            for g, base in ((g0, 0), (gn, 4)):
                for k in range(4):
                    new.append(carry[base + k] + g[KIND[k], i] * ref[k, i - shift])
            return tuple(new)

        return add

    final = (jnp.zeros((ny, nz), F32),) * 8
    final = lax.fori_loop(0, count, dot(early, 0), final)
    final = lax.fori_loop(count, rows, dot(src, count), final)
    for k in range(8):
        p[k] = final[k]

    for s in range(2):
        for side, at in ((0, 0), (1, ny - 1)):
            for which, g in ((0, g0), (1, gn)):
                for lo in range(0, rows, 8):
                    ends[4 * side + 2 * which + s, lo : lo + 8] = layer(
                        lambda r: g[s, lo + r, at : at + 1, :], ny, nz
                    )


def edge_kernel(rows, y_last, y_first, low, high, add):
    nz = add.shape[2]
    rate = 0.5 * ADVECTION
    for side, mine, far, sign in ((0, y_first, low, rate), (4, y_last, high, -rate)):
        for r in range(rows // 8):
            x = pl.ds(r * 8, 8)
            face = (0.5 * CROSS_RATE) * (mine[4, x] + far[4, x])
            faces = (face, THERMAL_RATIO * face)
            adv = sign * mine[1, x]
            both = [adv + c for c in faces]
            for k in range(4):
                s = KIND[k]
                add[side + k, x] = both[s] * far[k, x] - faces[s] * mine[k, x]


def ends_kernel(rows, ny, add, ends, p, tie, out):
    nz = out.shape[2]
    sub = lax.broadcasted_iota(jnp.int32, (ny, 128), 0)
    for j in range(nz // 128):
        z = pl.ds(j * 128, 128)
        sums = []
        for side in (0, 4):
            total = [None] * 8
            for r in range(rows // 8):
                x = pl.ds(r * 8, 8)
                g = [ends[side + q, x, z] for q in range(4)]
                for k in range(4):
                    h = add[side + k, x, z]
                    for slot, c in ((k, g[KIND[k]]), (4 + k, g[2 + KIND[k]])):
                        part = c * h
                        total[slot] = part if total[slot] is None else total[slot] + part
            sums.append(total)
        for slot in range(8):
            add_low = jnp.sum(sums[0][slot], axis=0, keepdims=True)
            add_high = jnp.sum(sums[1][slot], axis=0, keepdims=True)
            both = jnp.where(sub == 0, add_low, jnp.where(sub == ny - 1, add_high, 0.0))
            out[slot, :, z] = p[slot, :, z] + both


def side_bit(level):
    return jnp.bitwise_and(jnp.right_shift(lax.axis_index("line"), level), 1) == 0


def join(left, right):
    face = left[V_LAST] + right[V_FIRST]
    joint, new, ratio = {}, {}, []
    for s in range(2):
        resist = 1.0 / ((0.5 * STIFF * SCALES[s]) * face)
        r = 1.0 / (resist + left[GNN[s]] + right[G00[s]])
        ratio.append(r)
        a, b = left[G0N[s]], right[G0N[s]]
        joint[R_ + s] = r
        joint[GA + s] = a
        joint[GB + s] = b
        new[G00[s]] = left[G00[s]] - r * a * a
        new[GNN[s]] = right[GNN[s]] - r * b * b
        new[G0N[s]] = r * a * b
    rate = 0.5 * ADVECTION
    for k in range(4):
        s = KIND[k]
        add_a = -rate * left[F_LAST] * right[F_FIRST + k]
        add_b = rate * right[F_FIRST] * left[F_LAST + k]
        e = ratio[s] * (left[GNN[s]] * add_a - right[G00[s]] * add_b)
        joint[CA + k] = add_a - e
        joint[CB + k] = add_b + e
        new[F_FIRST + k] = left[F_FIRST + k]
        new[F_LAST + k] = right[F_LAST + k]
    new[V_FIRST] = left[V_FIRST]
    new[V_LAST] = right[V_LAST]
    return joint, new


def sided(low_side, mine, theirs):
    left = {p: jnp.where(low_side, mine[p], theirs[p]) for p in mine}
    right = {p: jnp.where(low_side, theirs[p], mine[p]) for p in mine}
    return left, right


def pair_kernel(own, other, *refs):
    joint, out = refs[-2:]
    low_side = side_bit(0)
    planes = range(PLANES)
    found, new = join(*sided(low_side, {p: own[p] for p in planes}, {p: other[p] for p in planes}))
    for plane in range(JOINT):
        joint[plane] = found[plane]
    width = out.shape[2]
    for plane in planes:
        out[plane] = jnp.where(low_side, new[plane][:, :width], new[plane][:, width:])


def chips_kernel(levels, own, *refs):
    others = refs[: 2 ** (levels - 1) - 1]
    joints = refs[-(2 * levels - 3) : len(refs) - (levels - 2)]
    consts = refs[len(refs) - (levels - 2) :]
    blocks = [{p: x[p] for p in range(PLANES)} for x in (own, *others)]
    zero = jnp.zeros_like(own[0])
    ends = [{p: zero for p in range(8)} for _ in blocks]
    for level in range(1, levels):
        low_side = side_bit(level)
        joined, new_ends = [], []
        for j in range(0, len(blocks), 2):
            found, new = join(*sided(low_side, blocks[j], blocks[j + 1]))
            for plane in range(JOINT):
                joints[level - 1][j // 2, plane] = found[plane]
            joined.append(new)
            if level < levels - 1:
                left, right = sided(low_side, ends[j], ends[j + 1])
                both = {}
                for k in range(4):
                    _, both[k], both[4 + k] = up(found, k, left, right)
                new_ends.append(both)
        blocks, ends = joined, new_ends
        if level < levels - 1:
            for slot, x in enumerate(facing(level + 1, levels, ends[1], False)):
                consts[level - 1][slot] = x


def facing(level, levels, ends, mine):
    if level < levels - 1:
        return [ends[p] for p in range(8)]
    low_side = side_bit(level)
    if not mine:
        low_side = jnp.logical_not(low_side)
    return [jnp.where(low_side, ends[4 + k], ends[k]) for k in range(4)]


def source_kernel(rows, count, early, src, cpr, add, t):
    ny, nz = src.shape[2], src.shape[3]
    sub = lax.broadcasted_iota(jnp.int32, (ny, nz), 0)
    top, low = sub == ny - 1, sub == 0

    def down(ref, shift):
        def row(i, carry):
            prev = jnp.maximum(i - 1, 0)
            new = []
            for k in range(4):
                a = jnp.broadcast_to(add[k, pl.ds(i, 1), :], (ny, nz))
                b = jnp.broadcast_to(add[4 + k, pl.ds(i, 1), :], (ny, nz))
                x = ref[k, i - shift] + jnp.where(low, a, jnp.where(top, b, 0.0))
                x = x + cpr[KIND[k], prev] * carry[k]
                t[k, i] = x
                new.append(x)
            return tuple(new)

        return row

    state = (jnp.zeros((ny, nz), F32),) * 4
    state = lax.fori_loop(0, count, down(early, 0), state)
    lax.fori_loop(count, rows, down(src, count), state)


def back_kernel(rows, t, inv, cpr, part):
    end = rows - 1
    start = []
    for k in range(4):
        x = inv[KIND[k], end] * t[k, end]
        part[k, end] = x
        start.append(x)

    def row(j, carry):
        i = end - 1 - j
        new = []
        for k in range(4):
            s = KIND[k]
            x = inv[s, i] * t[k, i] + cpr[s, i] * carry[k]
            part[k, i] = x
            new.append(x)
        return tuple(new)

    lax.fori_loop(0, end, row, tuple(start))


def up(joint, k, left, right):
    s = KIND[k]
    d = left[4 + k] - right[k]
    flow = joint[R_ + s] * d
    first = left[k] + joint[GA + s] * (joint[CA + k] - flow)
    last = right[4 + k] + joint[GB + s] * (joint[CB + k] + flow)
    return d, first, last


def up_kernel(levels, own, other, joint, *refs):
    joints = refs[: levels - 1]
    out, diff = refs[levels : levels + 2]
    shares = refs[levels + 2 :]
    low_side = side_bit(0)
    width = out.shape[2]
    left, right = sided(low_side, {p: own[p] for p in range(8)}, {p: other[p] for p in range(8)})
    ends = {}
    for k in range(4):
        diff[k], first, last = up(joint, k, left, right)
        ends[k] = jnp.where(low_side, first[:, :width], first[:, width:])
        ends[4 + k] = jnp.where(low_side, last[:, :width], last[:, width:])
        out[k] = ends[k]
        out[4 + k] = ends[4 + k]
    for level in range(1, levels - 1):
        low_side = side_bit(level)
        joint = joints[level - 1].at[0]
        for k in range(4):
            s = KIND[k]
            first, last = ends[k], ends[4 + k]
            flow = joint[R_ + s] * jnp.where(low_side, last, -first)
            ends[k] = jnp.where(low_side, first, 0.0) - joint[GA + s] * flow
            ends[4 + k] = jnp.where(low_side, 0.0, last) + joint[GB + s] * flow
        for slot, x in enumerate(facing(level + 1, levels, ends, True)):
            shares[level - 1][slot] = x


def joint_flow(joint, k, d, into_first, into_last, low_side):
    s = KIND[k]
    flow = joint[R_ + s] * (d + joint[GA + s] * into_first - joint[GB + s] * into_last)
    first = jnp.where(low_side, into_first, joint[CB + k] + flow)
    last = jnp.where(low_side, joint[CA + k] - flow, into_last)
    return first, last


def settle_kernel(levels, own, *refs):
    pairs = 2 ** (levels - 1)
    others, refs = refs[: pairs - 1], refs[pairs - 1 :]
    joints, consts, out = refs[: levels - 1], refs[levels - 1 : -1], refs[-1]
    ends = {p: own[p] for p in range(8)}
    diffs = []
    for level in range(1, levels):
        low_side = side_bit(level)
        parts = others[2 ** (level - 1) - 1 : 2**level - 1]
        last_one = level == levels - 1
        beside = {}
        for p in range(4 if last_one and level > 1 else 8):
            total = consts[level - 2][p] if level > 1 else 0.0
            for part in parts:
                total = total + part[p]
            beside[p] = total
        across = []
        if last_one and level > 1:
            for k in range(4):
                x = beside[k]
                across.append(jnp.where(low_side, ends[4 + k] - x, x - ends[k]))
        else:
            left, right = sided(low_side, ends, beside)
            for k in range(4):
                d, ends[k], ends[4 + k] = up(joints[level - 1].at[0], k, left, right)
                across.append(d)
        diffs.append(across)
    for k in range(4):
        first = last = jnp.zeros_like(diffs[0][0])
        for level in range(levels - 1, 0, -1):
            first, last = joint_flow(
                joints[level - 1].at[0], k, diffs[level - 1][k], first, last, side_bit(level)
            )
        out[k] = first
        out[4 + k] = last


def final_kernel(rows, parts, own, other, joint, diff, part, g0, gn, out, flux, buf, sems):
    bit = jnp.bitwise_and(lax.axis_index("line"), 1)
    low_side = bit == 0
    width = own.shape[2]
    for k in range(8):
        flux[k, :, :width] = jnp.where(low_side, own[k], other[k])
        flux[k, :, width:] = jnp.where(low_side, other[k], own[k])
    for k in range(4):
        first, last = joint_flow(joint, k, diff[k], flux[k], flux[4 + k], low_side)
        flux[k] = first
        flux[4 + k] = last
    copies = []
    for c in range(parts):
        z = pl.ds(c * 128, 128)
        into = [flux[k, :, z] for k in range(8)]
        for i in range(rows):
            a = [g0[s, i, :, z] for s in range(2)]
            b = [gn[s, i, :, z] for s in range(2)]
            for k in range(4):
                s = KIND[k]
                buf[k, i, :, z] = part[k, i, :, z] + (a[s] * into[k] + b[s] * into[4 + k])
        copy = pltpu.make_async_copy(buf.at[:, :, :, z], out.at[:, :, :, z], sems.at[c])
        copy.start()
        copies.append(copy)
    for copy in copies:
        copy.wait()


def local(fields, viscosity):
    rows, ny, nz = viscosity.shape
    lines = lax.axis_size("line")
    cols = lax.axis_size("col")
    levels = lines.bit_length() - 1
    half = nz // 2
    cells = rows * ny * nz
    block = (rows, ny, nz)

    ring = [(i, (i + 1) % cols) for i in range(cols)]
    back_ring = [(b, a) for a, b in ring]

    def gather(at_level):
        found = {}
        for d in sorted(range(1, lines // 2), key=lambda d: (-d.bit_count(), d)):
            x = at_level[d.bit_length()]
            found[d] = lax.ppermute(x, "line", [(i, i ^ (d << 1)) for i in range(lines)])
        return [found[d] for d in sorted(found)]

    def swap(x, level):
        return lax.ppermute(x, "line", [(i, i ^ (1 << level)) for i in range(lines)])

    y_first, y_last = call(
        functools.partial(cut_kernel, ny),
        "cut",
        [(5, rows, nz), (5, rows, nz)],
        [fields, viscosity],
        scratch=[pltpu.SemaphoreType.DMA((2, 5))],
        in_hbm=(0, 1),
        moved=2 * cells,
    )
    low = lax.ppermute(y_last, "col", ring)
    high = lax.ppermute(y_first, "col", back_ring)

    inv, cpr, g0, gn, w = call(
        functools.partial(factor_kernel, rows),
        "factor",
        [(2,) + block] * 4 + [(PLANES, ny, nz)],
        [fields, viscosity],
        scratch=[VMEM((2,) + block, F32), pltpu.SemaphoreType.DMA((2,))],
        in_hbm=(0,),
        flops=10**9,
    )
    count = rows // 4
    (early,) = call(
        functools.partial(early_kernel, count),
        "early",
        [(4, count, ny, nz)],
        [fields, viscosity],
        scratch=[VMEM((4, count + 1, ny, nz), F32), pltpu.SemaphoreType.DMA],
        in_hbm=(0,),
        flops=4 * 10**9,
    )
    src, p, ends = call(
        functools.partial(explicit_kernel, count),
        "explicit",
        [(4, rows - count, ny, nz), (8, ny, nz), (8, rows, nz)],
        [fields, viscosity, g0, gn, early],
        scratch=[VMEM((4, rows - count + 1, ny, nz), F32), pltpu.SemaphoreType.DMA((3,))],
        in_hbm=(0,),
        flops=5 * 10**9,
    )
    pair, w = call(
        pair_kernel,
        "pair",
        [(JOINT, ny, nz), (PLANES, ny, half)],
        [w, swap(w, 0), early],
        moved=4 * ny * nz * 60,
    )
    pairs = lines // 2
    widths = [8] * (levels - 3) + [4]
    found = call(
        functools.partial(chips_kernel, levels),
        "chips",
        [(pairs >> level, JOINT, ny, half) for level in range(1, levels)]
        + [(width, ny, half) for width in widths],
        [w] + gather([w] * (levels + 1)) + [p],
        moved=4 * ny * half * 300,
    )
    joints, consts = list(found[: levels - 1]), list(found[levels - 1 :])

    (add,) = call(
        functools.partial(edge_kernel, rows),
        "edge",
        [(8, rows, nz)],
        [y_last, y_first, low, high],
        flops=8 * cells,
        moved=4 * cells,
    )
    (p,) = call(
        functools.partial(ends_kernel, rows, ny),
        "ends",
        [(8, ny, nz)],
        [add, ends, p, joints[0]],
        flops=6 * cells,
        moved=2 * cells,
    )
    (t,) = call(
        functools.partial(source_kernel, rows, count),
        "source",
        [(4,) + block],
        [early, src, cpr, add],
        flops=30 * cells,
        moved=24 * cells,
    )
    (part,) = call(
        functools.partial(back_kernel, rows),
        "back",
        [(4,) + block],
        [t, inv, cpr],
        flops=20 * cells,
        moved=24 * cells,
    )
    p, diff, *shares = call(
        functools.partial(up_kernel, levels),
        "up",
        [(8, ny, half), (4, ny, nz)] + [(width, ny, half) for width in widths],
        [p, swap(p, 0), pair] + joints + [t],
        moved=4 * ny * nz * 40,
    )
    (flux,) = call(
        functools.partial(settle_kernel, levels),
        "settle",
        [(8, ny, half)],
        [p] + gather([None, p] + shares) + joints + consts,
        moved=4 * ny * half * 100,
    )
    parts = nz // 128
    (out,) = call(
        functools.partial(final_kernel, rows, parts),
        "final",
        [(4,) + block],
        [flux, swap(flux, 0), pair, diff, part, g0, gn],
        scratch=[VMEM((8, ny, nz), F32), VMEM((4,) + block, F32), pltpu.SemaphoreType.DMA((parts,))],
        any_out=(0,),
        flops=16 * cells,
        moved=16 * cells,
    )
    return out


def solution(mesh):
    return jax.shard_map(
        local,
        mesh=mesh,
        in_specs=(P(None, "line", "col", None), P("line", "col", None)),
        out_specs=P(None, "line", "col", None),
        check_vma=False,
    )
```

```python
import functools

import jax
import jax.numpy as jnp
from jax import lax
from jax.experimental import pallas as pl
from jax.experimental.pallas import tpu as pltpu
from jax.sharding import PartitionSpec as P

STIFF = 3072
THERMAL_RATIO = 0.8
CROSS_RATE = 0.2
ADVECTION = 0.25
BUOYANCY = 2.0
SCALES = (1.0, THERMAL_RATIO)
KIND = (0, 0, 0, 1)

F32 = jnp.float32
VMEM = pltpu.VMEM
LIMIT = 24 * 1024 * 1024

G00, G0N, GNN = (0, 3), (1, 4), (2, 5)
V_FIRST, V_LAST, F_FIRST, F_LAST = 6, 7, 8, 12
PLANES = 16
R_, GA, GB, CA, CB = 0, 2, 4, 6, 10
JOINT = 14


def in_vmem(x):
    return pltpu.with_memory_space_constraint(x, VMEM)


def spec():
    return pl.BlockSpec(memory_space=VMEM)


def call(kernel, name, out_shapes, args, scratch=(), in_hbm=(), out_hbm=(), aliases={}, flops=0, moved=0):
    in_specs = []
    operands = []
    for i, x in enumerate(args):
        if i in in_hbm:
            in_specs.append(pl.BlockSpec(memory_space=pltpu.HBM))
            operands.append(pltpu.with_memory_space_constraint(x, pltpu.HBM))
        else:
            in_specs.append(spec())
            operands.append(in_vmem(x))
    out_shape = []
    out_specs = []
    for i, s in enumerate(out_shapes):
        if i in out_hbm:
            out_shape.append(pltpu.HBM(s, F32))
            out_specs.append(pl.BlockSpec(memory_space=pltpu.HBM))
        else:
            out_shape.append(VMEM(s, F32))
            out_specs.append(spec())
    return pl.pallas_call(
        kernel,
        out_shape=out_shape,
        in_specs=in_specs,
        out_specs=out_specs,
        scratch_shapes=list(scratch),
        input_output_aliases=aliases,
        compiler_params=pltpu.CompilerParams(vmem_limit_bytes=LIMIT),
        cost_estimate=pl.CostEstimate(flops=flops, bytes_accessed=moved, transcendentals=0),
        name=name,
    )(*operands)


def layer(read, ny, nz):
    sub = lax.broadcasted_iota(jnp.int32, (8, nz), 0)
    tile = jnp.broadcast_to(read(0), (8, nz))
    for r in range(1, 8):
        tile = jnp.where(sub == r, jnp.broadcast_to(read(r), (8, nz)), tile)
    return tile


def cut_kernel(ny, fields, visc, y_first, y_last, sems):
    copies = []
    for j, (at, out) in enumerate(((0, y_first), (ny - 1, y_last))):
        for k in range(4):
            copies.append(pltpu.make_async_copy(fields.at[k, :, at], out.at[k], sems.at[j, k]))
        copies.append(pltpu.make_async_copy(visc.at[:, at], out.at[4], sems.at[j, 4]))
    for copy in copies:
        copy.start()
    for copy in copies:
        copy.wait()


def factor_kernel(rows, fields_ref, visc, inv, cpr, g0, gn, w, tau, sems):
    copies = [
        pltpu.make_async_copy(fields_ref.at[:, 0], w.at[F_FIRST : F_FIRST + 4], sems.at[0]),
        pltpu.make_async_copy(fields_ref.at[:, rows - 1], w.at[F_LAST : F_LAST + 4], sems.at[1]),
    ]
    for copy in copies:
        copy.start()
    ny, nz = visc.shape[1], visc.shape[2]
    me = lax.axis_index("line")
    wall_low = jnp.where(me == 0, 1.0, 0.0).astype(F32)
    wall_high = jnp.where(me == lax.axis_size("line") - 1, 1.0, 0.0).astype(F32)
    one = jnp.ones((ny, nz), F32)

    def row(i, carry):
        low, v = carry[4], carry[5]
        after = visc[jnp.minimum(i + 1, rows - 1)]
        high = jnp.where(i == rows - 1, (0.5 * STIFF) * wall_high * v, (0.5 * STIFF) * (v + after))
        new = []
        for s in range(2):
            gain, running = carry[2 * s], carry[2 * s + 1]
            down = SCALES[s] * low if s else low
            up = SCALES[s] * high if s else high
            q = 1.0 + down * gain
            one_over = 1.0 / (q + up)
            coupling = up * one_over
            inv[s, i] = one_over
            cpr[s, i] = coupling
            tau[s, i] = running
            new += [q * one_over, coupling * running]
        return tuple(new) + (high, after)

    first = visc[0]
    lax.fori_loop(0, rows, row, (one,) * 4 + (wall_low * (0.5 * STIFF) * first, first))

    end = rows - 1
    start = []
    for s in range(2):
        a = inv[s, end] * tau[s, end]
        b = inv[s, end]
        g0[s, end] = a
        gn[s, end] = b
        w[G0N[s]] = a
        w[GNN[s]] = b
        start += [a, b]

    def back(j, carry):
        i = end - 1 - j
        new = []
        for s in range(2):
            c = cpr[s, i]
            a = inv[s, i] * tau[s, i] + c * carry[2 * s]
            b = c * carry[2 * s + 1]
            g0[s, i] = a
            gn[s, i] = b
            new += [a, b]
        return tuple(new)

    final = lax.fori_loop(0, end, back, tuple(start))
    for s in range(2):
        w[G00[s]] = final[2 * s]
    w[V_FIRST] = first
    w[V_LAST] = visc[rows - 1]
    for copy in copies:
        copy.wait()


def explicit_rows(first, count, base, start, fields, visc, src):
    rows, ny, nz = visc.shape
    lane = lax.broadcasted_iota(jnp.int32, (ny, nz), 1)
    sub = lax.broadcasted_iota(jnp.int32, (ny, nz), 0)
    z_top, z_low = lane == nz - 1, lane == 0
    y_top, y_low = sub == ny - 1, sub == 0

    def sides(x):
        return (
            pltpu.roll(x, ny - 1, 0),
            pltpu.roll(x, 1, 0),
            pltpu.roll(x, nz - 1, 1),
            pltpu.roll(x, 1, 1),
        )

    def row(i, _):
        f = [fields[k, i - base] for k in range(4)]
        v = visc[i]
        after, before = jnp.minimum(i + 1, rows - 1), jnp.maximum(i - 1, 0)
        vyn, vyp, vzn, vzp = sides(v)
        half = 0.5 * CROSS_RATE
        faces = [
            jnp.where(y_top, 0.0, half * (v + vyn)),
            jnp.where(y_low, 0.0, half * (v + vyp)),
            half * (v + jnp.where(z_top, 0.0, vzn)),
            half * (v + jnp.where(z_low, 0.0, vzp)),
        ]
        none = [y_top, y_low, z_top, z_low]
        total = (faces[0] + faces[1]) + (faces[2] + faces[3])
        adv = [(-0.5 * ADVECTION) * f[k] for k in range(3)]
        move = [adv[1], -adv[1], adv[2], -adv[2]]
        adv_after = jnp.where(i == rows - 1, 0.0, adv[0])
        adv_before = jnp.where(i == 0, 0.0, adv[0])
        weights, centre = [], []
        for s in range(2):
            scaled = [SCALES[s] * x if s else x for x in faces]
            weights.append([jnp.where(n, 0.0, x + m) for n, x, m in zip(none, scaled, move)])
            centre.append(1.0 - (SCALES[s] * total if s else total))
        for k in range(4):
            s = KIND[k]
            near = sides(f[k])
            out = centre[s] * f[k] + adv_after * fields[k, after - base] - adv_before * fields[k, before - base]
            for c, x in zip(weights[s], near):
                out = out + c * x
            if k == 2:
                out = out + BUOYANCY * f[3]
            src[k, i - start] = out
        return 0

    lax.fori_loop(first, first + count, row, 0)


def early_kernel(count, fields_ref, visc, src, fields, sem):
    copy = pltpu.make_async_copy(fields_ref.at[:, 0 : count + 1], fields, sem)
    copy.start()
    copy.wait()
    explicit_rows(0, count, 0, 0, fields, visc, src)


def explicit_kernel(count, fields_ref, visc, g0, gn, early, src, p, ends, fields, sems):
    rows, ny, nz = visc.shape
    cuts = [count - 1] + list(range(2 * count + 1, rows, count)) + [rows]
    copies = []
    for c, (lo, hi) in enumerate(zip(cuts, cuts[1:])):
        copies.append(
            pltpu.make_async_copy(
                fields_ref.at[:, lo:hi], fields.at[:, lo - cuts[0] : hi - cuts[0]], sems.at[c]
            )
        )
        copies[-1].start()
    for c, copy in enumerate(copies):
        copy.wait()
        explicit_rows((c + 1) * count, count, cuts[0], count, fields, visc, src)

    def dot(ref, shift):
        def add(i, carry):
            new = []
            for g, base in ((g0, 0), (gn, 4)):
                for k in range(4):
                    new.append(carry[base + k] + g[KIND[k], i] * ref[k, i - shift])
            return tuple(new)

        return add

    final = (jnp.zeros((ny, nz), F32),) * 8
    final = lax.fori_loop(0, count, dot(early, 0), final)
    final = lax.fori_loop(count, rows, dot(src, count), final)
    for k in range(8):
        p[k] = final[k]

    for s in range(2):
        for side, at in ((0, 0), (1, ny - 1)):
            for which, g in ((0, g0), (1, gn)):
                for lo in range(0, rows, 8):
                    ends[4 * side + 2 * which + s, lo : lo + 8] = layer(
                        lambda r: g[s, lo + r, at : at + 1, :], ny, nz
                    )


def edge_kernel(rows, y_last, y_first, low, high, add):
    nz = add.shape[2]
    rate = 0.5 * ADVECTION
    for side, mine, far, sign in ((0, y_first, low, rate), (4, y_last, high, -rate)):
        for r in range(rows // 8):
            x = pl.ds(r * 8, 8)
            face = (0.5 * CROSS_RATE) * (mine[4, x] + far[4, x])
            faces = (face, THERMAL_RATIO * face)
            adv = sign * mine[1, x]
            both = [adv + c for c in faces]
            for k in range(4):
                s = KIND[k]
                add[side + k, x] = both[s] * far[k, x] - faces[s] * mine[k, x]


def ends_kernel(rows, ny, add, ends, p, tie, out):
    nz = out.shape[2]
    sub = lax.broadcasted_iota(jnp.int32, (ny, 128), 0)
    for j in range(nz // 128):
        z = pl.ds(j * 128, 128)
        sums = []
        for side in (0, 4):
            total = [None] * 8
            for r in range(rows // 8):
                x = pl.ds(r * 8, 8)
                g = [ends[side + q, x, z] for q in range(4)]
                for k in range(4):
                    h = add[side + k, x, z]
                    for slot, c in ((k, g[KIND[k]]), (4 + k, g[2 + KIND[k]])):
                        part = c * h
                        total[slot] = part if total[slot] is None else total[slot] + part
            sums.append(total)
        for slot in range(8):
            add_low = jnp.sum(sums[0][slot], axis=0, keepdims=True)
            add_high = jnp.sum(sums[1][slot], axis=0, keepdims=True)
            both = jnp.where(sub == 0, add_low, jnp.where(sub == ny - 1, add_high, 0.0))
            out[slot, :, z] = p[slot, :, z] + both


def side_bit(level):
    return jnp.bitwise_and(jnp.right_shift(lax.axis_index("line"), level), 1) == 0


def join(left, right):
    face = left[V_LAST] + right[V_FIRST]
    joint, new, ratio = {}, {}, []
    for s in range(2):
        resist = 1.0 / ((0.5 * STIFF * SCALES[s]) * face)
        r = 1.0 / (resist + left[GNN[s]] + right[G00[s]])
        ratio.append(r)
        a, b = left[G0N[s]], right[G0N[s]]
        joint[R_ + s] = r
        joint[GA + s] = a
        joint[GB + s] = b
        new[G00[s]] = left[G00[s]] - r * a * a
        new[GNN[s]] = right[GNN[s]] - r * b * b
        new[G0N[s]] = r * a * b
    rate = 0.5 * ADVECTION
    for k in range(4):
        s = KIND[k]
        add_a = -rate * left[F_LAST] * right[F_FIRST + k]
        add_b = rate * right[F_FIRST] * left[F_LAST + k]
        e = ratio[s] * (left[GNN[s]] * add_a - right[G00[s]] * add_b)
        joint[CA + k] = add_a - e
        joint[CB + k] = add_b + e
        new[F_FIRST + k] = left[F_FIRST + k]
        new[F_LAST + k] = right[F_LAST + k]
    new[V_FIRST] = left[V_FIRST]
    new[V_LAST] = right[V_LAST]
    return joint, new


def sided(low_side, mine, theirs):
    left = {p: jnp.where(low_side, mine[p], theirs[p]) for p in mine}
    right = {p: jnp.where(low_side, theirs[p], mine[p]) for p in mine}
    return left, right


def pair_kernel(own, other, *refs):
    joint, out = refs[-2:]
    low_side = side_bit(0)
    planes = range(PLANES)
    found, new = join(*sided(low_side, {p: own[p] for p in planes}, {p: other[p] for p in planes}))
    for plane in range(JOINT):
        joint[plane] = found[plane]
    width = out.shape[2]
    for plane in planes:
        out[plane] = jnp.where(low_side, new[plane][:, :width], new[plane][:, width:])


def chips_kernel(levels, own, *refs):
    others = refs[: 2 ** (levels - 1) - 1]
    joints = refs[-(2 * levels - 3) : len(refs) - (levels - 2)]
    consts = refs[len(refs) - (levels - 2) :]
    blocks = [{p: x[p] for p in range(PLANES)} for x in (own, *others)]
    zero = jnp.zeros_like(own[0])
    ends = [{p: zero for p in range(8)} for _ in blocks]
    for level in range(1, levels):
        low_side = side_bit(level)
        joined, new_ends = [], []
        for j in range(0, len(blocks), 2):
            found, new = join(*sided(low_side, blocks[j], blocks[j + 1]))
            for plane in range(JOINT):
                joints[level - 1][j // 2, plane] = found[plane]
            joined.append(new)
            if level < levels - 1:
                left, right = sided(low_side, ends[j], ends[j + 1])
                both = {}
                for k in range(4):
                    _, both[k], both[4 + k] = up(found, k, left, right)
                new_ends.append(both)
        blocks, ends = joined, new_ends
        if level < levels - 1:
            for slot, x in enumerate(facing(level + 1, levels, ends[1], False)):
                consts[level - 1][slot] = x


def facing(level, levels, ends, mine):
    if level < levels - 1:
        return [ends[p] for p in range(8)]
    low_side = side_bit(level)
    if not mine:
        low_side = jnp.logical_not(low_side)
    return [jnp.where(low_side, ends[4 + k], ends[k]) for k in range(4)]


def source_kernel(rows, count, early, src, cpr, add, t):
    ny, nz = src.shape[2], src.shape[3]
    sub = lax.broadcasted_iota(jnp.int32, (ny, nz), 0)
    top, low = sub == ny - 1, sub == 0

    def down(ref, shift):
        def row(i, carry):
            prev = jnp.maximum(i - 1, 0)
            new = []
            for k in range(4):
                a = jnp.broadcast_to(add[k, pl.ds(i, 1), :], (ny, nz))
                b = jnp.broadcast_to(add[4 + k, pl.ds(i, 1), :], (ny, nz))
                x = ref[k, i - shift] + jnp.where(low, a, jnp.where(top, b, 0.0))
                x = x + cpr[KIND[k], prev] * carry[k]
                t[k, i] = x
                new.append(x)
            return tuple(new)

        return row

    state = (jnp.zeros((ny, nz), F32),) * 4
    state = lax.fori_loop(0, count, down(early, 0), state)
    lax.fori_loop(count, rows, down(src, count), state)


def back_kernel(rows, t, inv, cpr, part):
    end = rows - 1
    start = []
    for k in range(4):
        x = inv[KIND[k], end] * t[k, end]
        part[k, end] = x
        start.append(x)

    def row(j, carry):
        i = end - 1 - j
        new = []
        for k in range(4):
            s = KIND[k]
            x = inv[s, i] * t[k, i] + cpr[s, i] * carry[k]
            part[k, i] = x
            new.append(x)
        return tuple(new)

    lax.fori_loop(0, end, row, tuple(start))


def up(joint, k, left, right):
    s = KIND[k]
    d = left[4 + k] - right[k]
    flow = joint[R_ + s] * d
    first = left[k] + joint[GA + s] * (joint[CA + k] - flow)
    last = right[4 + k] + joint[GB + s] * (joint[CB + k] + flow)
    return d, first, last


def up_kernel(levels, own, other, joint, *refs):
    joints = refs[: levels - 1]
    out, diff = refs[levels : levels + 2]
    shares = refs[levels + 2 :]
    low_side = side_bit(0)
    width = out.shape[2]
    left, right = sided(low_side, {p: own[p] for p in range(8)}, {p: other[p] for p in range(8)})
    ends = {}
    for k in range(4):
        diff[k], first, last = up(joint, k, left, right)
        ends[k] = jnp.where(low_side, first[:, :width], first[:, width:])
        ends[4 + k] = jnp.where(low_side, last[:, :width], last[:, width:])
        out[k] = ends[k]
        out[4 + k] = ends[4 + k]
    for level in range(1, levels - 1):
        low_side = side_bit(level)
        joint = joints[level - 1].at[0]
        for k in range(4):
            s = KIND[k]
            first, last = ends[k], ends[4 + k]
            flow = joint[R_ + s] * jnp.where(low_side, last, -first)
            ends[k] = jnp.where(low_side, first, 0.0) - joint[GA + s] * flow
            ends[4 + k] = jnp.where(low_side, 0.0, last) + joint[GB + s] * flow
        for slot, x in enumerate(facing(level + 1, levels, ends, True)):
            shares[level - 1][slot] = x


def joint_flow(joint, k, d, into_first, into_last, low_side):
    s = KIND[k]
    flow = joint[R_ + s] * (d + joint[GA + s] * into_first - joint[GB + s] * into_last)
    first = jnp.where(low_side, into_first, joint[CB + k] + flow)
    last = jnp.where(low_side, joint[CA + k] - flow, into_last)
    return first, last


def settle_kernel(levels, own, *refs):
    pairs = 2 ** (levels - 1)
    others, refs = refs[: pairs - 1], refs[pairs - 1 :]
    joints, consts, out = refs[: levels - 1], refs[levels - 1 : -1], refs[-1]
    ends = {p: own[p] for p in range(8)}
    diffs = []
    for level in range(1, levels):
        low_side = side_bit(level)
        parts = others[2 ** (level - 1) - 1 : 2**level - 1]
        last_one = level == levels - 1
        beside = {}
        for p in range(4 if last_one and level > 1 else 8):
            total = consts[level - 2][p] if level > 1 else 0.0
            for part in parts:
                total = total + part[p]
            beside[p] = total
        across = []
        if last_one and level > 1:
            for k in range(4):
                x = beside[k]
                across.append(jnp.where(low_side, ends[4 + k] - x, x - ends[k]))
        else:
            left, right = sided(low_side, ends, beside)
            for k in range(4):
                d, ends[k], ends[4 + k] = up(joints[level - 1].at[0], k, left, right)
                across.append(d)
        diffs.append(across)
    for k in range(4):
        first = last = jnp.zeros_like(diffs[0][0])
        for level in range(levels - 1, 0, -1):
            first, last = joint_flow(
                joints[level - 1].at[0], k, diffs[level - 1][k], first, last, side_bit(level)
            )
        out[k] = first
        out[4 + k] = last


def final_kernel(mine, flux, joint, diff, part, g0, gn, *refs):
    out, buf, sems = refs[-3:]
    rows, half = buf.shape[1], buf.shape[3]
    low_side = side_bit(0)
    core = jnp.bitwise_and(lax.axis_index("line"), 1)
    offset = (core if mine else 1 - core) * half
    copies = []
    for c in range(half // 128):
        near = pl.ds(c * 128, 128)
        z = pl.ds(pl.multiple_of(offset + c * 128, 128), 128)
        across = {plane: joint[plane, :, z] for plane in range(JOINT)}
        into = [
            joint_flow(across, k, diff[k, :, z], flux[k, :, near], flux[4 + k, :, near], low_side)
            for k in range(4)
        ]
        for i in range(rows):
            a = [g0[s, i, :, z] for s in range(2)]
            b = [gn[s, i, :, z] for s in range(2)]
            for k in range(4):
                s = KIND[k]
                buf[k, i, :, near] = part[k, i, :, z] + (a[s] * into[k][0] + b[s] * into[k][1])
        copies.append(pltpu.make_async_copy(buf.at[:, :, :, near], out.at[:, :, :, z], sems.at[c]))
        copies[-1].start()
    for copy in copies:
        copy.wait()


def local(fields, viscosity):
    rows, ny, nz = viscosity.shape
    lines = lax.axis_size("line")
    cols = lax.axis_size("col")
    levels = lines.bit_length() - 1
    half = nz // 2
    cells = rows * ny * nz
    block = (rows, ny, nz)

    ring = [(i, (i + 1) % cols) for i in range(cols)]
    back_ring = [(b, a) for a, b in ring]

    def gather(at_level):
        found = {}
        for d in sorted(range(1, lines // 2), key=lambda d: (-d.bit_count(), d)):
            x = at_level[d.bit_length()]
            found[d] = lax.ppermute(x, "line", [(i, i ^ (d << 1)) for i in range(lines)])
        return [found[d] for d in sorted(found)]

    def swap(x, level):
        return lax.ppermute(x, "line", [(i, i ^ (1 << level)) for i in range(lines)])

    y_first, y_last = call(
        functools.partial(cut_kernel, ny),
        "cut",
        [(5, rows, nz), (5, rows, nz)],
        [fields, viscosity],
        scratch=[pltpu.SemaphoreType.DMA((2, 5))],
        in_hbm=(0, 1),
        moved=2 * cells,
    )
    low = lax.ppermute(y_last, "col", ring)
    high = lax.ppermute(y_first, "col", back_ring)

    inv, cpr, g0, gn, w = call(
        functools.partial(factor_kernel, rows),
        "factor",
        [(2,) + block] * 4 + [(PLANES, ny, nz)],
        [fields, viscosity],
        scratch=[VMEM((2,) + block, F32), pltpu.SemaphoreType.DMA((2,))],
        in_hbm=(0,),
        flops=10**9,
    )
    count = rows // 4
    (early,) = call(
        functools.partial(early_kernel, count),
        "early",
        [(4, count, ny, nz)],
        [fields, viscosity],
        scratch=[VMEM((4, count + 1, ny, nz), F32), pltpu.SemaphoreType.DMA],
        in_hbm=(0,),
        flops=4 * 10**9,
    )
    src, p, ends = call(
        functools.partial(explicit_kernel, count),
        "explicit",
        [(4, rows - count, ny, nz), (8, ny, nz), (8, rows, nz)],
        [fields, viscosity, g0, gn, early],
        scratch=[VMEM((4, rows - count + 1, ny, nz), F32), pltpu.SemaphoreType.DMA((3,))],
        in_hbm=(0,),
        flops=5 * 10**9,
    )
    pair, w = call(
        pair_kernel,
        "pair",
        [(JOINT, ny, nz), (PLANES, ny, half)],
        [w, swap(w, 0), early],
        moved=4 * ny * nz * 60,
    )
    pairs = lines // 2
    widths = [8] * (levels - 3) + [4]
    found = call(
        functools.partial(chips_kernel, levels),
        "chips",
        [(pairs >> level, JOINT, ny, half) for level in range(1, levels)]
        + [(width, ny, half) for width in widths],
        [w] + gather([w] * (levels + 1)) + [p],
        moved=4 * ny * half * 300,
    )
    joints, consts = list(found[: levels - 1]), list(found[levels - 1 :])

    (add,) = call(
        functools.partial(edge_kernel, rows),
        "edge",
        [(8, rows, nz)],
        [y_last, y_first, low, high],
        flops=8 * cells,
        moved=4 * cells,
    )
    (p,) = call(
        functools.partial(ends_kernel, rows, ny),
        "ends",
        [(8, ny, nz)],
        [add, ends, p, joints[0]],
        flops=6 * cells,
        moved=2 * cells,
    )
    (t,) = call(
        functools.partial(source_kernel, rows, count),
        "source",
        [(4,) + block],
        [early, src, cpr, add],
        flops=30 * cells,
        moved=24 * cells,
    )
    (part,) = call(
        functools.partial(back_kernel, rows),
        "back",
        [(4,) + block],
        [t, inv, cpr],
        flops=20 * cells,
        moved=24 * cells,
    )
    p, diff, *shares = call(
        functools.partial(up_kernel, levels),
        "up",
        [(8, ny, half), (4, ny, nz)] + [(width, ny, half) for width in widths],
        [p, swap(p, 0), pair] + joints + [part],
        moved=4 * ny * nz * 40,
    )
    (flux,) = call(
        functools.partial(settle_kernel, levels),
        "settle",
        [(8, ny, half)],
        [p] + gather([None, p] + shares) + joints + consts,
        moved=4 * ny * half * 100,
    )
    rest = [pair, diff, part, g0, gn]
    scratch = [VMEM((4, rows, ny, half), F32), pltpu.SemaphoreType.DMA((half // 128,))]
    (out,) = call(
        functools.partial(final_kernel, True),
        "final_own",
        [(4,) + block],
        [flux] + rest,
        scratch=scratch,
        out_hbm=(0,),
        flops=10**9,
    )
    (out,) = call(
        functools.partial(final_kernel, False),
        "final_other",
        [(4,) + block],
        [swap(flux, 0)] + rest + [out],
        scratch=scratch,
        in_hbm=(6,),
        out_hbm=(0,),
        aliases={6: 0},
        flops=10**9,
    )
    return out


def solution(mesh):
    return jax.shard_map(
        local,
        mesh=mesh,
        in_specs=(P(None, "line", "col", None), P("line", "col", None)),
        out_specs=P(None, "line", "col", None),
        check_vma=False,
    )
```

```python
import functools

import jax
import jax.numpy as jnp
from jax import lax
from jax.experimental import pallas as pl
from jax.experimental.pallas import tpu as pltpu
from jax.sharding import PartitionSpec as P

STIFF = 3072
THERMAL_RATIO = 0.8
CROSS_RATE = 0.2
ADVECTION = 0.25
BUOYANCY = 2.0
SCALES = (1.0, THERMAL_RATIO)
KIND = (0, 0, 0, 1)

F32 = jnp.float32
VMEM = pltpu.VMEM
LIMIT = 24 * 1024 * 1024

G00, G0N, GNN = (0, 3), (1, 4), (2, 5)
V_FIRST, V_LAST, F_FIRST, F_LAST = 6, 7, 8, 12
PLANES = 16
R_, GA, GB, CA, CB = 0, 2, 4, 6, 10
JOINT = 14


def in_vmem(x):
    return pltpu.with_memory_space_constraint(x, VMEM)


def spec():
    return pl.BlockSpec(memory_space=VMEM)


def call(kernel, name, out_shapes, args, scratch=(), in_hbm=(), out_hbm=(), aliases={}, flops=0, moved=0):
    in_specs = []
    operands = []
    for i, x in enumerate(args):
        if i in in_hbm:
            in_specs.append(pl.BlockSpec(memory_space=pltpu.HBM))
            operands.append(pltpu.with_memory_space_constraint(x, pltpu.HBM))
        else:
            in_specs.append(spec())
            operands.append(in_vmem(x))
    out_shape = []
    out_specs = []
    for i, s in enumerate(out_shapes):
        if i in out_hbm:
            out_shape.append(pltpu.HBM(s, F32))
            out_specs.append(pl.BlockSpec(memory_space=pltpu.HBM))
        else:
            out_shape.append(VMEM(s, F32))
            out_specs.append(spec())
    return pl.pallas_call(
        kernel,
        out_shape=out_shape,
        in_specs=in_specs,
        out_specs=out_specs,
        scratch_shapes=list(scratch),
        input_output_aliases=aliases,
        compiler_params=pltpu.CompilerParams(vmem_limit_bytes=LIMIT),
        cost_estimate=pl.CostEstimate(flops=flops, bytes_accessed=moved, transcendentals=0),
        name=name,
    )(*operands)


def layer(read, ny, nz):
    sub = lax.broadcasted_iota(jnp.int32, (8, nz), 0)
    tile = jnp.broadcast_to(read(0), (8, nz))
    for r in range(1, 8):
        tile = jnp.where(sub == r, jnp.broadcast_to(read(r), (8, nz)), tile)
    return tile


def cut_kernel(ny, fields, visc, y_first, y_last, sems):
    copies = []
    for j, (at, out) in enumerate(((0, y_first), (ny - 1, y_last))):
        for k in range(4):
            copies.append(pltpu.make_async_copy(fields.at[k, :, at], out.at[k], sems.at[j, k]))
        copies.append(pltpu.make_async_copy(visc.at[:, at], out.at[4], sems.at[j, 4]))
    for copy in copies:
        copy.start()
    for copy in copies:
        copy.wait()


def factor_kernel(rows, fields_ref, visc, inv, cpr, g0, gn, w, tau, sems):
    copies = [
        pltpu.make_async_copy(fields_ref.at[:, 0], w.at[F_FIRST : F_FIRST + 4], sems.at[0]),
        pltpu.make_async_copy(fields_ref.at[:, rows - 1], w.at[F_LAST : F_LAST + 4], sems.at[1]),
    ]
    for copy in copies:
        copy.start()
    ny, nz = visc.shape[1], visc.shape[2]
    me = lax.axis_index("line")
    wall_low = jnp.where(me == 0, 1.0, 0.0).astype(F32)
    wall_high = jnp.where(me == lax.axis_size("line") - 1, 1.0, 0.0).astype(F32)
    one = jnp.ones((ny, nz), F32)

    def row(i, carry):
        low, v = carry[4], carry[5]
        after = visc[jnp.minimum(i + 1, rows - 1)]
        high = jnp.where(i == rows - 1, (0.5 * STIFF) * wall_high * v, (0.5 * STIFF) * (v + after))
        new = []
        for s in range(2):
            gain, running = carry[2 * s], carry[2 * s + 1]
            down = SCALES[s] * low if s else low
            up = SCALES[s] * high if s else high
            q = 1.0 + down * gain
            one_over = 1.0 / (q + up)
            coupling = up * one_over
            inv[s, i] = one_over
            cpr[s, i] = coupling
            tau[s, i] = running
            new += [q * one_over, coupling * running]
        return tuple(new) + (high, after)

    first = visc[0]
    lax.fori_loop(0, rows, row, (one,) * 4 + (wall_low * (0.5 * STIFF) * first, first))

    end = rows - 1
    start = []
    for s in range(2):
        a = inv[s, end] * tau[s, end]
        b = inv[s, end]
        g0[s, end] = a
        gn[s, end] = b
        w[G0N[s]] = a
        w[GNN[s]] = b
        start += [a, b]

    def back(j, carry):
        i = end - 1 - j
        new = []
        for s in range(2):
            c = cpr[s, i]
            a = inv[s, i] * tau[s, i] + c * carry[2 * s]
            b = c * carry[2 * s + 1]
            g0[s, i] = a
            gn[s, i] = b
            new += [a, b]
        return tuple(new)

    final = lax.fori_loop(0, end, back, tuple(start))
    for s in range(2):
        w[G00[s]] = final[2 * s]
    w[V_FIRST] = first
    w[V_LAST] = visc[rows - 1]
    for copy in copies:
        copy.wait()


def explicit_rows(first, count, base, start, fields, visc, src):
    rows, ny, nz = visc.shape
    lane = lax.broadcasted_iota(jnp.int32, (ny, nz), 1)
    sub = lax.broadcasted_iota(jnp.int32, (ny, nz), 0)
    z_top, z_low = lane == nz - 1, lane == 0
    y_top, y_low = sub == ny - 1, sub == 0

    def sides(x):
        return (
            pltpu.roll(x, ny - 1, 0),
            pltpu.roll(x, 1, 0),
            pltpu.roll(x, nz - 1, 1),
            pltpu.roll(x, 1, 1),
        )

    def row(i, _):
        f = [fields[k, i - base] for k in range(4)]
        v = visc[i]
        after, before = jnp.minimum(i + 1, rows - 1), jnp.maximum(i - 1, 0)
        vyn, vyp, vzn, vzp = sides(v)
        half = 0.5 * CROSS_RATE
        faces = [
            jnp.where(y_top, 0.0, half * (v + vyn)),
            jnp.where(y_low, 0.0, half * (v + vyp)),
            half * (v + jnp.where(z_top, 0.0, vzn)),
            half * (v + jnp.where(z_low, 0.0, vzp)),
        ]
        none = [y_top, y_low, z_top, z_low]
        total = (faces[0] + faces[1]) + (faces[2] + faces[3])
        adv = [(-0.5 * ADVECTION) * f[k] for k in range(3)]
        move = [adv[1], -adv[1], adv[2], -adv[2]]
        adv_after = jnp.where(i == rows - 1, 0.0, adv[0])
        adv_before = jnp.where(i == 0, 0.0, adv[0])
        weights, centre = [], []
        for s in range(2):
            scaled = [SCALES[s] * x if s else x for x in faces]
            weights.append([jnp.where(n, 0.0, x + m) for n, x, m in zip(none, scaled, move)])
            centre.append(1.0 - (SCALES[s] * total if s else total))
        for k in range(4):
            s = KIND[k]
            near = sides(f[k])
            out = centre[s] * f[k] + adv_after * fields[k, after - base] - adv_before * fields[k, before - base]
            for c, x in zip(weights[s], near):
                out = out + c * x
            if k == 2:
                out = out + BUOYANCY * f[3]
            src[k, i - start] = out
        return 0

    lax.fori_loop(first, first + count, row, 0)


def early_kernel(count, fields_ref, visc, src, fields, sem):
    copy = pltpu.make_async_copy(fields_ref.at[:, 0 : count + 1], fields, sem)
    copy.start()
    copy.wait()
    explicit_rows(0, count, 0, 0, fields, visc, src)


def explicit_kernel(count, fields_ref, visc, g0, gn, early, src, p, ends, fields, sems):
    rows, ny, nz = visc.shape
    cuts = [count - 1] + list(range(2 * count + 1, rows, count)) + [rows]
    copies = []
    for c, (lo, hi) in enumerate(zip(cuts, cuts[1:])):
        copies.append(
            pltpu.make_async_copy(
                fields_ref.at[:, lo:hi], fields.at[:, lo - cuts[0] : hi - cuts[0]], sems.at[c]
            )
        )
        copies[-1].start()
    for c, copy in enumerate(copies):
        copy.wait()
        explicit_rows((c + 1) * count, count, cuts[0], count, fields, visc, src)

    def dot(ref, shift):
        def add(i, carry):
            new = []
            for g, base in ((g0, 0), (gn, 4)):
                for k in range(4):
                    new.append(carry[base + k] + g[KIND[k], i] * ref[k, i - shift])
            return tuple(new)

        return add

    final = (jnp.zeros((ny, nz), F32),) * 8
    final = lax.fori_loop(0, count, dot(early, 0), final)
    final = lax.fori_loop(count, rows, dot(src, count), final)
    for k in range(8):
        p[k] = final[k]

    for s in range(2):
        for side, at in ((0, 0), (1, ny - 1)):
            for which, g in ((0, g0), (1, gn)):
                for lo in range(0, rows, 8):
                    ends[4 * side + 2 * which + s, lo : lo + 8] = layer(
                        lambda r: g[s, lo + r, at : at + 1, :], ny, nz
                    )


def edge_kernel(rows, y_last, y_first, low, high, add):
    nz = add.shape[2]
    rate = 0.5 * ADVECTION
    for side, mine, far, sign in ((0, y_first, low, rate), (4, y_last, high, -rate)):
        for r in range(rows // 8):
            x = pl.ds(r * 8, 8)
            face = (0.5 * CROSS_RATE) * (mine[4, x] + far[4, x])
            faces = (face, THERMAL_RATIO * face)
            adv = sign * mine[1, x]
            both = [adv + c for c in faces]
            for k in range(4):
                s = KIND[k]
                add[side + k, x] = both[s] * far[k, x] - faces[s] * mine[k, x]


def ends_kernel(rows, ny, add, ends, p, tie, out):
    nz = out.shape[2]
    sub = lax.broadcasted_iota(jnp.int32, (ny, 128), 0)
    for j in range(nz // 128):
        z = pl.ds(j * 128, 128)
        sums = []
        for side in (0, 4):
            total = [None] * 8
            for r in range(rows // 8):
                x = pl.ds(r * 8, 8)
                g = [ends[side + q, x, z] for q in range(4)]
                for k in range(4):
                    h = add[side + k, x, z]
                    for slot, c in ((k, g[KIND[k]]), (4 + k, g[2 + KIND[k]])):
                        part = c * h
                        total[slot] = part if total[slot] is None else total[slot] + part
            sums.append(total)
        for slot in range(8):
            add_low = jnp.sum(sums[0][slot], axis=0, keepdims=True)
            add_high = jnp.sum(sums[1][slot], axis=0, keepdims=True)
            both = jnp.where(sub == 0, add_low, jnp.where(sub == ny - 1, add_high, 0.0))
            out[slot, :, z] = p[slot, :, z] + both


def side_bit(level):
    return jnp.bitwise_and(jnp.right_shift(lax.axis_index("line"), level), 1) == 0


def join(left, right):
    face = left[V_LAST] + right[V_FIRST]
    joint, new, ratio = {}, {}, []
    for s in range(2):
        resist = 1.0 / ((0.5 * STIFF * SCALES[s]) * face)
        r = 1.0 / (resist + left[GNN[s]] + right[G00[s]])
        ratio.append(r)
        a, b = left[G0N[s]], right[G0N[s]]
        joint[R_ + s] = r
        joint[GA + s] = a
        joint[GB + s] = b
        new[G00[s]] = left[G00[s]] - r * a * a
        new[GNN[s]] = right[GNN[s]] - r * b * b
        new[G0N[s]] = r * a * b
    rate = 0.5 * ADVECTION
    for k in range(4):
        s = KIND[k]
        add_a = -rate * left[F_LAST] * right[F_FIRST + k]
        add_b = rate * right[F_FIRST] * left[F_LAST + k]
        e = ratio[s] * (left[GNN[s]] * add_a - right[G00[s]] * add_b)
        joint[CA + k] = add_a - e
        joint[CB + k] = add_b + e
        new[F_FIRST + k] = left[F_FIRST + k]
        new[F_LAST + k] = right[F_LAST + k]
    new[V_FIRST] = left[V_FIRST]
    new[V_LAST] = right[V_LAST]
    return joint, new


def sided(low_side, mine, theirs):
    left = {p: jnp.where(low_side, mine[p], theirs[p]) for p in mine}
    right = {p: jnp.where(low_side, theirs[p], mine[p]) for p in mine}
    return left, right


def pair_kernel(own, other, *refs):
    joint, out = refs[-2:]
    low_side = side_bit(0)
    planes = range(PLANES)
    found, new = join(*sided(low_side, {p: own[p] for p in planes}, {p: other[p] for p in planes}))
    for plane in range(JOINT):
        joint[plane] = found[plane]
    width = out.shape[2]
    for plane in planes:
        out[plane] = jnp.where(low_side, new[plane][:, :width], new[plane][:, width:])


def chips_kernel(levels, own, *refs):
    others = refs[: 2 ** (levels - 1) - 1]
    joints = refs[-(2 * levels - 3) : len(refs) - (levels - 2)]
    consts = refs[len(refs) - (levels - 2) :]
    blocks = [{p: x[p] for p in range(PLANES)} for x in (own, *others)]
    zero = jnp.zeros_like(own[0])
    ends = [{p: zero for p in range(8)} for _ in blocks]
    for level in range(1, levels):
        low_side = side_bit(level)
        joined, new_ends = [], []
        for j in range(0, len(blocks), 2):
            found, new = join(*sided(low_side, blocks[j], blocks[j + 1]))
            for plane in range(JOINT):
                joints[level - 1][j // 2, plane] = found[plane]
            joined.append(new)
            if level < levels - 1:
                left, right = sided(low_side, ends[j], ends[j + 1])
                both = {}
                for k in range(4):
                    _, both[k], both[4 + k] = up(found, k, left, right)
                new_ends.append(both)
        blocks, ends = joined, new_ends
        if level < levels - 1:
            for slot, x in enumerate(facing(level + 1, levels, ends[1], False)):
                consts[level - 1][slot] = x


def facing(level, levels, ends, mine):
    if level < levels - 1:
        return [ends[p] for p in range(8)]
    low_side = side_bit(level)
    if not mine:
        low_side = jnp.logical_not(low_side)
    return [jnp.where(low_side, ends[4 + k], ends[k]) for k in range(4)]


def source_kernel(rows, count, early, src, cpr, add, t):
    ny, nz = src.shape[2], src.shape[3]
    sub = lax.broadcasted_iota(jnp.int32, (ny, nz), 0)
    top, low = sub == ny - 1, sub == 0

    def down(ref, shift):
        def row(i, carry):
            prev = jnp.maximum(i - 1, 0)
            new = []
            for k in range(4):
                a = jnp.broadcast_to(add[k, pl.ds(i, 1), :], (ny, nz))
                b = jnp.broadcast_to(add[4 + k, pl.ds(i, 1), :], (ny, nz))
                x = ref[k, i - shift] + jnp.where(low, a, jnp.where(top, b, 0.0))
                x = x + cpr[KIND[k], prev] * carry[k]
                t[k, i] = x
                new.append(x)
            return tuple(new)

        return row

    state = (jnp.zeros((ny, nz), F32),) * 4
    state = lax.fori_loop(0, count, down(early, 0), state)
    lax.fori_loop(count, rows, down(src, count), state)


def back_kernel(rows, t, inv, cpr, part):
    end = rows - 1
    start = []
    for k in range(4):
        x = inv[KIND[k], end] * t[k, end]
        part[k, end] = x
        start.append(x)

    def row(j, carry):
        i = end - 1 - j
        new = []
        for k in range(4):
            s = KIND[k]
            x = inv[s, i] * t[k, i] + cpr[s, i] * carry[k]
            part[k, i] = x
            new.append(x)
        return tuple(new)

    lax.fori_loop(0, end, row, tuple(start))


def up(joint, k, left, right):
    s = KIND[k]
    d = left[4 + k] - right[k]
    flow = joint[R_ + s] * d
    first = left[k] + joint[GA + s] * (joint[CA + k] - flow)
    last = right[4 + k] + joint[GB + s] * (joint[CB + k] + flow)
    return d, first, last


def up_kernel(levels, own, other, joint, *refs):
    joints = refs[: levels - 1]
    out, diff = refs[levels : levels + 2]
    shares = refs[levels + 2 :]
    low_side = side_bit(0)
    width = out.shape[2]
    left, right = sided(low_side, {p: own[p] for p in range(8)}, {p: other[p] for p in range(8)})
    ends = {}
    for k in range(4):
        diff[k], first, last = up(joint, k, left, right)
        ends[k] = jnp.where(low_side, first[:, :width], first[:, width:])
        ends[4 + k] = jnp.where(low_side, last[:, :width], last[:, width:])
        out[k] = ends[k]
        out[4 + k] = ends[4 + k]
    for level in range(1, levels - 1):
        low_side = side_bit(level)
        joint = joints[level - 1].at[0]
        for k in range(4):
            s = KIND[k]
            first, last = ends[k], ends[4 + k]
            flow = joint[R_ + s] * jnp.where(low_side, last, -first)
            ends[k] = jnp.where(low_side, first, 0.0) - joint[GA + s] * flow
            ends[4 + k] = jnp.where(low_side, 0.0, last) + joint[GB + s] * flow
        for slot, x in enumerate(facing(level + 1, levels, ends, True)):
            shares[level - 1][slot] = x


def joint_flow(joint, k, d, into_first, into_last, low_side):
    s = KIND[k]
    flow = joint[R_ + s] * (d + joint[GA + s] * into_first - joint[GB + s] * into_last)
    first = jnp.where(low_side, into_first, joint[CB + k] + flow)
    last = jnp.where(low_side, joint[CA + k] - flow, into_last)
    return first, last


def beside_kernel(levels, *refs):
    parts, refs = list(refs[: 2 ** (levels - 1) - levels]), refs[2 ** (levels - 1) - levels :]
    consts, outs = refs[: levels - 2], refs[levels - 2 :]
    for level in range(2, levels):
        here = [parts.pop(0) for _ in range(2 ** (level - 1) - 1)]
        for p in range(outs[level - 2].shape[0]):
            total = consts[level - 2][p]
            for part in here:
                total = total + part[p]
            outs[level - 2][p] = total


def settle_kernel(levels, own, *refs):
    near, refs = refs[: levels - 1], refs[levels - 1 :]
    far, joints, out = refs[: levels - 2], refs[levels - 2 : -1], refs[-1]
    ends = {p: own[p] for p in range(8)}
    diffs = []
    for level in range(1, levels):
        low_side = side_bit(level)
        beside = {p: near[level - 1][p] for p in range(near[level - 1].shape[0])}
        if level > 1:
            beside = {p: x + far[level - 2][p] for p, x in beside.items()}
        across = []
        if len(beside) == 4:
            for k in range(4):
                x = beside[k]
                across.append(jnp.where(low_side, ends[4 + k] - x, x - ends[k]))
        else:
            left, right = sided(low_side, ends, beside)
            for k in range(4):
                d, ends[k], ends[4 + k] = up(joints[level - 1].at[0], k, left, right)
                across.append(d)
        diffs.append(across)
    for k in range(4):
        first = last = jnp.zeros_like(diffs[0][0])
        for level in range(levels - 1, 0, -1):
            first, last = joint_flow(
                joints[level - 1].at[0], k, diffs[level - 1][k], first, last, side_bit(level)
            )
        out[k] = first
        out[4 + k] = last


def final_kernel(mine, flux, joint, diff, part, g0, gn, *refs):
    out, buf, sems = refs[-3:]
    rows, half = buf.shape[1], buf.shape[3]
    low_side = side_bit(0)
    core = jnp.bitwise_and(lax.axis_index("line"), 1)
    offset = (core if mine else 1 - core) * half
    copies = []
    for c in range(half // 128):
        near = pl.ds(c * 128, 128)
        z = pl.ds(pl.multiple_of(offset + c * 128, 128), 128)
        across = {plane: joint[plane, :, z] for plane in range(JOINT)}
        into = [
            joint_flow(across, k, diff[k, :, z], flux[k, :, near], flux[4 + k, :, near], low_side)
            for k in range(4)
        ]
        for i in range(rows):
            a = [g0[s, i, :, z] for s in range(2)]
            b = [gn[s, i, :, z] for s in range(2)]
            for k in range(4):
                s = KIND[k]
                buf[k, i, :, near] = part[k, i, :, z] + (a[s] * into[k][0] + b[s] * into[k][1])
        copies.append(pltpu.make_async_copy(buf.at[:, :, :, near], out.at[:, :, :, z], sems.at[c]))
        copies[-1].start()
    for copy in copies:
        copy.wait()


def local(fields, viscosity):
    rows, ny, nz = viscosity.shape
    lines = lax.axis_size("line")
    cols = lax.axis_size("col")
    levels = lines.bit_length() - 1
    half = nz // 2
    cells = rows * ny * nz
    block = (rows, ny, nz)

    ring = [(i, (i + 1) % cols) for i in range(cols)]
    back_ring = [(b, a) for a, b in ring]

    def gather(at_level):
        found = {}
        for d in sorted(range(1, lines // 2), key=lambda d: (-d.bit_count(), d)):
            x = at_level[d.bit_length()]
            found[d] = lax.ppermute(x, "line", [(i, i ^ (d << 1)) for i in range(lines)])
        return [found[d] for d in sorted(found)]

    def swap(x, level):
        return lax.ppermute(x, "line", [(i, i ^ (1 << level)) for i in range(lines)])

    y_first, y_last = call(
        functools.partial(cut_kernel, ny),
        "cut",
        [(5, rows, nz), (5, rows, nz)],
        [fields, viscosity],
        scratch=[pltpu.SemaphoreType.DMA((2, 5))],
        in_hbm=(0, 1),
        moved=2 * cells,
    )
    low = lax.ppermute(y_last, "col", ring)
    high = lax.ppermute(y_first, "col", back_ring)

    inv, cpr, g0, gn, w = call(
        functools.partial(factor_kernel, rows),
        "factor",
        [(2,) + block] * 4 + [(PLANES, ny, nz)],
        [fields, viscosity],
        scratch=[VMEM((2,) + block, F32), pltpu.SemaphoreType.DMA((2,))],
        in_hbm=(0,),
        flops=10**9,
    )
    count = rows // 4
    (early,) = call(
        functools.partial(early_kernel, count),
        "early",
        [(4, count, ny, nz)],
        [fields, viscosity],
        scratch=[VMEM((4, count + 1, ny, nz), F32), pltpu.SemaphoreType.DMA],
        in_hbm=(0,),
        flops=4 * 10**9,
    )
    src, p, ends = call(
        functools.partial(explicit_kernel, count),
        "explicit",
        [(4, rows - count, ny, nz), (8, ny, nz), (8, rows, nz)],
        [fields, viscosity, g0, gn, early],
        scratch=[VMEM((4, rows - count + 1, ny, nz), F32), pltpu.SemaphoreType.DMA((3,))],
        in_hbm=(0,),
        flops=5 * 10**9,
    )
    pair, w = call(
        pair_kernel,
        "pair",
        [(JOINT, ny, nz), (PLANES, ny, half)],
        [w, swap(w, 0), early],
        moved=4 * ny * nz * 60,
    )
    pairs = lines // 2
    widths = [8] * (levels - 3) + [4]
    found = call(
        functools.partial(chips_kernel, levels),
        "chips",
        [(pairs >> level, JOINT, ny, half) for level in range(1, levels)]
        + [(width, ny, half) for width in widths],
        [w] + gather([w] * (levels + 1)) + [p],
        moved=4 * ny * half * 300,
    )
    joints, consts = list(found[: levels - 1]), list(found[levels - 1 :])

    (add,) = call(
        functools.partial(edge_kernel, rows),
        "edge",
        [(8, rows, nz)],
        [y_last, y_first, low, high],
        flops=8 * cells,
        moved=4 * cells,
    )
    (p,) = call(
        functools.partial(ends_kernel, rows, ny),
        "ends",
        [(8, ny, nz)],
        [add, ends, p, joints[0]],
        flops=6 * cells,
        moved=2 * cells,
    )
    (t,) = call(
        functools.partial(source_kernel, rows, count),
        "source",
        [(4,) + block],
        [early, src, cpr, add],
        flops=30 * cells,
        moved=24 * cells,
    )
    (part,) = call(
        functools.partial(back_kernel, rows),
        "back",
        [(4,) + block],
        [t, inv, cpr],
        flops=20 * cells,
        moved=24 * cells,
    )
    p, diff, *shares = call(
        functools.partial(up_kernel, levels),
        "up",
        [(8, ny, half), (4, ny, nz)] + [(width, ny, half) for width in widths],
        [p, swap(p, 0), pair] + joints + [part],
        moved=4 * ny * nz * 40,
    )
    others = dict(enumerate(gather([None, p] + shares), 1))
    near = [others.pop(1 << level) for level in range(levels - 1)]
    beside = call(
        functools.partial(beside_kernel, levels),
        "beside",
        [(width, ny, half) for width in widths],
        list(others.values()) + consts,
        flops=6 * 10**8,
    )
    (flux,) = call(
        functools.partial(settle_kernel, levels),
        "settle",
        [(8, ny, half)],
        [p] + near + list(beside) + joints,
        moved=4 * ny * half * 100,
    )
    rest = [pair, diff, part, g0, gn]
    scratch = [VMEM((4, rows, ny, half), F32), pltpu.SemaphoreType.DMA((half // 128,))]
    (out,) = call(
        functools.partial(final_kernel, True),
        "final_own",
        [(4,) + block],
        [flux] + rest,
        scratch=scratch,
        out_hbm=(0,),
        flops=10**9,
    )
    (out,) = call(
        functools.partial(final_kernel, False),
        "final_other",
        [(4,) + block],
        [swap(flux, 0)] + rest + [out],
        scratch=scratch,
        in_hbm=(6,),
        out_hbm=(0,),
        aliases={6: 0},
        flops=10**9,
    )
    return out


def solution(mesh):
    return jax.shard_map(
        local,
        mesh=mesh,
        in_specs=(P(None, "line", "col", None), P("line", "col", None)),
        out_specs=P(None, "line", "col", None),
        check_vma=False,
    )
```

```python
import functools

import jax
import jax.numpy as jnp
from jax import lax
from jax.experimental import pallas as pl
from jax.experimental.pallas import tpu as pltpu
from jax.sharding import PartitionSpec as P

STIFF = 3072
THERMAL_RATIO = 0.8
CROSS_RATE = 0.2
ADVECTION = 0.25
BUOYANCY = 2.0
SCALES = (1.0, THERMAL_RATIO)
KIND = (0, 0, 0, 1)

F32 = jnp.float32
VMEM = pltpu.VMEM
LIMIT = 24 * 1024 * 1024

G00, G0N, GNN = (0, 3), (1, 4), (2, 5)
V_FIRST, V_LAST, F_FIRST, F_LAST = 6, 7, 8, 12
PLANES = 16
R_, GA, GB, CA, CB = 0, 2, 4, 6, 10
JOINT = 14


def in_vmem(x):
    return pltpu.with_memory_space_constraint(x, VMEM)


def spec():
    return pl.BlockSpec(memory_space=VMEM)


def call(kernel, name, out_shapes, args, scratch=(), in_hbm=(), out_hbm=(), aliases={}, flops=0, moved=0):
    in_specs = []
    operands = []
    for i, x in enumerate(args):
        if i in in_hbm:
            in_specs.append(pl.BlockSpec(memory_space=pltpu.HBM))
            operands.append(pltpu.with_memory_space_constraint(x, pltpu.HBM))
        else:
            in_specs.append(spec())
            operands.append(in_vmem(x))
    out_shape = []
    out_specs = []
    for i, s in enumerate(out_shapes):
        if i in out_hbm:
            out_shape.append(pltpu.HBM(s, F32))
            out_specs.append(pl.BlockSpec(memory_space=pltpu.HBM))
        else:
            out_shape.append(VMEM(s, F32))
            out_specs.append(spec())
    return pl.pallas_call(
        kernel,
        out_shape=out_shape,
        in_specs=in_specs,
        out_specs=out_specs,
        scratch_shapes=list(scratch),
        input_output_aliases=aliases,
        compiler_params=pltpu.CompilerParams(vmem_limit_bytes=LIMIT),
        cost_estimate=pl.CostEstimate(flops=flops, bytes_accessed=moved, transcendentals=0),
        name=name,
    )(*operands)


def layer(read, ny, nz):
    sub = lax.broadcasted_iota(jnp.int32, (8, nz), 0)
    tile = jnp.broadcast_to(read(0), (8, nz))
    for r in range(1, 8):
        tile = jnp.where(sub == r, jnp.broadcast_to(read(r), (8, nz)), tile)
    return tile


def cut_kernel(ny, pieces, fields, visc, y_first, y_last, sems):
    step = visc.shape[0] // pieces
    copies = []
    for j, (at, out) in enumerate(((0, y_first), (ny - 1, y_last))):
        for k in range(5):
            for c in range(pieces):
                x = pl.ds(c * step, step)
                layer_of = visc.at[x, at] if k == 4 else fields.at[k, x, at]
                copies.append(pltpu.make_async_copy(layer_of, out.at[k, x], sems.at[j, k, c]))
    for copy in copies:
        copy.start()
    for copy in copies:
        copy.wait()


def factor_kernel(rows, fields_ref, visc, inv, cpr, g0, gn, w, tau, sems):
    copies = [
        pltpu.make_async_copy(fields_ref.at[:, 0], w.at[F_FIRST : F_FIRST + 4], sems.at[0]),
        pltpu.make_async_copy(fields_ref.at[:, rows - 1], w.at[F_LAST : F_LAST + 4], sems.at[1]),
    ]
    for copy in copies:
        copy.start()
    ny, nz = visc.shape[1], visc.shape[2]
    me = lax.axis_index("line")
    wall_low = jnp.where(me == 0, 1.0, 0.0).astype(F32)
    wall_high = jnp.where(me == lax.axis_size("line") - 1, 1.0, 0.0).astype(F32)
    one = jnp.ones((ny, nz), F32)

    def row(i, carry):
        low, v = carry[4], carry[5]
        after = visc[jnp.minimum(i + 1, rows - 1)]
        high = jnp.where(i == rows - 1, (0.5 * STIFF) * wall_high * v, (0.5 * STIFF) * (v + after))
        new = []
        for s in range(2):
            gain, running = carry[2 * s], carry[2 * s + 1]
            down = SCALES[s] * low if s else low
            up = SCALES[s] * high if s else high
            q = 1.0 + down * gain
            one_over = 1.0 / (q + up)
            coupling = up * one_over
            inv[s, i] = one_over
            cpr[s, i] = coupling
            tau[s, i] = running
            new += [q * one_over, coupling * running]
        return tuple(new) + (high, after)

    first = visc[0]
    lax.fori_loop(0, rows, row, (one,) * 4 + (wall_low * (0.5 * STIFF) * first, first))

    end = rows - 1
    start = []
    for s in range(2):
        a = inv[s, end] * tau[s, end]
        b = inv[s, end]
        g0[s, end] = a
        gn[s, end] = b
        w[G0N[s]] = a
        w[GNN[s]] = b
        start += [a, b]

    def back(j, carry):
        i = end - 1 - j
        new = []
        for s in range(2):
            c = cpr[s, i]
            a = inv[s, i] * tau[s, i] + c * carry[2 * s]
            b = c * carry[2 * s + 1]
            g0[s, i] = a
            gn[s, i] = b
            new += [a, b]
        return tuple(new)

    final = lax.fori_loop(0, end, back, tuple(start))
    for s in range(2):
        w[G00[s]] = final[2 * s]
    w[V_FIRST] = first
    w[V_LAST] = visc[rows - 1]
    for copy in copies:
        copy.wait()


def explicit_rows(first, count, base, start, fields, visc, src):
    rows, ny, nz = visc.shape
    lane = lax.broadcasted_iota(jnp.int32, (ny, nz), 1)
    sub = lax.broadcasted_iota(jnp.int32, (ny, nz), 0)
    z_top, z_low = lane == nz - 1, lane == 0
    y_top, y_low = sub == ny - 1, sub == 0

    def sides(x):
        return (
            pltpu.roll(x, ny - 1, 0),
            pltpu.roll(x, 1, 0),
            pltpu.roll(x, nz - 1, 1),
            pltpu.roll(x, 1, 1),
        )

    def row(i, _):
        f = [fields[k, i - base] for k in range(4)]
        v = visc[i]
        after, before = jnp.minimum(i + 1, rows - 1), jnp.maximum(i - 1, 0)
        vyn, vyp, vzn, vzp = sides(v)
        half = 0.5 * CROSS_RATE
        faces = [
            jnp.where(y_top, 0.0, half * (v + vyn)),
            jnp.where(y_low, 0.0, half * (v + vyp)),
            half * (v + jnp.where(z_top, 0.0, vzn)),
            half * (v + jnp.where(z_low, 0.0, vzp)),
        ]
        none = [y_top, y_low, z_top, z_low]
        total = (faces[0] + faces[1]) + (faces[2] + faces[3])
        adv = [(-0.5 * ADVECTION) * f[k] for k in range(3)]
        move = [adv[1], -adv[1], adv[2], -adv[2]]
        adv_after = jnp.where(i == rows - 1, 0.0, adv[0])
        adv_before = jnp.where(i == 0, 0.0, adv[0])
        weights, centre = [], []
        for s in range(2):
            scaled = [SCALES[s] * x if s else x for x in faces]
            weights.append([jnp.where(n, 0.0, x + m) for n, x, m in zip(none, scaled, move)])
            centre.append(1.0 - (SCALES[s] * total if s else total))
        for k in range(4):
            s = KIND[k]
            near = sides(f[k])
            out = centre[s] * f[k] + adv_after * fields[k, after - base] - adv_before * fields[k, before - base]
            for c, x in zip(weights[s], near):
                out = out + c * x
            if k == 2:
                out = out + BUOYANCY * f[3]
            src[k, i - start] = out
        return 0

    lax.fori_loop(first, first + count, row, 0)


def early_kernel(count, fields_ref, visc, src, fields, sem):
    copy = pltpu.make_async_copy(fields_ref.at[:, 0 : count + 1], fields, sem)
    copy.start()
    copy.wait()
    explicit_rows(0, count, 0, 0, fields, visc, src)


def explicit_kernel(count, fields_ref, visc, g0, gn, early, src, p, ends, fields, sems):
    rows, ny, nz = visc.shape
    cuts = [count - 1] + list(range(2 * count + 1, rows, count)) + [rows]
    copies = []
    for c, (lo, hi) in enumerate(zip(cuts, cuts[1:])):
        copies.append(
            pltpu.make_async_copy(
                fields_ref.at[:, lo:hi], fields.at[:, lo - cuts[0] : hi - cuts[0]], sems.at[c]
            )
        )
        copies[-1].start()
    for c, copy in enumerate(copies):
        copy.wait()
        explicit_rows((c + 1) * count, count, cuts[0], count, fields, visc, src)

    def dot(ref, shift):
        def add(i, carry):
            new = []
            for g, base in ((g0, 0), (gn, 4)):
                for k in range(4):
                    new.append(carry[base + k] + g[KIND[k], i] * ref[k, i - shift])
            return tuple(new)

        return add

    final = (jnp.zeros((ny, nz), F32),) * 8
    final = lax.fori_loop(0, count, dot(early, 0), final)
    final = lax.fori_loop(count, rows, dot(src, count), final)
    for k in range(8):
        p[k] = final[k]

    for s in range(2):
        for side, at in ((0, 0), (1, ny - 1)):
            for which, g in ((0, g0), (1, gn)):
                for lo in range(0, rows, 8):
                    ends[4 * side + 2 * which + s, lo : lo + 8] = layer(
                        lambda r: g[s, lo + r, at : at + 1, :], ny, nz
                    )


def edge_kernel(rows, y_last, y_first, low, high, add):
    nz = add.shape[2]
    rate = 0.5 * ADVECTION
    for side, mine, far, sign in ((0, y_first, low, rate), (4, y_last, high, -rate)):
        for r in range(rows // 8):
            x = pl.ds(r * 8, 8)
            face = (0.5 * CROSS_RATE) * (mine[4, x] + far[4, x])
            faces = (face, THERMAL_RATIO * face)
            adv = sign * mine[1, x]
            both = [adv + c for c in faces]
            for k in range(4):
                s = KIND[k]
                add[side + k, x] = both[s] * far[k, x] - faces[s] * mine[k, x]


def ends_kernel(rows, ny, add, ends, p, tie, out):
    nz = out.shape[2]
    sub = lax.broadcasted_iota(jnp.int32, (ny, 128), 0)
    for j in range(nz // 128):
        z = pl.ds(j * 128, 128)
        sums = []
        for side in (0, 4):
            total = [None] * 8
            for r in range(rows // 8):
                x = pl.ds(r * 8, 8)
                g = [ends[side + q, x, z] for q in range(4)]
                for k in range(4):
                    h = add[side + k, x, z]
                    for slot, c in ((k, g[KIND[k]]), (4 + k, g[2 + KIND[k]])):
                        part = c * h
                        total[slot] = part if total[slot] is None else total[slot] + part
            sums.append(total)
        for slot in range(8):
            add_low = jnp.sum(sums[0][slot], axis=0, keepdims=True)
            add_high = jnp.sum(sums[1][slot], axis=0, keepdims=True)
            both = jnp.where(sub == 0, add_low, jnp.where(sub == ny - 1, add_high, 0.0))
            out[slot, :, z] = p[slot, :, z] + both


def side_bit(level):
    return jnp.bitwise_and(jnp.right_shift(lax.axis_index("line"), level), 1) == 0


def join(left, right):
    face = left[V_LAST] + right[V_FIRST]
    joint, new, ratio = {}, {}, []
    for s in range(2):
        resist = 1.0 / ((0.5 * STIFF * SCALES[s]) * face)
        r = 1.0 / (resist + left[GNN[s]] + right[G00[s]])
        ratio.append(r)
        a, b = left[G0N[s]], right[G0N[s]]
        joint[R_ + s] = r
        joint[GA + s] = a
        joint[GB + s] = b
        new[G00[s]] = left[G00[s]] - r * a * a
        new[GNN[s]] = right[GNN[s]] - r * b * b
        new[G0N[s]] = r * a * b
    rate = 0.5 * ADVECTION
    for k in range(4):
        s = KIND[k]
        add_a = -rate * left[F_LAST] * right[F_FIRST + k]
        add_b = rate * right[F_FIRST] * left[F_LAST + k]
        e = ratio[s] * (left[GNN[s]] * add_a - right[G00[s]] * add_b)
        joint[CA + k] = add_a - e
        joint[CB + k] = add_b + e
        new[F_FIRST + k] = left[F_FIRST + k]
        new[F_LAST + k] = right[F_LAST + k]
    new[V_FIRST] = left[V_FIRST]
    new[V_LAST] = right[V_LAST]
    return joint, new


def sided(low_side, mine, theirs):
    left = {p: jnp.where(low_side, mine[p], theirs[p]) for p in mine}
    right = {p: jnp.where(low_side, theirs[p], mine[p]) for p in mine}
    return left, right


def pair_kernel(own, other, *refs):
    joint, out = refs[-2:]
    low_side = side_bit(0)
    planes = range(PLANES)
    found, new = join(*sided(low_side, {p: own[p] for p in planes}, {p: other[p] for p in planes}))
    for plane in range(JOINT):
        joint[plane] = found[plane]
    width = out.shape[2]
    for plane in planes:
        out[plane] = jnp.where(low_side, new[plane][:, :width], new[plane][:, width:])


def chips_kernel(levels, own, *refs):
    others = refs[: 2 ** (levels - 1) - 1]
    joints = refs[-(2 * levels - 3) : len(refs) - (levels - 2)]
    consts = refs[len(refs) - (levels - 2) :]
    blocks = [{p: x[p] for p in range(PLANES)} for x in (own, *others)]
    zero = jnp.zeros_like(own[0])
    ends = [{p: zero for p in range(8)} for _ in blocks]
    for level in range(1, levels):
        low_side = side_bit(level)
        joined, new_ends = [], []
        for j in range(0, len(blocks), 2):
            found, new = join(*sided(low_side, blocks[j], blocks[j + 1]))
            for plane in range(JOINT):
                joints[level - 1][j // 2, plane] = found[plane]
            joined.append(new)
            if level < levels - 1:
                left, right = sided(low_side, ends[j], ends[j + 1])
                both = {}
                for k in range(4):
                    _, both[k], both[4 + k] = up(found, k, left, right)
                new_ends.append(both)
        blocks, ends = joined, new_ends
        if level < levels - 1:
            for slot, x in enumerate(facing(level + 1, levels, ends[1], False)):
                consts[level - 1][slot] = x


def facing(level, levels, ends, mine):
    if level < levels - 1:
        return [ends[p] for p in range(8)]
    low_side = side_bit(level)
    if not mine:
        low_side = jnp.logical_not(low_side)
    return [jnp.where(low_side, ends[4 + k], ends[k]) for k in range(4)]


def source_kernel(rows, count, early, src, cpr, add, t):
    ny, nz = src.shape[2], src.shape[3]
    sub = lax.broadcasted_iota(jnp.int32, (ny, nz), 0)
    top, low = sub == ny - 1, sub == 0

    def down(ref, shift):
        def row(i, carry):
            prev = jnp.maximum(i - 1, 0)
            new = []
            for k in range(4):
                a = jnp.broadcast_to(add[k, pl.ds(i, 1), :], (ny, nz))
                b = jnp.broadcast_to(add[4 + k, pl.ds(i, 1), :], (ny, nz))
                x = ref[k, i - shift] + jnp.where(low, a, jnp.where(top, b, 0.0))
                x = x + cpr[KIND[k], prev] * carry[k]
                t[k, i] = x
                new.append(x)
            return tuple(new)

        return row

    state = (jnp.zeros((ny, nz), F32),) * 4
    state = lax.fori_loop(0, count, down(early, 0), state)
    lax.fori_loop(count, rows, down(src, count), state)


def back_kernel(rows, t, inv, cpr, part):
    end = rows - 1
    start = []
    for k in range(4):
        x = inv[KIND[k], end] * t[k, end]
        part[k, end] = x
        start.append(x)

    def row(j, carry):
        i = end - 1 - j
        new = []
        for k in range(4):
            s = KIND[k]
            x = inv[s, i] * t[k, i] + cpr[s, i] * carry[k]
            part[k, i] = x
            new.append(x)
        return tuple(new)

    lax.fori_loop(0, end, row, tuple(start))


def up(joint, k, left, right):
    s = KIND[k]
    d = left[4 + k] - right[k]
    flow = joint[R_ + s] * d
    first = left[k] + joint[GA + s] * (joint[CA + k] - flow)
    last = right[4 + k] + joint[GB + s] * (joint[CB + k] + flow)
    return d, first, last


def up_kernel(levels, own, other, joint, *refs):
    joints = refs[: levels - 1]
    out, diff = refs[levels : levels + 2]
    shares = refs[levels + 2 :]
    low_side = side_bit(0)
    width = out.shape[2]
    left, right = sided(low_side, {p: own[p] for p in range(8)}, {p: other[p] for p in range(8)})
    ends = {}
    for k in range(4):
        diff[k], first, last = up(joint, k, left, right)
        ends[k] = jnp.where(low_side, first[:, :width], first[:, width:])
        ends[4 + k] = jnp.where(low_side, last[:, :width], last[:, width:])
        out[k] = ends[k]
        out[4 + k] = ends[4 + k]
    for level in range(1, levels - 1):
        low_side = side_bit(level)
        joint = joints[level - 1].at[0]
        for k in range(4):
            s = KIND[k]
            first, last = ends[k], ends[4 + k]
            flow = joint[R_ + s] * jnp.where(low_side, last, -first)
            ends[k] = jnp.where(low_side, first, 0.0) - joint[GA + s] * flow
            ends[4 + k] = jnp.where(low_side, 0.0, last) + joint[GB + s] * flow
        for slot, x in enumerate(facing(level + 1, levels, ends, True)):
            shares[level - 1][slot] = x


def joint_flow(joint, k, d, into_first, into_last, low_side):
    s = KIND[k]
    flow = joint[R_ + s] * (d + joint[GA + s] * into_first - joint[GB + s] * into_last)
    first = jnp.where(low_side, into_first, joint[CB + k] + flow)
    last = jnp.where(low_side, joint[CA + k] - flow, into_last)
    return first, last


def beside_kernel(levels, *refs):
    parts, refs = list(refs[: 2 ** (levels - 1) - levels]), refs[2 ** (levels - 1) - levels :]
    consts, outs = refs[: levels - 2], refs[levels - 2 :]
    for level in range(2, levels):
        here = [parts.pop(0) for _ in range(2 ** (level - 1) - 1)]
        for p in range(outs[level - 2].shape[0]):
            total = consts[level - 2][p]
            for part in here:
                total = total + part[p]
            outs[level - 2][p] = total


def settle_kernel(levels, own, *refs):
    near, refs = refs[: levels - 1], refs[levels - 1 :]
    far, joints, out = refs[: levels - 2], refs[levels - 2 : -1], refs[-1]
    ends = {p: own[p] for p in range(8)}
    diffs = []
    for level in range(1, levels):
        low_side = side_bit(level)
        beside = {p: near[level - 1][p] for p in range(near[level - 1].shape[0])}
        if level > 1:
            beside = {p: x + far[level - 2][p] for p, x in beside.items()}
        across = []
        if len(beside) == 4:
            for k in range(4):
                x = beside[k]
                across.append(jnp.where(low_side, ends[4 + k] - x, x - ends[k]))
        else:
            left, right = sided(low_side, ends, beside)
            for k in range(4):
                d, ends[k], ends[4 + k] = up(joints[level - 1].at[0], k, left, right)
                across.append(d)
        diffs.append(across)
    for k in range(4):
        first = last = jnp.zeros_like(diffs[0][0])
        for level in range(levels - 1, 0, -1):
            first, last = joint_flow(
                joints[level - 1].at[0], k, diffs[level - 1][k], first, last, side_bit(level)
            )
        out[k] = first
        out[4 + k] = last


def final_kernel(mine, flux, joint, diff, part, g0, gn, *refs):
    out, buf, sems = refs[-3:]
    rows, half = buf.shape[1], buf.shape[3]
    low_side = side_bit(0)
    core = jnp.bitwise_and(lax.axis_index("line"), 1)
    offset = (core if mine else 1 - core) * half
    copies = []
    for c in range(half // 128):
        near = pl.ds(c * 128, 128)
        z = pl.ds(pl.multiple_of(offset + c * 128, 128), 128)
        across = {plane: joint[plane, :, z] for plane in range(JOINT)}
        into = [
            joint_flow(across, k, diff[k, :, z], flux[k, :, near], flux[4 + k, :, near], low_side)
            for k in range(4)
        ]
        for i in range(rows):
            a = [g0[s, i, :, z] for s in range(2)]
            b = [gn[s, i, :, z] for s in range(2)]
            for k in range(4):
                s = KIND[k]
                buf[k, i, :, near] = part[k, i, :, z] + (a[s] * into[k][0] + b[s] * into[k][1])
        copies.append(pltpu.make_async_copy(buf.at[:, :, :, near], out.at[:, :, :, z], sems.at[c]))
        copies[-1].start()
    for copy in copies:
        copy.wait()


def local(fields, viscosity):
    rows, ny, nz = viscosity.shape
    lines = lax.axis_size("line")
    cols = lax.axis_size("col")
    levels = lines.bit_length() - 1
    half = nz // 2
    cells = rows * ny * nz
    block = (rows, ny, nz)

    ring = [(i, (i + 1) % cols) for i in range(cols)]
    back_ring = [(b, a) for a, b in ring]

    def gather(at_level):
        found = {}
        for d in sorted(range(1, lines // 2), key=lambda d: (-d.bit_count(), d)):
            x = at_level[d.bit_length()]
            found[d] = lax.ppermute(x, "line", [(i, i ^ (d << 1)) for i in range(lines)])
        return [found[d] for d in sorted(found)]

    def swap(x, level):
        return lax.ppermute(x, "line", [(i, i ^ (1 << level)) for i in range(lines)])

    pieces = 2 if rows % 16 == 0 else 1
    y_first, y_last = call(
        functools.partial(cut_kernel, ny, pieces),
        "cut",
        [(5, rows, nz), (5, rows, nz)],
        [fields, viscosity],
        scratch=[pltpu.SemaphoreType.DMA((2, 5, pieces))],
        in_hbm=(0, 1),
        moved=2 * cells,
    )
    low = lax.ppermute(y_last, "col", ring)
    high = lax.ppermute(y_first, "col", back_ring)

    inv, cpr, g0, gn, w = call(
        functools.partial(factor_kernel, rows),
        "factor",
        [(2,) + block] * 4 + [(PLANES, ny, nz)],
        [fields, viscosity],
        scratch=[VMEM((2,) + block, F32), pltpu.SemaphoreType.DMA((2,))],
        in_hbm=(0,),
        flops=10**9,
    )
    count = rows // 4
    (early,) = call(
        functools.partial(early_kernel, count),
        "early",
        [(4, count, ny, nz)],
        [fields, viscosity],
        scratch=[VMEM((4, count + 1, ny, nz), F32), pltpu.SemaphoreType.DMA],
        in_hbm=(0,),
        flops=4 * 10**9,
    )
    src, p, ends = call(
        functools.partial(explicit_kernel, count),
        "explicit",
        [(4, rows - count, ny, nz), (8, ny, nz), (8, rows, nz)],
        [fields, viscosity, g0, gn, early],
        scratch=[VMEM((4, rows - count + 1, ny, nz), F32), pltpu.SemaphoreType.DMA((3,))],
        in_hbm=(0,),
        flops=5 * 10**9,
    )
    pair, w = call(
        pair_kernel,
        "pair",
        [(JOINT, ny, nz), (PLANES, ny, half)],
        [w, swap(w, 0), early],
        moved=4 * ny * nz * 60,
    )
    pairs = lines // 2
    widths = [8] * (levels - 3) + [4]
    found = call(
        functools.partial(chips_kernel, levels),
        "chips",
        [(pairs >> level, JOINT, ny, half) for level in range(1, levels)]
        + [(width, ny, half) for width in widths],
        [w] + gather([w] * (levels + 1)) + [p],
        moved=4 * ny * half * 300,
    )
    joints, consts = list(found[: levels - 1]), list(found[levels - 1 :])

    (add,) = call(
        functools.partial(edge_kernel, rows),
        "edge",
        [(8, rows, nz)],
        [y_last, y_first, low, high],
        flops=8 * cells,
        moved=4 * cells,
    )
    (p,) = call(
        functools.partial(ends_kernel, rows, ny),
        "ends",
        [(8, ny, nz)],
        [add, ends, p, joints[0]],
        flops=6 * cells,
        moved=2 * cells,
    )
    (t,) = call(
        functools.partial(source_kernel, rows, count),
        "source",
        [(4,) + block],
        [early, src, cpr, add],
        flops=30 * cells,
        moved=24 * cells,
    )
    (part,) = call(
        functools.partial(back_kernel, rows),
        "back",
        [(4,) + block],
        [t, inv, cpr],
        flops=20 * cells,
        moved=24 * cells,
    )
    p, diff, *shares = call(
        functools.partial(up_kernel, levels),
        "up",
        [(8, ny, half), (4, ny, nz)] + [(width, ny, half) for width in widths],
        [p, swap(p, 0), pair] + joints + [part],
        moved=4 * ny * nz * 40,
    )
    others = dict(enumerate(gather([None, p] + shares), 1))
    near = [others.pop(1 << level) for level in range(levels - 1)]
    beside = call(
        functools.partial(beside_kernel, levels),
        "beside",
        [(width, ny, half) for width in widths],
        list(others.values()) + consts,
        flops=10**9,
    )
    (flux,) = call(
        functools.partial(settle_kernel, levels),
        "settle",
        [(8, ny, half)],
        [p] + near + list(beside) + joints,
        moved=4 * ny * half * 100,
    )
    rest = [pair, diff, part, g0, gn]
    scratch = [VMEM((4, rows, ny, half), F32), pltpu.SemaphoreType.DMA((half // 128,))]
    (out,) = call(
        functools.partial(final_kernel, True),
        "final_own",
        [(4,) + block],
        [flux] + rest,
        scratch=scratch,
        out_hbm=(0,),
        flops=10**9,
    )
    (out,) = call(
        functools.partial(final_kernel, False),
        "final_other",
        [(4,) + block],
        [swap(flux, 0)] + rest + [out],
        scratch=scratch,
        in_hbm=(6,),
        out_hbm=(0,),
        aliases={6: 0},
        flops=10**9,
    )
    return out


def solution(mesh):
    return jax.shard_map(
        local,
        mesh=mesh,
        in_specs=(P(None, "line", "col", None), P("line", "col", None)),
        out_specs=P(None, "line", "col", None),
        check_vma=False,
    )
```

```python
import functools

import jax
import jax.numpy as jnp
from jax import lax
from jax.experimental import pallas as pl
from jax.experimental.pallas import tpu as pltpu
from jax.sharding import PartitionSpec as P

STIFF = 3072
THERMAL_RATIO = 0.8
CROSS_RATE = 0.2
ADVECTION = 0.25
BUOYANCY = 2.0
SCALES = (1.0, THERMAL_RATIO)
KIND = (0, 0, 0, 1)

F32 = jnp.float32
VMEM = pltpu.VMEM
LIMIT = 24 * 1024 * 1024

G00, G0N, GNN = (0, 3), (1, 4), (2, 5)
V_FIRST, V_LAST, F_FIRST, F_LAST = 6, 7, 8, 12
PLANES = 16
R_, GA, GB, CA, CB = 0, 2, 4, 6, 10
JOINT = 14


def in_vmem(x):
    return pltpu.with_memory_space_constraint(x, VMEM)


def spec():
    return pl.BlockSpec(memory_space=VMEM)


def call(kernel, name, out_shapes, args, scratch=(), in_hbm=(), out_hbm=(), aliases={}, flops=0, moved=0):
    in_specs = []
    operands = []
    for i, x in enumerate(args):
        if i in in_hbm:
            in_specs.append(pl.BlockSpec(memory_space=pltpu.HBM))
            operands.append(pltpu.with_memory_space_constraint(x, pltpu.HBM))
        else:
            in_specs.append(spec())
            operands.append(in_vmem(x))
    out_shape = []
    out_specs = []
    for i, s in enumerate(out_shapes):
        if i in out_hbm:
            out_shape.append(pltpu.HBM(s, F32))
            out_specs.append(pl.BlockSpec(memory_space=pltpu.HBM))
        else:
            out_shape.append(VMEM(s, F32))
            out_specs.append(spec())
    return pl.pallas_call(
        kernel,
        out_shape=out_shape,
        in_specs=in_specs,
        out_specs=out_specs,
        scratch_shapes=list(scratch),
        input_output_aliases=aliases,
        compiler_params=pltpu.CompilerParams(vmem_limit_bytes=LIMIT),
        cost_estimate=pl.CostEstimate(flops=flops, bytes_accessed=moved, transcendentals=0),
        name=name,
    )(*operands)


def layer(read, ny, nz):
    sub = lax.broadcasted_iota(jnp.int32, (8, nz), 0)
    tile = jnp.broadcast_to(read(0), (8, nz))
    for r in range(1, 8):
        tile = jnp.where(sub == r, jnp.broadcast_to(read(r), (8, nz)), tile)
    return tile


def cut_kernel(at, fields, visc, *refs):
    out, sems = refs[-2:]
    copies = [pltpu.make_async_copy(fields.at[k, :, at], out.at[k], sems.at[k]) for k in range(4)]
    copies.append(pltpu.make_async_copy(visc.at[:, at], out.at[4], sems.at[4]))
    for copy in copies:
        copy.start()
    for copy in copies:
        copy.wait()


def factor_kernel(rows, fields_ref, visc, inv, cpr, g0, gn, w, tau, sems):
    copies = [
        pltpu.make_async_copy(fields_ref.at[:, 0], w.at[F_FIRST : F_FIRST + 4], sems.at[0]),
        pltpu.make_async_copy(fields_ref.at[:, rows - 1], w.at[F_LAST : F_LAST + 4], sems.at[1]),
    ]
    for copy in copies:
        copy.start()
    ny, nz = visc.shape[1], visc.shape[2]
    me = lax.axis_index("line")
    wall_low = jnp.where(me == 0, 1.0, 0.0).astype(F32)
    wall_high = jnp.where(me == lax.axis_size("line") - 1, 1.0, 0.0).astype(F32)
    one = jnp.ones((ny, nz), F32)

    def row(i, carry):
        low, v = carry[4], carry[5]
        after = visc[jnp.minimum(i + 1, rows - 1)]
        high = jnp.where(i == rows - 1, (0.5 * STIFF) * wall_high * v, (0.5 * STIFF) * (v + after))
        new = []
        for s in range(2):
            gain, running = carry[2 * s], carry[2 * s + 1]
            down = SCALES[s] * low if s else low
            up = SCALES[s] * high if s else high
            q = 1.0 + down * gain
            one_over = 1.0 / (q + up)
            coupling = up * one_over
            inv[s, i] = one_over
            cpr[s, i] = coupling
            tau[s, i] = running
            new += [q * one_over, coupling * running]
        return tuple(new) + (high, after)

    first = visc[0]
    lax.fori_loop(0, rows, row, (one,) * 4 + (wall_low * (0.5 * STIFF) * first, first))

    end = rows - 1
    start = []
    for s in range(2):
        a = inv[s, end] * tau[s, end]
        b = inv[s, end]
        g0[s, end] = a
        gn[s, end] = b
        w[G0N[s]] = a
        w[GNN[s]] = b
        start += [a, b]

    def back(j, carry):
        i = end - 1 - j
        new = []
        for s in range(2):
            c = cpr[s, i]
            a = inv[s, i] * tau[s, i] + c * carry[2 * s]
            b = c * carry[2 * s + 1]
            g0[s, i] = a
            gn[s, i] = b
            new += [a, b]
        return tuple(new)

    final = lax.fori_loop(0, end, back, tuple(start))
    for s in range(2):
        w[G00[s]] = final[2 * s]
    w[V_FIRST] = first
    w[V_LAST] = visc[rows - 1]
    for copy in copies:
        copy.wait()


def explicit_rows(first, count, base, start, fields, visc, src):
    rows, ny, nz = visc.shape
    lane = lax.broadcasted_iota(jnp.int32, (ny, nz), 1)
    sub = lax.broadcasted_iota(jnp.int32, (ny, nz), 0)
    z_top, z_low = lane == nz - 1, lane == 0
    y_top, y_low = sub == ny - 1, sub == 0

    def sides(x):
        return (
            pltpu.roll(x, ny - 1, 0),
            pltpu.roll(x, 1, 0),
            pltpu.roll(x, nz - 1, 1),
            pltpu.roll(x, 1, 1),
        )

    def row(i, _):
        f = [fields[k, i - base] for k in range(4)]
        v = visc[i]
        after, before = jnp.minimum(i + 1, rows - 1), jnp.maximum(i - 1, 0)
        vyn, vyp, vzn, vzp = sides(v)
        half = 0.5 * CROSS_RATE
        faces = [
            jnp.where(y_top, 0.0, half * (v + vyn)),
            jnp.where(y_low, 0.0, half * (v + vyp)),
            half * (v + jnp.where(z_top, 0.0, vzn)),
            half * (v + jnp.where(z_low, 0.0, vzp)),
        ]
        none = [y_top, y_low, z_top, z_low]
        total = (faces[0] + faces[1]) + (faces[2] + faces[3])
        adv = [(-0.5 * ADVECTION) * f[k] for k in range(3)]
        move = [adv[1], -adv[1], adv[2], -adv[2]]
        adv_after = jnp.where(i == rows - 1, 0.0, adv[0])
        adv_before = jnp.where(i == 0, 0.0, adv[0])
        weights, centre = [], []
        for s in range(2):
            scaled = [SCALES[s] * x if s else x for x in faces]
            weights.append([jnp.where(n, 0.0, x + m) for n, x, m in zip(none, scaled, move)])
            centre.append(1.0 - (SCALES[s] * total if s else total))
        for k in range(4):
            s = KIND[k]
            near = sides(f[k])
            out = centre[s] * f[k] + adv_after * fields[k, after - base] - adv_before * fields[k, before - base]
            for c, x in zip(weights[s], near):
                out = out + c * x
            if k == 2:
                out = out + BUOYANCY * f[3]
            src[k, i - start] = out
        return 0

    lax.fori_loop(first, first + count, row, 0)


def early_kernel(count, fields_ref, visc, src, fields, sem):
    copy = pltpu.make_async_copy(fields_ref.at[:, 0 : count + 1], fields, sem)
    copy.start()
    copy.wait()
    explicit_rows(0, count, 0, 0, fields, visc, src)


def explicit_kernel(count, fields_ref, visc, g0, gn, early, src, p, ends, fields, sems):
    rows, ny, nz = visc.shape
    cuts = [count - 1] + list(range(2 * count + 1, rows, count)) + [rows]
    copies = []
    for c, (lo, hi) in enumerate(zip(cuts, cuts[1:])):
        copies.append(
            pltpu.make_async_copy(
                fields_ref.at[:, lo:hi], fields.at[:, lo - cuts[0] : hi - cuts[0]], sems.at[c]
            )
        )
        copies[-1].start()
    for c, copy in enumerate(copies):
        copy.wait()
        explicit_rows((c + 1) * count, count, cuts[0], count, fields, visc, src)

    def dot(ref, shift):
        def add(i, carry):
            new = []
            for g, base in ((g0, 0), (gn, 4)):
                for k in range(4):
                    new.append(carry[base + k] + g[KIND[k], i] * ref[k, i - shift])
            return tuple(new)

        return add

    final = (jnp.zeros((ny, nz), F32),) * 8
    final = lax.fori_loop(0, count, dot(early, 0), final)
    final = lax.fori_loop(count, rows, dot(src, count), final)
    for k in range(8):
        p[k] = final[k]

    for s in range(2):
        for side, at in ((0, 0), (1, ny - 1)):
            for which, g in ((0, g0), (1, gn)):
                for lo in range(0, rows, 8):
                    ends[4 * side + 2 * which + s, lo : lo + 8] = layer(
                        lambda r: g[s, lo + r, at : at + 1, :], ny, nz
                    )


def edge_kernel(rows, y_last, y_first, low, high, add):
    nz = add.shape[2]
    rate = 0.5 * ADVECTION
    for side, mine, far, sign in ((0, y_first, low, rate), (4, y_last, high, -rate)):
        for r in range(rows // 8):
            x = pl.ds(r * 8, 8)
            face = (0.5 * CROSS_RATE) * (mine[4, x] + far[4, x])
            faces = (face, THERMAL_RATIO * face)
            adv = sign * mine[1, x]
            both = [adv + c for c in faces]
            for k in range(4):
                s = KIND[k]
                add[side + k, x] = both[s] * far[k, x] - faces[s] * mine[k, x]


def ends_kernel(rows, ny, add, ends, p, tie, out):
    nz = out.shape[2]
    sub = lax.broadcasted_iota(jnp.int32, (ny, 128), 0)
    for j in range(nz // 128):
        z = pl.ds(j * 128, 128)
        sums = []
        for side in (0, 4):
            total = [None] * 8
            for r in range(rows // 8):
                x = pl.ds(r * 8, 8)
                g = [ends[side + q, x, z] for q in range(4)]
                for k in range(4):
                    h = add[side + k, x, z]
                    for slot, c in ((k, g[KIND[k]]), (4 + k, g[2 + KIND[k]])):
                        part = c * h
                        total[slot] = part if total[slot] is None else total[slot] + part
            sums.append(total)
        for slot in range(8):
            add_low = jnp.sum(sums[0][slot], axis=0, keepdims=True)
            add_high = jnp.sum(sums[1][slot], axis=0, keepdims=True)
            both = jnp.where(sub == 0, add_low, jnp.where(sub == ny - 1, add_high, 0.0))
            out[slot, :, z] = p[slot, :, z] + both


def side_bit(level):
    return jnp.bitwise_and(jnp.right_shift(lax.axis_index("line"), level), 1) == 0


def join(left, right):
    face = left[V_LAST] + right[V_FIRST]
    joint, new, ratio = {}, {}, []
    for s in range(2):
        resist = 1.0 / ((0.5 * STIFF * SCALES[s]) * face)
        r = 1.0 / (resist + left[GNN[s]] + right[G00[s]])
        ratio.append(r)
        a, b = left[G0N[s]], right[G0N[s]]
        joint[R_ + s] = r
        joint[GA + s] = a
        joint[GB + s] = b
        new[G00[s]] = left[G00[s]] - r * a * a
        new[GNN[s]] = right[GNN[s]] - r * b * b
        new[G0N[s]] = r * a * b
    rate = 0.5 * ADVECTION
    for k in range(4):
        s = KIND[k]
        add_a = -rate * left[F_LAST] * right[F_FIRST + k]
        add_b = rate * right[F_FIRST] * left[F_LAST + k]
        e = ratio[s] * (left[GNN[s]] * add_a - right[G00[s]] * add_b)
        joint[CA + k] = add_a - e
        joint[CB + k] = add_b + e
        new[F_FIRST + k] = left[F_FIRST + k]
        new[F_LAST + k] = right[F_LAST + k]
    new[V_FIRST] = left[V_FIRST]
    new[V_LAST] = right[V_LAST]
    return joint, new


def sided(low_side, mine, theirs):
    left = {p: jnp.where(low_side, mine[p], theirs[p]) for p in mine}
    right = {p: jnp.where(low_side, theirs[p], mine[p]) for p in mine}
    return left, right


def pair_kernel(own, other, *refs):
    joint, out = refs[-2:]
    low_side = side_bit(0)
    planes = range(PLANES)
    found, new = join(*sided(low_side, {p: own[p] for p in planes}, {p: other[p] for p in planes}))
    for plane in range(JOINT):
        joint[plane] = found[plane]
    width = out.shape[2]
    for plane in planes:
        out[plane] = jnp.where(low_side, new[plane][:, :width], new[plane][:, width:])


def chips_kernel(levels, own, *refs):
    others = refs[: 2 ** (levels - 1) - 1]
    joints = refs[-(2 * levels - 3) : len(refs) - (levels - 2)]
    consts = refs[len(refs) - (levels - 2) :]
    blocks = [{p: x[p] for p in range(PLANES)} for x in (own, *others)]
    zero = jnp.zeros_like(own[0])
    ends = [{p: zero for p in range(8)} for _ in blocks]
    for level in range(1, levels):
        low_side = side_bit(level)
        joined, new_ends = [], []
        for j in range(0, len(blocks), 2):
            found, new = join(*sided(low_side, blocks[j], blocks[j + 1]))
            for plane in range(JOINT):
                joints[level - 1][j // 2, plane] = found[plane]
            joined.append(new)
            if level < levels - 1:
                left, right = sided(low_side, ends[j], ends[j + 1])
                both = {}
                for k in range(4):
                    _, both[k], both[4 + k] = up(found, k, left, right)
                new_ends.append(both)
        blocks, ends = joined, new_ends
        if level < levels - 1:
            for slot, x in enumerate(facing(level + 1, levels, ends[1], False)):
                consts[level - 1][slot] = x


def facing(level, levels, ends, mine):
    if level < levels - 1:
        return [ends[p] for p in range(8)]
    low_side = side_bit(level)
    if not mine:
        low_side = jnp.logical_not(low_side)
    return [jnp.where(low_side, ends[4 + k], ends[k]) for k in range(4)]


def source_kernel(rows, count, early, src, cpr, add, t):
    ny, nz = src.shape[2], src.shape[3]
    sub = lax.broadcasted_iota(jnp.int32, (ny, nz), 0)
    top, low = sub == ny - 1, sub == 0

    def down(ref, shift):
        def row(i, carry):
            prev = jnp.maximum(i - 1, 0)
            new = []
            for k in range(4):
                a = jnp.broadcast_to(add[k, pl.ds(i, 1), :], (ny, nz))
                b = jnp.broadcast_to(add[4 + k, pl.ds(i, 1), :], (ny, nz))
                x = ref[k, i - shift] + jnp.where(low, a, jnp.where(top, b, 0.0))
                x = x + cpr[KIND[k], prev] * carry[k]
                t[k, i] = x
                new.append(x)
            return tuple(new)

        return row

    state = (jnp.zeros((ny, nz), F32),) * 4
    state = lax.fori_loop(0, count, down(early, 0), state)
    lax.fori_loop(count, rows, down(src, count), state)


def back_kernel(rows, t, inv, cpr, part):
    end = rows - 1
    start = []
    for k in range(4):
        x = inv[KIND[k], end] * t[k, end]
        part[k, end] = x
        start.append(x)

    def row(j, carry):
        i = end - 1 - j
        new = []
        for k in range(4):
            s = KIND[k]
            x = inv[s, i] * t[k, i] + cpr[s, i] * carry[k]
            part[k, i] = x
            new.append(x)
        return tuple(new)

    lax.fori_loop(0, end, row, tuple(start))


def up(joint, k, left, right):
    s = KIND[k]
    d = left[4 + k] - right[k]
    flow = joint[R_ + s] * d
    first = left[k] + joint[GA + s] * (joint[CA + k] - flow)
    last = right[4 + k] + joint[GB + s] * (joint[CB + k] + flow)
    return d, first, last


def up_kernel(levels, own, other, joint, *refs):
    joints = refs[: levels - 1]
    out, diff = refs[levels : levels + 2]
    shares = refs[levels + 2 :]
    low_side = side_bit(0)
    width = out.shape[2]
    left, right = sided(low_side, {p: own[p] for p in range(8)}, {p: other[p] for p in range(8)})
    ends = {}
    for k in range(4):
        diff[k], first, last = up(joint, k, left, right)
        ends[k] = jnp.where(low_side, first[:, :width], first[:, width:])
        ends[4 + k] = jnp.where(low_side, last[:, :width], last[:, width:])
        out[k] = ends[k]
        out[4 + k] = ends[4 + k]
    for level in range(1, levels - 1):
        low_side = side_bit(level)
        joint = joints[level - 1].at[0]
        for k in range(4):
            s = KIND[k]
            first, last = ends[k], ends[4 + k]
            flow = joint[R_ + s] * jnp.where(low_side, last, -first)
            ends[k] = jnp.where(low_side, first, 0.0) - joint[GA + s] * flow
            ends[4 + k] = jnp.where(low_side, 0.0, last) + joint[GB + s] * flow
        for slot, x in enumerate(facing(level + 1, levels, ends, True)):
            shares[level - 1][slot] = x


def joint_flow(joint, k, d, into_first, into_last, low_side):
    s = KIND[k]
    flow = joint[R_ + s] * (d + joint[GA + s] * into_first - joint[GB + s] * into_last)
    first = jnp.where(low_side, into_first, joint[CB + k] + flow)
    last = jnp.where(low_side, joint[CA + k] - flow, into_last)
    return first, last


def beside_kernel(levels, *refs):
    parts, refs = list(refs[: 2 ** (levels - 1) - levels]), refs[2 ** (levels - 1) - levels :]
    consts, outs = refs[: levels - 2], refs[levels - 2 :]
    for level in range(2, levels):
        here = [parts.pop(0) for _ in range(2 ** (level - 1) - 1)]
        for p in range(outs[level - 2].shape[0]):
            total = consts[level - 2][p]
            for part in here:
                total = total + part[p]
            outs[level - 2][p] = total


def settle_kernel(levels, own, *refs):
    near, refs = refs[: levels - 1], refs[levels - 1 :]
    far, joints, out = refs[: levels - 2], refs[levels - 2 : -1], refs[-1]
    ends = {p: own[p] for p in range(8)}
    diffs = []
    for level in range(1, levels):
        low_side = side_bit(level)
        beside = {p: near[level - 1][p] for p in range(near[level - 1].shape[0])}
        if level > 1:
            beside = {p: x + far[level - 2][p] for p, x in beside.items()}
        across = []
        if len(beside) == 4:
            for k in range(4):
                x = beside[k]
                across.append(jnp.where(low_side, ends[4 + k] - x, x - ends[k]))
        else:
            left, right = sided(low_side, ends, beside)
            for k in range(4):
                d, ends[k], ends[4 + k] = up(joints[level - 1].at[0], k, left, right)
                across.append(d)
        diffs.append(across)
    for k in range(4):
        first = last = jnp.zeros_like(diffs[0][0])
        for level in range(levels - 1, 0, -1):
            first, last = joint_flow(
                joints[level - 1].at[0], k, diffs[level - 1][k], first, last, side_bit(level)
            )
        out[k] = first
        out[4 + k] = last


def final_kernel(mine, parts, flux, joint, diff, part, g0, gn, *refs):
    out, buf, sems = refs[-3:]
    rows, half = buf.shape[1], buf.shape[3]
    low_side = side_bit(0)
    core = jnp.bitwise_and(lax.axis_index("line"), 1)
    offset = (core if mine else 1 - core) * half
    copies = []
    for c in range(half // 128):
        near = pl.ds(c * 128, 128)
        z = pl.ds(pl.multiple_of(offset + c * 128, 128), 128)
        across = {plane: joint[plane, :, z] for plane in range(JOINT)}
        into = [
            joint_flow(across, k, diff[k, :, z], flux[k, :, near], flux[4 + k, :, near], low_side)
            for k in range(4)
        ]
        for r in range(parts):
            x = pl.ds(r * (rows // parts), rows // parts)
            for i in range(x.start, x.start + x.size):
                a = [g0[s, i, :, z] for s in range(2)]
                b = [gn[s, i, :, z] for s in range(2)]
                for k in range(4):
                    s = KIND[k]
                    buf[k, i, :, near] = part[k, i, :, z] + (a[s] * into[k][0] + b[s] * into[k][1])
            copies.append(
                pltpu.make_async_copy(
                    buf.at[:, x, :, near], out.at[:, x, :, z], sems.at[c * parts + r]
                )
            )
            copies[-1].start()
    for copy in copies:
        copy.wait()


def local(fields, viscosity):
    rows, ny, nz = viscosity.shape
    lines = lax.axis_size("line")
    cols = lax.axis_size("col")
    levels = lines.bit_length() - 1
    half = nz // 2
    cells = rows * ny * nz
    block = (rows, ny, nz)

    ring = [(i, (i + 1) % cols) for i in range(cols)]
    back_ring = [(b, a) for a, b in ring]

    def gather(at_level):
        found = {}
        for d in sorted(range(1, lines // 2), key=lambda d: (-d.bit_count(), d)):
            x = at_level[d.bit_length()]
            found[d] = lax.ppermute(x, "line", [(i, i ^ (d << 1)) for i in range(lines)])
        return [found[d] for d in sorted(found)]

    def swap(x, level):
        return lax.ppermute(x, "line", [(i, i ^ (1 << level)) for i in range(lines)])

    def cut(at, name, order, flops):
        return call(
            functools.partial(cut_kernel, at),
            name,
            [(5, rows, nz)],
            [fields, viscosity] + order,
            scratch=[pltpu.SemaphoreType.DMA((5,))],
            in_hbm=(0, 1),
            flops=flops,
        )[0]

    y_last = cut(ny - 1, "cut_last", [], 5 * 10**8)
    low = lax.ppermute(y_last, "col", ring)
    y_first = cut(0, "cut_first", [y_last], 5 * 10**8)
    high = lax.ppermute(y_first, "col", back_ring)

    inv, cpr, g0, gn, w = call(
        functools.partial(factor_kernel, rows),
        "factor",
        [(2,) + block] * 4 + [(PLANES, ny, nz)],
        [fields, viscosity],
        scratch=[VMEM((2,) + block, F32), pltpu.SemaphoreType.DMA((2,))],
        in_hbm=(0,),
        flops=10**9,
    )
    count = rows // 4
    (early,) = call(
        functools.partial(early_kernel, count),
        "early",
        [(4, count, ny, nz)],
        [fields, viscosity],
        scratch=[VMEM((4, count + 1, ny, nz), F32), pltpu.SemaphoreType.DMA],
        in_hbm=(0,),
        flops=4 * 10**9,
    )
    src, p, ends = call(
        functools.partial(explicit_kernel, count),
        "explicit",
        [(4, rows - count, ny, nz), (8, ny, nz), (8, rows, nz)],
        [fields, viscosity, g0, gn, early],
        scratch=[VMEM((4, rows - count + 1, ny, nz), F32), pltpu.SemaphoreType.DMA((3,))],
        in_hbm=(0,),
        flops=5 * 10**9,
    )
    pair, w = call(
        pair_kernel,
        "pair",
        [(JOINT, ny, nz), (PLANES, ny, half)],
        [w, swap(w, 0), early],
        moved=4 * ny * nz * 60,
    )
    pairs = lines // 2
    widths = [8] * (levels - 3) + [4]
    found = call(
        functools.partial(chips_kernel, levels),
        "chips",
        [(pairs >> level, JOINT, ny, half) for level in range(1, levels)]
        + [(width, ny, half) for width in widths],
        [w] + gather([w] * (levels + 1)) + [p],
        moved=4 * ny * half * 300,
    )
    joints, consts = list(found[: levels - 1]), list(found[levels - 1 :])

    (add,) = call(
        functools.partial(edge_kernel, rows),
        "edge",
        [(8, rows, nz)],
        [y_last, y_first, low, high],
        flops=8 * cells,
        moved=4 * cells,
    )
    (p,) = call(
        functools.partial(ends_kernel, rows, ny),
        "ends",
        [(8, ny, nz)],
        [add, ends, p, joints[0]],
        flops=6 * cells,
        moved=2 * cells,
    )
    (t,) = call(
        functools.partial(source_kernel, rows, count),
        "source",
        [(4,) + block],
        [early, src, cpr, add],
        flops=30 * cells,
        moved=24 * cells,
    )
    (part,) = call(
        functools.partial(back_kernel, rows),
        "back",
        [(4,) + block],
        [t, inv, cpr],
        flops=20 * cells,
        moved=24 * cells,
    )
    p, diff, *shares = call(
        functools.partial(up_kernel, levels),
        "up",
        [(8, ny, half), (4, ny, nz)] + [(width, ny, half) for width in widths],
        [p, swap(p, 0), pair] + joints + [part],
        moved=4 * ny * nz * 40,
    )
    others = dict(enumerate(gather([None, p] + shares), 1))
    near = [others.pop(1 << level) for level in range(levels - 1)]
    beside = call(
        functools.partial(beside_kernel, levels),
        "beside",
        [(width, ny, half) for width in widths],
        list(others.values()) + consts,
        flops=6 * 10**8,
    )
    (flux,) = call(
        functools.partial(settle_kernel, levels),
        "settle",
        [(8, ny, half)],
        [p] + near + list(beside) + joints,
        moved=4 * ny * half * 100,
    )
    rest = [pair, diff, part, g0, gn]
    parts = 4 if rows % 4 == 0 else 1
    scratch = [VMEM((4, rows, ny, half), F32), pltpu.SemaphoreType.DMA((half // 128 * parts,))]
    (out,) = call(
        functools.partial(final_kernel, True, parts),
        "final_own",
        [(4,) + block],
        [flux] + rest,
        scratch=scratch,
        out_hbm=(0,),
        flops=10**9,
    )
    (out,) = call(
        functools.partial(final_kernel, False, parts),
        "final_other",
        [(4,) + block],
        [swap(flux, 0)] + rest + [out],
        scratch=scratch,
        in_hbm=(6,),
        out_hbm=(0,),
        aliases={6: 0},
        flops=10**9,
    )
    return out


def solution(mesh):
    return jax.shard_map(
        local,
        mesh=mesh,
        in_specs=(P(None, "line", "col", None), P("line", "col", None)),
        out_specs=P(None, "line", "col", None),
        check_vma=False,
    )
```

```python
import functools

import jax
import jax.numpy as jnp
from jax import lax
from jax.experimental import pallas as pl
from jax.experimental.pallas import tpu as pltpu
from jax.sharding import PartitionSpec as P

STIFF = 3072
THERMAL_RATIO = 0.8
CROSS_RATE = 0.2
ADVECTION = 0.25
BUOYANCY = 2.0
SCALES = (1.0, THERMAL_RATIO)
KIND = (0, 0, 0, 1)

F32 = jnp.float32
VMEM = pltpu.VMEM
LIMIT = 24 * 1024 * 1024

G00, G0N, GNN = (0, 3), (1, 4), (2, 5)
V_FIRST, V_LAST, F_FIRST, F_LAST = 6, 7, 8, 12
PLANES = 16
R_, GA, GB, CA, CB = 0, 2, 4, 6, 10
JOINT = 14


def in_vmem(x):
    return pltpu.with_memory_space_constraint(x, VMEM)


def spec():
    return pl.BlockSpec(memory_space=VMEM)


def call(kernel, name, out_shapes, args, scratch=(), in_hbm=(), any_out=(), flops=0, moved=0):
    in_specs = []
    operands = []
    for i, x in enumerate(args):
        if i in in_hbm:
            in_specs.append(pl.BlockSpec(memory_space=pltpu.HBM))
            operands.append(pltpu.with_memory_space_constraint(x, pltpu.HBM))
        else:
            in_specs.append(spec())
            operands.append(in_vmem(x))
    out_shape = []
    out_specs = []
    for i, s in enumerate(out_shapes):
        if i in any_out:
            out_shape.append(jax.ShapeDtypeStruct(s, F32))
            out_specs.append(pl.BlockSpec(memory_space=pl.ANY))
        else:
            out_shape.append(VMEM(s, F32))
            out_specs.append(spec())
    return pl.pallas_call(
        kernel,
        out_shape=out_shape,
        in_specs=in_specs,
        out_specs=out_specs,
        scratch_shapes=list(scratch),
        compiler_params=pltpu.CompilerParams(vmem_limit_bytes=LIMIT),
        cost_estimate=pl.CostEstimate(flops=flops, bytes_accessed=moved, transcendentals=0),
        name=name,
    )(*operands)


def layer(read, ny, nz):
    sub = lax.broadcasted_iota(jnp.int32, (8, nz), 0)
    tile = jnp.broadcast_to(read(0), (8, nz))
    for r in range(1, 8):
        tile = jnp.where(sub == r, jnp.broadcast_to(read(r), (8, nz)), tile)
    return tile


def cut_kernel(ny, fields, visc, y_first, y_last, sems):
    copies = []
    for j, (at, out) in enumerate(((0, y_first), (ny - 1, y_last))):
        for k in range(4):
            copies.append(pltpu.make_async_copy(fields.at[k, :, at], out.at[k], sems.at[j, k]))
        copies.append(pltpu.make_async_copy(visc.at[:, at], out.at[4], sems.at[j, 4]))
    for copy in copies:
        copy.start()
    for copy in copies:
        copy.wait()


def factor_kernel(rows, fields_ref, visc, inv, cpr, g0, gn, w, tau, sems):
    copies = [
        pltpu.make_async_copy(fields_ref.at[:, 0], w.at[F_FIRST : F_FIRST + 4], sems.at[0]),
        pltpu.make_async_copy(fields_ref.at[:, rows - 1], w.at[F_LAST : F_LAST + 4], sems.at[1]),
    ]
    for copy in copies:
        copy.start()
    ny, nz = visc.shape[1], visc.shape[2]
    me = lax.axis_index("line")
    wall_low = jnp.where(me == 0, 1.0, 0.0).astype(F32)
    wall_high = jnp.where(me == lax.axis_size("line") - 1, 1.0, 0.0).astype(F32)
    one = jnp.ones((ny, nz), F32)

    def row(i, carry):
        low, v = carry[4], carry[5]
        after = visc[jnp.minimum(i + 1, rows - 1)]
        high = jnp.where(i == rows - 1, (0.5 * STIFF) * wall_high * v, (0.5 * STIFF) * (v + after))
        new = []
        for s in range(2):
            gain, running = carry[2 * s], carry[2 * s + 1]
            down = SCALES[s] * low if s else low
            up = SCALES[s] * high if s else high
            q = 1.0 + down * gain
            one_over = 1.0 / (q + up)
            coupling = up * one_over
            inv[s, i] = one_over
            cpr[s, i] = coupling
            tau[s, i] = running
            new += [q * one_over, coupling * running]
        return tuple(new) + (high, after)

    first = visc[0]
    lax.fori_loop(0, rows, row, (one,) * 4 + (wall_low * (0.5 * STIFF) * first, first))

    end = rows - 1
    start = []
    for s in range(2):
        a = inv[s, end] * tau[s, end]
        b = inv[s, end]
        g0[s, end] = a
        gn[s, end] = b
        w[G0N[s]] = a
        w[GNN[s]] = b
        start += [a, b]

    def back(j, carry):
        i = end - 1 - j
        new = []
        for s in range(2):
            c = cpr[s, i]
            a = inv[s, i] * tau[s, i] + c * carry[2 * s]
            b = c * carry[2 * s + 1]
            g0[s, i] = a
            gn[s, i] = b
            new += [a, b]
        return tuple(new)

    final = lax.fori_loop(0, end, back, tuple(start))
    for s in range(2):
        w[G00[s]] = final[2 * s]
    w[V_FIRST] = first
    w[V_LAST] = visc[rows - 1]
    for copy in copies:
        copy.wait()


def explicit_rows(first, count, base, start, fields, visc, src):
    rows, ny, nz = visc.shape
    lane = lax.broadcasted_iota(jnp.int32, (ny, nz), 1)
    sub = lax.broadcasted_iota(jnp.int32, (ny, nz), 0)
    z_top, z_low = lane == nz - 1, lane == 0
    y_top, y_low = sub == ny - 1, sub == 0

    def sides(x):
        return (
            pltpu.roll(x, ny - 1, 0),
            pltpu.roll(x, 1, 0),
            pltpu.roll(x, nz - 1, 1),
            pltpu.roll(x, 1, 1),
        )

    def row(i, _):
        f = [fields[k, i - base] for k in range(4)]
        v = visc[i]
        after, before = jnp.minimum(i + 1, rows - 1), jnp.maximum(i - 1, 0)
        vyn, vyp, vzn, vzp = sides(v)
        half = 0.5 * CROSS_RATE
        faces = [
            jnp.where(y_top, 0.0, half * (v + vyn)),
            jnp.where(y_low, 0.0, half * (v + vyp)),
            half * (v + jnp.where(z_top, 0.0, vzn)),
            half * (v + jnp.where(z_low, 0.0, vzp)),
        ]
        none = [y_top, y_low, z_top, z_low]
        total = (faces[0] + faces[1]) + (faces[2] + faces[3])
        adv = [(-0.5 * ADVECTION) * f[k] for k in range(3)]
        move = [adv[1], -adv[1], adv[2], -adv[2]]
        adv_after = jnp.where(i == rows - 1, 0.0, adv[0])
        adv_before = jnp.where(i == 0, 0.0, adv[0])
        weights, centre = [], []
        for s in range(2):
            scaled = [SCALES[s] * x if s else x for x in faces]
            weights.append([jnp.where(n, 0.0, x + m) for n, x, m in zip(none, scaled, move)])
            centre.append(1.0 - (SCALES[s] * total if s else total))
        for k in range(4):
            s = KIND[k]
            near = sides(f[k])
            out = centre[s] * f[k] + adv_after * fields[k, after - base] - adv_before * fields[k, before - base]
            for c, x in zip(weights[s], near):
                out = out + c * x
            if k == 2:
                out = out + BUOYANCY * f[3]
            src[k, i - start] = out
        return 0

    lax.fori_loop(first, first + count, row, 0)


def early_kernel(count, fields_ref, visc, src, fields, sem):
    copy = pltpu.make_async_copy(fields_ref.at[:, 0 : count + 1], fields, sem)
    copy.start()
    copy.wait()
    explicit_rows(0, count, 0, 0, fields, visc, src)


def explicit_kernel(count, fields_ref, visc, g0, gn, early, src, p, ends, fields, sems):
    rows, ny, nz = visc.shape
    cuts = [count - 1] + list(range(2 * count + 1, rows, count)) + [rows]
    copies = []
    for c, (lo, hi) in enumerate(zip(cuts, cuts[1:])):
        copies.append(
            pltpu.make_async_copy(
                fields_ref.at[:, lo:hi], fields.at[:, lo - cuts[0] : hi - cuts[0]], sems.at[c]
            )
        )
        copies[-1].start()
    for c, copy in enumerate(copies):
        copy.wait()
        explicit_rows((c + 1) * count, count, cuts[0], count, fields, visc, src)

    def dot(ref, shift):
        def add(i, carry):
            new = []
            for g, base in ((g0, 0), (gn, 4)):
                for k in range(4):
                    new.append(carry[base + k] + g[KIND[k], i] * ref[k, i - shift])
            return tuple(new)

        return add

    final = (jnp.zeros((ny, nz), F32),) * 8
    final = lax.fori_loop(0, count, dot(early, 0), final)
    final = lax.fori_loop(count, rows, dot(src, count), final)
    for k in range(8):
        p[k] = final[k]

    for s in range(2):
        for side, at in ((0, 0), (1, ny - 1)):
            for which, g in ((0, g0), (1, gn)):
                for lo in range(0, rows, 8):
                    ends[4 * side + 2 * which + s, lo : lo + 8] = layer(
                        lambda r: g[s, lo + r, at : at + 1, :], ny, nz
                    )


def edge_kernel(rows, y_last, y_first, low, high, add):
    nz = add.shape[2]
    rate = 0.5 * ADVECTION
    for side, mine, far, sign in ((0, y_first, low, rate), (4, y_last, high, -rate)):
        for r in range(rows // 8):
            x = pl.ds(r * 8, 8)
            face = (0.5 * CROSS_RATE) * (mine[4, x] + far[4, x])
            faces = (face, THERMAL_RATIO * face)
            adv = sign * mine[1, x]
            both = [adv + c for c in faces]
            for k in range(4):
                s = KIND[k]
                add[side + k, x] = both[s] * far[k, x] - faces[s] * mine[k, x]


def ends_kernel(rows, ny, add, ends, p, tie, out):
    nz = out.shape[2]
    sub = lax.broadcasted_iota(jnp.int32, (ny, 128), 0)
    for j in range(nz // 128):
        z = pl.ds(j * 128, 128)
        sums = []
        for side in (0, 4):
            total = [None] * 8
            for r in range(rows // 8):
                x = pl.ds(r * 8, 8)
                g = [ends[side + q, x, z] for q in range(4)]
                for k in range(4):
                    h = add[side + k, x, z]
                    for slot, c in ((k, g[KIND[k]]), (4 + k, g[2 + KIND[k]])):
                        part = c * h
                        total[slot] = part if total[slot] is None else total[slot] + part
            sums.append(total)
        for slot in range(8):
            add_low = jnp.sum(sums[0][slot], axis=0, keepdims=True)
            add_high = jnp.sum(sums[1][slot], axis=0, keepdims=True)
            both = jnp.where(sub == 0, add_low, jnp.where(sub == ny - 1, add_high, 0.0))
            out[slot, :, z] = p[slot, :, z] + both


def side_bit(level):
    return jnp.bitwise_and(jnp.right_shift(lax.axis_index("line"), level), 1) == 0


def join(left, right):
    face = left[V_LAST] + right[V_FIRST]
    joint, new, ratio = {}, {}, []
    for s in range(2):
        resist = 1.0 / ((0.5 * STIFF * SCALES[s]) * face)
        r = 1.0 / (resist + left[GNN[s]] + right[G00[s]])
        ratio.append(r)
        a, b = left[G0N[s]], right[G0N[s]]
        joint[R_ + s] = r
        joint[GA + s] = a
        joint[GB + s] = b
        new[G00[s]] = left[G00[s]] - r * a * a
        new[GNN[s]] = right[GNN[s]] - r * b * b
        new[G0N[s]] = r * a * b
    rate = 0.5 * ADVECTION
    for k in range(4):
        s = KIND[k]
        add_a = -rate * left[F_LAST] * right[F_FIRST + k]
        add_b = rate * right[F_FIRST] * left[F_LAST + k]
        e = ratio[s] * (left[GNN[s]] * add_a - right[G00[s]] * add_b)
        joint[CA + k] = add_a - e
        joint[CB + k] = add_b + e
        new[F_FIRST + k] = left[F_FIRST + k]
        new[F_LAST + k] = right[F_LAST + k]
    new[V_FIRST] = left[V_FIRST]
    new[V_LAST] = right[V_LAST]
    return joint, new


def sided(low_side, mine, theirs):
    left = {p: jnp.where(low_side, mine[p], theirs[p]) for p in mine}
    right = {p: jnp.where(low_side, theirs[p], mine[p]) for p in mine}
    return left, right


def pair_kernel(own, other, *refs):
    joint, out = refs[-2:]
    low_side = side_bit(0)
    planes = range(PLANES)
    found, new = join(*sided(low_side, {p: own[p] for p in planes}, {p: other[p] for p in planes}))
    for plane in range(JOINT):
        joint[plane] = found[plane]
    width = out.shape[2]
    for plane in planes:
        out[plane] = jnp.where(low_side, new[plane][:, :width], new[plane][:, width:])


def chips_kernel(levels, own, *refs):
    others, joints = refs[: 2 ** (levels - 1) - 1], refs[-(levels - 1) :]
    blocks = [{p: x[p] for p in range(PLANES)} for x in (own, *others)]
    for level in range(1, levels):
        low_side = side_bit(level)
        joined = []
        for j in range(0, len(blocks), 2):
            found, new = join(*sided(low_side, blocks[j], blocks[j + 1]))
            for plane in range(JOINT):
                joints[level - 1][j // 2, plane] = found[plane]
            joined.append(new)
        blocks = joined


def source_kernel(rows, count, early, src, cpr, add, t):
    ny, nz = src.shape[2], src.shape[3]
    sub = lax.broadcasted_iota(jnp.int32, (ny, nz), 0)
    top, low = sub == ny - 1, sub == 0

    def down(ref, shift):
        def row(i, carry):
            prev = jnp.maximum(i - 1, 0)
            new = []
            for k in range(4):
                a = jnp.broadcast_to(add[k, pl.ds(i, 1), :], (ny, nz))
                b = jnp.broadcast_to(add[4 + k, pl.ds(i, 1), :], (ny, nz))
                x = ref[k, i - shift] + jnp.where(low, a, jnp.where(top, b, 0.0))
                x = x + cpr[KIND[k], prev] * carry[k]
                t[k, i] = x
                new.append(x)
            return tuple(new)

        return row

    state = (jnp.zeros((ny, nz), F32),) * 4
    state = lax.fori_loop(0, count, down(early, 0), state)
    lax.fori_loop(count, rows, down(src, count), state)


def back_kernel(rows, t, inv, cpr, part):
    end = rows - 1
    start = []
    for k in range(4):
        x = inv[KIND[k], end] * t[k, end]
        part[k, end] = x
        start.append(x)

    def row(j, carry):
        i = end - 1 - j
        new = []
        for k in range(4):
            s = KIND[k]
            x = inv[s, i] * t[k, i] + cpr[s, i] * carry[k]
            part[k, i] = x
            new.append(x)
        return tuple(new)

    lax.fori_loop(0, end, row, tuple(start))


def up(joint, k, left, right):
    s = KIND[k]
    d = left[4 + k] - right[k]
    flow = joint[R_ + s] * d
    first = left[k] + joint[GA + s] * (joint[CA + k] - flow)
    last = right[4 + k] + joint[GB + s] * (joint[CB + k] + flow)
    return d, first, last


def up_kernel(own, other, joint, *refs):
    out, diff = refs[-2:]
    low_side = side_bit(0)
    width = out.shape[2]
    left, right = sided(low_side, {p: own[p] for p in range(8)}, {p: other[p] for p in range(8)})
    for k in range(4):
        diff[k], first, last = up(joint, k, left, right)
        out[k] = jnp.where(low_side, first[:, :width], first[:, width:])
        out[4 + k] = jnp.where(low_side, last[:, :width], last[:, width:])


def joint_flow(joint, k, d, into_first, into_last, low_side):
    s = KIND[k]
    flow = joint[R_ + s] * (d + joint[GA + s] * into_first - joint[GB + s] * into_last)
    first = jnp.where(low_side, into_first, joint[CB + k] + flow)
    last = jnp.where(low_side, joint[CA + k] - flow, into_last)
    return first, last


def gathered(levels, own, ref, planes):
    mine = jnp.right_shift(lax.axis_index("line"), 1)
    blocks = [{p: own[p] for p in planes}]
    for d in range(1, 2 ** (levels - 1)):
        at = jnp.bitwise_xor(mine, d)
        blocks.append({p: ref[at, p] for p in planes})
    return blocks


def settle_kernel(levels, own, *refs):
    others, joints, out = refs[0], refs[-levels:-1], refs[-1]
    blocks = gathered(levels, own, others, range(8))
    diffs = []
    for level in range(1, levels):
        low_side = side_bit(level)
        joined = []
        for j in range(0, len(blocks), 2):
            left, right = sided(low_side, blocks[j], blocks[j + 1])
            joint = joints[level - 1].at[j // 2]
            new, across = {}, []
            for k in range(4):
                d, new[k], new[4 + k] = up(joint, k, left, right)
                across.append(d)
            joined.append(new)
            if j == 0:
                diffs.append(across)
        blocks = joined
    for k in range(4):
        first = last = jnp.zeros_like(diffs[0][0])
        for level in range(levels - 1, 0, -1):
            first, last = joint_flow(
                joints[level - 1].at[0], k, diffs[level - 1][k], first, last, side_bit(level)
            )
        out[k] = first
        out[4 + k] = last


def final_kernel(rows, parts, own, other, joint, diff, part, g0, gn, out, flux, buf, sems):
    bit = jnp.bitwise_and(lax.axis_index("line"), 1)
    low_side = bit == 0
    width = own.shape[2]
    for k in range(8):
        flux[k, :, :width] = jnp.where(low_side, own[k], other[k])
        flux[k, :, width:] = jnp.where(low_side, other[k], own[k])
    for k in range(4):
        first, last = joint_flow(joint, k, diff[k], flux[k], flux[4 + k], low_side)
        flux[k] = first
        flux[4 + k] = last
    copies = []
    for c in range(parts):
        z = pl.ds(c * 128, 128)
        into = [flux[k, :, z] for k in range(8)]
        for i in range(rows):
            a = [g0[s, i, :, z] for s in range(2)]
            b = [gn[s, i, :, z] for s in range(2)]
            for k in range(4):
                s = KIND[k]
                buf[k, i, :, z] = part[k, i, :, z] + (a[s] * into[k] + b[s] * into[4 + k])
        copy = pltpu.make_async_copy(buf.at[:, :, :, z], out.at[:, :, :, z], sems.at[c])
        copy.start()
        copies.append(copy)
    for copy in copies:
        copy.wait()


def local(fields, viscosity):
    rows, ny, nz = viscosity.shape
    lines = lax.axis_size("line")
    cols = lax.axis_size("col")
    levels = lines.bit_length() - 1
    half = nz // 2
    cells = rows * ny * nz
    block = (rows, ny, nz)

    ring = [(i, (i + 1) % cols) for i in range(cols)]
    back_ring = [(b, a) for a, b in ring]

    def gather(x):
        found = {}
        for d in sorted(range(1, lines // 2), key=lambda d: (-d.bit_count(), d)):
            found[d] = lax.ppermute(x, "line", [(i, i ^ (d << 1)) for i in range(lines)])
        return [found[d] for d in sorted(found)]

    def swap(x, level):
        return lax.ppermute(x, "line", [(i, i ^ (1 << level)) for i in range(lines)])

    y_first, y_last = call(
        functools.partial(cut_kernel, ny),
        "cut",
        [(5, rows, nz), (5, rows, nz)],
        [fields, viscosity],
        scratch=[pltpu.SemaphoreType.DMA((2, 5))],
        in_hbm=(0, 1),
        moved=2 * cells,
    )
    low = lax.ppermute(y_last, "col", ring)
    high = lax.ppermute(y_first, "col", back_ring)

    inv, cpr, g0, gn, w = call(
        functools.partial(factor_kernel, rows),
        "factor",
        [(2,) + block] * 4 + [(PLANES, ny, nz)],
        [fields, viscosity],
        scratch=[VMEM((2,) + block, F32), pltpu.SemaphoreType.DMA((2,))],
        in_hbm=(0,),
        flops=10**9,
    )
    count = rows // 4
    (early,) = call(
        functools.partial(early_kernel, count),
        "early",
        [(4, count, ny, nz)],
        [fields, viscosity],
        scratch=[VMEM((4, count + 1, ny, nz), F32), pltpu.SemaphoreType.DMA],
        in_hbm=(0,),
        flops=4 * 10**9,
    )
    src, p, ends = call(
        functools.partial(explicit_kernel, count),
        "explicit",
        [(4, rows - count, ny, nz), (8, ny, nz), (8, rows, nz)],
        [fields, viscosity, g0, gn, early],
        scratch=[VMEM((4, rows - count + 1, ny, nz), F32), pltpu.SemaphoreType.DMA((3,))],
        in_hbm=(0,),
        flops=5 * 10**9,
    )
    pair, w = call(
        pair_kernel,
        "pair",
        [(JOINT, ny, nz), (PLANES, ny, half)],
        [w, swap(w, 0), early],
        moved=4 * ny * nz * 60,
    )
    pairs = lines // 2
    joints = call(
        functools.partial(chips_kernel, levels),
        "chips",
        [(pairs >> level, JOINT, ny, half) for level in range(1, levels)],
        [w] + gather(w) + [p],
        moved=4 * ny * half * 300,
    )

    (add,) = call(
        functools.partial(edge_kernel, rows),
        "edge",
        [(8, rows, nz)],
        [y_last, y_first, low, high],
        flops=8 * cells,
        moved=4 * cells,
    )
    (p,) = call(
        functools.partial(ends_kernel, rows, ny),
        "ends",
        [(8, ny, nz)],
        [add, ends, p, joints[0]],
        flops=6 * cells,
        moved=2 * cells,
    )
    (t,) = call(
        functools.partial(source_kernel, rows, count),
        "source",
        [(4,) + block],
        [early, src, cpr, add],
        flops=30 * cells,
        moved=24 * cells,
    )
    (part,) = call(
        functools.partial(back_kernel, rows),
        "back",
        [(4,) + block],
        [t, inv, cpr],
        flops=20 * cells,
        moved=24 * cells,
    )
    p, diff = call(
        up_kernel,
        "up",
        [(8, ny, half), (4, ny, nz)],
        [p, swap(p, 0), pair, t],
        moved=4 * ny * nz * 40,
    )
    groups = [[i for i in range(lines) if i % 2 == side] for side in range(2)]
    (flux,) = call(
        functools.partial(settle_kernel, levels),
        "settle",
        [(8, ny, half)],
        [p, lax.all_gather(p, "line", axis_index_groups=groups)] + list(joints),
        moved=4 * ny * half * 100,
    )
    parts = nz // 128
    (out,) = call(
        functools.partial(final_kernel, rows, parts),
        "final",
        [(4,) + block],
        [flux, swap(flux, 0), pair, diff, part, g0, gn],
        scratch=[VMEM((8, ny, nz), F32), VMEM((4,) + block, F32), pltpu.SemaphoreType.DMA((parts,))],
        any_out=(0,),
        flops=16 * cells,
        moved=16 * cells,
    )
    return out


def solution(mesh):
    return jax.shard_map(
        local,
        mesh=mesh,
        in_specs=(P(None, "line", "col", None), P("line", "col", None)),
        out_specs=P(None, "line", "col", None),
        check_vma=False,
    )
```

```python
import functools

import jax
import jax.numpy as jnp
from jax import lax
from jax.experimental import pallas as pl
from jax.experimental.pallas import tpu as pltpu
from jax.sharding import PartitionSpec as P

STIFF = 3072
THERMAL_RATIO = 0.8
CROSS_RATE = 0.2
ADVECTION = 0.25
BUOYANCY = 2.0
SCALES = (1.0, THERMAL_RATIO)
KIND = (0, 0, 0, 1)

F32 = jnp.float32
VMEM = pltpu.VMEM
LIMIT = 24 * 1024 * 1024

G00, G0N, GNN = (0, 3), (1, 4), (2, 5)
V_FIRST, V_LAST, F_FIRST, F_LAST = 6, 7, 8, 12
PLANES = 16
R_, GA, GB, CA, CB = 0, 2, 4, 6, 10
JOINT = 14


def in_vmem(x):
    return pltpu.with_memory_space_constraint(x, VMEM)


def spec():
    return pl.BlockSpec(memory_space=VMEM)


def call(kernel, name, out_shapes, args, scratch=(), in_hbm=(), out_hbm=(), aliases={}, flops=0, moved=0):
    in_specs = []
    operands = []
    for i, x in enumerate(args):
        if i in in_hbm:
            in_specs.append(pl.BlockSpec(memory_space=pltpu.HBM))
            operands.append(pltpu.with_memory_space_constraint(x, pltpu.HBM))
        else:
            in_specs.append(spec())
            operands.append(in_vmem(x))
    out_shape = []
    out_specs = []
    for i, s in enumerate(out_shapes):
        if i in out_hbm:
            out_shape.append(pltpu.HBM(s, F32))
            out_specs.append(pl.BlockSpec(memory_space=pltpu.HBM))
        else:
            out_shape.append(VMEM(s, F32))
            out_specs.append(spec())
    return pl.pallas_call(
        kernel,
        out_shape=out_shape,
        in_specs=in_specs,
        out_specs=out_specs,
        scratch_shapes=list(scratch),
        input_output_aliases=aliases,
        compiler_params=pltpu.CompilerParams(vmem_limit_bytes=LIMIT),
        cost_estimate=pl.CostEstimate(flops=flops, bytes_accessed=moved, transcendentals=0),
        name=name,
    )(*operands)


def layer(read, ny, nz):
    sub = lax.broadcasted_iota(jnp.int32, (8, nz), 0)
    tile = jnp.broadcast_to(read(0), (8, nz))
    for r in range(1, 8):
        tile = jnp.where(sub == r, jnp.broadcast_to(read(r), (8, nz)), tile)
    return tile


def cut_kernel(at, fields, visc, *refs):
    out, sems = refs[-2:]
    copies = [pltpu.make_async_copy(fields.at[k, :, at], out.at[k], sems.at[k]) for k in range(4)]
    copies.append(pltpu.make_async_copy(visc.at[:, at], out.at[4], sems.at[4]))
    for copy in copies:
        copy.start()
    for copy in copies:
        copy.wait()


def factor_kernel(rows, fields_ref, visc, inv, cpr, g0, gn, w, tau, sems):
    copies = [
        pltpu.make_async_copy(fields_ref.at[:, 0], w.at[F_FIRST : F_FIRST + 4], sems.at[0]),
        pltpu.make_async_copy(fields_ref.at[:, rows - 1], w.at[F_LAST : F_LAST + 4], sems.at[1]),
    ]
    for copy in copies:
        copy.start()
    ny, nz = visc.shape[1], visc.shape[2]
    me = lax.axis_index("line")
    wall_low = jnp.where(me == 0, 1.0, 0.0).astype(F32)
    wall_high = jnp.where(me == lax.axis_size("line") - 1, 1.0, 0.0).astype(F32)
    one = jnp.ones((ny, nz), F32)

    def row(i, carry):
        low, v = carry[4], carry[5]
        after = visc[jnp.minimum(i + 1, rows - 1)]
        high = jnp.where(i == rows - 1, (0.5 * STIFF) * wall_high * v, (0.5 * STIFF) * (v + after))
        new = []
        for s in range(2):
            gain, running = carry[2 * s], carry[2 * s + 1]
            down = SCALES[s] * low if s else low
            up = SCALES[s] * high if s else high
            q = 1.0 + down * gain
            one_over = 1.0 / (q + up)
            coupling = up * one_over
            inv[s, i] = one_over
            cpr[s, i] = coupling
            tau[s, i] = running
            new += [q * one_over, coupling * running]
        return tuple(new) + (high, after)

    first = visc[0]
    lax.fori_loop(0, rows, row, (one,) * 4 + (wall_low * (0.5 * STIFF) * first, first))

    end = rows - 1
    start = []
    for s in range(2):
        a = inv[s, end] * tau[s, end]
        b = inv[s, end]
        g0[s, end] = a
        gn[s, end] = b
        w[G0N[s]] = a
        w[GNN[s]] = b
        start += [a, b]

    def back(j, carry):
        i = end - 1 - j
        new = []
        for s in range(2):
            c = cpr[s, i]
            a = inv[s, i] * tau[s, i] + c * carry[2 * s]
            b = c * carry[2 * s + 1]
            g0[s, i] = a
            gn[s, i] = b
            new += [a, b]
        return tuple(new)

    final = lax.fori_loop(0, end, back, tuple(start))
    for s in range(2):
        w[G00[s]] = final[2 * s]
    w[V_FIRST] = first
    w[V_LAST] = visc[rows - 1]
    for copy in copies:
        copy.wait()


def explicit_rows(first, count, base, start, fields, visc, src):
    rows, ny, nz = visc.shape
    lane = lax.broadcasted_iota(jnp.int32, (ny, nz), 1)
    sub = lax.broadcasted_iota(jnp.int32, (ny, nz), 0)
    z_top, z_low = lane == nz - 1, lane == 0
    y_top, y_low = sub == ny - 1, sub == 0

    def sides(x):
        return (
            pltpu.roll(x, ny - 1, 0),
            pltpu.roll(x, 1, 0),
            pltpu.roll(x, nz - 1, 1),
            pltpu.roll(x, 1, 1),
        )

    def row(i, _):
        f = [fields[k, i - base] for k in range(4)]
        v = visc[i]
        after, before = jnp.minimum(i + 1, rows - 1), jnp.maximum(i - 1, 0)
        vyn, vyp, vzn, vzp = sides(v)
        half = 0.5 * CROSS_RATE
        faces = [
            jnp.where(y_top, 0.0, half * (v + vyn)),
            jnp.where(y_low, 0.0, half * (v + vyp)),
            half * (v + jnp.where(z_top, 0.0, vzn)),
            half * (v + jnp.where(z_low, 0.0, vzp)),
        ]
        none = [y_top, y_low, z_top, z_low]
        total = (faces[0] + faces[1]) + (faces[2] + faces[3])
        adv = [(-0.5 * ADVECTION) * f[k] for k in range(3)]
        move = [adv[1], -adv[1], adv[2], -adv[2]]
        adv_after = jnp.where(i == rows - 1, 0.0, adv[0])
        adv_before = jnp.where(i == 0, 0.0, adv[0])
        weights, centre = [], []
        for s in range(2):
            scaled = [SCALES[s] * x if s else x for x in faces]
            weights.append([jnp.where(n, 0.0, x + m) for n, x, m in zip(none, scaled, move)])
            centre.append(1.0 - (SCALES[s] * total if s else total))
        for k in range(4):
            s = KIND[k]
            near = sides(f[k])
            out = centre[s] * f[k] + adv_after * fields[k, after - base] - adv_before * fields[k, before - base]
            for c, x in zip(weights[s], near):
                out = out + c * x
            if k == 2:
                out = out + BUOYANCY * f[3]
            src[k, i - start] = out
        return 0

    lax.fori_loop(first, first + count, row, 0)


def early_kernel(count, fields_ref, visc, src, fields, sem):
    copy = pltpu.make_async_copy(fields_ref.at[:, 0 : count + 1], fields, sem)
    copy.start()
    copy.wait()
    explicit_rows(0, count, 0, 0, fields, visc, src)


def explicit_kernel(count, fields_ref, visc, g0, gn, early, src, p, ends, fields, sems):
    rows, ny, nz = visc.shape
    cuts = [count - 1] + list(range(2 * count + 1, rows, count)) + [rows]
    copies = []
    for c, (lo, hi) in enumerate(zip(cuts, cuts[1:])):
        copies.append(
            pltpu.make_async_copy(
                fields_ref.at[:, lo:hi], fields.at[:, lo - cuts[0] : hi - cuts[0]], sems.at[c]
            )
        )
        copies[-1].start()
    for c, copy in enumerate(copies):
        copy.wait()
        explicit_rows((c + 1) * count, count, cuts[0], count, fields, visc, src)

    def dot(ref, shift):
        def add(i, carry):
            new = []
            for g, base in ((g0, 0), (gn, 4)):
                for k in range(4):
                    new.append(carry[base + k] + g[KIND[k], i] * ref[k, i - shift])
            return tuple(new)

        return add

    final = (jnp.zeros((ny, nz), F32),) * 8
    final = lax.fori_loop(0, count, dot(early, 0), final)
    final = lax.fori_loop(count, rows, dot(src, count), final)
    for k in range(8):
        p[k] = final[k]

    for s in range(2):
        for side, at in ((0, 0), (1, ny - 1)):
            for which, g in ((0, g0), (1, gn)):
                for lo in range(0, rows, 8):
                    ends[4 * side + 2 * which + s, lo : lo + 8] = layer(
                        lambda r: g[s, lo + r, at : at + 1, :], ny, nz
                    )


def edge_kernel(rows, ny, y_last, y_first, low, high, ends, p, *refs):
    add, out = refs[-2:]
    nz = out.shape[2]
    sub = lax.broadcasted_iota(jnp.int32, (ny, 128), 0)
    rate = 0.5 * ADVECTION
    for j in range(nz // 128):
        z = pl.ds(j * 128, 128)
        sums = []
        for side, mine, far, sign in ((0, y_first, low, rate), (4, y_last, high, -rate)):
            total = [None] * 8
            for r in range(rows // 8):
                x = pl.ds(r * 8, 8)
                face = (0.5 * CROSS_RATE) * (mine[4, x, z] + far[4, x, z])
                faces = (face, THERMAL_RATIO * face)
                adv = sign * mine[1, x, z]
                both = [adv + c for c in faces]
                g = [ends[side + q, x, z] for q in range(4)]
                for k in range(4):
                    s = KIND[k]
                    h = both[s] * far[k, x, z] - faces[s] * mine[k, x, z]
                    add[side + k, x, z] = h
                    for slot, c in ((k, g[s]), (4 + k, g[2 + s])):
                        part = c * h
                        total[slot] = part if total[slot] is None else total[slot] + part
            sums.append(total)
        for slot in range(8):
            add_low = jnp.sum(sums[0][slot], axis=0, keepdims=True)
            add_high = jnp.sum(sums[1][slot], axis=0, keepdims=True)
            both = jnp.where(sub == 0, add_low, jnp.where(sub == ny - 1, add_high, 0.0))
            out[slot, :, z] = p[slot, :, z] + both


def side_bit(level):
    return jnp.bitwise_and(jnp.right_shift(lax.axis_index("line"), level), 1) == 0


def join(left, right):
    face = left[V_LAST] + right[V_FIRST]
    joint, new, ratio = {}, {}, []
    for s in range(2):
        resist = 1.0 / ((0.5 * STIFF * SCALES[s]) * face)
        r = 1.0 / (resist + left[GNN[s]] + right[G00[s]])
        ratio.append(r)
        a, b = left[G0N[s]], right[G0N[s]]
        joint[R_ + s] = r
        joint[GA + s] = a
        joint[GB + s] = b
        new[G00[s]] = left[G00[s]] - r * a * a
        new[GNN[s]] = right[GNN[s]] - r * b * b
        new[G0N[s]] = r * a * b
    rate = 0.5 * ADVECTION
    for k in range(4):
        s = KIND[k]
        add_a = -rate * left[F_LAST] * right[F_FIRST + k]
        add_b = rate * right[F_FIRST] * left[F_LAST + k]
        e = ratio[s] * (left[GNN[s]] * add_a - right[G00[s]] * add_b)
        joint[CA + k] = add_a - e
        joint[CB + k] = add_b + e
        new[F_FIRST + k] = left[F_FIRST + k]
        new[F_LAST + k] = right[F_LAST + k]
    new[V_FIRST] = left[V_FIRST]
    new[V_LAST] = right[V_LAST]
    return joint, new


def sided(low_side, mine, theirs):
    left = {p: jnp.where(low_side, mine[p], theirs[p]) for p in mine}
    right = {p: jnp.where(low_side, theirs[p], mine[p]) for p in mine}
    return left, right


def pair_kernel(own, other, *refs):
    joint, out = refs[-2:]
    low_side = side_bit(0)
    planes = range(PLANES)
    found, new = join(*sided(low_side, {p: own[p] for p in planes}, {p: other[p] for p in planes}))
    for plane in range(JOINT):
        joint[plane] = found[plane]
    width = out.shape[2]
    for plane in planes:
        out[plane] = jnp.where(low_side, new[plane][:, :width], new[plane][:, width:])


def chips_kernel(levels, own, *refs):
    others = refs[: 2 ** (levels - 1) - 1]
    joints = refs[-(2 * levels - 3) : len(refs) - (levels - 2)]
    consts = refs[len(refs) - (levels - 2) :]
    blocks = [{p: x[p] for p in range(PLANES)} for x in (own, *others)]
    zero = jnp.zeros_like(own[0])
    ends = [{p: zero for p in range(8)} for _ in blocks]
    for level in range(1, levels):
        low_side = side_bit(level)
        joined, new_ends = [], []
        for j in range(0, len(blocks), 2):
            found, new = join(*sided(low_side, blocks[j], blocks[j + 1]))
            for plane in range(JOINT):
                joints[level - 1][j // 2, plane] = found[plane]
            joined.append(new)
            if level < levels - 1:
                left, right = sided(low_side, ends[j], ends[j + 1])
                both = {}
                for k in range(4):
                    _, both[k], both[4 + k] = up(found, k, left, right)
                new_ends.append(both)
        blocks, ends = joined, new_ends
        if level < levels - 1:
            for slot, x in enumerate(facing(level + 1, levels, ends[1], False)):
                consts[level - 1][slot] = x


def facing(level, levels, ends, mine):
    if level < levels - 1:
        return [ends[p] for p in range(8)]
    low_side = side_bit(level)
    if not mine:
        low_side = jnp.logical_not(low_side)
    return [jnp.where(low_side, ends[4 + k], ends[k]) for k in range(4)]


def source_kernel(rows, count, early, src, cpr, add, t):
    ny, nz = src.shape[2], src.shape[3]
    sub = lax.broadcasted_iota(jnp.int32, (ny, nz), 0)
    top, low = sub == ny - 1, sub == 0

    def down(ref, shift):
        def row(i, carry):
            prev = jnp.maximum(i - 1, 0)
            new = []
            for k in range(4):
                a = jnp.broadcast_to(add[k, pl.ds(i, 1), :], (ny, nz))
                b = jnp.broadcast_to(add[4 + k, pl.ds(i, 1), :], (ny, nz))
                x = ref[k, i - shift] + jnp.where(low, a, jnp.where(top, b, 0.0))
                x = x + cpr[KIND[k], prev] * carry[k]
                t[k, i] = x
                new.append(x)
            return tuple(new)

        return row

    state = (jnp.zeros((ny, nz), F32),) * 4
    state = lax.fori_loop(0, count, down(early, 0), state)
    lax.fori_loop(count, rows, down(src, count), state)


def back_kernel(rows, t, inv, cpr, part):
    end = rows - 1
    start = []
    for k in range(4):
        x = inv[KIND[k], end] * t[k, end]
        part[k, end] = x
        start.append(x)

    def row(j, carry):
        i = end - 1 - j
        new = []
        for k in range(4):
            s = KIND[k]
            x = inv[s, i] * t[k, i] + cpr[s, i] * carry[k]
            part[k, i] = x
            new.append(x)
        return tuple(new)

    lax.fori_loop(0, end, row, tuple(start))


def up(joint, k, left, right):
    s = KIND[k]
    d = left[4 + k] - right[k]
    flow = joint[R_ + s] * d
    first = left[k] + joint[GA + s] * (joint[CA + k] - flow)
    last = right[4 + k] + joint[GB + s] * (joint[CB + k] + flow)
    return d, first, last


def up_kernel(levels, own, other, joint, *refs):
    joints = refs[: levels - 1]
    out, diff = refs[levels : levels + 2]
    shares = refs[levels + 2 :]
    low_side = side_bit(0)
    width = out.shape[2]
    left, right = sided(low_side, {p: own[p] for p in range(8)}, {p: other[p] for p in range(8)})
    ends = {}
    for k in range(4):
        diff[k], first, last = up(joint, k, left, right)
        ends[k] = jnp.where(low_side, first[:, :width], first[:, width:])
        ends[4 + k] = jnp.where(low_side, last[:, :width], last[:, width:])
        out[k] = ends[k]
        out[4 + k] = ends[4 + k]
    for level in range(1, levels - 1):
        low_side = side_bit(level)
        joint = joints[level - 1].at[0]
        for k in range(4):
            s = KIND[k]
            first, last = ends[k], ends[4 + k]
            flow = joint[R_ + s] * jnp.where(low_side, last, -first)
            ends[k] = jnp.where(low_side, first, 0.0) - joint[GA + s] * flow
            ends[4 + k] = jnp.where(low_side, 0.0, last) + joint[GB + s] * flow
        for slot, x in enumerate(facing(level + 1, levels, ends, True)):
            shares[level - 1][slot] = x


def joint_flow(joint, k, d, into_first, into_last, low_side):
    s = KIND[k]
    flow = joint[R_ + s] * (d + joint[GA + s] * into_first - joint[GB + s] * into_last)
    first = jnp.where(low_side, into_first, joint[CB + k] + flow)
    last = jnp.where(low_side, joint[CA + k] - flow, into_last)
    return first, last


def beside_kernel(levels, *refs):
    parts, refs = list(refs[: 2 ** (levels - 1) - levels]), refs[2 ** (levels - 1) - levels :]
    consts, outs = refs[: levels - 2], refs[levels - 2 :]
    for level in range(2, levels):
        here = [parts.pop(0) for _ in range(2 ** (level - 1) - 1)]
        for p in range(outs[level - 2].shape[0]):
            total = consts[level - 2][p]
            for part in here:
                total = total + part[p]
            outs[level - 2][p] = total


def settle_kernel(levels, own, *refs):
    near, refs = refs[: levels - 1], refs[levels - 1 :]
    far, joints, out = refs[: levels - 2], refs[levels - 2 : -1], refs[-1]
    ends = {p: own[p] for p in range(8)}
    diffs = []
    for level in range(1, levels):
        low_side = side_bit(level)
        beside = {p: near[level - 1][p] for p in range(near[level - 1].shape[0])}
        if level > 1:
            beside = {p: x + far[level - 2][p] for p, x in beside.items()}
        across = []
        if len(beside) == 4:
            for k in range(4):
                x = beside[k]
                across.append(jnp.where(low_side, ends[4 + k] - x, x - ends[k]))
        else:
            left, right = sided(low_side, ends, beside)
            for k in range(4):
                d, ends[k], ends[4 + k] = up(joints[level - 1].at[0], k, left, right)
                across.append(d)
        diffs.append(across)
    for k in range(4):
        first = last = jnp.zeros_like(diffs[0][0])
        for level in range(levels - 1, 0, -1):
            first, last = joint_flow(
                joints[level - 1].at[0], k, diffs[level - 1][k], first, last, side_bit(level)
            )
        out[k] = first
        out[4 + k] = last


def final_kernel(mine, parts, flux, joint, diff, part, g0, gn, *refs):
    out, buf, sems = refs[-3:]
    rows, half = buf.shape[1], buf.shape[3]
    low_side = side_bit(0)
    core = jnp.bitwise_and(lax.axis_index("line"), 1)
    offset = (core if mine else 1 - core) * half
    copies = []
    for c in range(half // 128):
        near = pl.ds(c * 128, 128)
        z = pl.ds(pl.multiple_of(offset + c * 128, 128), 128)
        across = {plane: joint[plane, :, z] for plane in range(JOINT)}
        into = [
            joint_flow(across, k, diff[k, :, z], flux[k, :, near], flux[4 + k, :, near], low_side)
            for k in range(4)
        ]
        for r in range(parts):
            x = pl.ds(r * (rows // parts), rows // parts)
            for i in range(x.start, x.start + x.size):
                a = [g0[s, i, :, z] for s in range(2)]
                b = [gn[s, i, :, z] for s in range(2)]
                for k in range(4):
                    s = KIND[k]
                    buf[k, i, :, near] = part[k, i, :, z] + (a[s] * into[k][0] + b[s] * into[k][1])
            copies.append(
                pltpu.make_async_copy(
                    buf.at[:, x, :, near], out.at[:, x, :, z], sems.at[c * parts + r]
                )
            )
            copies[-1].start()
    for copy in copies:
        copy.wait()


def local(fields, viscosity):
    rows, ny, nz = viscosity.shape
    lines = lax.axis_size("line")
    cols = lax.axis_size("col")
    levels = lines.bit_length() - 1
    half = nz // 2
    cells = rows * ny * nz
    block = (rows, ny, nz)

    ring = [(i, (i + 1) % cols) for i in range(cols)]
    back_ring = [(b, a) for a, b in ring]

    def gather(at_level):
        found = {}
        for d in sorted(range(1, lines // 2), key=lambda d: (-d.bit_count(), d)):
            x = at_level[d.bit_length()]
            found[d] = lax.ppermute(x, "line", [(i, i ^ (d << 1)) for i in range(lines)])
        return [found[d] for d in sorted(found)]

    def swap(x, level):
        return lax.ppermute(x, "line", [(i, i ^ (1 << level)) for i in range(lines)])

    def cut(at, name, order, flops):
        return call(
            functools.partial(cut_kernel, at),
            name,
            [(5, rows, nz)],
            [fields, viscosity] + order,
            scratch=[pltpu.SemaphoreType.DMA((5,))],
            in_hbm=(0, 1),
            flops=flops,
        )[0]

    y_last = cut(ny - 1, "cut_last", [], 5 * 10**8)
    low = lax.ppermute(y_last, "col", ring)
    y_first = cut(0, "cut_first", [y_last], 5 * 10**8)
    high = lax.ppermute(y_first, "col", back_ring)

    inv, cpr, g0, gn, w = call(
        functools.partial(factor_kernel, rows),
        "factor",
        [(2,) + block] * 4 + [(PLANES, ny, nz)],
        [fields, viscosity],
        scratch=[VMEM((2,) + block, F32), pltpu.SemaphoreType.DMA((2,))],
        in_hbm=(0,),
        flops=10**9,
    )
    count = rows // 4
    (early,) = call(
        functools.partial(early_kernel, count),
        "early",
        [(4, count, ny, nz)],
        [fields, viscosity],
        scratch=[VMEM((4, count + 1, ny, nz), F32), pltpu.SemaphoreType.DMA],
        in_hbm=(0,),
        flops=4 * 10**9,
    )
    src, p, ends = call(
        functools.partial(explicit_kernel, count),
        "explicit",
        [(4, rows - count, ny, nz), (8, ny, nz), (8, rows, nz)],
        [fields, viscosity, g0, gn, early],
        scratch=[VMEM((4, rows - count + 1, ny, nz), F32), pltpu.SemaphoreType.DMA((3,))],
        in_hbm=(0,),
        flops=5 * 10**9,
    )
    pair, w = call(
        pair_kernel,
        "pair",
        [(JOINT, ny, nz), (PLANES, ny, half)],
        [w, swap(w, 0), early],
        moved=4 * ny * nz * 60,
    )
    pairs = lines // 2
    widths = [8] * (levels - 3) + [4]
    found = call(
        functools.partial(chips_kernel, levels),
        "chips",
        [(pairs >> level, JOINT, ny, half) for level in range(1, levels)]
        + [(width, ny, half) for width in widths],
        [w] + gather([w] * (levels + 1)) + [p],
        moved=4 * ny * half * 300,
    )
    joints, consts = list(found[: levels - 1]), list(found[levels - 1 :])

    add, p = call(
        functools.partial(edge_kernel, rows, ny),
        "edge",
        [(8, rows, nz), (8, ny, nz)],
        [y_last, y_first, low, high, ends, p, joints[0]],
        flops=5 * 10**8,
    )
    (t,) = call(
        functools.partial(source_kernel, rows, count),
        "source",
        [(4,) + block],
        [early, src, cpr, add],
        flops=30 * cells,
        moved=24 * cells,
    )
    (part,) = call(
        functools.partial(back_kernel, rows),
        "back",
        [(4,) + block],
        [t, inv, cpr],
        flops=20 * cells,
        moved=24 * cells,
    )
    p, diff, *shares = call(
        functools.partial(up_kernel, levels),
        "up",
        [(8, ny, half), (4, ny, nz)] + [(width, ny, half) for width in widths],
        [p, swap(p, 0), pair] + joints + [part],
        moved=4 * ny * nz * 40,
    )
    others = dict(enumerate(gather([None, p] + shares), 1))
    near = [others.pop(1 << level) for level in range(levels - 1)]
    beside = call(
        functools.partial(beside_kernel, levels),
        "beside",
        [(width, ny, half) for width in widths],
        list(others.values()) + consts,
        flops=6 * 10**8,
    )
    (flux,) = call(
        functools.partial(settle_kernel, levels),
        "settle",
        [(8, ny, half)],
        [p] + near + list(beside) + joints,
        moved=4 * ny * half * 100,
    )
    rest = [pair, diff, part, g0, gn]
    parts = 4 if rows % 4 == 0 else 1
    scratch = [VMEM((4, rows, ny, half), F32), pltpu.SemaphoreType.DMA((half // 128 * parts,))]
    (out,) = call(
        functools.partial(final_kernel, True, parts),
        "final_own",
        [(4,) + block],
        [flux] + rest,
        scratch=scratch,
        out_hbm=(0,),
        flops=10**9,
    )
    (out,) = call(
        functools.partial(final_kernel, False, parts),
        "final_other",
        [(4,) + block],
        [swap(flux, 0)] + rest + [out],
        scratch=scratch,
        in_hbm=(6,),
        out_hbm=(0,),
        aliases={6: 0},
        flops=10**9,
    )
    return out


def solution(mesh):
    return jax.shard_map(
        local,
        mesh=mesh,
        in_specs=(P(None, "line", "col", None), P("line", "col", None)),
        out_specs=P(None, "line", "col", None),
        check_vma=False,
    )
```

```python
import functools

import jax
import jax.numpy as jnp
from jax import lax
from jax.experimental import pallas as pl
from jax.experimental.pallas import tpu as pltpu
from jax.sharding import PartitionSpec as P

STIFF = 3072
THERMAL_RATIO = 0.8
CROSS_RATE = 0.2
ADVECTION = 0.25
BUOYANCY = 2.0
SCALES = (1.0, THERMAL_RATIO)
KIND = (0, 0, 0, 1)

F32 = jnp.float32
VMEM = pltpu.VMEM
LIMIT = 24 * 1024 * 1024

G00, G0N, GNN = (0, 3), (1, 4), (2, 5)
V_FIRST, V_LAST, F_FIRST, F_LAST = 6, 7, 8, 12
PLANES = 16
R_, GA, GB, CA, CB = 0, 2, 4, 6, 10
JOINT = 14


def in_vmem(x):
    return pltpu.with_memory_space_constraint(x, VMEM)


def spec():
    return pl.BlockSpec(memory_space=VMEM)


def call(kernel, name, out_shapes, args, scratch=(), in_hbm=(), out_hbm=(), aliases={}, flops=0, moved=0):
    in_specs = []
    operands = []
    for i, x in enumerate(args):
        if i in in_hbm:
            in_specs.append(pl.BlockSpec(memory_space=pltpu.HBM))
            operands.append(pltpu.with_memory_space_constraint(x, pltpu.HBM))
        else:
            in_specs.append(spec())
            operands.append(in_vmem(x))
    out_shape = []
    out_specs = []
    for i, s in enumerate(out_shapes):
        if i in out_hbm:
            out_shape.append(pltpu.HBM(s, F32))
            out_specs.append(pl.BlockSpec(memory_space=pltpu.HBM))
        else:
            out_shape.append(VMEM(s, F32))
            out_specs.append(spec())
    return pl.pallas_call(
        kernel,
        out_shape=out_shape,
        in_specs=in_specs,
        out_specs=out_specs,
        scratch_shapes=list(scratch),
        input_output_aliases=aliases,
        compiler_params=pltpu.CompilerParams(vmem_limit_bytes=LIMIT),
        cost_estimate=pl.CostEstimate(flops=flops, bytes_accessed=moved, transcendentals=0),
        name=name,
    )(*operands)


def layer(read, ny, nz):
    sub = lax.broadcasted_iota(jnp.int32, (8, nz), 0)
    tile = jnp.broadcast_to(read(0), (8, nz))
    for r in range(1, 8):
        tile = jnp.where(sub == r, jnp.broadcast_to(read(r), (8, nz)), tile)
    return tile


def col_odd():
    return jnp.bitwise_and(lax.axis_index("col"), 1) == 1


def cut_kernel(ny, fields, visc, first_out, second_out, sems):
    def run(ats):
        copies = []
        for j, (at, out) in enumerate(zip(ats, (first_out, second_out))):
            for k in range(4):
                copies.append(pltpu.make_async_copy(fields.at[k, :, at], out.at[k], sems.at[j, k]))
            copies.append(pltpu.make_async_copy(visc.at[:, at], out.at[4], sems.at[j, 4]))
        for copy in copies:
            copy.start()
        for copy in copies:
            copy.wait()

    odd = col_odd()
    pl.when(odd)(lambda: run((ny - 1, 0)))
    pl.when(jnp.logical_not(odd))(lambda: run((0, ny - 1)))


def factor_kernel(rows, fields_ref, visc, inv, cpr, g0, gn, w, tau, sems):
    copies = [
        pltpu.make_async_copy(fields_ref.at[:, 0], w.at[F_FIRST : F_FIRST + 4], sems.at[0]),
        pltpu.make_async_copy(fields_ref.at[:, rows - 1], w.at[F_LAST : F_LAST + 4], sems.at[1]),
    ]
    for copy in copies:
        copy.start()
    ny, nz = visc.shape[1], visc.shape[2]
    me = lax.axis_index("line")
    wall_low = jnp.where(me == 0, 1.0, 0.0).astype(F32)
    wall_high = jnp.where(me == lax.axis_size("line") - 1, 1.0, 0.0).astype(F32)
    one = jnp.ones((ny, nz), F32)

    def row(i, carry):
        low, v = carry[4], carry[5]
        after = visc[jnp.minimum(i + 1, rows - 1)]
        high = jnp.where(i == rows - 1, (0.5 * STIFF) * wall_high * v, (0.5 * STIFF) * (v + after))
        new = []
        for s in range(2):
            gain, running = carry[2 * s], carry[2 * s + 1]
            down = SCALES[s] * low if s else low
            up = SCALES[s] * high if s else high
            q = 1.0 + down * gain
            one_over = 1.0 / (q + up)
            coupling = up * one_over
            inv[s, i] = one_over
            cpr[s, i] = coupling
            tau[s, i] = running
            new += [q * one_over, coupling * running]
        return tuple(new) + (high, after)

    first = visc[0]
    lax.fori_loop(0, rows, row, (one,) * 4 + (wall_low * (0.5 * STIFF) * first, first))

    end = rows - 1
    start = []
    for s in range(2):
        a = inv[s, end] * tau[s, end]
        b = inv[s, end]
        g0[s, end] = a
        gn[s, end] = b
        w[G0N[s]] = a
        w[GNN[s]] = b
        start += [a, b]

    def back(j, carry):
        i = end - 1 - j
        new = []
        for s in range(2):
            c = cpr[s, i]
            a = inv[s, i] * tau[s, i] + c * carry[2 * s]
            b = c * carry[2 * s + 1]
            g0[s, i] = a
            gn[s, i] = b
            new += [a, b]
        return tuple(new)

    final = lax.fori_loop(0, end, back, tuple(start))
    for s in range(2):
        w[G00[s]] = final[2 * s]
    w[V_FIRST] = first
    w[V_LAST] = visc[rows - 1]
    for copy in copies:
        copy.wait()


def explicit_rows(first, count, base, start, fields, visc, src):
    rows, ny, nz = visc.shape
    lane = lax.broadcasted_iota(jnp.int32, (ny, nz), 1)
    sub = lax.broadcasted_iota(jnp.int32, (ny, nz), 0)
    z_top, z_low = lane == nz - 1, lane == 0
    y_top, y_low = sub == ny - 1, sub == 0

    def sides(x):
        return (
            pltpu.roll(x, ny - 1, 0),
            pltpu.roll(x, 1, 0),
            pltpu.roll(x, nz - 1, 1),
            pltpu.roll(x, 1, 1),
        )

    def row(i, _):
        f = [fields[k, i - base] for k in range(4)]
        v = visc[i]
        after, before = jnp.minimum(i + 1, rows - 1), jnp.maximum(i - 1, 0)
        vyn, vyp, vzn, vzp = sides(v)
        half = 0.5 * CROSS_RATE
        faces = [
            jnp.where(y_top, 0.0, half * (v + vyn)),
            jnp.where(y_low, 0.0, half * (v + vyp)),
            half * (v + jnp.where(z_top, 0.0, vzn)),
            half * (v + jnp.where(z_low, 0.0, vzp)),
        ]
        none = [y_top, y_low, z_top, z_low]
        total = (faces[0] + faces[1]) + (faces[2] + faces[3])
        adv = [(-0.5 * ADVECTION) * f[k] for k in range(3)]
        move = [adv[1], -adv[1], adv[2], -adv[2]]
        adv_after = jnp.where(i == rows - 1, 0.0, adv[0])
        adv_before = jnp.where(i == 0, 0.0, adv[0])
        weights, centre = [], []
        for s in range(2):
            scaled = [SCALES[s] * x if s else x for x in faces]
            weights.append([jnp.where(n, 0.0, x + m) for n, x, m in zip(none, scaled, move)])
            centre.append(1.0 - (SCALES[s] * total if s else total))
        for k in range(4):
            s = KIND[k]
            near = sides(f[k])
            out = centre[s] * f[k] + adv_after * fields[k, after - base] - adv_before * fields[k, before - base]
            for c, x in zip(weights[s], near):
                out = out + c * x
            if k == 2:
                out = out + BUOYANCY * f[3]
            src[k, i - start] = out
        return 0

    lax.fori_loop(first, first + count, row, 0)


def early_kernel(count, fields_ref, visc, src, fields, sem):
    copy = pltpu.make_async_copy(fields_ref.at[:, 0 : count + 1], fields, sem)
    copy.start()
    copy.wait()
    explicit_rows(0, count, 0, 0, fields, visc, src)


def explicit_kernel(count, fields_ref, visc, g0, gn, early, src, p, ends, fields, sems):
    rows, ny, nz = visc.shape
    cuts = [count - 1] + list(range(2 * count + 1, rows, count)) + [rows]
    copies = []
    for c, (lo, hi) in enumerate(zip(cuts, cuts[1:])):
        copies.append(
            pltpu.make_async_copy(
                fields_ref.at[:, lo:hi], fields.at[:, lo - cuts[0] : hi - cuts[0]], sems.at[c]
            )
        )
        copies[-1].start()
    for c, copy in enumerate(copies):
        copy.wait()
        explicit_rows((c + 1) * count, count, cuts[0], count, fields, visc, src)

    def dot(ref, shift):
        def add(i, carry):
            new = []
            for g, base in ((g0, 0), (gn, 4)):
                for k in range(4):
                    new.append(carry[base + k] + g[KIND[k], i] * ref[k, i - shift])
            return tuple(new)

        return add

    final = (jnp.zeros((ny, nz), F32),) * 8
    final = lax.fori_loop(0, count, dot(early, 0), final)
    final = lax.fori_loop(count, rows, dot(src, count), final)
    for k in range(8):
        p[k] = final[k]

    for s in range(2):
        for side, at in ((0, 0), (1, ny - 1)):
            for which, g in ((0, g0), (1, gn)):
                for lo in range(0, rows, 8):
                    ends[4 * side + 2 * which + s, lo : lo + 8] = layer(
                        lambda r: g[s, lo + r, at : at + 1, :], ny, nz
                    )


def edge_kernel(rows, ny, sent_one, sent_two, got_one, got_two, ends, p, *refs):
    add, out = refs[-2:]
    nz = out.shape[2]
    sub = lax.broadcasted_iota(jnp.int32, (ny, 128), 0)
    rate = 0.5 * ADVECTION
    odd = col_odd()
    slots = (
        (jnp.where(odd, 4, 0), sent_one, got_one, jnp.where(odd, -rate, rate).astype(F32)),
        (jnp.where(odd, 0, 4), sent_two, got_two, jnp.where(odd, rate, -rate).astype(F32)),
    )
    for j in range(nz // 128):
        z = pl.ds(j * 128, 128)
        sums = []
        for side, mine, far, sign in slots:
            total = [None] * 8
            for r in range(rows // 8):
                x = pl.ds(r * 8, 8)
                face = (0.5 * CROSS_RATE) * (mine[4, x, z] + far[4, x, z])
                faces = (face, THERMAL_RATIO * face)
                adv = sign * mine[1, x, z]
                both = [adv + c for c in faces]
                g = [ends[side + q, x, z] for q in range(4)]
                for k in range(4):
                    s = KIND[k]
                    h = both[s] * far[k, x, z] - faces[s] * mine[k, x, z]
                    add[side + k, x, z] = h
                    for slot, c in ((k, g[s]), (4 + k, g[2 + s])):
                        part = c * h
                        total[slot] = part if total[slot] is None else total[slot] + part
            sums.append(total)
        for slot in range(8):
            add_one = jnp.sum(sums[0][slot], axis=0, keepdims=True)
            add_two = jnp.sum(sums[1][slot], axis=0, keepdims=True)
            add_low = jnp.where(odd, add_two, add_one)
            add_high = jnp.where(odd, add_one, add_two)
            both = jnp.where(sub == 0, add_low, jnp.where(sub == ny - 1, add_high, 0.0))
            out[slot, :, z] = p[slot, :, z] + both


def side_bit(level):
    return jnp.bitwise_and(jnp.right_shift(lax.axis_index("line"), level), 1) == 0


def join(left, right):
    face = left[V_LAST] + right[V_FIRST]
    joint, new, ratio = {}, {}, []
    for s in range(2):
        resist = 1.0 / ((0.5 * STIFF * SCALES[s]) * face)
        r = 1.0 / (resist + left[GNN[s]] + right[G00[s]])
        ratio.append(r)
        a, b = left[G0N[s]], right[G0N[s]]
        joint[R_ + s] = r
        joint[GA + s] = a
        joint[GB + s] = b
        new[G00[s]] = left[G00[s]] - r * a * a
        new[GNN[s]] = right[GNN[s]] - r * b * b
        new[G0N[s]] = r * a * b
    rate = 0.5 * ADVECTION
    for k in range(4):
        s = KIND[k]
        add_a = -rate * left[F_LAST] * right[F_FIRST + k]
        add_b = rate * right[F_FIRST] * left[F_LAST + k]
        e = ratio[s] * (left[GNN[s]] * add_a - right[G00[s]] * add_b)
        joint[CA + k] = add_a - e
        joint[CB + k] = add_b + e
        new[F_FIRST + k] = left[F_FIRST + k]
        new[F_LAST + k] = right[F_LAST + k]
    new[V_FIRST] = left[V_FIRST]
    new[V_LAST] = right[V_LAST]
    return joint, new


def sided(low_side, mine, theirs):
    left = {p: jnp.where(low_side, mine[p], theirs[p]) for p in mine}
    right = {p: jnp.where(low_side, theirs[p], mine[p]) for p in mine}
    return left, right


def pair_kernel(own, other, *refs):
    joint, out = refs[-2:]
    low_side = side_bit(0)
    planes = range(PLANES)
    found, new = join(*sided(low_side, {p: own[p] for p in planes}, {p: other[p] for p in planes}))
    for plane in range(JOINT):
        joint[plane] = found[plane]
    width = out.shape[2]
    for plane in planes:
        out[plane] = jnp.where(low_side, new[plane][:, :width], new[plane][:, width:])


def chips_kernel(levels, own, *refs):
    others = refs[: 2 ** (levels - 1) - 1]
    joints = refs[-(2 * levels - 3) : len(refs) - (levels - 2)]
    consts = refs[len(refs) - (levels - 2) :]
    blocks = [{p: x[p] for p in range(PLANES)} for x in (own, *others)]
    zero = jnp.zeros_like(own[0])
    ends = [{p: zero for p in range(8)} for _ in blocks]
    for level in range(1, levels):
        low_side = side_bit(level)
        joined, new_ends = [], []
        for j in range(0, len(blocks), 2):
            found, new = join(*sided(low_side, blocks[j], blocks[j + 1]))
            for plane in range(JOINT):
                joints[level - 1][j // 2, plane] = found[plane]
            joined.append(new)
            if level < levels - 1:
                left, right = sided(low_side, ends[j], ends[j + 1])
                both = {}
                for k in range(4):
                    _, both[k], both[4 + k] = up(found, k, left, right)
                new_ends.append(both)
        blocks, ends = joined, new_ends
        if level < levels - 1:
            for slot, x in enumerate(facing(level + 1, levels, ends[1], False)):
                consts[level - 1][slot] = x


def facing(level, levels, ends, mine):
    if level < levels - 1:
        return [ends[p] for p in range(8)]
    low_side = side_bit(level)
    if not mine:
        low_side = jnp.logical_not(low_side)
    return [jnp.where(low_side, ends[4 + k], ends[k]) for k in range(4)]


def source_kernel(rows, count, early, src, cpr, add, t):
    ny, nz = src.shape[2], src.shape[3]
    sub = lax.broadcasted_iota(jnp.int32, (ny, nz), 0)
    top, low = sub == ny - 1, sub == 0

    def down(ref, shift):
        def row(i, carry):
            prev = jnp.maximum(i - 1, 0)
            new = []
            for k in range(4):
                a = jnp.broadcast_to(add[k, pl.ds(i, 1), :], (ny, nz))
                b = jnp.broadcast_to(add[4 + k, pl.ds(i, 1), :], (ny, nz))
                x = ref[k, i - shift] + jnp.where(low, a, jnp.where(top, b, 0.0))
                x = x + cpr[KIND[k], prev] * carry[k]
                t[k, i] = x
                new.append(x)
            return tuple(new)

        return row

    state = (jnp.zeros((ny, nz), F32),) * 4
    state = lax.fori_loop(0, count, down(early, 0), state)
    lax.fori_loop(count, rows, down(src, count), state)


def back_kernel(rows, t, inv, cpr, part):
    end = rows - 1
    start = []
    for k in range(4):
        x = inv[KIND[k], end] * t[k, end]
        part[k, end] = x
        start.append(x)

    def row(j, carry):
        i = end - 1 - j
        new = []
        for k in range(4):
            s = KIND[k]
            x = inv[s, i] * t[k, i] + cpr[s, i] * carry[k]
            part[k, i] = x
            new.append(x)
        return tuple(new)

    lax.fori_loop(0, end, row, tuple(start))


def up(joint, k, left, right):
    s = KIND[k]
    d = left[4 + k] - right[k]
    flow = joint[R_ + s] * d
    first = left[k] + joint[GA + s] * (joint[CA + k] - flow)
    last = right[4 + k] + joint[GB + s] * (joint[CB + k] + flow)
    return d, first, last


def up_kernel(levels, own, other, joint, *refs):
    joints = refs[: levels - 1]
    out, diff = refs[levels : levels + 2]
    shares = refs[levels + 2 :]
    low_side = side_bit(0)
    width = out.shape[2]
    left, right = sided(low_side, {p: own[p] for p in range(8)}, {p: other[p] for p in range(8)})
    ends = {}
    for k in range(4):
        diff[k], first, last = up(joint, k, left, right)
        ends[k] = jnp.where(low_side, first[:, :width], first[:, width:])
        ends[4 + k] = jnp.where(low_side, last[:, :width], last[:, width:])
        out[k] = ends[k]
        out[4 + k] = ends[4 + k]
    for level in range(1, levels - 1):
        low_side = side_bit(level)
        joint = joints[level - 1].at[0]
        for k in range(4):
            s = KIND[k]
            first, last = ends[k], ends[4 + k]
            flow = joint[R_ + s] * jnp.where(low_side, last, -first)
            ends[k] = jnp.where(low_side, first, 0.0) - joint[GA + s] * flow
            ends[4 + k] = jnp.where(low_side, 0.0, last) + joint[GB + s] * flow
        for slot, x in enumerate(facing(level + 1, levels, ends, True)):
            shares[level - 1][slot] = x


def joint_flow(joint, k, d, into_first, into_last, low_side):
    s = KIND[k]
    flow = joint[R_ + s] * (d + joint[GA + s] * into_first - joint[GB + s] * into_last)
    first = jnp.where(low_side, into_first, joint[CB + k] + flow)
    last = jnp.where(low_side, joint[CA + k] - flow, into_last)
    return first, last


def beside_kernel(levels, *refs):
    parts, refs = list(refs[: 2 ** (levels - 1) - levels]), refs[2 ** (levels - 1) - levels :]
    consts, outs = refs[: levels - 2], refs[levels - 2 :]
    for level in range(2, levels):
        here = [parts.pop(0) for _ in range(2 ** (level - 1) - 1)]
        for p in range(outs[level - 2].shape[0]):
            total = consts[level - 2][p]
            for part in here:
                total = total + part[p]
            outs[level - 2][p] = total


def settle_kernel(levels, own, *refs):
    near, refs = refs[: levels - 1], refs[levels - 1 :]
    far, joints, out = refs[: levels - 2], refs[levels - 2 : -1], refs[-1]
    ends = {p: own[p] for p in range(8)}
    diffs = []
    for level in range(1, levels):
        low_side = side_bit(level)
        beside = {p: near[level - 1][p] for p in range(near[level - 1].shape[0])}
        if level > 1:
            beside = {p: x + far[level - 2][p] for p, x in beside.items()}
        across = []
        if len(beside) == 4:
            for k in range(4):
                x = beside[k]
                across.append(jnp.where(low_side, ends[4 + k] - x, x - ends[k]))
        else:
            left, right = sided(low_side, ends, beside)
            for k in range(4):
                d, ends[k], ends[4 + k] = up(joints[level - 1].at[0], k, left, right)
                across.append(d)
        diffs.append(across)
    for k in range(4):
        first = last = jnp.zeros_like(diffs[0][0])
        for level in range(levels - 1, 0, -1):
            first, last = joint_flow(
                joints[level - 1].at[0], k, diffs[level - 1][k], first, last, side_bit(level)
            )
        out[k] = first
        out[4 + k] = last


def final_kernel(mine, parts, flux, joint, diff, part, g0, gn, *refs):
    out, buf, sems = refs[-3:]
    rows, half = buf.shape[1], buf.shape[3]
    low_side = side_bit(0)
    core = jnp.bitwise_and(lax.axis_index("line"), 1)
    offset = (core if mine else 1 - core) * half
    copies = []
    for c in range(half // 128):
        near = pl.ds(c * 128, 128)
        z = pl.ds(pl.multiple_of(offset + c * 128, 128), 128)
        across = {plane: joint[plane, :, z] for plane in range(JOINT)}
        into = [
            joint_flow(across, k, diff[k, :, z], flux[k, :, near], flux[4 + k, :, near], low_side)
            for k in range(4)
        ]
        for r in range(parts):
            x = pl.ds(r * (rows // parts), rows // parts)
            for i in range(x.start, x.start + x.size):
                a = [g0[s, i, :, z] for s in range(2)]
                b = [gn[s, i, :, z] for s in range(2)]
                for k in range(4):
                    s = KIND[k]
                    buf[k, i, :, near] = part[k, i, :, z] + (a[s] * into[k][0] + b[s] * into[k][1])
            copies.append(
                pltpu.make_async_copy(
                    buf.at[:, x, :, near], out.at[:, x, :, z], sems.at[c * parts + r]
                )
            )
            copies[-1].start()
    for copy in copies:
        copy.wait()


def local(fields, viscosity):
    rows, ny, nz = viscosity.shape
    lines = lax.axis_size("line")
    cols = lax.axis_size("col")
    levels = lines.bit_length() - 1
    half = nz // 2
    cells = rows * ny * nz
    block = (rows, ny, nz)

    across = [(i, (i + 1) % cols if i % 2 else (i - 1) % cols) for i in range(cols)]
    inside = [(i, (i - 1) % cols if i % 2 else (i + 1) % cols) for i in range(cols)]

    def gather(at_level):
        found = {}
        for d in sorted(range(1, lines // 2), key=lambda d: (-d.bit_count(), d)):
            x = at_level[d.bit_length()]
            found[d] = lax.ppermute(x, "line", [(i, i ^ (d << 1)) for i in range(lines)])
        return [found[d] for d in sorted(found)]

    def swap(x, level):
        return lax.ppermute(x, "line", [(i, i ^ (1 << level)) for i in range(lines)])

    sent_one, sent_two = call(
        functools.partial(cut_kernel, ny),
        "cut",
        [(5, rows, nz), (5, rows, nz)],
        [fields, viscosity],
        scratch=[pltpu.SemaphoreType.DMA((2, 5))],
        in_hbm=(0, 1),
        moved=2 * cells,
    )
    got_one = lax.ppermute(sent_one, "col", across)
    got_two = lax.ppermute(sent_two, "col", inside)

    inv, cpr, g0, gn, w = call(
        functools.partial(factor_kernel, rows),
        "factor",
        [(2,) + block] * 4 + [(PLANES, ny, nz)],
        [fields, viscosity],
        scratch=[VMEM((2,) + block, F32), pltpu.SemaphoreType.DMA((2,))],
        in_hbm=(0,),
        flops=10**9,
    )
    count = rows // 4
    (early,) = call(
        functools.partial(early_kernel, count),
        "early",
        [(4, count, ny, nz)],
        [fields, viscosity],
        scratch=[VMEM((4, count + 1, ny, nz), F32), pltpu.SemaphoreType.DMA],
        in_hbm=(0,),
        flops=4 * 10**9,
    )
    src, p, ends = call(
        functools.partial(explicit_kernel, count),
        "explicit",
        [(4, rows - count, ny, nz), (8, ny, nz), (8, rows, nz)],
        [fields, viscosity, g0, gn, early],
        scratch=[VMEM((4, rows - count + 1, ny, nz), F32), pltpu.SemaphoreType.DMA((3,))],
        in_hbm=(0,),
        flops=5 * 10**9,
    )
    pair, w = call(
        pair_kernel,
        "pair",
        [(JOINT, ny, nz), (PLANES, ny, half)],
        [w, swap(w, 0), early],
        moved=4 * ny * nz * 60,
    )
    pairs = lines // 2
    widths = [8] * (levels - 3) + [4]
    found = call(
        functools.partial(chips_kernel, levels),
        "chips",
        [(pairs >> level, JOINT, ny, half) for level in range(1, levels)]
        + [(width, ny, half) for width in widths],
        [w] + gather([w] * (levels + 1)) + [p],
        moved=4 * ny * half * 300,
    )
    joints, consts = list(found[: levels - 1]), list(found[levels - 1 :])

    add, p = call(
        functools.partial(edge_kernel, rows, ny),
        "edge",
        [(8, rows, nz), (8, ny, nz)],
        [sent_one, sent_two, got_one, got_two, ends, p, joints[0]],
        flops=5 * 10**8,
    )
    (t,) = call(
        functools.partial(source_kernel, rows, count),
        "source",
        [(4,) + block],
        [early, src, cpr, add],
        flops=30 * cells,
        moved=24 * cells,
    )
    (part,) = call(
        functools.partial(back_kernel, rows),
        "back",
        [(4,) + block],
        [t, inv, cpr],
        flops=20 * cells,
        moved=24 * cells,
    )
    p, diff, *shares = call(
        functools.partial(up_kernel, levels),
        "up",
        [(8, ny, half), (4, ny, nz)] + [(width, ny, half) for width in widths],
        [p, swap(p, 0), pair] + joints + [part],
        moved=4 * ny * nz * 40,
    )
    others = dict(enumerate(gather([None, p] + shares), 1))
    near = [others.pop(1 << level) for level in range(levels - 1)]
    beside = call(
        functools.partial(beside_kernel, levels),
        "beside",
        [(width, ny, half) for width in widths],
        list(others.values()) + consts,
        flops=6 * 10**8,
    )
    (flux,) = call(
        functools.partial(settle_kernel, levels),
        "settle",
        [(8, ny, half)],
        [p] + near + list(beside) + joints,
        moved=4 * ny * half * 100,
    )
    rest = [pair, diff, part, g0, gn]
    parts = 4 if rows % 4 == 0 else 1
    scratch = [VMEM((4, rows, ny, half), F32), pltpu.SemaphoreType.DMA((half // 128 * parts,))]
    (out,) = call(
        functools.partial(final_kernel, True, parts),
        "final_own",
        [(4,) + block],
        [flux] + rest,
        scratch=scratch,
        out_hbm=(0,),
        flops=10**9,
    )
    (out,) = call(
        functools.partial(final_kernel, False, parts),
        "final_other",
        [(4,) + block],
        [swap(flux, 0)] + rest + [out],
        scratch=scratch,
        in_hbm=(6,),
        out_hbm=(0,),
        aliases={6: 0},
        flops=10**9,
    )
    return out


def solution(mesh):
    return jax.shard_map(
        local,
        mesh=mesh,
        in_specs=(P(None, "line", "col", None), P("line", "col", None)),
        out_specs=P(None, "line", "col", None),
        check_vma=False,
    )
```

```python
import functools

import jax
import jax.numpy as jnp
from jax import lax
from jax.experimental import pallas as pl
from jax.experimental.pallas import tpu as pltpu
from jax.sharding import PartitionSpec as P

STIFF = 3072
THERMAL_RATIO = 0.8
CROSS_RATE = 0.2
ADVECTION = 0.25
BUOYANCY = 2.0
SCALES = (1.0, THERMAL_RATIO)
KIND = (0, 0, 0, 1)

F32 = jnp.float32
VMEM = pltpu.VMEM
LIMIT = 24 * 1024 * 1024

G00, G0N, GNN = (0, 3), (1, 4), (2, 5)
V_FIRST, V_LAST, F_FIRST, F_LAST = 6, 7, 8, 12
PLANES = 16
R_, GA, GB, CA, CB = 0, 2, 4, 6, 10
JOINT = 14


def in_vmem(x):
    return pltpu.with_memory_space_constraint(x, VMEM)


def spec():
    return pl.BlockSpec(memory_space=VMEM)


def call(kernel, name, out_shapes, args, scratch=(), in_hbm=(), out_hbm=(), aliases={}, flops=0, moved=0):
    in_specs = []
    operands = []
    for i, x in enumerate(args):
        if i in in_hbm:
            in_specs.append(pl.BlockSpec(memory_space=pltpu.HBM))
            operands.append(pltpu.with_memory_space_constraint(x, pltpu.HBM))
        else:
            in_specs.append(spec())
            operands.append(in_vmem(x))
    out_shape = []
    out_specs = []
    for i, s in enumerate(out_shapes):
        if i in out_hbm:
            out_shape.append(pltpu.HBM(s, F32))
            out_specs.append(pl.BlockSpec(memory_space=pltpu.HBM))
        else:
            out_shape.append(VMEM(s, F32))
            out_specs.append(spec())
    return pl.pallas_call(
        kernel,
        out_shape=out_shape,
        in_specs=in_specs,
        out_specs=out_specs,
        scratch_shapes=list(scratch),
        input_output_aliases=aliases,
        compiler_params=pltpu.CompilerParams(vmem_limit_bytes=LIMIT),
        cost_estimate=pl.CostEstimate(flops=flops, bytes_accessed=moved, transcendentals=0),
        name=name,
    )(*operands)


def layer(read, ny, nz):
    sub = lax.broadcasted_iota(jnp.int32, (8, nz), 0)
    tile = jnp.broadcast_to(read(0), (8, nz))
    for r in range(1, 8):
        tile = jnp.where(sub == r, jnp.broadcast_to(read(r), (8, nz)), tile)
    return tile


def cut_kernel(ny, fields, visc, y_first, y_last, sems):
    copies = []
    for j, (at, out) in enumerate(((0, y_first), (ny - 1, y_last))):
        for k in range(4):
            copies.append(pltpu.make_async_copy(fields.at[k, :, at], out.at[k], sems.at[j, k]))
        copies.append(pltpu.make_async_copy(visc.at[:, at], out.at[4], sems.at[j, 4]))
    for copy in copies:
        copy.start()
    for copy in copies:
        copy.wait()


def factor_kernel(rows, fields_ref, visc, inv, cpr, g0, gn, w, tau, sems):
    copies = [
        pltpu.make_async_copy(fields_ref.at[:, 0], w.at[F_FIRST : F_FIRST + 4], sems.at[0]),
        pltpu.make_async_copy(fields_ref.at[:, rows - 1], w.at[F_LAST : F_LAST + 4], sems.at[1]),
    ]
    for copy in copies:
        copy.start()
    ny, nz = visc.shape[1], visc.shape[2]
    me = lax.axis_index("line")
    wall_low = jnp.where(me == 0, 1.0, 0.0).astype(F32)
    wall_high = jnp.where(me == lax.axis_size("line") - 1, 1.0, 0.0).astype(F32)
    one = jnp.ones((ny, nz), F32)

    def row(i, carry):
        low, v = carry[4], carry[5]
        after = visc[jnp.minimum(i + 1, rows - 1)]
        high = jnp.where(i == rows - 1, (0.5 * STIFF) * wall_high * v, (0.5 * STIFF) * (v + after))
        new = []
        for s in range(2):
            gain, running = carry[2 * s], carry[2 * s + 1]
            down = SCALES[s] * low if s else low
            up = SCALES[s] * high if s else high
            q = 1.0 + down * gain
            one_over = 1.0 / (q + up)
            coupling = up * one_over
            inv[s, i] = one_over
            cpr[s, i] = coupling
            tau[s, i] = running
            new += [q * one_over, coupling * running]
        return tuple(new) + (high, after)

    first = visc[0]
    lax.fori_loop(0, rows, row, (one,) * 4 + (wall_low * (0.5 * STIFF) * first, first))

    end = rows - 1
    start = []
    for s in range(2):
        a = inv[s, end] * tau[s, end]
        b = inv[s, end]
        g0[s, end] = a
        gn[s, end] = b
        w[G0N[s]] = a
        w[GNN[s]] = b
        start += [a, b]

    def back(j, carry):
        i = end - 1 - j
        new = []
        for s in range(2):
            c = cpr[s, i]
            a = inv[s, i] * tau[s, i] + c * carry[2 * s]
            b = c * carry[2 * s + 1]
            g0[s, i] = a
            gn[s, i] = b
            new += [a, b]
        return tuple(new)

    final = lax.fori_loop(0, end, back, tuple(start))
    for s in range(2):
        w[G00[s]] = final[2 * s]
    w[V_FIRST] = first
    w[V_LAST] = visc[rows - 1]
    for copy in copies:
        copy.wait()


def explicit_rows(first, count, base, start, fields, visc, src):
    rows, ny, nz = visc.shape
    lane = lax.broadcasted_iota(jnp.int32, (ny, nz), 1)
    sub = lax.broadcasted_iota(jnp.int32, (ny, nz), 0)
    z_top, z_low = lane == nz - 1, lane == 0
    y_top, y_low = sub == ny - 1, sub == 0

    def sides(x):
        return (
            pltpu.roll(x, ny - 1, 0),
            pltpu.roll(x, 1, 0),
            pltpu.roll(x, nz - 1, 1),
            pltpu.roll(x, 1, 1),
        )

    def row(i, _):
        f = [fields[k, i - base] for k in range(4)]
        v = visc[i]
        after, before = jnp.minimum(i + 1, rows - 1), jnp.maximum(i - 1, 0)
        vyn, vyp, vzn, vzp = sides(v)
        half = 0.5 * CROSS_RATE
        faces = [
            jnp.where(y_top, 0.0, half * (v + vyn)),
            jnp.where(y_low, 0.0, half * (v + vyp)),
            half * (v + jnp.where(z_top, 0.0, vzn)),
            half * (v + jnp.where(z_low, 0.0, vzp)),
        ]
        none = [y_top, y_low, z_top, z_low]
        total = (faces[0] + faces[1]) + (faces[2] + faces[3])
        adv = [(-0.5 * ADVECTION) * f[k] for k in range(3)]
        move = [adv[1], -adv[1], adv[2], -adv[2]]
        adv_after = jnp.where(i == rows - 1, 0.0, adv[0])
        adv_before = jnp.where(i == 0, 0.0, adv[0])
        weights, centre = [], []
        for s in range(2):
            scaled = [SCALES[s] * x if s else x for x in faces]
            weights.append([jnp.where(n, 0.0, x + m) for n, x, m in zip(none, scaled, move)])
            centre.append(1.0 - (SCALES[s] * total if s else total))
        for k in range(4):
            s = KIND[k]
            near = sides(f[k])
            out = centre[s] * f[k] + adv_after * fields[k, after - base] - adv_before * fields[k, before - base]
            for c, x in zip(weights[s], near):
                out = out + c * x
            if k == 2:
                out = out + BUOYANCY * f[3]
            src[k, i - start] = out
        return 0

    lax.fori_loop(first, first + count, row, 0)


def early_kernel(count, fields_ref, visc, src, fields, sem):
    copy = pltpu.make_async_copy(fields_ref.at[:, 0 : count + 1], fields, sem)
    copy.start()
    copy.wait()
    explicit_rows(0, count, 0, 0, fields, visc, src)


def explicit_kernel(count, fields_ref, visc, g0, gn, early, src, p, ends, fields, sems):
    rows, ny, nz = visc.shape
    cuts = [count - 1] + list(range(2 * count + 1, rows, count)) + [rows]
    copies = []
    for c, (lo, hi) in enumerate(zip(cuts, cuts[1:])):
        copies.append(
            pltpu.make_async_copy(
                fields_ref.at[:, lo:hi], fields.at[:, lo - cuts[0] : hi - cuts[0]], sems.at[c]
            )
        )
        copies[-1].start()
    for c, copy in enumerate(copies):
        copy.wait()
        explicit_rows((c + 1) * count, count, cuts[0], count, fields, visc, src)

    def dot(ref, shift):
        def add(i, carry):
            new = []
            for g, base in ((g0, 0), (gn, 4)):
                for k in range(4):
                    new.append(carry[base + k] + g[KIND[k], i] * ref[k, i - shift])
            return tuple(new)

        return add

    final = (jnp.zeros((ny, nz), F32),) * 8
    final = lax.fori_loop(0, count, dot(early, 0), final)
    final = lax.fori_loop(count, rows, dot(src, count), final)
    for k in range(8):
        p[k] = final[k]

    for s in range(2):
        for side, at in ((0, 0), (1, ny - 1)):
            for which, g in ((0, g0), (1, gn)):
                for lo in range(0, rows, 8):
                    ends[4 * side + 2 * which + s, lo : lo + 8] = layer(
                        lambda r: g[s, lo + r, at : at + 1, :], ny, nz
                    )


def edge_kernel(rows, ny, y_last, y_first, low, high, ends, p, *refs):
    add, out = refs[-2:]
    nz = out.shape[2]
    sub = lax.broadcasted_iota(jnp.int32, (ny, 128), 0)
    rate = 0.5 * ADVECTION
    for j in range(nz // 128):
        z = pl.ds(j * 128, 128)
        sums = []
        for side, mine, far, sign in ((0, y_first, low, rate), (4, y_last, high, -rate)):
            total = [None] * 8
            for r in range(rows // 8):
                x = pl.ds(r * 8, 8)
                face = (0.5 * CROSS_RATE) * (mine[4, x, z] + far[4, x, z])
                faces = (face, THERMAL_RATIO * face)
                adv = sign * mine[1, x, z]
                both = [adv + c for c in faces]
                g = [ends[side + q, x, z] for q in range(4)]
                for k in range(4):
                    s = KIND[k]
                    h = both[s] * far[k, x, z] - faces[s] * mine[k, x, z]
                    add[side + k, x, z] = h
                    for slot, c in ((k, g[s]), (4 + k, g[2 + s])):
                        part = c * h
                        total[slot] = part if total[slot] is None else total[slot] + part
            sums.append(total)
        for slot in range(8):
            add_low = jnp.sum(sums[0][slot], axis=0, keepdims=True)
            add_high = jnp.sum(sums[1][slot], axis=0, keepdims=True)
            both = jnp.where(sub == 0, add_low, jnp.where(sub == ny - 1, add_high, 0.0))
            out[slot, :, z] = p[slot, :, z] + both


def side_bit(level):
    return jnp.bitwise_and(jnp.right_shift(lax.axis_index("line"), level), 1) == 0


def join(left, right):
    face = left[V_LAST] + right[V_FIRST]
    joint, new, ratio = {}, {}, []
    for s in range(2):
        resist = 1.0 / ((0.5 * STIFF * SCALES[s]) * face)
        r = 1.0 / (resist + left[GNN[s]] + right[G00[s]])
        ratio.append(r)
        a, b = left[G0N[s]], right[G0N[s]]
        joint[R_ + s] = r
        joint[GA + s] = a
        joint[GB + s] = b
        new[G00[s]] = left[G00[s]] - r * a * a
        new[GNN[s]] = right[GNN[s]] - r * b * b
        new[G0N[s]] = r * a * b
    rate = 0.5 * ADVECTION
    for k in range(4):
        s = KIND[k]
        add_a = -rate * left[F_LAST] * right[F_FIRST + k]
        add_b = rate * right[F_FIRST] * left[F_LAST + k]
        e = ratio[s] * (left[GNN[s]] * add_a - right[G00[s]] * add_b)
        joint[CA + k] = add_a - e
        joint[CB + k] = add_b + e
        new[F_FIRST + k] = left[F_FIRST + k]
        new[F_LAST + k] = right[F_LAST + k]
    new[V_FIRST] = left[V_FIRST]
    new[V_LAST] = right[V_LAST]
    return joint, new


def sided(low_side, mine, theirs):
    left = {p: jnp.where(low_side, mine[p], theirs[p]) for p in mine}
    right = {p: jnp.where(low_side, theirs[p], mine[p]) for p in mine}
    return left, right


def pair_kernel(own, other, *refs):
    joint, out = refs[-2:]
    low_side = side_bit(0)
    planes = range(PLANES)
    found, new = join(*sided(low_side, {p: own[p] for p in planes}, {p: other[p] for p in planes}))
    for plane in range(JOINT):
        joint[plane] = found[plane]
    width = out.shape[2]
    for plane in planes:
        out[plane] = jnp.where(low_side, new[plane][:, :width], new[plane][:, width:])


def chips_kernel(levels, own, *refs):
    others = refs[: 2 ** (levels - 1) - 1]
    joints = refs[-(2 * levels - 3) : len(refs) - (levels - 2)]
    consts = refs[len(refs) - (levels - 2) :]
    blocks = [{p: x[p] for p in range(PLANES)} for x in (own, *others)]
    zero = jnp.zeros_like(own[0])
    ends = [{p: zero for p in range(8)} for _ in blocks]
    for level in range(1, levels):
        low_side = side_bit(level)
        joined, new_ends = [], []
        for j in range(0, len(blocks), 2):
            found, new = join(*sided(low_side, blocks[j], blocks[j + 1]))
            for plane in range(JOINT):
                joints[level - 1][j // 2, plane] = found[plane]
            joined.append(new)
            if level < levels - 1:
                left, right = sided(low_side, ends[j], ends[j + 1])
                both = {}
                for k in range(4):
                    _, both[k], both[4 + k] = up(found, k, left, right)
                new_ends.append(both)
        blocks, ends = joined, new_ends
        if level < levels - 1:
            for slot, x in enumerate(facing(level + 1, levels, ends[1], False)):
                consts[level - 1][slot] = x


def facing(level, levels, ends, mine):
    if level < levels - 1:
        return [ends[p] for p in range(8)]
    low_side = side_bit(level)
    if not mine:
        low_side = jnp.logical_not(low_side)
    return [jnp.where(low_side, ends[4 + k], ends[k]) for k in range(4)]


def source_kernel(rows, count, early, src, cpr, add, t):
    ny, nz = src.shape[2], src.shape[3]
    sub = lax.broadcasted_iota(jnp.int32, (ny, nz), 0)
    top, low = sub == ny - 1, sub == 0

    def down(ref, shift):
        def row(i, carry):
            prev = jnp.maximum(i - 1, 0)
            new = []
            for k in range(4):
                a = jnp.broadcast_to(add[k, pl.ds(i, 1), :], (ny, nz))
                b = jnp.broadcast_to(add[4 + k, pl.ds(i, 1), :], (ny, nz))
                x = ref[k, i - shift] + jnp.where(low, a, jnp.where(top, b, 0.0))
                x = x + cpr[KIND[k], prev] * carry[k]
                t[k, i] = x
                new.append(x)
            return tuple(new)

        return row

    state = (jnp.zeros((ny, nz), F32),) * 4
    state = lax.fori_loop(0, count, down(early, 0), state)
    lax.fori_loop(count, rows, down(src, count), state)


def back_kernel(rows, t, inv, cpr, part):
    end = rows - 1
    start = []
    for k in range(4):
        x = inv[KIND[k], end] * t[k, end]
        part[k, end] = x
        start.append(x)

    def row(j, carry):
        i = end - 1 - j
        new = []
        for k in range(4):
            s = KIND[k]
            x = inv[s, i] * t[k, i] + cpr[s, i] * carry[k]
            part[k, i] = x
            new.append(x)
        return tuple(new)

    lax.fori_loop(0, end, row, tuple(start))


def up(joint, k, left, right):
    s = KIND[k]
    d = left[4 + k] - right[k]
    flow = joint[R_ + s] * d
    first = left[k] + joint[GA + s] * (joint[CA + k] - flow)
    last = right[4 + k] + joint[GB + s] * (joint[CB + k] + flow)
    return d, first, last


def up_kernel(levels, own, other, joint, *refs):
    joints = refs[: levels - 1]
    out, diff = refs[levels : levels + 2]
    shares = refs[levels + 2 :]
    low_side = side_bit(0)
    width = out.shape[2]
    left, right = sided(low_side, {p: own[p] for p in range(8)}, {p: other[p] for p in range(8)})
    ends = {}
    for k in range(4):
        diff[k], first, last = up(joint, k, left, right)
        ends[k] = jnp.where(low_side, first[:, :width], first[:, width:])
        ends[4 + k] = jnp.where(low_side, last[:, :width], last[:, width:])
        out[k] = ends[k]
        out[4 + k] = ends[4 + k]
    for level in range(1, levels - 1):
        low_side = side_bit(level)
        joint = joints[level - 1].at[0]
        for k in range(4):
            s = KIND[k]
            first, last = ends[k], ends[4 + k]
            flow = joint[R_ + s] * jnp.where(low_side, last, -first)
            ends[k] = jnp.where(low_side, first, 0.0) - joint[GA + s] * flow
            ends[4 + k] = jnp.where(low_side, 0.0, last) + joint[GB + s] * flow
        for slot, x in enumerate(facing(level + 1, levels, ends, True)):
            shares[level - 1][slot] = x


def joint_flow(joint, k, d, into_first, into_last, low_side):
    s = KIND[k]
    flow = joint[R_ + s] * (d + joint[GA + s] * into_first - joint[GB + s] * into_last)
    first = jnp.where(low_side, into_first, joint[CB + k] + flow)
    last = jnp.where(low_side, joint[CA + k] - flow, into_last)
    return first, last


def beside_kernel(levels, *refs):
    parts, refs = list(refs[: 2 ** (levels - 1) - levels]), refs[2 ** (levels - 1) - levels :]
    consts, outs = refs[: levels - 2], refs[levels - 2 :]
    for level in range(2, levels):
        here = [parts.pop(0) for _ in range(2 ** (level - 1) - 1)]
        for p in range(outs[level - 2].shape[0]):
            total = consts[level - 2][p]
            for part in here:
                total = total + part[p]
            outs[level - 2][p] = total


def settle_kernel(levels, own, *refs):
    near, refs = refs[: levels - 1], refs[levels - 1 :]
    far, joints, out = refs[: levels - 2], refs[levels - 2 : -1], refs[-1]
    ends = {p: own[p] for p in range(8)}
    diffs = []
    for level in range(1, levels):
        low_side = side_bit(level)
        beside = {p: near[level - 1][p] for p in range(near[level - 1].shape[0])}
        if level > 1:
            beside = {p: x + far[level - 2][p] for p, x in beside.items()}
        across = []
        if len(beside) == 4:
            for k in range(4):
                x = beside[k]
                across.append(jnp.where(low_side, ends[4 + k] - x, x - ends[k]))
        else:
            left, right = sided(low_side, ends, beside)
            for k in range(4):
                d, ends[k], ends[4 + k] = up(joints[level - 1].at[0], k, left, right)
                across.append(d)
        diffs.append(across)
    for k in range(4):
        first = last = jnp.zeros_like(diffs[0][0])
        for level in range(levels - 1, 0, -1):
            first, last = joint_flow(
                joints[level - 1].at[0], k, diffs[level - 1][k], first, last, side_bit(level)
            )
        out[k] = first
        out[4 + k] = last


def final_kernel(mine, parts, flux, joint, diff, part, g0, gn, *refs):
    out, buf, sems = refs[-3:]
    rows, half = buf.shape[1], buf.shape[3]
    low_side = side_bit(0)
    core = jnp.bitwise_and(lax.axis_index("line"), 1)
    offset = (core if mine else 1 - core) * half
    chunks, into = [], []
    for c in range(half // 128):
        near = pl.ds(c * 128, 128)
        z = pl.ds(pl.multiple_of(offset + c * 128, 128), 128)
        across = {plane: joint[plane, :, z] for plane in range(JOINT)}
        chunks.append((near, z))
        into.append(
            [
                joint_flow(across, k, diff[k, :, z], flux[k, :, near], flux[4 + k, :, near], low_side)
                for k in range(4)
            ]
        )
    copies = []
    step = rows // parts
    for r in range(parts):
        for (near, z), ends in zip(chunks, into):
            for i in range(r * step, (r + 1) * step):
                a = [g0[s, i, :, z] for s in range(2)]
                b = [gn[s, i, :, z] for s in range(2)]
                for k in range(4):
                    s = KIND[k]
                    buf[k, i, :, near] = part[k, i, :, z] + (a[s] * ends[k][0] + b[s] * ends[k][1])
        x = pl.ds(r * step, step)
        lanes = pl.ds(pl.multiple_of(offset, 128), half)
        copies.append(pltpu.make_async_copy(buf.at[:, x], out.at[:, x, :, lanes], sems.at[r]))
        copies[-1].start()
    for copy in copies:
        copy.wait()


def local(fields, viscosity):
    rows, ny, nz = viscosity.shape
    lines = lax.axis_size("line")
    cols = lax.axis_size("col")
    levels = lines.bit_length() - 1
    half = nz // 2
    cells = rows * ny * nz
    block = (rows, ny, nz)

    ring = [(i, (i + 1) % cols) for i in range(cols)]
    back_ring = [(b, a) for a, b in ring]

    def gather(at_level):
        found = {}
        for d in sorted(range(1, lines // 2), key=lambda d: (-d.bit_count(), d)):
            x = at_level[d.bit_length()]
            found[d] = lax.ppermute(x, "line", [(i, i ^ (d << 1)) for i in range(lines)])
        return [found[d] for d in sorted(found)]

    def swap(x, level):
        return lax.ppermute(x, "line", [(i, i ^ (1 << level)) for i in range(lines)])

    y_first, y_last = call(
        functools.partial(cut_kernel, ny),
        "cut",
        [(5, rows, nz), (5, rows, nz)],
        [fields, viscosity],
        scratch=[pltpu.SemaphoreType.DMA((2, 5))],
        in_hbm=(0, 1),
        moved=2 * cells,
    )
    low = lax.ppermute(y_last, "col", ring)
    high = lax.ppermute(y_first, "col", back_ring)

    inv, cpr, g0, gn, w = call(
        functools.partial(factor_kernel, rows),
        "factor",
        [(2,) + block] * 4 + [(PLANES, ny, nz)],
        [fields, viscosity],
        scratch=[VMEM((2,) + block, F32), pltpu.SemaphoreType.DMA((2,))],
        in_hbm=(0,),
        flops=10**9,
    )
    count = rows // 4
    (early,) = call(
        functools.partial(early_kernel, count),
        "early",
        [(4, count, ny, nz)],
        [fields, viscosity],
        scratch=[VMEM((4, count + 1, ny, nz), F32), pltpu.SemaphoreType.DMA],
        in_hbm=(0,),
        flops=4 * 10**9,
    )
    src, p, ends = call(
        functools.partial(explicit_kernel, count),
        "explicit",
        [(4, rows - count, ny, nz), (8, ny, nz), (8, rows, nz)],
        [fields, viscosity, g0, gn, early],
        scratch=[VMEM((4, rows - count + 1, ny, nz), F32), pltpu.SemaphoreType.DMA((3,))],
        in_hbm=(0,),
        flops=5 * 10**9,
    )
    pair, w = call(
        pair_kernel,
        "pair",
        [(JOINT, ny, nz), (PLANES, ny, half)],
        [w, swap(w, 0), early],
        moved=4 * ny * nz * 60,
    )
    pairs = lines // 2
    widths = [8] * (levels - 3) + [4]
    found = call(
        functools.partial(chips_kernel, levels),
        "chips",
        [(pairs >> level, JOINT, ny, half) for level in range(1, levels)]
        + [(width, ny, half) for width in widths],
        [w] + gather([w] * (levels + 1)) + [p],
        moved=4 * ny * half * 300,
    )
    joints, consts = list(found[: levels - 1]), list(found[levels - 1 :])

    add, p = call(
        functools.partial(edge_kernel, rows, ny),
        "edge",
        [(8, rows, nz), (8, ny, nz)],
        [y_last, y_first, low, high, ends, p, joints[0]],
        flops=5 * 10**8,
    )
    (t,) = call(
        functools.partial(source_kernel, rows, count),
        "source",
        [(4,) + block],
        [early, src, cpr, add],
        flops=30 * cells,
        moved=24 * cells,
    )
    (part,) = call(
        functools.partial(back_kernel, rows),
        "back",
        [(4,) + block],
        [t, inv, cpr],
        flops=20 * cells,
        moved=24 * cells,
    )
    p, diff, *shares = call(
        functools.partial(up_kernel, levels),
        "up",
        [(8, ny, half), (4, ny, nz)] + [(width, ny, half) for width in widths],
        [p, swap(p, 0), pair] + joints + [part],
        moved=4 * ny * nz * 40,
    )
    others = dict(enumerate(gather([None, p] + shares), 1))
    near = [others.pop(1 << level) for level in range(levels - 1)]
    beside = call(
        functools.partial(beside_kernel, levels),
        "beside",
        [(width, ny, half) for width in widths],
        list(others.values()) + consts,
        flops=6 * 10**8,
    )
    (flux,) = call(
        functools.partial(settle_kernel, levels),
        "settle",
        [(8, ny, half)],
        [p] + near + list(beside) + joints,
        moved=4 * ny * half * 100,
    )
    rest = [pair, diff, part, g0, gn]
    parts = 8 if rows % 8 == 0 else 1
    scratch = [VMEM((4, rows, ny, half), F32), pltpu.SemaphoreType.DMA((parts,))]
    (out,) = call(
        functools.partial(final_kernel, True, parts),
        "final_own",
        [(4,) + block],
        [flux] + rest,
        scratch=scratch,
        out_hbm=(0,),
        flops=10**9,
    )
    (out,) = call(
        functools.partial(final_kernel, False, parts),
        "final_other",
        [(4,) + block],
        [swap(flux, 0)] + rest + [out],
        scratch=scratch,
        in_hbm=(6,),
        out_hbm=(0,),
        aliases={6: 0},
        flops=10**9,
    )
    return out


def solution(mesh):
    return jax.shard_map(
        local,
        mesh=mesh,
        in_specs=(P(None, "line", "col", None), P("line", "col", None)),
        out_specs=P(None, "line", "col", None),
        check_vma=False,
    )
```

```python
import functools

import jax
import jax.numpy as jnp
from jax import lax
from jax.experimental import pallas as pl
from jax.experimental.pallas import tpu as pltpu
from jax.sharding import PartitionSpec as P

STIFF = 3072
THERMAL_RATIO = 0.8
CROSS_RATE = 0.2
ADVECTION = 0.25
BUOYANCY = 2.0
SCALES = (1.0, THERMAL_RATIO)
KIND = (0, 0, 0, 1)

F32 = jnp.float32
VMEM = pltpu.VMEM
LIMIT = 24 * 1024 * 1024

G00, G0N, GNN = (0, 3), (1, 4), (2, 5)
V_FIRST, V_LAST, F_FIRST, F_LAST = 6, 7, 8, 12
PLANES = 16
R_, GA, GB, CA, CB = 0, 2, 4, 6, 10
JOINT = 14


def in_vmem(x):
    return pltpu.with_memory_space_constraint(x, VMEM)


def spec():
    return pl.BlockSpec(memory_space=VMEM)


def call(kernel, name, out_shapes, args, scratch=(), in_hbm=(), out_hbm=(), aliases={}, flops=0, moved=0):
    in_specs = []
    operands = []
    for i, x in enumerate(args):
        if i in in_hbm:
            in_specs.append(pl.BlockSpec(memory_space=pltpu.HBM))
            operands.append(pltpu.with_memory_space_constraint(x, pltpu.HBM))
        else:
            in_specs.append(spec())
            operands.append(in_vmem(x))
    out_shape = []
    out_specs = []
    for i, s in enumerate(out_shapes):
        if i in out_hbm:
            out_shape.append(pltpu.HBM(s, F32))
            out_specs.append(pl.BlockSpec(memory_space=pltpu.HBM))
        else:
            out_shape.append(VMEM(s, F32))
            out_specs.append(spec())
    return pl.pallas_call(
        kernel,
        out_shape=out_shape,
        in_specs=in_specs,
        out_specs=out_specs,
        scratch_shapes=list(scratch),
        input_output_aliases=aliases,
        compiler_params=pltpu.CompilerParams(vmem_limit_bytes=LIMIT),
        cost_estimate=pl.CostEstimate(flops=flops, bytes_accessed=moved, transcendentals=0),
        name=name,
    )(*operands)


def layer(read, ny, nz):
    sub = lax.broadcasted_iota(jnp.int32, (8, nz), 0)
    tile = jnp.broadcast_to(read(0), (8, nz))
    for r in range(1, 8):
        tile = jnp.where(sub == r, jnp.broadcast_to(read(r), (8, nz)), tile)
    return tile


def col_odd():
    return jnp.bitwise_and(lax.axis_index("col"), 1) == 1


def cut_kernel(ny, fields, visc, first_out, second_out, sems):
    def run(ats):
        copies = []
        for j, (at, out) in enumerate(zip(ats, (first_out, second_out))):
            for k in range(4):
                copies.append(pltpu.make_async_copy(fields.at[k, :, at], out.at[k], sems.at[j, k]))
            copies.append(pltpu.make_async_copy(visc.at[:, at], out.at[4], sems.at[j, 4]))
        for copy in copies:
            copy.start()
        for copy in copies:
            copy.wait()

    odd = col_odd()
    pl.when(odd)(lambda: run((ny - 1, 0)))
    pl.when(jnp.logical_not(odd))(lambda: run((0, ny - 1)))


def factor_kernel(rows, fields_ref, visc, inv, cpr, g0, gn, w, tau, sems):
    copies = [
        pltpu.make_async_copy(fields_ref.at[:, 0], w.at[F_FIRST : F_FIRST + 4], sems.at[0]),
        pltpu.make_async_copy(fields_ref.at[:, rows - 1], w.at[F_LAST : F_LAST + 4], sems.at[1]),
    ]
    for copy in copies:
        copy.start()
    ny, nz = visc.shape[1], visc.shape[2]
    me = lax.axis_index("line")
    wall_low = jnp.where(me == 0, 1.0, 0.0).astype(F32)
    wall_high = jnp.where(me == lax.axis_size("line") - 1, 1.0, 0.0).astype(F32)
    one = jnp.ones((ny, nz), F32)

    def row(i, carry):
        low, v = carry[4], carry[5]
        after = visc[jnp.minimum(i + 1, rows - 1)]
        high = jnp.where(i == rows - 1, (0.5 * STIFF) * wall_high * v, (0.5 * STIFF) * (v + after))
        new = []
        for s in range(2):
            gain, running = carry[2 * s], carry[2 * s + 1]
            down = SCALES[s] * low if s else low
            up = SCALES[s] * high if s else high
            q = 1.0 + down * gain
            one_over = 1.0 / (q + up)
            coupling = up * one_over
            inv[s, i] = one_over
            cpr[s, i] = coupling
            tau[s, i] = running
            new += [q * one_over, coupling * running]
        return tuple(new) + (high, after)

    first = visc[0]
    lax.fori_loop(0, rows, row, (one,) * 4 + (wall_low * (0.5 * STIFF) * first, first))

    end = rows - 1
    start = []
    for s in range(2):
        a = inv[s, end] * tau[s, end]
        b = inv[s, end]
        g0[s, end] = a
        gn[s, end] = b
        w[G0N[s]] = a
        w[GNN[s]] = b
        start += [a, b]

    def back(j, carry):
        i = end - 1 - j
        new = []
        for s in range(2):
            c = cpr[s, i]
            a = inv[s, i] * tau[s, i] + c * carry[2 * s]
            b = c * carry[2 * s + 1]
            g0[s, i] = a
            gn[s, i] = b
            new += [a, b]
        return tuple(new)

    final = lax.fori_loop(0, end, back, tuple(start))
    for s in range(2):
        w[G00[s]] = final[2 * s]
    w[V_FIRST] = first
    w[V_LAST] = visc[rows - 1]
    for copy in copies:
        copy.wait()


def explicit_rows(first, count, base, start, fields, visc, src):
    rows, ny, nz = visc.shape
    lane = lax.broadcasted_iota(jnp.int32, (ny, nz), 1)
    sub = lax.broadcasted_iota(jnp.int32, (ny, nz), 0)
    z_top, z_low = lane == nz - 1, lane == 0
    y_top, y_low = sub == ny - 1, sub == 0

    def sides(x):
        return (
            pltpu.roll(x, ny - 1, 0),
            pltpu.roll(x, 1, 0),
            pltpu.roll(x, nz - 1, 1),
            pltpu.roll(x, 1, 1),
        )

    def row(i, _):
        f = [fields[k, i - base] for k in range(4)]
        v = visc[i]
        after, before = jnp.minimum(i + 1, rows - 1), jnp.maximum(i - 1, 0)
        vyn, vyp, vzn, vzp = sides(v)
        half = 0.5 * CROSS_RATE
        faces = [
            jnp.where(y_top, 0.0, half * (v + vyn)),
            jnp.where(y_low, 0.0, half * (v + vyp)),
            half * (v + jnp.where(z_top, 0.0, vzn)),
            half * (v + jnp.where(z_low, 0.0, vzp)),
        ]
        none = [y_top, y_low, z_top, z_low]
        total = (faces[0] + faces[1]) + (faces[2] + faces[3])
        adv = [(-0.5 * ADVECTION) * f[k] for k in range(3)]
        move = [adv[1], -adv[1], adv[2], -adv[2]]
        adv_after = jnp.where(i == rows - 1, 0.0, adv[0])
        adv_before = jnp.where(i == 0, 0.0, adv[0])
        weights, centre = [], []
        for s in range(2):
            scaled = [SCALES[s] * x if s else x for x in faces]
            weights.append([jnp.where(n, 0.0, x + m) for n, x, m in zip(none, scaled, move)])
            centre.append(1.0 - (SCALES[s] * total if s else total))
        for k in range(4):
            s = KIND[k]
            near = sides(f[k])
            out = centre[s] * f[k] + adv_after * fields[k, after - base] - adv_before * fields[k, before - base]
            for c, x in zip(weights[s], near):
                out = out + c * x
            if k == 2:
                out = out + BUOYANCY * f[3]
            src[k, i - start] = out
        return 0

    lax.fori_loop(first, first + count, row, 0)


def early_kernel(count, fields_ref, visc, src, fields, sem):
    copy = pltpu.make_async_copy(fields_ref.at[:, 0 : count + 1], fields, sem)
    copy.start()
    copy.wait()
    explicit_rows(0, count, 0, 0, fields, visc, src)


def explicit_kernel(count, fields_ref, visc, g0, gn, early, src, p, ends, fields, sems):
    rows, ny, nz = visc.shape
    cuts = [count - 1] + list(range(2 * count + 1, rows, count)) + [rows]
    copies = []
    for c, (lo, hi) in enumerate(zip(cuts, cuts[1:])):
        copies.append(
            pltpu.make_async_copy(
                fields_ref.at[:, lo:hi], fields.at[:, lo - cuts[0] : hi - cuts[0]], sems.at[c]
            )
        )
        copies[-1].start()
    for c, copy in enumerate(copies):
        copy.wait()
        explicit_rows((c + 1) * count, count, cuts[0], count, fields, visc, src)

    def dot(ref, shift):
        def add(i, carry):
            new = []
            for g, base in ((g0, 0), (gn, 4)):
                for k in range(4):
                    new.append(carry[base + k] + g[KIND[k], i] * ref[k, i - shift])
            return tuple(new)

        return add

    final = (jnp.zeros((ny, nz), F32),) * 8
    final = lax.fori_loop(0, count, dot(early, 0), final)
    final = lax.fori_loop(count, rows, dot(src, count), final)
    for k in range(8):
        p[k] = final[k]

    for s in range(2):
        for side, at in ((0, 0), (1, ny - 1)):
            for which, g in ((0, g0), (1, gn)):
                for lo in range(0, rows, 8):
                    ends[4 * side + 2 * which + s, lo : lo + 8] = layer(
                        lambda r: g[s, lo + r, at : at + 1, :], ny, nz
                    )


def edge_kernel(rows, ny, sent_two, sent_one, got_two, got_one, ends, p, *refs):
    add, out = refs[-2:]
    nz = out.shape[2]
    sub = lax.broadcasted_iota(jnp.int32, (ny, 128), 0)
    rate = 0.5 * ADVECTION
    odd = col_odd()
    slots = (
        (jnp.where(odd, 4, 0), sent_one, got_one, jnp.where(odd, -rate, rate).astype(F32)),
        (jnp.where(odd, 0, 4), sent_two, got_two, jnp.where(odd, rate, -rate).astype(F32)),
    )
    for j in range(nz // 128):
        z = pl.ds(j * 128, 128)
        sums = []
        for side, mine, far, sign in slots:
            total = [None] * 8
            for r in range(rows // 8):
                x = pl.ds(r * 8, 8)
                face = (0.5 * CROSS_RATE) * (mine[4, x, z] + far[4, x, z])
                faces = (face, THERMAL_RATIO * face)
                adv = sign * mine[1, x, z]
                both = [adv + c for c in faces]
                g = [ends[side + q, x, z] for q in range(4)]
                for k in range(4):
                    s = KIND[k]
                    h = both[s] * far[k, x, z] - faces[s] * mine[k, x, z]
                    add[side + k, x, z] = h
                    for slot, c in ((k, g[s]), (4 + k, g[2 + s])):
                        part = c * h
                        total[slot] = part if total[slot] is None else total[slot] + part
            sums.append(total)
        for slot in range(8):
            add_one = jnp.sum(sums[0][slot], axis=0, keepdims=True)
            add_two = jnp.sum(sums[1][slot], axis=0, keepdims=True)
            add_low = jnp.where(odd, add_two, add_one)
            add_high = jnp.where(odd, add_one, add_two)
            both = jnp.where(sub == 0, add_low, jnp.where(sub == ny - 1, add_high, 0.0))
            out[slot, :, z] = p[slot, :, z] + both


def side_bit(level):
    return jnp.bitwise_and(jnp.right_shift(lax.axis_index("line"), level), 1) == 0


def join(left, right):
    face = left[V_LAST] + right[V_FIRST]
    joint, new, ratio = {}, {}, []
    for s in range(2):
        resist = 1.0 / ((0.5 * STIFF * SCALES[s]) * face)
        r = 1.0 / (resist + left[GNN[s]] + right[G00[s]])
        ratio.append(r)
        a, b = left[G0N[s]], right[G0N[s]]
        joint[R_ + s] = r
        joint[GA + s] = a
        joint[GB + s] = b
        new[G00[s]] = left[G00[s]] - r * a * a
        new[GNN[s]] = right[GNN[s]] - r * b * b
        new[G0N[s]] = r * a * b
    rate = 0.5 * ADVECTION
    for k in range(4):
        s = KIND[k]
        add_a = -rate * left[F_LAST] * right[F_FIRST + k]
        add_b = rate * right[F_FIRST] * left[F_LAST + k]
        e = ratio[s] * (left[GNN[s]] * add_a - right[G00[s]] * add_b)
        joint[CA + k] = add_a - e
        joint[CB + k] = add_b + e
        new[F_FIRST + k] = left[F_FIRST + k]
        new[F_LAST + k] = right[F_LAST + k]
    new[V_FIRST] = left[V_FIRST]
    new[V_LAST] = right[V_LAST]
    return joint, new


def sided(low_side, mine, theirs):
    left = {p: jnp.where(low_side, mine[p], theirs[p]) for p in mine}
    right = {p: jnp.where(low_side, theirs[p], mine[p]) for p in mine}
    return left, right


def pair_kernel(own, other, *refs):
    joint, out = refs[-2:]
    low_side = side_bit(0)
    planes = range(PLANES)
    found, new = join(*sided(low_side, {p: own[p] for p in planes}, {p: other[p] for p in planes}))
    for plane in range(JOINT):
        joint[plane] = found[plane]
    width = out.shape[2]
    for plane in planes:
        out[plane] = jnp.where(low_side, new[plane][:, :width], new[plane][:, width:])


def chips_kernel(levels, own, *refs):
    others = refs[: 2 ** (levels - 1) - 1]
    joints = refs[-(2 * levels - 3) : len(refs) - (levels - 2)]
    consts = refs[len(refs) - (levels - 2) :]
    blocks = [{p: x[p] for p in range(PLANES)} for x in (own, *others)]
    zero = jnp.zeros_like(own[0])
    ends = [{p: zero for p in range(8)} for _ in blocks]
    for level in range(1, levels):
        low_side = side_bit(level)
        joined, new_ends = [], []
        for j in range(0, len(blocks), 2):
            found, new = join(*sided(low_side, blocks[j], blocks[j + 1]))
            for plane in range(JOINT):
                joints[level - 1][j // 2, plane] = found[plane]
            joined.append(new)
            if level < levels - 1:
                left, right = sided(low_side, ends[j], ends[j + 1])
                both = {}
                for k in range(4):
                    _, both[k], both[4 + k] = up(found, k, left, right)
                new_ends.append(both)
        blocks, ends = joined, new_ends
        if level < levels - 1:
            for slot, x in enumerate(facing(level + 1, levels, ends[1], False)):
                consts[level - 1][slot] = x


def facing(level, levels, ends, mine):
    if level < levels - 1:
        return [ends[p] for p in range(8)]
    low_side = side_bit(level)
    if not mine:
        low_side = jnp.logical_not(low_side)
    return [jnp.where(low_side, ends[4 + k], ends[k]) for k in range(4)]


def source_kernel(rows, count, early, src, cpr, add, t):
    ny, nz = src.shape[2], src.shape[3]
    sub = lax.broadcasted_iota(jnp.int32, (ny, nz), 0)
    top, low = sub == ny - 1, sub == 0

    def down(ref, shift):
        def row(i, carry):
            prev = jnp.maximum(i - 1, 0)
            new = []
            for k in range(4):
                a = jnp.broadcast_to(add[k, pl.ds(i, 1), :], (ny, nz))
                b = jnp.broadcast_to(add[4 + k, pl.ds(i, 1), :], (ny, nz))
                x = ref[k, i - shift] + jnp.where(low, a, jnp.where(top, b, 0.0))
                x = x + cpr[KIND[k], prev] * carry[k]
                t[k, i] = x
                new.append(x)
            return tuple(new)

        return row

    state = (jnp.zeros((ny, nz), F32),) * 4
    state = lax.fori_loop(0, count, down(early, 0), state)
    lax.fori_loop(count, rows, down(src, count), state)


def back_kernel(rows, t, inv, cpr, part):
    end = rows - 1
    start = []
    for k in range(4):
        x = inv[KIND[k], end] * t[k, end]
        part[k, end] = x
        start.append(x)

    def row(j, carry):
        i = end - 1 - j
        new = []
        for k in range(4):
            s = KIND[k]
            x = inv[s, i] * t[k, i] + cpr[s, i] * carry[k]
            part[k, i] = x
            new.append(x)
        return tuple(new)

    lax.fori_loop(0, end, row, tuple(start))


def up(joint, k, left, right):
    s = KIND[k]
    d = left[4 + k] - right[k]
    flow = joint[R_ + s] * d
    first = left[k] + joint[GA + s] * (joint[CA + k] - flow)
    last = right[4 + k] + joint[GB + s] * (joint[CB + k] + flow)
    return d, first, last


def up_kernel(levels, own, other, joint, *refs):
    joints = refs[: levels - 1]
    out, diff = refs[levels : levels + 2]
    shares = refs[levels + 2 :]
    low_side = side_bit(0)
    width = out.shape[2]
    left, right = sided(low_side, {p: own[p] for p in range(8)}, {p: other[p] for p in range(8)})
    ends = {}
    for k in range(4):
        diff[k], first, last = up(joint, k, left, right)
        ends[k] = jnp.where(low_side, first[:, :width], first[:, width:])
        ends[4 + k] = jnp.where(low_side, last[:, :width], last[:, width:])
        out[k] = ends[k]
        out[4 + k] = ends[4 + k]
    for level in range(1, levels - 1):
        low_side = side_bit(level)
        joint = joints[level - 1].at[0]
        for k in range(4):
            s = KIND[k]
            first, last = ends[k], ends[4 + k]
            flow = joint[R_ + s] * jnp.where(low_side, last, -first)
            ends[k] = jnp.where(low_side, first, 0.0) - joint[GA + s] * flow
            ends[4 + k] = jnp.where(low_side, 0.0, last) + joint[GB + s] * flow
        for slot, x in enumerate(facing(level + 1, levels, ends, True)):
            shares[level - 1][slot] = x


def joint_flow(joint, k, d, into_first, into_last, low_side):
    s = KIND[k]
    flow = joint[R_ + s] * (d + joint[GA + s] * into_first - joint[GB + s] * into_last)
    first = jnp.where(low_side, into_first, joint[CB + k] + flow)
    last = jnp.where(low_side, joint[CA + k] - flow, into_last)
    return first, last


def beside_kernel(levels, *refs):
    parts, refs = list(refs[: 2 ** (levels - 1) - levels]), refs[2 ** (levels - 1) - levels :]
    consts, outs = refs[: levels - 2], refs[levels - 2 :]
    for level in range(2, levels):
        here = [parts.pop(0) for _ in range(2 ** (level - 1) - 1)]
        for p in range(outs[level - 2].shape[0]):
            total = consts[level - 2][p]
            for part in here:
                total = total + part[p]
            outs[level - 2][p] = total


def settle_kernel(levels, own, *refs):
    near, refs = refs[: levels - 1], refs[levels - 1 :]
    far, joints, out = refs[: levels - 2], refs[levels - 2 : -1], refs[-1]
    ends = {p: own[p] for p in range(8)}
    diffs = []
    for level in range(1, levels):
        low_side = side_bit(level)
        beside = {p: near[level - 1][p] for p in range(near[level - 1].shape[0])}
        if level > 1:
            beside = {p: x + far[level - 2][p] for p, x in beside.items()}
        across = []
        if len(beside) == 4:
            for k in range(4):
                x = beside[k]
                across.append(jnp.where(low_side, ends[4 + k] - x, x - ends[k]))
        else:
            left, right = sided(low_side, ends, beside)
            for k in range(4):
                d, ends[k], ends[4 + k] = up(joints[level - 1].at[0], k, left, right)
                across.append(d)
        diffs.append(across)
    for k in range(4):
        first = last = jnp.zeros_like(diffs[0][0])
        for level in range(levels - 1, 0, -1):
            first, last = joint_flow(
                joints[level - 1].at[0], k, diffs[level - 1][k], first, last, side_bit(level)
            )
        out[k] = first
        out[4 + k] = last


def final_kernel(mine, parts, flux, joint, diff, part, g0, gn, *refs):
    out, buf, sems = refs[-3:]
    rows, half = buf.shape[1], buf.shape[3]
    low_side = side_bit(0)
    core = jnp.bitwise_and(lax.axis_index("line"), 1)
    offset = (core if mine else 1 - core) * half
    copies = []
    for c in range(half // 128):
        near = pl.ds(c * 128, 128)
        z = pl.ds(pl.multiple_of(offset + c * 128, 128), 128)
        across = {plane: joint[plane, :, z] for plane in range(JOINT)}
        into = [
            joint_flow(across, k, diff[k, :, z], flux[k, :, near], flux[4 + k, :, near], low_side)
            for k in range(4)
        ]
        for r in range(parts):
            x = pl.ds(r * (rows // parts), rows // parts)
            for i in range(x.start, x.start + x.size):
                a = [g0[s, i, :, z] for s in range(2)]
                b = [gn[s, i, :, z] for s in range(2)]
                for k in range(4):
                    s = KIND[k]
                    buf[k, i, :, near] = part[k, i, :, z] + (a[s] * into[k][0] + b[s] * into[k][1])
            copies.append(
                pltpu.make_async_copy(
                    buf.at[:, x, :, near], out.at[:, x, :, z], sems.at[c * parts + r]
                )
            )
            copies[-1].start()
    for copy in copies:
        copy.wait()


def local(fields, viscosity):
    rows, ny, nz = viscosity.shape
    lines = lax.axis_size("line")
    cols = lax.axis_size("col")
    levels = lines.bit_length() - 1
    half = nz // 2
    cells = rows * ny * nz
    block = (rows, ny, nz)

    across = [(i, (i + 1) % cols if i % 2 else (i - 1) % cols) for i in range(cols)]
    inside = [(i, (i - 1) % cols if i % 2 else (i + 1) % cols) for i in range(cols)]

    def gather(at_level):
        found = {}
        for d in sorted(range(1, lines // 2), key=lambda d: (-d.bit_count(), d)):
            x = at_level[d.bit_length()]
            found[d] = lax.ppermute(x, "line", [(i, i ^ (d << 1)) for i in range(lines)])
        return [found[d] for d in sorted(found)]

    def swap(x, level):
        return lax.ppermute(x, "line", [(i, i ^ (1 << level)) for i in range(lines)])

    sent_one, sent_two = call(
        functools.partial(cut_kernel, ny),
        "cut",
        [(5, rows, nz), (5, rows, nz)],
        [fields, viscosity],
        scratch=[pltpu.SemaphoreType.DMA((2, 5))],
        in_hbm=(0, 1),
        moved=2 * cells,
    )
    got_one = lax.ppermute(sent_one, "col", across)
    got_two = lax.ppermute(sent_two, "col", inside)

    inv, cpr, g0, gn, w = call(
        functools.partial(factor_kernel, rows),
        "factor",
        [(2,) + block] * 4 + [(PLANES, ny, nz)],
        [fields, viscosity],
        scratch=[VMEM((2,) + block, F32), pltpu.SemaphoreType.DMA((2,))],
        in_hbm=(0,),
        flops=10**9,
    )
    count = rows // 4
    (early,) = call(
        functools.partial(early_kernel, count),
        "early",
        [(4, count, ny, nz)],
        [fields, viscosity],
        scratch=[VMEM((4, count + 1, ny, nz), F32), pltpu.SemaphoreType.DMA],
        in_hbm=(0,),
        flops=4 * 10**9,
    )
    src, p, ends = call(
        functools.partial(explicit_kernel, count),
        "explicit",
        [(4, rows - count, ny, nz), (8, ny, nz), (8, rows, nz)],
        [fields, viscosity, g0, gn, early],
        scratch=[VMEM((4, rows - count + 1, ny, nz), F32), pltpu.SemaphoreType.DMA((3,))],
        in_hbm=(0,),
        flops=5 * 10**9,
    )
    pair, w = call(
        pair_kernel,
        "pair",
        [(JOINT, ny, nz), (PLANES, ny, half)],
        [w, swap(w, 0), early],
        moved=4 * ny * nz * 60,
    )
    pairs = lines // 2
    widths = [8] * (levels - 3) + [4]
    found = call(
        functools.partial(chips_kernel, levels),
        "chips",
        [(pairs >> level, JOINT, ny, half) for level in range(1, levels)]
        + [(width, ny, half) for width in widths],
        [w] + gather([w] * (levels + 1)) + [p],
        moved=4 * ny * half * 300,
    )
    joints, consts = list(found[: levels - 1]), list(found[levels - 1 :])

    add, p = call(
        functools.partial(edge_kernel, rows, ny),
        "edge",
        [(8, rows, nz), (8, ny, nz)],
        [sent_two, sent_one, got_two, got_one, ends, p, joints[0]],
        flops=5 * 10**8,
    )
    (t,) = call(
        functools.partial(source_kernel, rows, count),
        "source",
        [(4,) + block],
        [early, src, cpr, add],
        flops=30 * cells,
        moved=24 * cells,
    )
    (part,) = call(
        functools.partial(back_kernel, rows),
        "back",
        [(4,) + block],
        [t, inv, cpr],
        flops=20 * cells,
        moved=24 * cells,
    )
    p, diff, *shares = call(
        functools.partial(up_kernel, levels),
        "up",
        [(8, ny, half), (4, ny, nz)] + [(width, ny, half) for width in widths],
        [p, swap(p, 0), pair] + joints + [part],
        moved=4 * ny * nz * 40,
    )
    others = dict(enumerate(gather([None, p] + shares), 1))
    near = [others.pop(1 << level) for level in range(levels - 1)]
    beside = call(
        functools.partial(beside_kernel, levels),
        "beside",
        [(width, ny, half) for width in widths],
        list(others.values()) + consts,
        flops=6 * 10**8,
    )
    (flux,) = call(
        functools.partial(settle_kernel, levels),
        "settle",
        [(8, ny, half)],
        [p] + near + list(beside) + joints,
        moved=4 * ny * half * 100,
    )
    rest = [pair, diff, part, g0, gn]
    parts = 4 if rows % 4 == 0 else 1
    scratch = [VMEM((4, rows, ny, half), F32), pltpu.SemaphoreType.DMA((half // 128 * parts,))]
    (out,) = call(
        functools.partial(final_kernel, True, parts),
        "final_own",
        [(4,) + block],
        [flux] + rest,
        scratch=scratch,
        out_hbm=(0,),
        flops=10**9,
    )
    (out,) = call(
        functools.partial(final_kernel, False, parts),
        "final_other",
        [(4,) + block],
        [swap(flux, 0)] + rest + [out],
        scratch=scratch,
        in_hbm=(6,),
        out_hbm=(0,),
        aliases={6: 0},
        flops=10**9,
    )
    return out


def solution(mesh):
    return jax.shard_map(
        local,
        mesh=mesh,
        in_specs=(P(None, "line", "col", None), P("line", "col", None)),
        out_specs=P(None, "line", "col", None),
        check_vma=False,
    )
```

```python
import functools

import jax
import jax.numpy as jnp
from jax import lax
from jax.experimental import pallas as pl
from jax.experimental.pallas import tpu as pltpu
from jax.sharding import PartitionSpec as P

STIFF = 3072
THERMAL_RATIO = 0.8
CROSS_RATE = 0.2
ADVECTION = 0.25
BUOYANCY = 2.0
SCALES = (1.0, THERMAL_RATIO)
KIND = (0, 0, 0, 1)

F32 = jnp.float32
VMEM = pltpu.VMEM
LIMIT = 24 * 1024 * 1024

G00, G0N, GNN = (0, 3), (1, 4), (2, 5)
V_FIRST, V_LAST, F_FIRST, F_LAST = 6, 7, 8, 12
PLANES = 16
R_, GA, GB, CA, CB = 0, 2, 4, 6, 10
JOINT = 14


def in_vmem(x):
    return pltpu.with_memory_space_constraint(x, VMEM)


def spec():
    return pl.BlockSpec(memory_space=VMEM)


def call(kernel, name, out_shapes, args, scratch=(), in_hbm=(), out_hbm=(), aliases={}, flops=0, moved=0):
    in_specs = []
    operands = []
    for i, x in enumerate(args):
        if i in in_hbm:
            in_specs.append(pl.BlockSpec(memory_space=pltpu.HBM))
            operands.append(pltpu.with_memory_space_constraint(x, pltpu.HBM))
        else:
            in_specs.append(spec())
            operands.append(in_vmem(x))
    out_shape = []
    out_specs = []
    for i, s in enumerate(out_shapes):
        if i in out_hbm:
            out_shape.append(pltpu.HBM(s, F32))
            out_specs.append(pl.BlockSpec(memory_space=pltpu.HBM))
        else:
            out_shape.append(VMEM(s, F32))
            out_specs.append(spec())
    return pl.pallas_call(
        kernel,
        out_shape=out_shape,
        in_specs=in_specs,
        out_specs=out_specs,
        scratch_shapes=list(scratch),
        input_output_aliases=aliases,
        compiler_params=pltpu.CompilerParams(vmem_limit_bytes=LIMIT),
        cost_estimate=pl.CostEstimate(flops=flops, bytes_accessed=moved, transcendentals=0),
        name=name,
    )(*operands)


def layer(read, ny, nz):
    sub = lax.broadcasted_iota(jnp.int32, (8, nz), 0)
    tile = jnp.broadcast_to(read(0), (8, nz))
    for r in range(1, 8):
        tile = jnp.where(sub == r, jnp.broadcast_to(read(r), (8, nz)), tile)
    return tile


def cut_kernel(ny, fields, visc, y_first, y_last, sems):
    copies = []
    for j, (at, out) in enumerate(((0, y_first), (ny - 1, y_last))):
        for k in range(4):
            copies.append(pltpu.make_async_copy(fields.at[k, :, at], out.at[k], sems.at[j, k]))
        copies.append(pltpu.make_async_copy(visc.at[:, at], out.at[4], sems.at[j, 4]))
    for copy in copies:
        copy.start()
    for copy in copies:
        copy.wait()


def factor_kernel(rows, fields_ref, visc, inv, cpr, g0, gn, w, tau, sems):
    copies = [
        pltpu.make_async_copy(fields_ref.at[:, 0], w.at[F_FIRST : F_FIRST + 4], sems.at[0]),
        pltpu.make_async_copy(fields_ref.at[:, rows - 1], w.at[F_LAST : F_LAST + 4], sems.at[1]),
    ]
    for copy in copies:
        copy.start()
    ny, nz = visc.shape[1], visc.shape[2]
    me = lax.axis_index("line")
    wall_low = jnp.where(me == 0, 1.0, 0.0).astype(F32)
    wall_high = jnp.where(me == lax.axis_size("line") - 1, 1.0, 0.0).astype(F32)
    one = jnp.ones((ny, nz), F32)

    def row(i, carry):
        low, v = carry[4], carry[5]
        after = visc[jnp.minimum(i + 1, rows - 1)]
        high = jnp.where(i == rows - 1, (0.5 * STIFF) * wall_high * v, (0.5 * STIFF) * (v + after))
        new = []
        for s in range(2):
            gain, running = carry[2 * s], carry[2 * s + 1]
            down = SCALES[s] * low if s else low
            up = SCALES[s] * high if s else high
            q = 1.0 + down * gain
            one_over = 1.0 / (q + up)
            coupling = up * one_over
            inv[s, i] = one_over
            cpr[s, i] = coupling
            tau[s, i] = running
            new += [q * one_over, coupling * running]
        return tuple(new) + (high, after)

    first = visc[0]
    lax.fori_loop(0, rows, row, (one,) * 4 + (wall_low * (0.5 * STIFF) * first, first))

    end = rows - 1
    start = []
    for s in range(2):
        a = inv[s, end] * tau[s, end]
        b = inv[s, end]
        g0[s, end] = a
        gn[s, end] = b
        w[G0N[s]] = a
        w[GNN[s]] = b
        start += [a, b]

    def back(j, carry):
        i = end - 1 - j
        new = []
        for s in range(2):
            c = cpr[s, i]
            a = inv[s, i] * tau[s, i] + c * carry[2 * s]
            b = c * carry[2 * s + 1]
            g0[s, i] = a
            gn[s, i] = b
            new += [a, b]
        return tuple(new)

    final = lax.fori_loop(0, end, back, tuple(start))
    for s in range(2):
        w[G00[s]] = final[2 * s]
    w[V_FIRST] = first
    w[V_LAST] = visc[rows - 1]
    for copy in copies:
        copy.wait()


def explicit_rows(first, count, base, start, fields, visc, src):
    rows, ny, nz = visc.shape
    lane = lax.broadcasted_iota(jnp.int32, (ny, nz), 1)
    sub = lax.broadcasted_iota(jnp.int32, (ny, nz), 0)
    z_top, z_low = lane == nz - 1, lane == 0
    y_top, y_low = sub == ny - 1, sub == 0

    def sides(x):
        return (
            pltpu.roll(x, ny - 1, 0),
            pltpu.roll(x, 1, 0),
            pltpu.roll(x, nz - 1, 1),
            pltpu.roll(x, 1, 1),
        )

    def row(i, _):
        f = [fields[k, i - base] for k in range(4)]
        v = visc[i]
        after, before = jnp.minimum(i + 1, rows - 1), jnp.maximum(i - 1, 0)
        vyn, vyp, vzn, vzp = sides(v)
        half = 0.5 * CROSS_RATE
        faces = [
            jnp.where(y_top, 0.0, half * (v + vyn)),
            jnp.where(y_low, 0.0, half * (v + vyp)),
            half * (v + jnp.where(z_top, 0.0, vzn)),
            half * (v + jnp.where(z_low, 0.0, vzp)),
        ]
        none = [y_top, y_low, z_top, z_low]
        total = (faces[0] + faces[1]) + (faces[2] + faces[3])
        adv = [(-0.5 * ADVECTION) * f[k] for k in range(3)]
        move = [adv[1], -adv[1], adv[2], -adv[2]]
        adv_after = jnp.where(i == rows - 1, 0.0, adv[0])
        adv_before = jnp.where(i == 0, 0.0, adv[0])
        weights, centre = [], []
        for s in range(2):
            scaled = [SCALES[s] * x if s else x for x in faces]
            weights.append([jnp.where(n, 0.0, x + m) for n, x, m in zip(none, scaled, move)])
            centre.append(1.0 - (SCALES[s] * total if s else total))
        for k in range(4):
            s = KIND[k]
            near = sides(f[k])
            out = centre[s] * f[k] + adv_after * fields[k, after - base] - adv_before * fields[k, before - base]
            for c, x in zip(weights[s], near):
                out = out + c * x
            if k == 2:
                out = out + BUOYANCY * f[3]
            src[k, i - start] = out
        return 0

    lax.fori_loop(first, first + count, row, 0)


def early_kernel(count, fields_ref, visc, src, fields, sem):
    copy = pltpu.make_async_copy(fields_ref.at[:, 0 : count + 1], fields, sem)
    copy.start()
    copy.wait()
    explicit_rows(0, count, 0, 0, fields, visc, src)


def explicit_kernel(count, fields_ref, visc, g0, gn, early, src, p, ends, fields, sems):
    rows, ny, nz = visc.shape
    cuts = [count - 1] + list(range(2 * count + 1, rows, count)) + [rows]
    copies = []
    for c, (lo, hi) in enumerate(zip(cuts, cuts[1:])):
        copies.append(
            pltpu.make_async_copy(
                fields_ref.at[:, lo:hi], fields.at[:, lo - cuts[0] : hi - cuts[0]], sems.at[c]
            )
        )
        copies[-1].start()
    for c, copy in enumerate(copies):
        copy.wait()
        explicit_rows((c + 1) * count, count, cuts[0], count, fields, visc, src)

    def dot(ref, shift):
        def add(i, carry):
            new = []
            for g, base in ((g0, 0), (gn, 4)):
                for k in range(4):
                    new.append(carry[base + k] + g[KIND[k], i] * ref[k, i - shift])
            return tuple(new)

        return add

    final = (jnp.zeros((ny, nz), F32),) * 8
    final = lax.fori_loop(0, count, dot(early, 0), final)
    final = lax.fori_loop(count, rows, dot(src, count), final)
    for k in range(8):
        p[k] = final[k]

    for s in range(2):
        for side, at in ((0, 0), (1, ny - 1)):
            for which, g in ((0, g0), (1, gn)):
                for lo in range(0, rows, 8):
                    ends[4 * side + 2 * which + s, lo : lo + 8] = layer(
                        lambda r: g[s, lo + r, at : at + 1, :], ny, nz
                    )


def edge_kernel(rows, ny, y_last, y_first, low, high, ends, p, *refs):
    add, keep, send = refs[-3:]
    nz = add.shape[2]
    half = nz // 2
    low_core = side_bit(0)
    values = {}
    sub = lax.broadcasted_iota(jnp.int32, (ny, 128), 0)
    rate = 0.5 * ADVECTION
    for j in range(nz // 128):
        z = pl.ds(j * 128, 128)
        sums = []
        for side, mine, far, sign in ((0, y_first, low, rate), (4, y_last, high, -rate)):
            total = [None] * 8
            for r in range(rows // 8):
                x = pl.ds(r * 8, 8)
                face = (0.5 * CROSS_RATE) * (mine[4, x, z] + far[4, x, z])
                faces = (face, THERMAL_RATIO * face)
                adv = sign * mine[1, x, z]
                both = [adv + c for c in faces]
                g = [ends[side + q, x, z] for q in range(4)]
                for k in range(4):
                    s = KIND[k]
                    h = both[s] * far[k, x, z] - faces[s] * mine[k, x, z]
                    add[side + k, x, z] = h
                    for slot, c in ((k, g[s]), (4 + k, g[2 + s])):
                        part = c * h
                        total[slot] = part if total[slot] is None else total[slot] + part
            sums.append(total)
        for slot in range(8):
            add_low = jnp.sum(sums[0][slot], axis=0, keepdims=True)
            add_high = jnp.sum(sums[1][slot], axis=0, keepdims=True)
            both = jnp.where(sub == 0, add_low, jnp.where(sub == ny - 1, add_high, 0.0))
            values[slot, j] = p[slot, :, z] + both
    for slot in range(8):
        for c in range(half // 128):
            near = pl.ds(c * 128, 128)
            one, two = values[slot, c], values[slot, c + half // 128]
            keep[slot, :, near] = jnp.where(low_core, one, two)
            send[slot, :, near] = jnp.where(low_core, two, one)


def side_bit(level):
    return jnp.bitwise_and(jnp.right_shift(lax.axis_index("line"), level), 1) == 0


def join(left, right):
    face = left[V_LAST] + right[V_FIRST]
    joint, new, ratio = {}, {}, []
    for s in range(2):
        resist = 1.0 / ((0.5 * STIFF * SCALES[s]) * face)
        r = 1.0 / (resist + left[GNN[s]] + right[G00[s]])
        ratio.append(r)
        a, b = left[G0N[s]], right[G0N[s]]
        joint[R_ + s] = r
        joint[GA + s] = a
        joint[GB + s] = b
        new[G00[s]] = left[G00[s]] - r * a * a
        new[GNN[s]] = right[GNN[s]] - r * b * b
        new[G0N[s]] = r * a * b
    rate = 0.5 * ADVECTION
    for k in range(4):
        s = KIND[k]
        add_a = -rate * left[F_LAST] * right[F_FIRST + k]
        add_b = rate * right[F_FIRST] * left[F_LAST + k]
        e = ratio[s] * (left[GNN[s]] * add_a - right[G00[s]] * add_b)
        joint[CA + k] = add_a - e
        joint[CB + k] = add_b + e
        new[F_FIRST + k] = left[F_FIRST + k]
        new[F_LAST + k] = right[F_LAST + k]
    new[V_FIRST] = left[V_FIRST]
    new[V_LAST] = right[V_LAST]
    return joint, new


def sided(low_side, mine, theirs):
    left = {p: jnp.where(low_side, mine[p], theirs[p]) for p in mine}
    right = {p: jnp.where(low_side, theirs[p], mine[p]) for p in mine}
    return left, right


def pair_kernel(own, other, *refs):
    joint, out = refs[-2:]
    low_side = side_bit(0)
    planes = range(PLANES)
    found, new = join(*sided(low_side, {p: own[p] for p in planes}, {p: other[p] for p in planes}))
    width = out.shape[2]
    for plane in range(JOINT):
        joint[plane] = jnp.where(low_side, found[plane][:, :width], found[plane][:, width:])
    for plane in planes:
        out[plane] = jnp.where(low_side, new[plane][:, :width], new[plane][:, width:])


def chips_kernel(levels, own, *refs):
    others = refs[: 2 ** (levels - 1) - 1]
    joints = refs[-(2 * levels - 3) : len(refs) - (levels - 2)]
    consts = refs[len(refs) - (levels - 2) :]
    blocks = [{p: x[p] for p in range(PLANES)} for x in (own, *others)]
    zero = jnp.zeros_like(own[0])
    ends = [{p: zero for p in range(8)} for _ in blocks]
    for level in range(1, levels):
        low_side = side_bit(level)
        joined, new_ends = [], []
        for j in range(0, len(blocks), 2):
            found, new = join(*sided(low_side, blocks[j], blocks[j + 1]))
            for plane in range(JOINT):
                joints[level - 1][j // 2, plane] = found[plane]
            joined.append(new)
            if level < levels - 1:
                left, right = sided(low_side, ends[j], ends[j + 1])
                both = {}
                for k in range(4):
                    _, both[k], both[4 + k] = up(found, k, left, right)
                new_ends.append(both)
        blocks, ends = joined, new_ends
        if level < levels - 1:
            for slot, x in enumerate(facing(level + 1, levels, ends[1], False)):
                consts[level - 1][slot] = x


def facing(level, levels, ends, mine):
    if level < levels - 1:
        return [ends[p] for p in range(8)]
    low_side = side_bit(level)
    if not mine:
        low_side = jnp.logical_not(low_side)
    return [jnp.where(low_side, ends[4 + k], ends[k]) for k in range(4)]


def source_kernel(rows, count, early, src, cpr, add, t):
    ny, nz = src.shape[2], src.shape[3]
    sub = lax.broadcasted_iota(jnp.int32, (ny, nz), 0)
    top, low = sub == ny - 1, sub == 0

    def down(ref, shift):
        def row(i, carry):
            prev = jnp.maximum(i - 1, 0)
            new = []
            for k in range(4):
                a = jnp.broadcast_to(add[k, pl.ds(i, 1), :], (ny, nz))
                b = jnp.broadcast_to(add[4 + k, pl.ds(i, 1), :], (ny, nz))
                x = ref[k, i - shift] + jnp.where(low, a, jnp.where(top, b, 0.0))
                x = x + cpr[KIND[k], prev] * carry[k]
                t[k, i] = x
                new.append(x)
            return tuple(new)

        return row

    state = (jnp.zeros((ny, nz), F32),) * 4
    state = lax.fori_loop(0, count, down(early, 0), state)
    lax.fori_loop(count, rows, down(src, count), state)


def back_kernel(rows, t, inv, cpr, part):
    end = rows - 1
    start = []
    for k in range(4):
        x = inv[KIND[k], end] * t[k, end]
        part[k, end] = x
        start.append(x)

    def row(j, carry):
        i = end - 1 - j
        new = []
        for k in range(4):
            s = KIND[k]
            x = inv[s, i] * t[k, i] + cpr[s, i] * carry[k]
            part[k, i] = x
            new.append(x)
        return tuple(new)

    lax.fori_loop(0, end, row, tuple(start))


def up(joint, k, left, right):
    s = KIND[k]
    d = left[4 + k] - right[k]
    flow = joint[R_ + s] * d
    first = left[k] + joint[GA + s] * (joint[CA + k] - flow)
    last = right[4 + k] + joint[GB + s] * (joint[CB + k] + flow)
    return d, first, last


def up_kernel(levels, own, other, joint, *refs):
    joints = refs[: levels - 1]
    out, diff = refs[levels : levels + 2]
    shares = refs[levels + 2 :]
    low_side = side_bit(0)
    left, right = sided(low_side, {p: own[p] for p in range(8)}, {p: other[p] for p in range(8)})
    ends = {}
    for k in range(4):
        diff[k], ends[k], ends[4 + k] = up(joint, k, left, right)
        out[k] = ends[k]
        out[4 + k] = ends[4 + k]
    for level in range(1, levels - 1):
        low_side = side_bit(level)
        joint = joints[level - 1].at[0]
        for k in range(4):
            s = KIND[k]
            first, last = ends[k], ends[4 + k]
            flow = joint[R_ + s] * jnp.where(low_side, last, -first)
            ends[k] = jnp.where(low_side, first, 0.0) - joint[GA + s] * flow
            ends[4 + k] = jnp.where(low_side, 0.0, last) + joint[GB + s] * flow
        for slot, x in enumerate(facing(level + 1, levels, ends, True)):
            shares[level - 1][slot] = x


def joint_flow(joint, k, d, into_first, into_last, low_side):
    s = KIND[k]
    flow = joint[R_ + s] * (d + joint[GA + s] * into_first - joint[GB + s] * into_last)
    first = jnp.where(low_side, into_first, joint[CB + k] + flow)
    last = jnp.where(low_side, joint[CA + k] - flow, into_last)
    return first, last


def beside_kernel(levels, *refs):
    parts, refs = list(refs[: 2 ** (levels - 1) - levels]), refs[2 ** (levels - 1) - levels :]
    consts, outs = refs[: levels - 2], refs[levels - 2 :]
    for level in range(2, levels):
        here = [parts.pop(0) for _ in range(2 ** (level - 1) - 1)]
        for p in range(outs[level - 2].shape[0]):
            total = consts[level - 2][p]
            for part in here:
                total = total + part[p]
            outs[level - 2][p] = total


def settle_kernel(levels, own, *refs):
    near, refs = refs[: levels - 1], refs[levels - 1 :]
    far, joints = refs[: levels - 2], refs[levels - 2 : 2 * levels - 3]
    pair, diff, out, send = refs[2 * levels - 3 :]
    ends = {p: own[p] for p in range(8)}
    diffs = []
    for level in range(1, levels):
        low_side = side_bit(level)
        beside = {p: near[level - 1][p] for p in range(near[level - 1].shape[0])}
        if level > 1:
            beside = {p: x + far[level - 2][p] for p, x in beside.items()}
        across = []
        if len(beside) == 4:
            for k in range(4):
                x = beside[k]
                across.append(jnp.where(low_side, ends[4 + k] - x, x - ends[k]))
        else:
            left, right = sided(low_side, ends, beside)
            for k in range(4):
                d, ends[k], ends[4 + k] = up(joints[level - 1].at[0], k, left, right)
                across.append(d)
        diffs.append(across)
    for k in range(4):
        first = last = jnp.zeros_like(diffs[0][0])
        for level in range(levels - 1, 0, -1):
            first, last = joint_flow(
                joints[level - 1].at[0], k, diffs[level - 1][k], first, last, side_bit(level)
            )
        low_side = side_bit(0)
        s = KIND[k]
        flow = pair[R_ + s] * (diff[k] + pair[GA + s] * first - pair[GB + s] * last)
        low_last, high_first = pair[CA + k] - flow, pair[CB + k] + flow
        out[k] = jnp.where(low_side, first, high_first)
        out[4 + k] = jnp.where(low_side, low_last, last)
        send[k] = jnp.where(low_side, high_first, first)
        send[4 + k] = jnp.where(low_side, last, low_last)


def final_kernel(mine, parts, flux, part, g0, gn, *refs):
    out, buf, sems = refs[-3:]
    rows, half = buf.shape[1], buf.shape[3]
    core = jnp.bitwise_and(lax.axis_index("line"), 1)
    offset = (core if mine else 1 - core) * half
    step = rows // parts
    copies = []
    for c in range(half // 128):
        near = pl.ds(c * 128, 128)
        z = pl.ds(pl.multiple_of(offset + c * 128, 128), 128)
        into = [flux[k, :, near] for k in range(8)]
        for r in range(parts):
            for i in range(r * step, (r + 1) * step):
                a = [g0[s, i, :, z] for s in range(2)]
                b = [gn[s, i, :, z] for s in range(2)]
                for k in range(4):
                    s = KIND[k]
                    buf[k, i, :, near] = part[k, i, :, z] + (a[s] * into[k] + b[s] * into[4 + k])
            x = pl.ds(r * step, step)
            copies.append(
                pltpu.make_async_copy(
                    buf.at[:, x, :, near], out.at[:, x, :, z], sems.at[c * parts + r]
                )
            )
            copies[-1].start()
    for copy in copies:
        copy.wait()


def local(fields, viscosity):
    rows, ny, nz = viscosity.shape
    lines = lax.axis_size("line")
    cols = lax.axis_size("col")
    levels = lines.bit_length() - 1
    half = nz // 2
    cells = rows * ny * nz
    block = (rows, ny, nz)

    ring = [(i, (i + 1) % cols) for i in range(cols)]
    back_ring = [(b, a) for a, b in ring]

    def gather(at_level):
        found = {}
        for d in sorted(range(1, lines // 2), key=lambda d: (-d.bit_count(), d)):
            x = at_level[d.bit_length()]
            found[d] = lax.ppermute(x, "line", [(i, i ^ (d << 1)) for i in range(lines)])
        return [found[d] for d in sorted(found)]

    def swap(x, level):
        return lax.ppermute(x, "line", [(i, i ^ (1 << level)) for i in range(lines)])

    y_first, y_last = call(
        functools.partial(cut_kernel, ny),
        "cut",
        [(5, rows, nz), (5, rows, nz)],
        [fields, viscosity],
        scratch=[pltpu.SemaphoreType.DMA((2, 5))],
        in_hbm=(0, 1),
        moved=2 * cells,
    )
    low = lax.ppermute(y_last, "col", ring)
    high = lax.ppermute(y_first, "col", back_ring)

    inv, cpr, g0, gn, w = call(
        functools.partial(factor_kernel, rows),
        "factor",
        [(2,) + block] * 4 + [(PLANES, ny, nz)],
        [fields, viscosity],
        scratch=[VMEM((2,) + block, F32), pltpu.SemaphoreType.DMA((2,))],
        in_hbm=(0,),
        flops=10**9,
    )
    count = rows // 4
    (early,) = call(
        functools.partial(early_kernel, count),
        "early",
        [(4, count, ny, nz)],
        [fields, viscosity],
        scratch=[VMEM((4, count + 1, ny, nz), F32), pltpu.SemaphoreType.DMA],
        in_hbm=(0,),
        flops=4 * 10**9,
    )
    src, p, ends = call(
        functools.partial(explicit_kernel, count),
        "explicit",
        [(4, rows - count, ny, nz), (8, ny, nz), (8, rows, nz)],
        [fields, viscosity, g0, gn, early],
        scratch=[VMEM((4, rows - count + 1, ny, nz), F32), pltpu.SemaphoreType.DMA((3,))],
        in_hbm=(0,),
        flops=5 * 10**9,
    )
    pair, w = call(
        pair_kernel,
        "pair",
        [(JOINT, ny, half), (PLANES, ny, half)],
        [w, swap(w, 0), early],
        moved=4 * ny * nz * 60,
    )
    pairs = lines // 2
    widths = [8] * (levels - 3) + [4]
    found = call(
        functools.partial(chips_kernel, levels),
        "chips",
        [(pairs >> level, JOINT, ny, half) for level in range(1, levels)]
        + [(width, ny, half) for width in widths],
        [w] + gather([w] * (levels + 1)) + [p],
        moved=4 * ny * half * 300,
    )
    joints, consts = list(found[: levels - 1]), list(found[levels - 1 :])

    add, p, sent = call(
        functools.partial(edge_kernel, rows, ny),
        "edge",
        [(8, rows, nz), (8, ny, half), (8, ny, half)],
        [y_last, y_first, low, high, ends, p, joints[0]],
        flops=5 * 10**8,
    )
    (t,) = call(
        functools.partial(source_kernel, rows, count),
        "source",
        [(4,) + block],
        [early, src, cpr, add],
        flops=30 * cells,
        moved=24 * cells,
    )
    (part,) = call(
        functools.partial(back_kernel, rows),
        "back",
        [(4,) + block],
        [t, inv, cpr],
        flops=20 * cells,
        moved=24 * cells,
    )
    p, diff, *shares = call(
        functools.partial(up_kernel, levels),
        "up",
        [(8, ny, half), (4, ny, half)] + [(width, ny, half) for width in widths],
        [p, swap(sent, 0), pair] + joints + [part],
        moved=4 * ny * nz * 40,
    )
    others = dict(enumerate(gather([None, p] + shares), 1))
    near = [others.pop(1 << level) for level in range(levels - 1)]
    beside = call(
        functools.partial(beside_kernel, levels),
        "beside",
        [(width, ny, half) for width in widths],
        list(others.values()) + consts,
        flops=6 * 10**8,
    )
    flux, sent = call(
        functools.partial(settle_kernel, levels),
        "settle",
        [(8, ny, half)] * 2,
        [p] + near + list(beside) + joints + [pair, diff],
        moved=4 * ny * half * 100,
    )
    rest = [part, g0, gn]
    parts = 4 if rows % 4 == 0 else 1
    scratch = [VMEM((4, rows, ny, half), F32), pltpu.SemaphoreType.DMA((half // 128 * parts,))]
    (out,) = call(
        functools.partial(final_kernel, True, parts),
        "final_own",
        [(4,) + block],
        [flux] + rest,
        scratch=scratch,
        out_hbm=(0,),
        flops=10**9,
    )
    (out,) = call(
        functools.partial(final_kernel, False, parts),
        "final_other",
        [(4,) + block],
        [swap(sent, 0)] + rest + [out],
        scratch=scratch,
        in_hbm=(4,),
        out_hbm=(0,),
        aliases={4: 0},
        flops=10**9,
    )
    return out


def solution(mesh):
    return jax.shard_map(
        local,
        mesh=mesh,
        in_specs=(P(None, "line", "col", None), P("line", "col", None)),
        out_specs=P(None, "line", "col", None),
        check_vma=False,
    )
```

```python
import functools

import jax
import jax.numpy as jnp
from jax import lax
from jax.experimental import pallas as pl
from jax.experimental.pallas import tpu as pltpu
from jax.sharding import PartitionSpec as P

STIFF = 3072
THERMAL_RATIO = 0.8
CROSS_RATE = 0.2
ADVECTION = 0.25
BUOYANCY = 2.0
SCALES = (1.0, THERMAL_RATIO)
KIND = (0, 0, 0, 1)

F32 = jnp.float32
VMEM = pltpu.VMEM
LIMIT = 24 * 1024 * 1024

G00, G0N, GNN = (0, 3), (1, 4), (2, 5)
V_FIRST, V_LAST, F_FIRST, F_LAST = 6, 7, 8, 12
PLANES = 16
R_, GA, GB, CA, CB = 0, 2, 4, 6, 10
JOINT = 14


def in_vmem(x):
    return pltpu.with_memory_space_constraint(x, VMEM)


def spec():
    return pl.BlockSpec(memory_space=VMEM)


def call(kernel, name, out_shapes, args, scratch=(), in_hbm=(), out_hbm=(), aliases={}, flops=0, moved=0):
    in_specs = []
    operands = []
    for i, x in enumerate(args):
        if i in in_hbm:
            in_specs.append(pl.BlockSpec(memory_space=pltpu.HBM))
            operands.append(pltpu.with_memory_space_constraint(x, pltpu.HBM))
        else:
            in_specs.append(spec())
            operands.append(in_vmem(x))
    out_shape = []
    out_specs = []
    for i, s in enumerate(out_shapes):
        if i in out_hbm:
            out_shape.append(pltpu.HBM(s, F32))
            out_specs.append(pl.BlockSpec(memory_space=pltpu.HBM))
        else:
            out_shape.append(VMEM(s, F32))
            out_specs.append(spec())
    return pl.pallas_call(
        kernel,
        out_shape=out_shape,
        in_specs=in_specs,
        out_specs=out_specs,
        scratch_shapes=list(scratch),
        input_output_aliases=aliases,
        compiler_params=pltpu.CompilerParams(vmem_limit_bytes=LIMIT),
        cost_estimate=pl.CostEstimate(flops=flops, bytes_accessed=moved, transcendentals=0),
        name=name,
    )(*operands)


def layer(read, ny, nz):
    sub = lax.broadcasted_iota(jnp.int32, (8, nz), 0)
    tile = jnp.broadcast_to(read(0), (8, nz))
    for r in range(1, 8):
        tile = jnp.where(sub == r, jnp.broadcast_to(read(r), (8, nz)), tile)
    return tile


def cut_kernel(ny, fields, visc, y_first, y_last, sems):
    copies = []
    for j, (at, out) in enumerate(((0, y_first), (ny - 1, y_last))):
        for k in range(4):
            copies.append(pltpu.make_async_copy(fields.at[k, :, at], out.at[k], sems.at[j, k]))
        copies.append(pltpu.make_async_copy(visc.at[:, at], out.at[4], sems.at[j, 4]))
    for copy in copies:
        copy.start()
    for copy in copies:
        copy.wait()


def factor_kernel(rows, fields_ref, visc, inv, cpr, g0, gn, w, tau, sems):
    copies = [
        pltpu.make_async_copy(fields_ref.at[:, 0], w.at[F_FIRST : F_FIRST + 4], sems.at[0]),
        pltpu.make_async_copy(fields_ref.at[:, rows - 1], w.at[F_LAST : F_LAST + 4], sems.at[1]),
    ]
    for copy in copies:
        copy.start()
    ny, nz = visc.shape[1], visc.shape[2]
    me = lax.axis_index("line")
    wall_low = jnp.where(me == 0, 1.0, 0.0).astype(F32)
    wall_high = jnp.where(me == lax.axis_size("line") - 1, 1.0, 0.0).astype(F32)
    one = jnp.ones((ny, nz), F32)

    def row(i, carry):
        low, v = carry[4], carry[5]
        after = visc[jnp.minimum(i + 1, rows - 1)]
        high = jnp.where(i == rows - 1, (0.5 * STIFF) * wall_high * v, (0.5 * STIFF) * (v + after))
        new = []
        for s in range(2):
            gain, running = carry[2 * s], carry[2 * s + 1]
            down = SCALES[s] * low if s else low
            up = SCALES[s] * high if s else high
            q = 1.0 + down * gain
            one_over = 1.0 / (q + up)
            coupling = up * one_over
            inv[s, i] = one_over
            cpr[s, i] = coupling
            tau[s, i] = running
            new += [q * one_over, coupling * running]
        return tuple(new) + (high, after)

    first = visc[0]
    lax.fori_loop(0, rows, row, (one,) * 4 + (wall_low * (0.5 * STIFF) * first, first))

    end = rows - 1
    start = []
    for s in range(2):
        a = inv[s, end] * tau[s, end]
        b = inv[s, end]
        g0[s, end] = a
        gn[s, end] = b
        w[G0N[s]] = a
        w[GNN[s]] = b
        start += [a, b]

    def back(j, carry):
        i = end - 1 - j
        new = []
        for s in range(2):
            c = cpr[s, i]
            a = inv[s, i] * tau[s, i] + c * carry[2 * s]
            b = c * carry[2 * s + 1]
            g0[s, i] = a
            gn[s, i] = b
            new += [a, b]
        return tuple(new)

    final = lax.fori_loop(0, end, back, tuple(start))
    for s in range(2):
        w[G00[s]] = final[2 * s]
    w[V_FIRST] = first
    w[V_LAST] = visc[rows - 1]
    for copy in copies:
        copy.wait()


def explicit_rows(first, count, base, start, fields, visc, src):
    rows, ny, nz = visc.shape
    lane = lax.broadcasted_iota(jnp.int32, (ny, nz), 1)
    sub = lax.broadcasted_iota(jnp.int32, (ny, nz), 0)
    z_top, z_low = lane == nz - 1, lane == 0
    y_top, y_low = sub == ny - 1, sub == 0

    def sides(x):
        return (
            pltpu.roll(x, ny - 1, 0),
            pltpu.roll(x, 1, 0),
            pltpu.roll(x, nz - 1, 1),
            pltpu.roll(x, 1, 1),
        )

    def row(i, _):
        f = [fields[k, i - base] for k in range(4)]
        v = visc[i]
        after, before = jnp.minimum(i + 1, rows - 1), jnp.maximum(i - 1, 0)
        vyn, vyp, vzn, vzp = sides(v)
        half = 0.5 * CROSS_RATE
        faces = [
            jnp.where(y_top, 0.0, half * (v + vyn)),
            jnp.where(y_low, 0.0, half * (v + vyp)),
            half * (v + jnp.where(z_top, 0.0, vzn)),
            half * (v + jnp.where(z_low, 0.0, vzp)),
        ]
        none = [y_top, y_low, z_top, z_low]
        total = (faces[0] + faces[1]) + (faces[2] + faces[3])
        adv = [(-0.5 * ADVECTION) * f[k] for k in range(3)]
        move = [adv[1], -adv[1], adv[2], -adv[2]]
        adv_after = jnp.where(i == rows - 1, 0.0, adv[0])
        adv_before = jnp.where(i == 0, 0.0, adv[0])
        weights, centre = [], []
        for s in range(2):
            scaled = [SCALES[s] * x if s else x for x in faces]
            weights.append([jnp.where(n, 0.0, x + m) for n, x, m in zip(none, scaled, move)])
            centre.append(1.0 - (SCALES[s] * total if s else total))
        for k in range(4):
            s = KIND[k]
            near = sides(f[k])
            out = centre[s] * f[k] + adv_after * fields[k, after - base] - adv_before * fields[k, before - base]
            for c, x in zip(weights[s], near):
                out = out + c * x
            if k == 2:
                out = out + BUOYANCY * f[3]
            src[k, i - start] = out
        return 0

    lax.fori_loop(first, first + count, row, 0)


def early_kernel(count, fields_ref, visc, src, fields, sem):
    copy = pltpu.make_async_copy(fields_ref.at[:, 0 : count + 1], fields, sem)
    copy.start()
    copy.wait()
    explicit_rows(0, count, 0, 0, fields, visc, src)


def explicit_kernel(count, fields_ref, visc, g0, gn, early, src, p, ends, fields, sems):
    rows, ny, nz = visc.shape
    cuts = [count - 1] + list(range(2 * count + 1, rows, count)) + [rows]
    copies = []
    for c, (lo, hi) in enumerate(zip(cuts, cuts[1:])):
        copies.append(
            pltpu.make_async_copy(
                fields_ref.at[:, lo:hi], fields.at[:, lo - cuts[0] : hi - cuts[0]], sems.at[c]
            )
        )
        copies[-1].start()
    for c, copy in enumerate(copies):
        copy.wait()
        explicit_rows((c + 1) * count, count, cuts[0], count, fields, visc, src)

    def dot(ref, shift):
        def add(i, carry):
            new = []
            for g, base in ((g0, 0), (gn, 4)):
                for k in range(4):
                    new.append(carry[base + k] + g[KIND[k], i] * ref[k, i - shift])
            return tuple(new)

        return add

    final = (jnp.zeros((ny, nz), F32),) * 8
    final = lax.fori_loop(0, count, dot(early, 0), final)
    final = lax.fori_loop(count, rows, dot(src, count), final)
    for k in range(8):
        p[k] = final[k]

    for s in range(2):
        for side, at in ((0, 0), (1, ny - 1)):
            for which, g in ((0, g0), (1, gn)):
                for lo in range(0, rows, 8):
                    ends[4 * side + 2 * which + s, lo : lo + 8] = layer(
                        lambda r: g[s, lo + r, at : at + 1, :], ny, nz
                    )


def edge_sums(rows, side, mine, far, sign, ends, add, z):
    total = [None] * 8
    for r in range(rows // 8):
        x = pl.ds(r * 8, 8)
        face = (0.5 * CROSS_RATE) * (mine[4, x, z] + far[4, x, z])
        faces = (face, THERMAL_RATIO * face)
        adv = sign * mine[1, x, z]
        both = [adv + c for c in faces]
        g = [ends[side + q, x, z] for q in range(4)]
        for k in range(4):
            s = KIND[k]
            h = both[s] * far[k, x, z] - faces[s] * mine[k, x, z]
            add[k, x, z] = h
            for slot, c in ((k, g[s]), (4 + k, g[2 + s])):
                part = c * h
                total[slot] = part if total[slot] is None else total[slot] + part
    return [jnp.sum(x, axis=0, keepdims=True) for x in total]


def low_kernel(rows, ny, mine, far, ends, p, *refs):
    add, out = refs[-2:]
    sub = lax.broadcasted_iota(jnp.int32, (ny, 128), 0)
    for j in range(add.shape[2] // 128):
        z = pl.ds(j * 128, 128)
        sums = edge_sums(rows, 0, mine, far, 0.5 * ADVECTION, ends, add, z)
        for slot in range(8):
            out[slot, :, z] = p[slot, :, z] + jnp.where(sub == 0, sums[slot], 0.0)


def high_kernel(rows, ny, mine, far, ends, p, *refs):
    add, keep, send = refs[-3:]
    half = add.shape[2] // 2
    low_core = side_bit(0)
    values = {}
    sub = lax.broadcasted_iota(jnp.int32, (ny, 128), 0)
    for j in range(2 * half // 128):
        z = pl.ds(j * 128, 128)
        sums = edge_sums(rows, 4, mine, far, -0.5 * ADVECTION, ends, add, z)
        for slot in range(8):
            values[slot, j] = p[slot, :, z] + jnp.where(sub == ny - 1, sums[slot], 0.0)
    for slot in range(8):
        for c in range(half // 128):
            near = pl.ds(c * 128, 128)
            one, two = values[slot, c], values[slot, c + half // 128]
            keep[slot, :, near] = jnp.where(low_core, one, two)
            send[slot, :, near] = jnp.where(low_core, two, one)


def side_bit(level):
    return jnp.bitwise_and(jnp.right_shift(lax.axis_index("line"), level), 1) == 0


def join(left, right):
    face = left[V_LAST] + right[V_FIRST]
    joint, new, ratio = {}, {}, []
    for s in range(2):
        resist = 1.0 / ((0.5 * STIFF * SCALES[s]) * face)
        r = 1.0 / (resist + left[GNN[s]] + right[G00[s]])
        ratio.append(r)
        a, b = left[G0N[s]], right[G0N[s]]
        joint[R_ + s] = r
        joint[GA + s] = a
        joint[GB + s] = b
        new[G00[s]] = left[G00[s]] - r * a * a
        new[GNN[s]] = right[GNN[s]] - r * b * b
        new[G0N[s]] = r * a * b
    rate = 0.5 * ADVECTION
    for k in range(4):
        s = KIND[k]
        add_a = -rate * left[F_LAST] * right[F_FIRST + k]
        add_b = rate * right[F_FIRST] * left[F_LAST + k]
        e = ratio[s] * (left[GNN[s]] * add_a - right[G00[s]] * add_b)
        joint[CA + k] = add_a - e
        joint[CB + k] = add_b + e
        new[F_FIRST + k] = left[F_FIRST + k]
        new[F_LAST + k] = right[F_LAST + k]
    new[V_FIRST] = left[V_FIRST]
    new[V_LAST] = right[V_LAST]
    return joint, new


def sided(low_side, mine, theirs):
    left = {p: jnp.where(low_side, mine[p], theirs[p]) for p in mine}
    right = {p: jnp.where(low_side, theirs[p], mine[p]) for p in mine}
    return left, right


def pair_kernel(own, other, *refs):
    joint, out = refs[-2:]
    low_side = side_bit(0)
    planes = range(PLANES)
    found, new = join(*sided(low_side, {p: own[p] for p in planes}, {p: other[p] for p in planes}))
    width = out.shape[2]
    for plane in range(JOINT):
        joint[plane] = jnp.where(low_side, found[plane][:, :width], found[plane][:, width:])
    for plane in planes:
        out[plane] = jnp.where(low_side, new[plane][:, :width], new[plane][:, width:])


def chips_kernel(levels, own, *refs):
    others = refs[: 2 ** (levels - 1) - 1]
    joints = refs[-(2 * levels - 3) : len(refs) - (levels - 2)]
    consts = refs[len(refs) - (levels - 2) :]
    blocks = [{p: x[p] for p in range(PLANES)} for x in (own, *others)]
    zero = jnp.zeros_like(own[0])
    ends = [{p: zero for p in range(8)} for _ in blocks]
    for level in range(1, levels):
        low_side = side_bit(level)
        joined, new_ends = [], []
        for j in range(0, len(blocks), 2):
            found, new = join(*sided(low_side, blocks[j], blocks[j + 1]))
            for plane in range(JOINT):
                joints[level - 1][j // 2, plane] = found[plane]
            joined.append(new)
            if level < levels - 1:
                left, right = sided(low_side, ends[j], ends[j + 1])
                both = {}
                for k in range(4):
                    _, both[k], both[4 + k] = up(found, k, left, right)
                new_ends.append(both)
        blocks, ends = joined, new_ends
        if level < levels - 1:
            for slot, x in enumerate(facing(level + 1, levels, ends[1], False)):
                consts[level - 1][slot] = x


def facing(level, levels, ends, mine):
    if level < levels - 1:
        return [ends[p] for p in range(8)]
    low_side = side_bit(level)
    if not mine:
        low_side = jnp.logical_not(low_side)
    return [jnp.where(low_side, ends[4 + k], ends[k]) for k in range(4)]


def source_kernel(rows, count, early, src, cpr, add_low, add_high, t):
    ny, nz = src.shape[2], src.shape[3]
    sub = lax.broadcasted_iota(jnp.int32, (ny, nz), 0)
    top, low = sub == ny - 1, sub == 0

    def down(ref, shift):
        def row(i, carry):
            prev = jnp.maximum(i - 1, 0)
            new = []
            for k in range(4):
                a = jnp.broadcast_to(add_low[k, pl.ds(i, 1), :], (ny, nz))
                b = jnp.broadcast_to(add_high[k, pl.ds(i, 1), :], (ny, nz))
                x = ref[k, i - shift] + jnp.where(low, a, jnp.where(top, b, 0.0))
                x = x + cpr[KIND[k], prev] * carry[k]
                t[k, i] = x
                new.append(x)
            return tuple(new)

        return row

    state = (jnp.zeros((ny, nz), F32),) * 4
    state = lax.fori_loop(0, count, down(early, 0), state)
    lax.fori_loop(count, rows, down(src, count), state)


def back_kernel(rows, t, inv, cpr, part):
    end = rows - 1
    start = []
    for k in range(4):
        x = inv[KIND[k], end] * t[k, end]
        part[k, end] = x
        start.append(x)

    def row(j, carry):
        i = end - 1 - j
        new = []
        for k in range(4):
            s = KIND[k]
            x = inv[s, i] * t[k, i] + cpr[s, i] * carry[k]
            part[k, i] = x
            new.append(x)
        return tuple(new)

    lax.fori_loop(0, end, row, tuple(start))


def up(joint, k, left, right):
    s = KIND[k]
    d = left[4 + k] - right[k]
    flow = joint[R_ + s] * d
    first = left[k] + joint[GA + s] * (joint[CA + k] - flow)
    last = right[4 + k] + joint[GB + s] * (joint[CB + k] + flow)
    return d, first, last


def up_kernel(levels, own, other, joint, *refs):
    joints = refs[: levels - 1]
    out, diff = refs[levels : levels + 2]
    shares = refs[levels + 2 :]
    low_side = side_bit(0)
    left, right = sided(low_side, {p: own[p] for p in range(8)}, {p: other[p] for p in range(8)})
    ends = {}
    for k in range(4):
        diff[k], ends[k], ends[4 + k] = up(joint, k, left, right)
        out[k] = ends[k]
        out[4 + k] = ends[4 + k]
    for level in range(1, levels - 1):
        low_side = side_bit(level)
        joint = joints[level - 1].at[0]
        for k in range(4):
            s = KIND[k]
            first, last = ends[k], ends[4 + k]
            flow = joint[R_ + s] * jnp.where(low_side, last, -first)
            ends[k] = jnp.where(low_side, first, 0.0) - joint[GA + s] * flow
            ends[4 + k] = jnp.where(low_side, 0.0, last) + joint[GB + s] * flow
        for slot, x in enumerate(facing(level + 1, levels, ends, True)):
            shares[level - 1][slot] = x


def joint_flow(joint, k, d, into_first, into_last, low_side):
    s = KIND[k]
    flow = joint[R_ + s] * (d + joint[GA + s] * into_first - joint[GB + s] * into_last)
    first = jnp.where(low_side, into_first, joint[CB + k] + flow)
    last = jnp.where(low_side, joint[CA + k] - flow, into_last)
    return first, last


def beside_kernel(levels, *refs):
    parts, refs = list(refs[: 2 ** (levels - 1) - levels]), refs[2 ** (levels - 1) - levels :]
    consts, outs = refs[: levels - 2], refs[levels - 2 :]
    for level in range(2, levels):
        here = [parts.pop(0) for _ in range(2 ** (level - 1) - 1)]
        for p in range(outs[level - 2].shape[0]):
            total = consts[level - 2][p]
            for part in here:
                total = total + part[p]
            outs[level - 2][p] = total


def settle_kernel(levels, own, *refs):
    near, refs = refs[: levels - 1], refs[levels - 1 :]
    far, joints = refs[: levels - 2], refs[levels - 2 : 2 * levels - 3]
    pair, diff, out, send = refs[2 * levels - 3 :]
    ends = {p: own[p] for p in range(8)}
    diffs = []
    for level in range(1, levels):
        low_side = side_bit(level)
        beside = {p: near[level - 1][p] for p in range(near[level - 1].shape[0])}
        if level > 1:
            beside = {p: x + far[level - 2][p] for p, x in beside.items()}
        across = []
        if len(beside) == 4:
            for k in range(4):
                x = beside[k]
                across.append(jnp.where(low_side, ends[4 + k] - x, x - ends[k]))
        else:
            left, right = sided(low_side, ends, beside)
            for k in range(4):
                d, ends[k], ends[4 + k] = up(joints[level - 1].at[0], k, left, right)
                across.append(d)
        diffs.append(across)
    for k in range(4):
        first = last = jnp.zeros_like(diffs[0][0])
        for level in range(levels - 1, 0, -1):
            first, last = joint_flow(
                joints[level - 1].at[0], k, diffs[level - 1][k], first, last, side_bit(level)
            )
        low_side = side_bit(0)
        s = KIND[k]
        flow = pair[R_ + s] * (diff[k] + pair[GA + s] * first - pair[GB + s] * last)
        low_last, high_first = pair[CA + k] - flow, pair[CB + k] + flow
        out[k] = jnp.where(low_side, first, high_first)
        out[4 + k] = jnp.where(low_side, low_last, last)
        send[k] = jnp.where(low_side, high_first, first)
        send[4 + k] = jnp.where(low_side, last, low_last)


def final_kernel(mine, parts, flux, part, g0, gn, *refs):
    out, buf, sems = refs[-3:]
    rows, half = buf.shape[1], buf.shape[3]
    core = jnp.bitwise_and(lax.axis_index("line"), 1)
    offset = (core if mine else 1 - core) * half
    step = rows // parts
    copies = []
    for c in range(half // 128):
        near = pl.ds(c * 128, 128)
        z = pl.ds(pl.multiple_of(offset + c * 128, 128), 128)
        into = [flux[k, :, near] for k in range(8)]
        for r in range(parts):
            for i in range(r * step, (r + 1) * step):
                a = [g0[s, i, :, z] for s in range(2)]
                b = [gn[s, i, :, z] for s in range(2)]
                for k in range(4):
                    s = KIND[k]
                    buf[k, i, :, near] = part[k, i, :, z] + (a[s] * into[k] + b[s] * into[4 + k])
            x = pl.ds(r * step, step)
            copies.append(
                pltpu.make_async_copy(
                    buf.at[:, x, :, near], out.at[:, x, :, z], sems.at[c * parts + r]
                )
            )
            copies[-1].start()
    for copy in copies:
        copy.wait()


def local(fields, viscosity):
    rows, ny, nz = viscosity.shape
    lines = lax.axis_size("line")
    cols = lax.axis_size("col")
    levels = lines.bit_length() - 1
    half = nz // 2
    cells = rows * ny * nz
    block = (rows, ny, nz)

    ring = [(i, (i + 1) % cols) for i in range(cols)]
    back_ring = [(b, a) for a, b in ring]

    def gather(at_level):
        found = {}
        for d in sorted(range(1, lines // 2), key=lambda d: (-d.bit_count(), d)):
            x = at_level[d.bit_length()]
            found[d] = lax.ppermute(x, "line", [(i, i ^ (d << 1)) for i in range(lines)])
        return [found[d] for d in sorted(found)]

    def swap(x, level):
        return lax.ppermute(x, "line", [(i, i ^ (1 << level)) for i in range(lines)])

    y_first, y_last = call(
        functools.partial(cut_kernel, ny),
        "cut",
        [(5, rows, nz), (5, rows, nz)],
        [fields, viscosity],
        scratch=[pltpu.SemaphoreType.DMA((2, 5))],
        in_hbm=(0, 1),
        moved=2 * cells,
    )
    low = lax.ppermute(y_last, "col", ring)
    high = lax.ppermute(y_first, "col", back_ring)

    inv, cpr, g0, gn, w = call(
        functools.partial(factor_kernel, rows),
        "factor",
        [(2,) + block] * 4 + [(PLANES, ny, nz)],
        [fields, viscosity],
        scratch=[VMEM((2,) + block, F32), pltpu.SemaphoreType.DMA((2,))],
        in_hbm=(0,),
        flops=10**9,
    )
    count = rows // 4
    (early,) = call(
        functools.partial(early_kernel, count),
        "early",
        [(4, count, ny, nz)],
        [fields, viscosity],
        scratch=[VMEM((4, count + 1, ny, nz), F32), pltpu.SemaphoreType.DMA],
        in_hbm=(0,),
        flops=4 * 10**9,
    )
    src, p, ends = call(
        functools.partial(explicit_kernel, count),
        "explicit",
        [(4, rows - count, ny, nz), (8, ny, nz), (8, rows, nz)],
        [fields, viscosity, g0, gn, early],
        scratch=[VMEM((4, rows - count + 1, ny, nz), F32), pltpu.SemaphoreType.DMA((3,))],
        in_hbm=(0,),
        flops=5 * 10**9,
    )
    pair, w = call(
        pair_kernel,
        "pair",
        [(JOINT, ny, half), (PLANES, ny, half)],
        [w, swap(w, 0), early],
        moved=4 * ny * nz * 60,
    )
    pairs = lines // 2
    widths = [8] * (levels - 3) + [4]
    found = call(
        functools.partial(chips_kernel, levels),
        "chips",
        [(pairs >> level, JOINT, ny, half) for level in range(1, levels)]
        + [(width, ny, half) for width in widths],
        [w] + gather([w] * (levels + 1)) + [p],
        moved=4 * ny * half * 300,
    )
    joints, consts = list(found[: levels - 1]), list(found[levels - 1 :])

    add_low, p = call(
        functools.partial(low_kernel, rows, ny),
        "edge_low",
        [(4, rows, nz), (8, ny, nz)],
        [y_first, low, ends, p, joints[0]],
        flops=2 * 10**8,
    )
    add_high, p, sent = call(
        functools.partial(high_kernel, rows, ny),
        "edge_high",
        [(4, rows, nz), (8, ny, half), (8, ny, half)],
        [y_last, high, ends, p],
        flops=2 * 10**8,
    )
    (t,) = call(
        functools.partial(source_kernel, rows, count),
        "source",
        [(4,) + block],
        [early, src, cpr, add_low, add_high],
        flops=30 * cells,
        moved=24 * cells,
    )
    (part,) = call(
        functools.partial(back_kernel, rows),
        "back",
        [(4,) + block],
        [t, inv, cpr],
        flops=20 * cells,
        moved=24 * cells,
    )
    p, diff, *shares = call(
        functools.partial(up_kernel, levels),
        "up",
        [(8, ny, half), (4, ny, half)] + [(width, ny, half) for width in widths],
        [p, swap(sent, 0), pair] + joints + [part],
        moved=4 * ny * nz * 40,
    )
    others = dict(enumerate(gather([None, p] + shares), 1))
    near = [others.pop(1 << level) for level in range(levels - 1)]
    beside = call(
        functools.partial(beside_kernel, levels),
        "beside",
        [(width, ny, half) for width in widths],
        list(others.values()) + consts,
        flops=6 * 10**8,
    )
    flux, sent = call(
        functools.partial(settle_kernel, levels),
        "settle",
        [(8, ny, half)] * 2,
        [p] + near + list(beside) + joints + [pair, diff],
        moved=4 * ny * half * 100,
    )
    rest = [part, g0, gn]
    parts = 4 if rows % 4 == 0 else 1
    scratch = [VMEM((4, rows, ny, half), F32), pltpu.SemaphoreType.DMA((half // 128 * parts,))]
    (out,) = call(
        functools.partial(final_kernel, True, parts),
        "final_own",
        [(4,) + block],
        [flux] + rest,
        scratch=scratch,
        out_hbm=(0,),
        flops=10**9,
    )
    (out,) = call(
        functools.partial(final_kernel, False, parts),
        "final_other",
        [(4,) + block],
        [swap(sent, 0)] + rest + [out],
        scratch=scratch,
        in_hbm=(4,),
        out_hbm=(0,),
        aliases={4: 0},
        flops=10**9,
    )
    return out


def solution(mesh):
    return jax.shard_map(
        local,
        mesh=mesh,
        in_specs=(P(None, "line", "col", None), P("line", "col", None)),
        out_specs=P(None, "line", "col", None),
        check_vma=False,
    )
```

```python
import functools

import jax
import jax.numpy as jnp
from jax import lax
from jax.experimental import pallas as pl
from jax.experimental.pallas import tpu as pltpu
from jax.sharding import PartitionSpec as P

STIFF = 3072
THERMAL_RATIO = 0.8
CROSS_RATE = 0.2
ADVECTION = 0.25
BUOYANCY = 2.0
SCALES = (1.0, THERMAL_RATIO)
KIND = (0, 0, 0, 1)

F32 = jnp.float32
VMEM = pltpu.VMEM
LIMIT = 24 * 1024 * 1024

G00, G0N, GNN = (0, 3), (1, 4), (2, 5)
V_FIRST, V_LAST, F_FIRST, F_LAST = 6, 7, 8, 12
PLANES = 16
R_, GA, GB, CA, CB = 0, 2, 4, 6, 10
JOINT = 14


def in_vmem(x):
    return pltpu.with_memory_space_constraint(x, VMEM)


def spec():
    return pl.BlockSpec(memory_space=VMEM)


def call(kernel, name, out_shapes, args, scratch=(), in_hbm=(), out_hbm=(), aliases={}, flops=0, moved=0):
    in_specs = []
    operands = []
    for i, x in enumerate(args):
        if i in in_hbm:
            in_specs.append(pl.BlockSpec(memory_space=pltpu.HBM))
            operands.append(pltpu.with_memory_space_constraint(x, pltpu.HBM))
        else:
            in_specs.append(spec())
            operands.append(in_vmem(x))
    out_shape = []
    out_specs = []
    for i, s in enumerate(out_shapes):
        if i in out_hbm:
            out_shape.append(pltpu.HBM(s, F32))
            out_specs.append(pl.BlockSpec(memory_space=pltpu.HBM))
        else:
            out_shape.append(VMEM(s, F32))
            out_specs.append(spec())
    return pl.pallas_call(
        kernel,
        out_shape=out_shape,
        in_specs=in_specs,
        out_specs=out_specs,
        scratch_shapes=list(scratch),
        input_output_aliases=aliases,
        compiler_params=pltpu.CompilerParams(vmem_limit_bytes=LIMIT),
        cost_estimate=pl.CostEstimate(flops=flops, bytes_accessed=moved, transcendentals=0),
        name=name,
    )(*operands)


def layer(read, ny, nz):
    sub = lax.broadcasted_iota(jnp.int32, (8, nz), 0)
    tile = jnp.broadcast_to(read(0), (8, nz))
    for r in range(1, 8):
        tile = jnp.where(sub == r, jnp.broadcast_to(read(r), (8, nz)), tile)
    return tile


def cut_kernel(ny, fields, visc, y_first, y_last, sems):
    copies = []
    for j, (at, out) in enumerate(((0, y_first), (ny - 1, y_last))):
        for k in range(4):
            copies.append(pltpu.make_async_copy(fields.at[k, :, at], out.at[k], sems.at[j, k]))
        copies.append(pltpu.make_async_copy(visc.at[:, at], out.at[4], sems.at[j, 4]))
    for i, copy in enumerate(copies):
        copy.start(priority=i % 2)
    for copy in copies:
        copy.wait()


def factor_kernel(rows, fields_ref, visc, inv, cpr, g0, gn, w, tau, sems):
    copies = [
        pltpu.make_async_copy(fields_ref.at[:, 0], w.at[F_FIRST : F_FIRST + 4], sems.at[0]),
        pltpu.make_async_copy(fields_ref.at[:, rows - 1], w.at[F_LAST : F_LAST + 4], sems.at[1]),
    ]
    for copy in copies:
        copy.start()
    ny, nz = visc.shape[1], visc.shape[2]
    me = lax.axis_index("line")
    wall_low = jnp.where(me == 0, 1.0, 0.0).astype(F32)
    wall_high = jnp.where(me == lax.axis_size("line") - 1, 1.0, 0.0).astype(F32)
    one = jnp.ones((ny, nz), F32)

    def row(i, carry):
        low, v = carry[4], carry[5]
        after = visc[jnp.minimum(i + 1, rows - 1)]
        high = jnp.where(i == rows - 1, (0.5 * STIFF) * wall_high * v, (0.5 * STIFF) * (v + after))
        new = []
        for s in range(2):
            gain, running = carry[2 * s], carry[2 * s + 1]
            down = SCALES[s] * low if s else low
            up = SCALES[s] * high if s else high
            q = 1.0 + down * gain
            one_over = 1.0 / (q + up)
            coupling = up * one_over
            inv[s, i] = one_over
            cpr[s, i] = coupling
            tau[s, i] = running
            new += [q * one_over, coupling * running]
        return tuple(new) + (high, after)

    first = visc[0]
    lax.fori_loop(0, rows, row, (one,) * 4 + (wall_low * (0.5 * STIFF) * first, first))

    end = rows - 1
    start = []
    for s in range(2):
        a = inv[s, end] * tau[s, end]
        b = inv[s, end]
        g0[s, end] = a
        gn[s, end] = b
        w[G0N[s]] = a
        w[GNN[s]] = b
        start += [a, b]

    def back(j, carry):
        i = end - 1 - j
        new = []
        for s in range(2):
            c = cpr[s, i]
            a = inv[s, i] * tau[s, i] + c * carry[2 * s]
            b = c * carry[2 * s + 1]
            g0[s, i] = a
            gn[s, i] = b
            new += [a, b]
        return tuple(new)

    final = lax.fori_loop(0, end, back, tuple(start))
    for s in range(2):
        w[G00[s]] = final[2 * s]
    w[V_FIRST] = first
    w[V_LAST] = visc[rows - 1]
    for copy in copies:
        copy.wait()


def explicit_rows(first, count, base, start, fields, visc, src):
    rows, ny, nz = visc.shape
    lane = lax.broadcasted_iota(jnp.int32, (ny, nz), 1)
    sub = lax.broadcasted_iota(jnp.int32, (ny, nz), 0)
    z_top, z_low = lane == nz - 1, lane == 0
    y_top, y_low = sub == ny - 1, sub == 0

    def sides(x):
        return (
            pltpu.roll(x, ny - 1, 0),
            pltpu.roll(x, 1, 0),
            pltpu.roll(x, nz - 1, 1),
            pltpu.roll(x, 1, 1),
        )

    def row(i, _):
        f = [fields[k, i - base] for k in range(4)]
        v = visc[i]
        after, before = jnp.minimum(i + 1, rows - 1), jnp.maximum(i - 1, 0)
        vyn, vyp, vzn, vzp = sides(v)
        half = 0.5 * CROSS_RATE
        faces = [
            jnp.where(y_top, 0.0, half * (v + vyn)),
            jnp.where(y_low, 0.0, half * (v + vyp)),
            half * (v + jnp.where(z_top, 0.0, vzn)),
            half * (v + jnp.where(z_low, 0.0, vzp)),
        ]
        none = [y_top, y_low, z_top, z_low]
        total = (faces[0] + faces[1]) + (faces[2] + faces[3])
        adv = [(-0.5 * ADVECTION) * f[k] for k in range(3)]
        move = [adv[1], -adv[1], adv[2], -adv[2]]
        adv_after = jnp.where(i == rows - 1, 0.0, adv[0])
        adv_before = jnp.where(i == 0, 0.0, adv[0])
        weights, centre = [], []
        for s in range(2):
            scaled = [SCALES[s] * x if s else x for x in faces]
            weights.append([jnp.where(n, 0.0, x + m) for n, x, m in zip(none, scaled, move)])
            centre.append(1.0 - (SCALES[s] * total if s else total))
        for k in range(4):
            s = KIND[k]
            near = sides(f[k])
            out = centre[s] * f[k] + adv_after * fields[k, after - base] - adv_before * fields[k, before - base]
            for c, x in zip(weights[s], near):
                out = out + c * x
            if k == 2:
                out = out + BUOYANCY * f[3]
            src[k, i - start] = out
        return 0

    lax.fori_loop(first, first + count, row, 0)


def early_kernel(count, fields_ref, visc, src, fields, sem):
    copy = pltpu.make_async_copy(fields_ref.at[:, 0 : count + 1], fields, sem)
    copy.start()
    copy.wait()
    explicit_rows(0, count, 0, 0, fields, visc, src)


def explicit_kernel(count, fields_ref, visc, g0, gn, early, src, p, ends, fields, sems):
    rows, ny, nz = visc.shape
    cuts = [count - 1] + list(range(2 * count + 1, rows, count)) + [rows]
    copies = []
    for c, (lo, hi) in enumerate(zip(cuts, cuts[1:])):
        copies.append(
            pltpu.make_async_copy(
                fields_ref.at[:, lo:hi], fields.at[:, lo - cuts[0] : hi - cuts[0]], sems.at[c]
            )
        )
        copies[-1].start()
    for c, copy in enumerate(copies):
        copy.wait()
        explicit_rows((c + 1) * count, count, cuts[0], count, fields, visc, src)

    def dot(ref, shift):
        def add(i, carry):
            new = []
            for g, base in ((g0, 0), (gn, 4)):
                for k in range(4):
                    new.append(carry[base + k] + g[KIND[k], i] * ref[k, i - shift])
            return tuple(new)

        return add

    final = (jnp.zeros((ny, nz), F32),) * 8
    final = lax.fori_loop(0, count, dot(early, 0), final)
    final = lax.fori_loop(count, rows, dot(src, count), final)
    for k in range(8):
        p[k] = final[k]

    for s in range(2):
        for side, at in ((0, 0), (1, ny - 1)):
            for which, g in ((0, g0), (1, gn)):
                for lo in range(0, rows, 8):
                    ends[4 * side + 2 * which + s, lo : lo + 8] = layer(
                        lambda r: g[s, lo + r, at : at + 1, :], ny, nz
                    )


def edge_kernel(rows, ny, y_last, y_first, low, high, ends, p, *refs):
    add, keep, send = refs[-3:]
    nz = add.shape[2]
    half = nz // 2
    low_core = side_bit(0)
    values = {}
    sub = lax.broadcasted_iota(jnp.int32, (ny, 128), 0)
    rate = 0.5 * ADVECTION
    for j in range(nz // 128):
        z = pl.ds(j * 128, 128)
        sums = []
        for side, mine, far, sign in ((0, y_first, low, rate), (4, y_last, high, -rate)):
            total = [None] * 8
            for r in range(rows // 8):
                x = pl.ds(r * 8, 8)
                face = (0.5 * CROSS_RATE) * (mine[4, x, z] + far[4, x, z])
                faces = (face, THERMAL_RATIO * face)
                adv = sign * mine[1, x, z]
                both = [adv + c for c in faces]
                g = [ends[side + q, x, z] for q in range(4)]
                for k in range(4):
                    s = KIND[k]
                    h = both[s] * far[k, x, z] - faces[s] * mine[k, x, z]
                    add[side + k, x, z] = h
                    for slot, c in ((k, g[s]), (4 + k, g[2 + s])):
                        part = c * h
                        total[slot] = part if total[slot] is None else total[slot] + part
            sums.append(total)
        for slot in range(8):
            add_low = jnp.sum(sums[0][slot], axis=0, keepdims=True)
            add_high = jnp.sum(sums[1][slot], axis=0, keepdims=True)
            both = jnp.where(sub == 0, add_low, jnp.where(sub == ny - 1, add_high, 0.0))
            values[slot, j] = p[slot, :, z] + both
    for slot in range(8):
        for c in range(half // 128):
            near = pl.ds(c * 128, 128)
            one, two = values[slot, c], values[slot, c + half // 128]
            keep[slot, :, near] = jnp.where(low_core, one, two)
            send[slot, :, near] = jnp.where(low_core, two, one)


def side_bit(level):
    return jnp.bitwise_and(jnp.right_shift(lax.axis_index("line"), level), 1) == 0


def join(left, right):
    face = left[V_LAST] + right[V_FIRST]
    joint, new, ratio = {}, {}, []
    for s in range(2):
        resist = 1.0 / ((0.5 * STIFF * SCALES[s]) * face)
        r = 1.0 / (resist + left[GNN[s]] + right[G00[s]])
        ratio.append(r)
        a, b = left[G0N[s]], right[G0N[s]]
        joint[R_ + s] = r
        joint[GA + s] = a
        joint[GB + s] = b
        new[G00[s]] = left[G00[s]] - r * a * a
        new[GNN[s]] = right[GNN[s]] - r * b * b
        new[G0N[s]] = r * a * b
    rate = 0.5 * ADVECTION
    for k in range(4):
        s = KIND[k]
        add_a = -rate * left[F_LAST] * right[F_FIRST + k]
        add_b = rate * right[F_FIRST] * left[F_LAST + k]
        e = ratio[s] * (left[GNN[s]] * add_a - right[G00[s]] * add_b)
        joint[CA + k] = add_a - e
        joint[CB + k] = add_b + e
        new[F_FIRST + k] = left[F_FIRST + k]
        new[F_LAST + k] = right[F_LAST + k]
    new[V_FIRST] = left[V_FIRST]
    new[V_LAST] = right[V_LAST]
    return joint, new


def sided(low_side, mine, theirs):
    left = {p: jnp.where(low_side, mine[p], theirs[p]) for p in mine}
    right = {p: jnp.where(low_side, theirs[p], mine[p]) for p in mine}
    return left, right


def pair_kernel(own, other, *refs):
    joint, out = refs[-2:]
    low_side = side_bit(0)
    planes = range(PLANES)
    found, new = join(*sided(low_side, {p: own[p] for p in planes}, {p: other[p] for p in planes}))
    width = out.shape[2]
    for plane in range(JOINT):
        joint[plane] = jnp.where(low_side, found[plane][:, :width], found[plane][:, width:])
    for plane in planes:
        out[plane] = jnp.where(low_side, new[plane][:, :width], new[plane][:, width:])


def chips_kernel(levels, own, *refs):
    others = refs[: 2 ** (levels - 1) - 1]
    joints = refs[-(2 * levels - 3) : len(refs) - (levels - 2)]
    consts = refs[len(refs) - (levels - 2) :]
    blocks = [{p: x[p] for p in range(PLANES)} for x in (own, *others)]
    zero = jnp.zeros_like(own[0])
    ends = [{p: zero for p in range(8)} for _ in blocks]
    for level in range(1, levels):
        low_side = side_bit(level)
        joined, new_ends = [], []
        for j in range(0, len(blocks), 2):
            found, new = join(*sided(low_side, blocks[j], blocks[j + 1]))
            for plane in range(JOINT):
                joints[level - 1][j // 2, plane] = found[plane]
            joined.append(new)
            if level < levels - 1:
                left, right = sided(low_side, ends[j], ends[j + 1])
                both = {}
                for k in range(4):
                    _, both[k], both[4 + k] = up(found, k, left, right)
                new_ends.append(both)
        blocks, ends = joined, new_ends
        if level < levels - 1:
            for slot, x in enumerate(facing(level + 1, levels, ends[1], False)):
                consts[level - 1][slot] = x


def facing(level, levels, ends, mine):
    if level < levels - 1:
        return [ends[p] for p in range(8)]
    low_side = side_bit(level)
    if not mine:
        low_side = jnp.logical_not(low_side)
    return [jnp.where(low_side, ends[4 + k], ends[k]) for k in range(4)]


def source_kernel(rows, count, early, src, cpr, add, t):
    ny, nz = src.shape[2], src.shape[3]
    sub = lax.broadcasted_iota(jnp.int32, (ny, nz), 0)
    top, low = sub == ny - 1, sub == 0

    def down(ref, shift):
        def row(i, carry):
            prev = jnp.maximum(i - 1, 0)
            new = []
            for k in range(4):
                a = jnp.broadcast_to(add[k, pl.ds(i, 1), :], (ny, nz))
                b = jnp.broadcast_to(add[4 + k, pl.ds(i, 1), :], (ny, nz))
                x = ref[k, i - shift] + jnp.where(low, a, jnp.where(top, b, 0.0))
                x = x + cpr[KIND[k], prev] * carry[k]
                t[k, i] = x
                new.append(x)
            return tuple(new)

        return row

    state = (jnp.zeros((ny, nz), F32),) * 4
    state = lax.fori_loop(0, count, down(early, 0), state)
    lax.fori_loop(count, rows, down(src, count), state)


def back_kernel(rows, t, inv, cpr, part):
    end = rows - 1
    start = []
    for k in range(4):
        x = inv[KIND[k], end] * t[k, end]
        part[k, end] = x
        start.append(x)

    def row(j, carry):
        i = end - 1 - j
        new = []
        for k in range(4):
            s = KIND[k]
            x = inv[s, i] * t[k, i] + cpr[s, i] * carry[k]
            part[k, i] = x
            new.append(x)
        return tuple(new)

    lax.fori_loop(0, end, row, tuple(start))


def up(joint, k, left, right):
    s = KIND[k]
    d = left[4 + k] - right[k]
    flow = joint[R_ + s] * d
    first = left[k] + joint[GA + s] * (joint[CA + k] - flow)
    last = right[4 + k] + joint[GB + s] * (joint[CB + k] + flow)
    return d, first, last


def up_kernel(levels, own, other, joint, *refs):
    joints = refs[: levels - 1]
    out, diff = refs[levels : levels + 2]
    shares = refs[levels + 2 :]
    low_side = side_bit(0)
    left, right = sided(low_side, {p: own[p] for p in range(8)}, {p: other[p] for p in range(8)})
    ends = {}
    for k in range(4):
        diff[k], ends[k], ends[4 + k] = up(joint, k, left, right)
        out[k] = ends[k]
        out[4 + k] = ends[4 + k]
    for level in range(1, levels - 1):
        low_side = side_bit(level)
        joint = joints[level - 1].at[0]
        for k in range(4):
            s = KIND[k]
            first, last = ends[k], ends[4 + k]
            flow = joint[R_ + s] * jnp.where(low_side, last, -first)
            ends[k] = jnp.where(low_side, first, 0.0) - joint[GA + s] * flow
            ends[4 + k] = jnp.where(low_side, 0.0, last) + joint[GB + s] * flow
        for slot, x in enumerate(facing(level + 1, levels, ends, True)):
            shares[level - 1][slot] = x


def joint_flow(joint, k, d, into_first, into_last, low_side):
    s = KIND[k]
    flow = joint[R_ + s] * (d + joint[GA + s] * into_first - joint[GB + s] * into_last)
    first = jnp.where(low_side, into_first, joint[CB + k] + flow)
    last = jnp.where(low_side, joint[CA + k] - flow, into_last)
    return first, last


def beside_kernel(levels, *refs):
    parts, refs = list(refs[: 2 ** (levels - 1) - levels]), refs[2 ** (levels - 1) - levels :]
    consts, outs = refs[: levels - 2], refs[levels - 2 :]
    for level in range(2, levels):
        here = [parts.pop(0) for _ in range(2 ** (level - 1) - 1)]
        for p in range(outs[level - 2].shape[0]):
            total = consts[level - 2][p]
            for part in here:
                total = total + part[p]
            outs[level - 2][p] = total


def settle_kernel(levels, own, *refs):
    near, refs = refs[: levels - 1], refs[levels - 1 :]
    far, joints = refs[: levels - 2], refs[levels - 2 : 2 * levels - 3]
    pair, diff, out, send = refs[2 * levels - 3 :]
    ends = {p: own[p] for p in range(8)}
    diffs = []
    for level in range(1, levels):
        low_side = side_bit(level)
        beside = {p: near[level - 1][p] for p in range(near[level - 1].shape[0])}
        if level > 1:
            beside = {p: x + far[level - 2][p] for p, x in beside.items()}
        across = []
        if len(beside) == 4:
            for k in range(4):
                x = beside[k]
                across.append(jnp.where(low_side, ends[4 + k] - x, x - ends[k]))
        else:
            left, right = sided(low_side, ends, beside)
            for k in range(4):
                d, ends[k], ends[4 + k] = up(joints[level - 1].at[0], k, left, right)
                across.append(d)
        diffs.append(across)
    for k in range(4):
        first = last = jnp.zeros_like(diffs[0][0])
        for level in range(levels - 1, 0, -1):
            first, last = joint_flow(
                joints[level - 1].at[0], k, diffs[level - 1][k], first, last, side_bit(level)
            )
        low_side = side_bit(0)
        s = KIND[k]
        flow = pair[R_ + s] * (diff[k] + pair[GA + s] * first - pair[GB + s] * last)
        low_last, high_first = pair[CA + k] - flow, pair[CB + k] + flow
        out[k] = jnp.where(low_side, first, high_first)
        out[4 + k] = jnp.where(low_side, low_last, last)
        send[k] = jnp.where(low_side, high_first, first)
        send[4 + k] = jnp.where(low_side, last, low_last)


def final_kernel(mine, parts, flux, part, g0, gn, *refs):
    out, buf, sems = refs[-3:]
    rows, half = buf.shape[1], buf.shape[3]
    core = jnp.bitwise_and(lax.axis_index("line"), 1)
    offset = (core if mine else 1 - core) * half
    step = rows // parts
    copies = []
    for c in range(half // 128):
        near = pl.ds(c * 128, 128)
        z = pl.ds(pl.multiple_of(offset + c * 128, 128), 128)
        into = [flux[k, :, near] for k in range(8)]
        for r in range(parts):
            for i in range(r * step, (r + 1) * step):
                a = [g0[s, i, :, z] for s in range(2)]
                b = [gn[s, i, :, z] for s in range(2)]
                for k in range(4):
                    s = KIND[k]
                    buf[k, i, :, near] = part[k, i, :, z] + (a[s] * into[k] + b[s] * into[4 + k])
            x = pl.ds(r * step, step)
            copies.append(
                pltpu.make_async_copy(
                    buf.at[:, x, :, near], out.at[:, x, :, z], sems.at[c * parts + r]
                )
            )
            copies[-1].start(priority=len(copies) % 2)
    for copy in copies:
        copy.wait()


def local(fields, viscosity):
    rows, ny, nz = viscosity.shape
    lines = lax.axis_size("line")
    cols = lax.axis_size("col")
    levels = lines.bit_length() - 1
    half = nz // 2
    cells = rows * ny * nz
    block = (rows, ny, nz)

    ring = [(i, (i + 1) % cols) for i in range(cols)]
    back_ring = [(b, a) for a, b in ring]

    def gather(at_level):
        found = {}
        for d in sorted(range(1, lines // 2), key=lambda d: (-d.bit_count(), d)):
            x = at_level[d.bit_length()]
            found[d] = lax.ppermute(x, "line", [(i, i ^ (d << 1)) for i in range(lines)])
        return [found[d] for d in sorted(found)]

    def swap(x, level):
        return lax.ppermute(x, "line", [(i, i ^ (1 << level)) for i in range(lines)])

    y_first, y_last = call(
        functools.partial(cut_kernel, ny),
        "cut",
        [(5, rows, nz), (5, rows, nz)],
        [fields, viscosity],
        scratch=[pltpu.SemaphoreType.DMA((2, 5))],
        in_hbm=(0, 1),
        moved=2 * cells,
    )
    low = lax.ppermute(y_last, "col", ring)
    high = lax.ppermute(y_first, "col", back_ring)

    inv, cpr, g0, gn, w = call(
        functools.partial(factor_kernel, rows),
        "factor",
        [(2,) + block] * 4 + [(PLANES, ny, nz)],
        [fields, viscosity],
        scratch=[VMEM((2,) + block, F32), pltpu.SemaphoreType.DMA((2,))],
        in_hbm=(0,),
        flops=10**9,
    )
    count = rows // 4
    (early,) = call(
        functools.partial(early_kernel, count),
        "early",
        [(4, count, ny, nz)],
        [fields, viscosity],
        scratch=[VMEM((4, count + 1, ny, nz), F32), pltpu.SemaphoreType.DMA],
        in_hbm=(0,),
        flops=4 * 10**9,
    )
    src, p, ends = call(
        functools.partial(explicit_kernel, count),
        "explicit",
        [(4, rows - count, ny, nz), (8, ny, nz), (8, rows, nz)],
        [fields, viscosity, g0, gn, early],
        scratch=[VMEM((4, rows - count + 1, ny, nz), F32), pltpu.SemaphoreType.DMA((3,))],
        in_hbm=(0,),
        flops=5 * 10**9,
    )
    pair, w = call(
        pair_kernel,
        "pair",
        [(JOINT, ny, half), (PLANES, ny, half)],
        [w, swap(w, 0), early],
        moved=4 * ny * nz * 60,
    )
    pairs = lines // 2
    widths = [8] * (levels - 3) + [4]
    found = call(
        functools.partial(chips_kernel, levels),
        "chips",
        [(pairs >> level, JOINT, ny, half) for level in range(1, levels)]
        + [(width, ny, half) for width in widths],
        [w] + gather([w] * (levels + 1)) + [p],
        moved=4 * ny * half * 300,
    )
    joints, consts = list(found[: levels - 1]), list(found[levels - 1 :])

    add, p, sent = call(
        functools.partial(edge_kernel, rows, ny),
        "edge",
        [(8, rows, nz), (8, ny, half), (8, ny, half)],
        [y_last, y_first, low, high, ends, p, joints[0]],
        flops=5 * 10**8,
    )
    (t,) = call(
        functools.partial(source_kernel, rows, count),
        "source",
        [(4,) + block],
        [early, src, cpr, add],
        flops=30 * cells,
        moved=24 * cells,
    )
    (part,) = call(
        functools.partial(back_kernel, rows),
        "back",
        [(4,) + block],
        [t, inv, cpr],
        flops=20 * cells,
        moved=24 * cells,
    )
    p, diff, *shares = call(
        functools.partial(up_kernel, levels),
        "up",
        [(8, ny, half), (4, ny, half)] + [(width, ny, half) for width in widths],
        [p, swap(sent, 0), pair] + joints + [part],
        moved=4 * ny * nz * 40,
    )
    others = dict(enumerate(gather([None, p] + shares), 1))
    near = [others.pop(1 << level) for level in range(levels - 1)]
    beside = call(
        functools.partial(beside_kernel, levels),
        "beside",
        [(width, ny, half) for width in widths],
        list(others.values()) + consts,
        flops=6 * 10**8,
    )
    flux, sent = call(
        functools.partial(settle_kernel, levels),
        "settle",
        [(8, ny, half)] * 2,
        [p] + near + list(beside) + joints + [pair, diff],
        moved=4 * ny * half * 100,
    )
    rest = [part, g0, gn]
    parts = 4 if rows % 4 == 0 else 1
    scratch = [VMEM((4, rows, ny, half), F32), pltpu.SemaphoreType.DMA((half // 128 * parts,))]
    (out,) = call(
        functools.partial(final_kernel, True, parts),
        "final_own",
        [(4,) + block],
        [flux] + rest,
        scratch=scratch,
        out_hbm=(0,),
        flops=10**9,
    )
    (out,) = call(
        functools.partial(final_kernel, False, parts),
        "final_other",
        [(4,) + block],
        [swap(sent, 0)] + rest + [out],
        scratch=scratch,
        in_hbm=(4,),
        out_hbm=(0,),
        aliases={4: 0},
        flops=10**9,
    )
    return out


def solution(mesh):
    return jax.shard_map(
        local,
        mesh=mesh,
        in_specs=(P(None, "line", "col", None), P("line", "col", None)),
        out_specs=P(None, "line", "col", None),
        check_vma=False,
    )
```

```python
import functools

import jax
import jax.numpy as jnp
from jax import lax
from jax.experimental import pallas as pl
from jax.experimental.pallas import tpu as pltpu
from jax.sharding import PartitionSpec as P

STIFF = 3072
THERMAL_RATIO = 0.8
CROSS_RATE = 0.2
ADVECTION = 0.25
BUOYANCY = 2.0
SCALES = (1.0, THERMAL_RATIO)
KIND = (0, 0, 0, 1)

F32 = jnp.float32
VMEM = pltpu.VMEM
LIMIT = 24 * 1024 * 1024

G00, G0N, GNN = (0, 3), (1, 4), (2, 5)
V_FIRST, V_LAST, F_FIRST, F_LAST = 6, 7, 8, 12
PLANES = 16
R_, GA, GB, CA, CB = 0, 2, 4, 6, 10
JOINT = 14


def in_vmem(x):
    return pltpu.with_memory_space_constraint(x, VMEM)


def spec():
    return pl.BlockSpec(memory_space=VMEM)


def call(kernel, name, out_shapes, args, scratch=(), in_hbm=(), out_hbm=(), aliases={}, flops=0, moved=0):
    in_specs = []
    operands = []
    for i, x in enumerate(args):
        if i in in_hbm:
            in_specs.append(pl.BlockSpec(memory_space=pltpu.HBM))
            operands.append(pltpu.with_memory_space_constraint(x, pltpu.HBM))
        else:
            in_specs.append(spec())
            operands.append(in_vmem(x))
    out_shape = []
    out_specs = []
    for i, s in enumerate(out_shapes):
        if i in out_hbm:
            out_shape.append(pltpu.HBM(s, F32))
            out_specs.append(pl.BlockSpec(memory_space=pltpu.HBM))
        else:
            out_shape.append(VMEM(s, F32))
            out_specs.append(spec())
    return pl.pallas_call(
        kernel,
        out_shape=out_shape,
        in_specs=in_specs,
        out_specs=out_specs,
        scratch_shapes=list(scratch),
        input_output_aliases=aliases,
        compiler_params=pltpu.CompilerParams(vmem_limit_bytes=LIMIT),
        cost_estimate=pl.CostEstimate(flops=flops, bytes_accessed=moved, transcendentals=0),
        name=name,
    )(*operands)


def layer(read, ny, nz):
    sub = lax.broadcasted_iota(jnp.int32, (8, nz), 0)
    tile = jnp.broadcast_to(read(0), (8, nz))
    for r in range(1, 8):
        tile = jnp.where(sub == r, jnp.broadcast_to(read(r), (8, nz)), tile)
    return tile


def cut_kernel(ny, fields, visc, y_first, y_last, sems):
    copies = []
    for j, (at, out) in enumerate(((0, y_first), (ny - 1, y_last))):
        copies.append(pltpu.make_async_copy(fields.at[:, :, at], out.at[0:4], sems.at[j, 0]))
        copies.append(pltpu.make_async_copy(visc.at[:, at], out.at[4], sems.at[j, 1]))
    for copy in copies:
        copy.start()
    for copy in copies:
        copy.wait()


def factor_kernel(rows, fields_ref, visc, inv, cpr, g0, gn, w, tau, sems):
    copies = [
        pltpu.make_async_copy(fields_ref.at[:, 0], w.at[F_FIRST : F_FIRST + 4], sems.at[0]),
        pltpu.make_async_copy(fields_ref.at[:, rows - 1], w.at[F_LAST : F_LAST + 4], sems.at[1]),
    ]
    for copy in copies:
        copy.start()
    ny, nz = visc.shape[1], visc.shape[2]
    me = lax.axis_index("line")
    wall_low = jnp.where(me == 0, 1.0, 0.0).astype(F32)
    wall_high = jnp.where(me == lax.axis_size("line") - 1, 1.0, 0.0).astype(F32)
    one = jnp.ones((ny, nz), F32)

    def row(i, carry):
        low, v = carry[4], carry[5]
        after = visc[jnp.minimum(i + 1, rows - 1)]
        high = jnp.where(i == rows - 1, (0.5 * STIFF) * wall_high * v, (0.5 * STIFF) * (v + after))
        new = []
        for s in range(2):
            gain, running = carry[2 * s], carry[2 * s + 1]
            down = SCALES[s] * low if s else low
            up = SCALES[s] * high if s else high
            q = 1.0 + down * gain
            one_over = 1.0 / (q + up)
            coupling = up * one_over
            inv[s, i] = one_over
            cpr[s, i] = coupling
            tau[s, i] = running
            new += [q * one_over, coupling * running]
        return tuple(new) + (high, after)

    first = visc[0]
    lax.fori_loop(0, rows, row, (one,) * 4 + (wall_low * (0.5 * STIFF) * first, first))

    end = rows - 1
    start = []
    for s in range(2):
        a = inv[s, end] * tau[s, end]
        b = inv[s, end]
        g0[s, end] = a
        gn[s, end] = b
        w[G0N[s]] = a
        w[GNN[s]] = b
        start += [a, b]

    def back(j, carry):
        i = end - 1 - j
        new = []
        for s in range(2):
            c = cpr[s, i]
            a = inv[s, i] * tau[s, i] + c * carry[2 * s]
            b = c * carry[2 * s + 1]
            g0[s, i] = a
            gn[s, i] = b
            new += [a, b]
        return tuple(new)

    final = lax.fori_loop(0, end, back, tuple(start))
    for s in range(2):
        w[G00[s]] = final[2 * s]
    w[V_FIRST] = first
    w[V_LAST] = visc[rows - 1]
    for copy in copies:
        copy.wait()


def explicit_rows(first, count, base, start, fields, visc, src):
    rows, ny, nz = visc.shape
    lane = lax.broadcasted_iota(jnp.int32, (ny, nz), 1)
    sub = lax.broadcasted_iota(jnp.int32, (ny, nz), 0)
    z_top, z_low = lane == nz - 1, lane == 0
    y_top, y_low = sub == ny - 1, sub == 0

    def sides(x):
        return (
            pltpu.roll(x, ny - 1, 0),
            pltpu.roll(x, 1, 0),
            pltpu.roll(x, nz - 1, 1),
            pltpu.roll(x, 1, 1),
        )

    def row(i, _):
        f = [fields[k, i - base] for k in range(4)]
        v = visc[i]
        after, before = jnp.minimum(i + 1, rows - 1), jnp.maximum(i - 1, 0)
        vyn, vyp, vzn, vzp = sides(v)
        half = 0.5 * CROSS_RATE
        faces = [
            jnp.where(y_top, 0.0, half * (v + vyn)),
            jnp.where(y_low, 0.0, half * (v + vyp)),
            half * (v + jnp.where(z_top, 0.0, vzn)),
            half * (v + jnp.where(z_low, 0.0, vzp)),
        ]
        none = [y_top, y_low, z_top, z_low]
        total = (faces[0] + faces[1]) + (faces[2] + faces[3])
        adv = [(-0.5 * ADVECTION) * f[k] for k in range(3)]
        move = [adv[1], -adv[1], adv[2], -adv[2]]
        adv_after = jnp.where(i == rows - 1, 0.0, adv[0])
        adv_before = jnp.where(i == 0, 0.0, adv[0])
        weights, centre = [], []
        for s in range(2):
            scaled = [SCALES[s] * x if s else x for x in faces]
            weights.append([jnp.where(n, 0.0, x + m) for n, x, m in zip(none, scaled, move)])
            centre.append(1.0 - (SCALES[s] * total if s else total))
        for k in range(4):
            s = KIND[k]
            near = sides(f[k])
            out = centre[s] * f[k] + adv_after * fields[k, after - base] - adv_before * fields[k, before - base]
            for c, x in zip(weights[s], near):
                out = out + c * x
            if k == 2:
                out = out + BUOYANCY * f[3]
            src[k, i - start] = out
        return 0

    lax.fori_loop(first, first + count, row, 0)


def early_kernel(count, fields_ref, visc, src, fields, sem):
    copy = pltpu.make_async_copy(fields_ref.at[:, 0 : count + 1], fields, sem)
    copy.start()
    copy.wait()
    explicit_rows(0, count, 0, 0, fields, visc, src)


def explicit_kernel(count, fields_ref, visc, g0, gn, early, src, p, ends, fields, sems):
    rows, ny, nz = visc.shape
    cuts = [count - 1] + list(range(2 * count + 1, rows, count)) + [rows]
    copies = []
    for c, (lo, hi) in enumerate(zip(cuts, cuts[1:])):
        copies.append(
            pltpu.make_async_copy(
                fields_ref.at[:, lo:hi], fields.at[:, lo - cuts[0] : hi - cuts[0]], sems.at[c]
            )
        )
        copies[-1].start()
    for c, copy in enumerate(copies):
        copy.wait()
        explicit_rows((c + 1) * count, count, cuts[0], count, fields, visc, src)

    def dot(ref, shift):
        def add(i, carry):
            new = []
            for g, base in ((g0, 0), (gn, 4)):
                for k in range(4):
                    new.append(carry[base + k] + g[KIND[k], i] * ref[k, i - shift])
            return tuple(new)

        return add

    final = (jnp.zeros((ny, nz), F32),) * 8
    final = lax.fori_loop(0, count, dot(early, 0), final)
    final = lax.fori_loop(count, rows, dot(src, count), final)
    for k in range(8):
        p[k] = final[k]

    for s in range(2):
        for side, at in ((0, 0), (1, ny - 1)):
            for which, g in ((0, g0), (1, gn)):
                for lo in range(0, rows, 8):
                    ends[4 * side + 2 * which + s, lo : lo + 8] = layer(
                        lambda r: g[s, lo + r, at : at + 1, :], ny, nz
                    )


def edge_kernel(rows, ny, y_last, y_first, low, high, ends, p, *refs):
    add, keep, send = refs[-3:]
    nz = add.shape[2]
    half = nz // 2
    low_core = side_bit(0)
    values = {}
    sub = lax.broadcasted_iota(jnp.int32, (ny, 128), 0)
    rate = 0.5 * ADVECTION
    for j in range(nz // 128):
        z = pl.ds(j * 128, 128)
        sums = []
        for side, mine, far, sign in ((0, y_first, low, rate), (4, y_last, high, -rate)):
            total = [None] * 8
            for r in range(rows // 8):
                x = pl.ds(r * 8, 8)
                face = (0.5 * CROSS_RATE) * (mine[4, x, z] + far[4, x, z])
                faces = (face, THERMAL_RATIO * face)
                adv = sign * mine[1, x, z]
                both = [adv + c for c in faces]
                g = [ends[side + q, x, z] for q in range(4)]
                for k in range(4):
                    s = KIND[k]
                    h = both[s] * far[k, x, z] - faces[s] * mine[k, x, z]
                    add[side + k, x, z] = h
                    for slot, c in ((k, g[s]), (4 + k, g[2 + s])):
                        part = c * h
                        total[slot] = part if total[slot] is None else total[slot] + part
            sums.append(total)
        for slot in range(8):
            add_low = jnp.sum(sums[0][slot], axis=0, keepdims=True)
            add_high = jnp.sum(sums[1][slot], axis=0, keepdims=True)
            both = jnp.where(sub == 0, add_low, jnp.where(sub == ny - 1, add_high, 0.0))
            values[slot, j] = p[slot, :, z] + both
    for slot in range(8):
        for c in range(half // 128):
            near = pl.ds(c * 128, 128)
            one, two = values[slot, c], values[slot, c + half // 128]
            keep[slot, :, near] = jnp.where(low_core, one, two)
            send[slot, :, near] = jnp.where(low_core, two, one)


def side_bit(level):
    return jnp.bitwise_and(jnp.right_shift(lax.axis_index("line"), level), 1) == 0


def join(left, right):
    face = left[V_LAST] + right[V_FIRST]
    joint, new, ratio = {}, {}, []
    for s in range(2):
        resist = 1.0 / ((0.5 * STIFF * SCALES[s]) * face)
        r = 1.0 / (resist + left[GNN[s]] + right[G00[s]])
        ratio.append(r)
        a, b = left[G0N[s]], right[G0N[s]]
        joint[R_ + s] = r
        joint[GA + s] = a
        joint[GB + s] = b
        new[G00[s]] = left[G00[s]] - r * a * a
        new[GNN[s]] = right[GNN[s]] - r * b * b
        new[G0N[s]] = r * a * b
    rate = 0.5 * ADVECTION
    for k in range(4):
        s = KIND[k]
        add_a = -rate * left[F_LAST] * right[F_FIRST + k]
        add_b = rate * right[F_FIRST] * left[F_LAST + k]
        e = ratio[s] * (left[GNN[s]] * add_a - right[G00[s]] * add_b)
        joint[CA + k] = add_a - e
        joint[CB + k] = add_b + e
        new[F_FIRST + k] = left[F_FIRST + k]
        new[F_LAST + k] = right[F_LAST + k]
    new[V_FIRST] = left[V_FIRST]
    new[V_LAST] = right[V_LAST]
    return joint, new


def sided(low_side, mine, theirs):
    left = {p: jnp.where(low_side, mine[p], theirs[p]) for p in mine}
    right = {p: jnp.where(low_side, theirs[p], mine[p]) for p in mine}
    return left, right


def pair_kernel(own, other, *refs):
    joint, out = refs[-2:]
    low_side = side_bit(0)
    planes = range(PLANES)
    found, new = join(*sided(low_side, {p: own[p] for p in planes}, {p: other[p] for p in planes}))
    width = out.shape[2]
    for plane in range(JOINT):
        joint[plane] = jnp.where(low_side, found[plane][:, :width], found[plane][:, width:])
    for plane in planes:
        out[plane] = jnp.where(low_side, new[plane][:, :width], new[plane][:, width:])


def chips_kernel(levels, own, *refs):
    others = refs[: 2 ** (levels - 1) - 1]
    joints = refs[-(2 * levels - 3) : len(refs) - (levels - 2)]
    consts = refs[len(refs) - (levels - 2) :]
    blocks = [{p: x[p] for p in range(PLANES)} for x in (own, *others)]
    zero = jnp.zeros_like(own[0])
    ends = [{p: zero for p in range(8)} for _ in blocks]
    for level in range(1, levels):
        low_side = side_bit(level)
        joined, new_ends = [], []
        for j in range(0, len(blocks), 2):
            found, new = join(*sided(low_side, blocks[j], blocks[j + 1]))
            for plane in range(JOINT):
                joints[level - 1][j // 2, plane] = found[plane]
            joined.append(new)
            if level < levels - 1:
                left, right = sided(low_side, ends[j], ends[j + 1])
                both = {}
                for k in range(4):
                    _, both[k], both[4 + k] = up(found, k, left, right)
                new_ends.append(both)
        blocks, ends = joined, new_ends
        if level < levels - 1:
            for slot, x in enumerate(facing(level + 1, levels, ends[1], False)):
                consts[level - 1][slot] = x


def facing(level, levels, ends, mine):
    if level < levels - 1:
        return [ends[p] for p in range(8)]
    low_side = side_bit(level)
    if not mine:
        low_side = jnp.logical_not(low_side)
    return [jnp.where(low_side, ends[4 + k], ends[k]) for k in range(4)]


def source_kernel(rows, count, early, src, cpr, add, t):
    ny, nz = src.shape[2], src.shape[3]
    sub = lax.broadcasted_iota(jnp.int32, (ny, nz), 0)
    top, low = sub == ny - 1, sub == 0

    def down(ref, shift):
        def row(i, carry):
            prev = jnp.maximum(i - 1, 0)
            new = []
            for k in range(4):
                a = jnp.broadcast_to(add[k, pl.ds(i, 1), :], (ny, nz))
                b = jnp.broadcast_to(add[4 + k, pl.ds(i, 1), :], (ny, nz))
                x = ref[k, i - shift] + jnp.where(low, a, jnp.where(top, b, 0.0))
                x = x + cpr[KIND[k], prev] * carry[k]
                t[k, i] = x
                new.append(x)
            return tuple(new)

        return row

    state = (jnp.zeros((ny, nz), F32),) * 4
    state = lax.fori_loop(0, count, down(early, 0), state)
    lax.fori_loop(count, rows, down(src, count), state)


def back_kernel(rows, t, inv, cpr, part):
    end = rows - 1
    start = []
    for k in range(4):
        x = inv[KIND[k], end] * t[k, end]
        part[k, end] = x
        start.append(x)

    def row(j, carry):
        i = end - 1 - j
        new = []
        for k in range(4):
            s = KIND[k]
            x = inv[s, i] * t[k, i] + cpr[s, i] * carry[k]
            part[k, i] = x
            new.append(x)
        return tuple(new)

    lax.fori_loop(0, end, row, tuple(start))


def up(joint, k, left, right):
    s = KIND[k]
    d = left[4 + k] - right[k]
    flow = joint[R_ + s] * d
    first = left[k] + joint[GA + s] * (joint[CA + k] - flow)
    last = right[4 + k] + joint[GB + s] * (joint[CB + k] + flow)
    return d, first, last


def up_kernel(levels, own, other, joint, *refs):
    joints = refs[: levels - 1]
    out, diff = refs[levels : levels + 2]
    shares = refs[levels + 2 :]
    low_side = side_bit(0)
    left, right = sided(low_side, {p: own[p] for p in range(8)}, {p: other[p] for p in range(8)})
    ends = {}
    for k in range(4):
        diff[k], ends[k], ends[4 + k] = up(joint, k, left, right)
        out[k] = ends[k]
        out[4 + k] = ends[4 + k]
    for level in range(1, levels - 1):
        low_side = side_bit(level)
        joint = joints[level - 1].at[0]
        for k in range(4):
            s = KIND[k]
            first, last = ends[k], ends[4 + k]
            flow = joint[R_ + s] * jnp.where(low_side, last, -first)
            ends[k] = jnp.where(low_side, first, 0.0) - joint[GA + s] * flow
            ends[4 + k] = jnp.where(low_side, 0.0, last) + joint[GB + s] * flow
        for slot, x in enumerate(facing(level + 1, levels, ends, True)):
            shares[level - 1][slot] = x


def joint_flow(joint, k, d, into_first, into_last, low_side):
    s = KIND[k]
    flow = joint[R_ + s] * (d + joint[GA + s] * into_first - joint[GB + s] * into_last)
    first = jnp.where(low_side, into_first, joint[CB + k] + flow)
    last = jnp.where(low_side, joint[CA + k] - flow, into_last)
    return first, last


def beside_kernel(levels, *refs):
    parts, refs = list(refs[: 2 ** (levels - 1) - levels]), refs[2 ** (levels - 1) - levels :]
    consts, outs = refs[: levels - 2], refs[levels - 2 :]
    for level in range(2, levels):
        here = [parts.pop(0) for _ in range(2 ** (level - 1) - 1)]
        for p in range(outs[level - 2].shape[0]):
            total = consts[level - 2][p]
            for part in here:
                total = total + part[p]
            outs[level - 2][p] = total


def settle_kernel(levels, own, *refs):
    near, refs = refs[: levels - 1], refs[levels - 1 :]
    far, joints = refs[: levels - 2], refs[levels - 2 : 2 * levels - 3]
    pair, diff, out, send = refs[2 * levels - 3 :]
    ends = {p: own[p] for p in range(8)}
    diffs = []
    for level in range(1, levels):
        low_side = side_bit(level)
        beside = {p: near[level - 1][p] for p in range(near[level - 1].shape[0])}
        if level > 1:
            beside = {p: x + far[level - 2][p] for p, x in beside.items()}
        across = []
        if len(beside) == 4:
            for k in range(4):
                x = beside[k]
                across.append(jnp.where(low_side, ends[4 + k] - x, x - ends[k]))
        else:
            left, right = sided(low_side, ends, beside)
            for k in range(4):
                d, ends[k], ends[4 + k] = up(joints[level - 1].at[0], k, left, right)
                across.append(d)
        diffs.append(across)
    for k in range(4):
        first = last = jnp.zeros_like(diffs[0][0])
        for level in range(levels - 1, 0, -1):
            first, last = joint_flow(
                joints[level - 1].at[0], k, diffs[level - 1][k], first, last, side_bit(level)
            )
        low_side = side_bit(0)
        s = KIND[k]
        flow = pair[R_ + s] * (diff[k] + pair[GA + s] * first - pair[GB + s] * last)
        low_last, high_first = pair[CA + k] - flow, pair[CB + k] + flow
        out[k] = jnp.where(low_side, first, high_first)
        out[4 + k] = jnp.where(low_side, low_last, last)
        send[k] = jnp.where(low_side, high_first, first)
        send[4 + k] = jnp.where(low_side, last, low_last)


def final_kernel(mine, parts, flux, part, g0, gn, *refs):
    out, buf, sems = refs[-3:]
    rows, half = buf.shape[1], buf.shape[3]
    core = jnp.bitwise_and(lax.axis_index("line"), 1)
    offset = (core if mine else 1 - core) * half
    step = rows // parts
    copies = []
    for c in range(half // 128):
        near = pl.ds(c * 128, 128)
        z = pl.ds(pl.multiple_of(offset + c * 128, 128), 128)
        into = [flux[k, :, near] for k in range(8)]
        for r in range(parts):
            for i in range(r * step, (r + 1) * step):
                a = [g0[s, i, :, z] for s in range(2)]
                b = [gn[s, i, :, z] for s in range(2)]
                for k in range(4):
                    s = KIND[k]
                    buf[k, i, :, near] = part[k, i, :, z] + (a[s] * into[k] + b[s] * into[4 + k])
            x = pl.ds(r * step, step)
            copies.append(
                pltpu.make_async_copy(
                    buf.at[:, x, :, near], out.at[:, x, :, z], sems.at[c * parts + r]
                )
            )
            copies[-1].start()
    for copy in copies:
        copy.wait()


def local(fields, viscosity):
    rows, ny, nz = viscosity.shape
    lines = lax.axis_size("line")
    cols = lax.axis_size("col")
    levels = lines.bit_length() - 1
    half = nz // 2
    cells = rows * ny * nz
    block = (rows, ny, nz)

    ring = [(i, (i + 1) % cols) for i in range(cols)]
    back_ring = [(b, a) for a, b in ring]

    def gather(at_level):
        found = {}
        for d in sorted(range(1, lines // 2), key=lambda d: (-d.bit_count(), d)):
            x = at_level[d.bit_length()]
            found[d] = lax.ppermute(x, "line", [(i, i ^ (d << 1)) for i in range(lines)])
        return [found[d] for d in sorted(found)]

    def swap(x, level):
        return lax.ppermute(x, "line", [(i, i ^ (1 << level)) for i in range(lines)])

    y_first, y_last = call(
        functools.partial(cut_kernel, ny),
        "cut",
        [(5, rows, nz), (5, rows, nz)],
        [fields, viscosity],
        scratch=[pltpu.SemaphoreType.DMA((2, 2))],
        in_hbm=(0, 1),
        moved=2 * cells,
    )
    low = lax.ppermute(y_last, "col", ring)
    high = lax.ppermute(y_first, "col", back_ring)

    inv, cpr, g0, gn, w = call(
        functools.partial(factor_kernel, rows),
        "factor",
        [(2,) + block] * 4 + [(PLANES, ny, nz)],
        [fields, viscosity],
        scratch=[VMEM((2,) + block, F32), pltpu.SemaphoreType.DMA((2,))],
        in_hbm=(0,),
        flops=10**9,
    )
    count = rows // 4
    (early,) = call(
        functools.partial(early_kernel, count),
        "early",
        [(4, count, ny, nz)],
        [fields, viscosity],
        scratch=[VMEM((4, count + 1, ny, nz), F32), pltpu.SemaphoreType.DMA],
        in_hbm=(0,),
        flops=4 * 10**9,
    )
    src, p, ends = call(
        functools.partial(explicit_kernel, count),
        "explicit",
        [(4, rows - count, ny, nz), (8, ny, nz), (8, rows, nz)],
        [fields, viscosity, g0, gn, early],
        scratch=[VMEM((4, rows - count + 1, ny, nz), F32), pltpu.SemaphoreType.DMA((3,))],
        in_hbm=(0,),
        flops=5 * 10**9,
    )
    pair, w = call(
        pair_kernel,
        "pair",
        [(JOINT, ny, half), (PLANES, ny, half)],
        [w, swap(w, 0), early],
        moved=4 * ny * nz * 60,
    )
    pairs = lines // 2
    widths = [8] * (levels - 3) + [4]
    found = call(
        functools.partial(chips_kernel, levels),
        "chips",
        [(pairs >> level, JOINT, ny, half) for level in range(1, levels)]
        + [(width, ny, half) for width in widths],
        [w] + gather([w] * (levels + 1)) + [p],
        moved=4 * ny * half * 300,
    )
    joints, consts = list(found[: levels - 1]), list(found[levels - 1 :])

    add, p, sent = call(
        functools.partial(edge_kernel, rows, ny),
        "edge",
        [(8, rows, nz), (8, ny, half), (8, ny, half)],
        [y_last, y_first, low, high, ends, p, joints[0]],
        flops=5 * 10**8,
    )
    (t,) = call(
        functools.partial(source_kernel, rows, count),
        "source",
        [(4,) + block],
        [early, src, cpr, add],
        flops=30 * cells,
        moved=24 * cells,
    )
    (part,) = call(
        functools.partial(back_kernel, rows),
        "back",
        [(4,) + block],
        [t, inv, cpr],
        flops=20 * cells,
        moved=24 * cells,
    )
    p, diff, *shares = call(
        functools.partial(up_kernel, levels),
        "up",
        [(8, ny, half), (4, ny, half)] + [(width, ny, half) for width in widths],
        [p, swap(sent, 0), pair] + joints + [part],
        moved=4 * ny * nz * 40,
    )
    others = dict(enumerate(gather([None, p] + shares), 1))
    near = [others.pop(1 << level) for level in range(levels - 1)]
    beside = call(
        functools.partial(beside_kernel, levels),
        "beside",
        [(width, ny, half) for width in widths],
        list(others.values()) + consts,
        flops=6 * 10**8,
    )
    flux, sent = call(
        functools.partial(settle_kernel, levels),
        "settle",
        [(8, ny, half)] * 2,
        [p] + near + list(beside) + joints + [pair, diff],
        moved=4 * ny * half * 100,
    )
    rest = [part, g0, gn]
    parts = 4 if rows % 4 == 0 else 1
    scratch = [VMEM((4, rows, ny, half), F32), pltpu.SemaphoreType.DMA((half // 128 * parts,))]
    (out,) = call(
        functools.partial(final_kernel, True, parts),
        "final_own",
        [(4,) + block],
        [flux] + rest,
        scratch=scratch,
        out_hbm=(0,),
        flops=10**9,
    )
    (out,) = call(
        functools.partial(final_kernel, False, parts),
        "final_other",
        [(4,) + block],
        [swap(sent, 0)] + rest + [out],
        scratch=scratch,
        in_hbm=(4,),
        out_hbm=(0,),
        aliases={4: 0},
        flops=10**9,
    )
    return out


def solution(mesh):
    return jax.shard_map(
        local,
        mesh=mesh,
        in_specs=(P(None, "line", "col", None), P("line", "col", None)),
        out_specs=P(None, "line", "col", None),
        check_vma=False,
    )
```
